32 devices in a mesh: seq: 8 (over z, y), chan: 4 (over x, core).
Axes of the slice: x: 2, y: 2, z: 4, core: 2. Of those that a mesh axis runs over, the one named last changes fastest.
Arguments:
- features: bfloat16 [4096, 512], P('seq', 'chan'), may hold values from -600 to 600
- pre_gate: bfloat16 [4096, 512], P('seq', 'chan'), may hold values from -6 to 6
- post_gate: bfloat16 [4096, 512], P('seq', 'chan'), may hold values from -6 to 6
- norm_gain: float32 [512], P('chan'), may hold values from 0.1 to 1.9
- skip_weight: float32 [512], P('chan'), may hold values from -4 to 4
- spectrum: float32 [2, 16, 512, 512], P(None, 'seq', None, 'chan'), may hold values from -6 to 6
Outputs:
- gated_out: bfloat16 [4096, 512], P('seq', 'chan')
The draws below stay inside these ranges and needn't reach their ends.
All inputs are finite; a program needn't handle non-finite values.
Results may differ from the reference program's by a relative error of at most 0.007.
Values may be sent and summed in bfloat16 or wider, within the bound.
No kernel may reach another device: no remote copies, remote signals or barrier semaphores. Data moves between devices by JAX's collectives and lax.ppermute only.
A program may use at most 64 MiB of HBM per device.

```python
import math
import jax
import jax.numpy as jnp
import numpy as np
from jax import lax

TOK_DEV = 512
CHANNELS = 512
SEQLEN = 4096
BINS = 8192
STRIDE = 16
N_SEQ = 8


def draw_features(key, part):
    folded = jax.random.fold_in(key, 17)
    base_key, chan_key, token_key = jax.random.split(folded, 3)
    channel_ramp = (jnp.arange(CHANNELS, dtype=jnp.float32) + jax.random.uniform(chan_key, (CHANNELS,))) / CHANNELS
    token_scale = jnp.exp(math.log(10.0) * jax.random.uniform(token_key, (SEQLEN, 1)))
    base_draw = jnp.clip(jax.random.normal(base_key, (SEQLEN, CHANNELS)), -6.0, 6.0)
    chan_scale = jnp.exp(math.log(10.0) * channel_ramp)
    return (base_draw * token_scale * chan_scale).astype(jnp.bfloat16)


def block_scale(stream_key, shape, pieces, least, top_value):
    loudness, own = 1.0, jax.random.fold_in(stream_key, 6)
    for axis_at, shards_of in pieces:
        heights = jnp.exp(jax.random.uniform(jax.random.fold_in(own, axis_at), (shards_of,), jnp.float32, least / len(pieces), top_value / len(pieces)))
        loudness = loudness * jnp.repeat(heights, shape[axis_at] // shards_of).reshape([-1 if axis == axis_at else 1 for axis in range(len(shape))])
    return loudness


def noise(stream_key, dims, scale, bound, cuts=(), held_as=jnp.bfloat16):
    entries = jax.random.normal(stream_key, dims, jnp.float32) * scale
    if len(cuts) > 0:
        entries = block_scale(stream_key, dims, cuts, -0.22, 0.18) * entries
    return jnp.clip(entries, min=-bound, max=bound).astype(held_as)


def setup_inputs(seed: int = 0) -> dict:
    key_list = jax.random.split(jax.random.key(seed), 7)
    features = draw_features(jax.random.fold_in(key_list[6], 71), 0)
    pre_gate = noise(key_list[1], (SEQLEN, CHANNELS), 1.0, 6.0, ((0, 8), (1, 4)))
    post_gate = noise(key_list[2], (SEQLEN, CHANNELS), 1.0, 6.0, ((0, 8), (1, 4)))
    norm_gain = jnp.clip(1.0 + 0.18 * jax.random.normal(key_list[3], (CHANNELS,), jnp.float32), 0.1, 1.9)
    skip_weight = noise(key_list[4], (CHANNELS,), 1.0, 4.0, ((0, 4),), jnp.float32)
    spectrum = noise(key_list[5], (2, STRIDE, TOK_DEV, CHANNELS), 1.0, 6.0, ((1, 8), (3, 4)), jnp.float32)
    return dict(features=features, pre_gate=pre_gate, post_gate=post_gate, norm_gain=norm_gain, skip_weight=skip_weight, spectrum=spectrum)


def reversed_digits(axis_count):
    levels = axis_count.bit_length() - 1
    positions = np.arange(axis_count)
    result = np.zeros(axis_count, np.int64)
    for bit_pos in range(levels):
        result = result + ((positions >> bit_pos & 1) << levels - 1 - bit_pos)
    return result

def convolve_block(packed):
    signal_block, filter_block = packed
    padded = jnp.concatenate([signal_block, jnp.zeros_like(signal_block)], axis=0)
    forward = jnp.fft.fft(padded, axis=0)
    response = filter_block[0] + 1j * filter_block[1]
    return jnp.real(jnp.fft.ifft(forward * response, axis=0))[:SEQLEN]

def reference(features, pre_gate, post_gate, norm_gain, skip_weight, spectrum):
    widened = features.astype(jnp.float32)
    mean_square = lax.optimization_barrier(jnp.mean(widened * widened, axis=1, keepdims=True))
    scaled = widened * lax.rsqrt(mean_square + 1e-06) * norm_gain
    signal = (scaled * pre_gate.astype(jnp.float32)).astype(jnp.bfloat16)
    digit_order = reversed_digits(N_SEQ)
    stride = 2 * N_SEQ
    slots = np.arange(stride)
    low_bins = 2 * digit_order[slots // 2] + slots % 2
    bin_index = (low_bins[:, None] + stride * np.arange(TOK_DEV)[None, :]).reshape(-1)
    inverse = np.argsort(bin_index)
    natural = spectrum.reshape(2, stride * TOK_DEV, CHANNELS)[:, inverse]
    group_size = min(CHANNELS, 64)
    blocks = CHANNELS // group_size
    signal_blocks = signal.astype(jnp.float32).reshape(SEQLEN, blocks, group_size).transpose(1, 0, 2)
    filter_blocks = natural.reshape(2, BINS, blocks, group_size).transpose(2, 0, 1, 3)
    per_block = lax.map(convolve_block, (signal_blocks, filter_blocks))
    convolved = per_block.transpose(1, 0, 2).reshape(SEQLEN, CHANNELS)
    gated = post_gate.astype(jnp.float32) * (convolved + skip_weight * signal.astype(jnp.float32))
    return gated.astype(jnp.bfloat16)
```

```python
import functools
import math

import jax
import jax.numpy as jnp
import numpy as np
from jax import lax
from jax.experimental import pallas as pl
from jax.experimental.pallas import tpu as pltpu
from jax.sharding import PartitionSpec as P

EPS = 1e-06
BF16 = jnp.bfloat16
F32 = jnp.float32
VMEM_LIMIT = 48 * 1024 * 1024


def reverse_bits(index, levels):
    return sum((index >> bit & 1) << levels - 1 - bit for bit in range(levels))


@functools.lru_cache(maxsize=None)
def tables(places, rows, width):
    levels = places.bit_length() - 1
    stride = 2 * places
    bins = stride * rows
    residues = np.array([2 * reverse_bits(place, levels) + parity for place in range(places) for parity in range(2)])
    angle = 2.0 * np.pi * ((residues[:, None] * np.arange(places)[None, :]) % stride) / stride
    same = np.eye(width)
    first = np.concatenate([np.kron(np.cos(angle), same), np.kron(-np.sin(angle), same)])
    last = first.T / bins
    angle = 2.0 * np.pi * ((residues[:, None] * np.arange(rows)[None, :]) % bins) / bins
    twist = np.stack([np.repeat(np.cos(angle), width, axis=0), np.repeat(np.sin(angle), width, axis=0)])
    series = np.arange(rows)
    angle = 2.0 * np.pi * ((series[:, None] * series[None, :]) % rows) / rows
    dft = np.stack([np.cos(angle), np.sin(angle)])
    return (
        first.astype(jnp.bfloat16),
        last.astype(jnp.bfloat16),
        twist.astype(np.float32),
        dft.astype(jnp.bfloat16),
    )


def spread_matrix(places, groups, width):
    return np.repeat(np.kron(np.eye(places), np.ones((1, groups))), width, axis=0).astype(np.float32)


def prepare_kernel(features_ref, pre_ref, gain_ref, spectrum_ref, scaled_ref, squares_ref, moved_ref):
    features = features_ref[...].astype(F32)
    turned = features.T
    squares_ref[...] = jnp.sum(turned * turned, axis=0, keepdims=True)
    scaled = features * gain_ref[...] * pre_ref[...].astype(F32)
    scaled_ref[...] = scaled.T.astype(BF16)
    for part in range(2):
        for parity in range(2):
            turned = spectrum_ref[part, parity].T.astype(BF16)
            if len(moved_ref.shape) == 5:
                moved_ref[:, part, parity] = turned.reshape(moved_ref.shape[0], moved_ref.shape[3], moved_ref.shape[4])
            else:
                moved_ref[part, parity] = turned


def matmul(left, right):
    return jnp.dot(left, right, preferred_element_type=F32)


def convolve_kernel(
    channels, scaled_ref, squares_ref, spread_ref, spectrum_ref, first_ref, last_ref, twist_ref, dft_ref, out_ref
):
    total = jnp.dot(spread_ref[...], squares_ref[...], precision=lax.Precision.HIGHEST, preferred_element_type=F32)
    scale = lax.rsqrt(total / channels + EPS)
    signal = (scaled_ref[...].astype(F32) * scale).astype(BF16)
    mixed = matmul(first_ref[...], signal)
    half = mixed.shape[0] // 2
    real, imag = mixed[:half], mixed[half:]
    cos_twist, sin_twist = twist_ref[0], twist_ref[1]
    turned_real = (real * cos_twist + imag * sin_twist).astype(BF16)
    turned_imag = (imag * cos_twist - real * sin_twist).astype(BF16)
    cos_dft, sin_dft = dft_ref[0], dft_ref[1]
    real = matmul(turned_real, cos_dft) + matmul(turned_imag, sin_dft)
    imag = matmul(turned_imag, cos_dft) - matmul(turned_real, sin_dft)
    if len(spectrum_ref.shape) == 5:
        response_real = spectrum_ref[:, 0].reshape(half, -1).astype(F32)
        response_imag = spectrum_ref[:, 1].reshape(half, -1).astype(F32)
    else:
        response_real = spectrum_ref[0].astype(F32)
        response_imag = spectrum_ref[1].astype(F32)
    product_real = (real * response_real - imag * response_imag).astype(BF16)
    product_imag = (real * response_imag + imag * response_real).astype(BF16)
    real = matmul(product_real, cos_dft) - matmul(product_imag, sin_dft)
    imag = matmul(product_imag, cos_dft) + matmul(product_real, sin_dft)
    turned_real = (real * cos_twist - imag * sin_twist).astype(BF16)
    turned_imag = (imag * cos_twist + real * sin_twist).astype(BF16)
    out_ref[...] = (matmul(last_ref[:, :half], turned_real) + matmul(last_ref[:, half:], turned_imag)).astype(BF16)


def finish_kernel(channels, conv_ref, scaled_ref, squares_ref, skip_ref, post_ref, out_ref):
    total = jnp.sum(squares_ref[...], axis=0, keepdims=True)
    scale = lax.rsqrt(total / channels + EPS)
    signal = (scaled_ref[...].astype(F32) * scale).astype(BF16).astype(F32)
    turned = conv_ref[...].astype(F32) + skip_ref[...] * signal
    out_ref[...] = (post_ref[...].astype(F32) * turned.T).astype(BF16)


def call(kernel, out_shape, flops, moved, *operands):
    return pl.pallas_call(
        kernel,
        out_shape=out_shape,
        compiler_params=pltpu.CompilerParams(vmem_limit_bytes=VMEM_LIMIT),
        cost_estimate=pl.CostEstimate(flops=flops, bytes_accessed=moved, transcendentals=0),
    )(*operands)


def exchange(value):
    return lax.all_to_all(value, "seq", split_axis=0, concat_axis=0, tiled=True)


def local(features, pre_gate, post_gate, norm_gain, skip_weight, spectrum):
    rows, wide = features.shape
    places = lax.axis_size("seq")
    groups = lax.axis_size("chan")
    channels = wide * groups
    width = wide // places
    direct = width % 16 == 0
    first, last, twist, dft = tables(places, rows, width)
    spread = spread_matrix(places, groups, width)
    moved_shape = (places, 2, 2, width, rows) if direct else (2, 2, wide, rows)
    scaled, squares, moved = call(
        prepare_kernel,
        (
            jax.ShapeDtypeStruct((wide, rows), BF16),
            jax.ShapeDtypeStruct((1, rows), F32),
            jax.ShapeDtypeStruct(moved_shape, BF16),
        ),
        10 * rows * wide,
        32 * rows * wide,
        features,
        pre_gate,
        norm_gain[None, :],
        spectrum,
    )
    if not direct:
        moved = moved.reshape(2, 2, places, width, rows).transpose(2, 0, 1, 3, 4)
    all_squares = lax.all_gather(squares, ("seq", "chan"), axis=0, tiled=True)
    signal = exchange(scaled.reshape(places, width, rows)).reshape(wide, rows)
    response = exchange(moved)
    if not direct:
        response = response.transpose(1, 0, 2, 3, 4).reshape(2, 2 * wide, rows)
    conv = call(
        functools.partial(convolve_kernel, channels),
        jax.ShapeDtypeStruct((wide, rows), BF16),
        16 * (2 * wide) * rows * rows,
        40 * rows * wide,
        signal,
        all_squares,
        spread,
        response,
        first,
        last,
        twist,
        dft,
    )
    conv = exchange(conv.reshape(places, width, rows)).reshape(wide, rows)
    own_squares = lax.dynamic_slice_in_dim(all_squares, lax.axis_index("seq") * groups, groups, axis=0)
    return call(
        functools.partial(finish_kernel, channels),
        jax.ShapeDtypeStruct((rows, wide), BF16),
        10 * rows * wide,
        10 * rows * wide,
        conv,
        scaled,
        own_squares,
        skip_weight[:, None],
        post_gate,
    )


def solution(mesh):
    return jax.shard_map(
        local,
        mesh=mesh,
        in_specs=(
            P("seq", "chan"),
            P("seq", "chan"),
            P("seq", "chan"),
            P("chan"),
            P("chan"),
            P(None, "seq", None, "chan"),
        ),
        out_specs=P("seq", "chan"),
        check_vma=False,
    )
```

```python
import functools
import math

import jax
import jax.numpy as jnp
import numpy as np
from jax import lax
from jax.experimental import pallas as pl
from jax.experimental.pallas import tpu as pltpu
from jax.sharding import PartitionSpec as P

EPS = 1e-06
BF16 = jnp.bfloat16
F32 = jnp.float32
VMEM_LIMIT = 48 * 1024 * 1024


def reverse_bits(index, levels):
    return sum((index >> bit & 1) << levels - 1 - bit for bit in range(levels))


@functools.lru_cache(maxsize=None)
def tables(places, rows, width):
    levels = places.bit_length() - 1
    stride = 2 * places
    bins = stride * rows
    residues = np.array([2 * reverse_bits(place, levels) + parity for place in range(places) for parity in range(2)])
    angle = 2.0 * np.pi * ((residues[:, None] * np.arange(places)[None, :]) % stride) / stride
    same = np.eye(width)
    first = np.concatenate([np.kron(np.cos(angle), same), np.kron(-np.sin(angle), same)])
    last = first.T / bins
    angle = 2.0 * np.pi * ((residues[:, None] * np.arange(rows)[None, :]) % bins) / bins
    twist = np.stack([np.repeat(np.cos(angle), width, axis=0), np.repeat(np.sin(angle), width, axis=0)])
    series = np.arange(rows)
    angle = 2.0 * np.pi * ((series[:, None] * series[None, :]) % rows) / rows
    dft = np.stack([np.cos(angle), np.sin(angle)])
    return (
        first.astype(jnp.bfloat16),
        last.astype(jnp.bfloat16),
        twist.astype(np.float32),
        dft.astype(jnp.bfloat16),
    )


def prepare_kernel(features_ref, spectrum_ref, squares_ref, moved_ref, features_in, spectrum_in, sems):
    blocks = [(part, parity) for part in range(2) for parity in range(2)]
    copies = [pltpu.make_async_copy(features_ref, features_in, sems.at[4])]
    for slot, block in enumerate(blocks):
        copies.append(pltpu.make_async_copy(spectrum_ref.at[block], spectrum_in.at[block], sems.at[slot]))
    for copy in copies:
        copy.start()
    copies[0].wait()
    turned = features_in[...].astype(F32).T
    squares_ref[...] = jnp.sum(turned * turned, axis=0, keepdims=True)
    for slot, (part, parity) in enumerate(blocks):
        copies[1 + slot].wait()
        turned = spectrum_in[part, parity].T.astype(BF16)
        if len(moved_ref.shape) == 5:
            moved_ref[:, part, parity] = turned.reshape(moved_ref.shape[0], moved_ref.shape[3], moved_ref.shape[4])
        else:
            moved_ref[part, parity] = turned


def signal_kernel(channels, features_ref, pre_ref, gain_ref, squares_ref, signal_ref):
    total = jnp.sum(squares_ref[...], axis=0, keepdims=True)
    scale = lax.rsqrt(total / channels + EPS)
    scaled = features_ref[...].astype(F32) * gain_ref[...] * pre_ref[...].astype(F32)
    signal_ref[...] = (scaled.T * scale).astype(BF16)


def matmul(left, right):
    return jnp.dot(left, right, preferred_element_type=F32)


def convolve_kernel(signal_ref, spectrum_ref, first_ref, last_ref, twist_ref, dft_ref, out_ref):
    signal = signal_ref[...]
    mixed = matmul(first_ref[...], signal)
    half = mixed.shape[0] // 2
    real, imag = mixed[:half], mixed[half:]
    cos_twist, sin_twist = twist_ref[0], twist_ref[1]
    turned_real = (real * cos_twist + imag * sin_twist).astype(BF16)
    turned_imag = (imag * cos_twist - real * sin_twist).astype(BF16)
    cos_dft, sin_dft = dft_ref[0], dft_ref[1]
    real = matmul(turned_real, cos_dft) + matmul(turned_imag, sin_dft)
    imag = matmul(turned_imag, cos_dft) - matmul(turned_real, sin_dft)
    if len(spectrum_ref.shape) == 5:
        response_real = spectrum_ref[:, 0].reshape(half, -1).astype(F32)
        response_imag = spectrum_ref[:, 1].reshape(half, -1).astype(F32)
    else:
        response_real = spectrum_ref[0].astype(F32)
        response_imag = spectrum_ref[1].astype(F32)
    product_real = (real * response_real - imag * response_imag).astype(BF16)
    product_imag = (real * response_imag + imag * response_real).astype(BF16)
    real = matmul(product_real, cos_dft) - matmul(product_imag, sin_dft)
    imag = matmul(product_imag, cos_dft) + matmul(product_real, sin_dft)
    turned_real = (real * cos_twist - imag * sin_twist).astype(BF16)
    turned_imag = (imag * cos_twist + real * sin_twist).astype(BF16)
    out_ref[...] = (matmul(last_ref[:, :half], turned_real) + matmul(last_ref[:, half:], turned_imag)).astype(BF16)


def finish_kernel(conv_ref, signal_ref, skip_ref, post_ref, out_ref):
    turned = conv_ref[...].astype(F32) + skip_ref[...] * signal_ref[...].astype(F32)
    out_ref[...] = (post_ref[...].astype(F32) * turned.T).astype(BF16)


def call(kernel, out_shape, flops, moved, *operands, **options):
    return pl.pallas_call(
        kernel,
        out_shape=out_shape,
        compiler_params=pltpu.CompilerParams(vmem_limit_bytes=VMEM_LIMIT),
        cost_estimate=pl.CostEstimate(flops=flops, bytes_accessed=moved, transcendentals=0),
        **options,
    )(*operands)


def exchange(value):
    return lax.all_to_all(value, "seq", split_axis=0, concat_axis=0, tiled=True)


def local(features, pre_gate, post_gate, norm_gain, skip_weight, spectrum):
    rows, wide = features.shape
    places = lax.axis_size("seq")
    groups = lax.axis_size("chan")
    channels = wide * groups
    width = wide // places
    direct = width % 16 == 0
    first, last, twist, dft = tables(places, rows, width)
    moved_shape = (places, 2, 2, width, rows) if direct else (2, 2, wide, rows)
    squares, moved = call(
        prepare_kernel,
        (
            jax.ShapeDtypeStruct((1, rows), F32),
            jax.ShapeDtypeStruct(moved_shape, BF16),
        ),
        10 * rows * wide,
        26 * rows * wide,
        features,
        spectrum,
        in_specs=[pl.BlockSpec(memory_space=pl.ANY)] * 2,
        scratch_shapes=[
            pltpu.VMEM(features.shape, BF16),
            pltpu.VMEM(spectrum.shape, F32),
            pltpu.SemaphoreType.DMA((5,)),
        ],
    )
    if not direct:
        moved = moved.reshape(2, 2, places, width, rows).transpose(2, 0, 1, 3, 4)
    response = exchange(moved)
    group_squares = lax.all_gather(squares, "chan", axis=0, tiled=True)
    signal = call(
        functools.partial(signal_kernel, channels),
        jax.ShapeDtypeStruct((wide, rows), BF16),
        10 * rows * wide,
        6 * rows * wide,
        features,
        pre_gate,
        norm_gain[None, :],
        group_squares,
    )
    gathered = exchange(signal.reshape(places, width, rows)).reshape(wide, rows)
    if not direct:
        response = response.transpose(1, 0, 2, 3, 4).reshape(2, 2 * wide, rows)
    conv = call(
        convolve_kernel,
        jax.ShapeDtypeStruct((wide, rows), BF16),
        16 * (2 * wide) * rows * rows,
        40 * rows * wide,
        gathered,
        response,
        first,
        last,
        twist,
        dft,
    )
    conv = exchange(conv.reshape(places, width, rows)).reshape(wide, rows)
    return call(
        finish_kernel,
        jax.ShapeDtypeStruct((rows, wide), BF16),
        10 * rows * wide,
        10 * rows * wide,
        conv,
        signal,
        skip_weight[:, None],
        post_gate,
    )


def solution(mesh):
    return jax.shard_map(
        local,
        mesh=mesh,
        in_specs=(
            P("seq", "chan"),
            P("seq", "chan"),
            P("seq", "chan"),
            P("chan"),
            P("chan"),
            P(None, "seq", None, "chan"),
        ),
        out_specs=P("seq", "chan"),
        check_vma=False,
    )
```

```python
import functools
import math

import jax
import jax.numpy as jnp
import numpy as np
from jax import lax
from jax.experimental import pallas as pl
from jax.experimental.pallas import tpu as pltpu
from jax.sharding import PartitionSpec as P

EPS = 1e-06
BF16 = jnp.bfloat16
F32 = jnp.float32
VMEM_LIMIT = 48 * 1024 * 1024


def reverse_bits(index, levels):
    return sum((index >> bit & 1) << levels - 1 - bit for bit in range(levels))


@functools.lru_cache(maxsize=None)
def tables(places, rows, width):
    levels = places.bit_length() - 1
    stride = 2 * places
    bins = stride * rows
    residues = np.array([2 * reverse_bits(place, levels) + parity for place in range(places) for parity in range(2)])
    angle = 2.0 * np.pi * ((residues[:, None] * np.arange(places)[None, :]) % stride) / stride
    same = np.eye(width)
    first = np.concatenate([np.kron(np.cos(angle), same), np.kron(-np.sin(angle), same)])
    last = first.T / bins
    angle = 2.0 * np.pi * ((residues[:, None] * np.arange(rows)[None, :]) % bins) / bins
    twist = np.stack([np.repeat(np.cos(angle), width, axis=0), np.repeat(np.sin(angle), width, axis=0)])
    series = np.arange(rows)
    angle = 2.0 * np.pi * ((series[:, None] * series[None, :]) % rows) / rows
    dft = np.stack([np.cos(angle), np.sin(angle)])
    return (
        first.astype(jnp.bfloat16),
        last.astype(jnp.bfloat16),
        twist.astype(np.float32),
        dft.astype(jnp.bfloat16),
    )


def prepare_kernel(
    features_ref, pre_ref, gain_ref, spectrum_ref, squares_ref, scaled_ref, packed_ref, features_in, spectrum_in, sems
):
    blocks = [(part, parity) for part in range(2) for parity in range(2)]
    copies = [pltpu.make_async_copy(features_ref, features_in, sems.at[4])]
    for slot, block in enumerate(blocks):
        copies.append(pltpu.make_async_copy(spectrum_ref.at[block], spectrum_in.at[block], sems.at[slot]))
    for copy in copies:
        copy.start()

    def put(slot, turned):
        if len(packed_ref.shape) == 4:
            packed_ref[:, slot] = turned.reshape(packed_ref.shape[0], packed_ref.shape[2], packed_ref.shape[3])
        else:
            packed_ref[slot] = turned

    copies[0].wait()
    features = features_in[...].astype(F32)
    turned = features.T
    squares_ref[...] = jnp.sum(turned * turned, axis=0, keepdims=True)
    scaled = (features * gain_ref[...] * pre_ref[...].astype(F32)).T.astype(BF16)
    scaled_ref[...] = scaled
    put(4, scaled)
    for slot, block in enumerate(blocks):
        copies[1 + slot].wait()
        put(slot, spectrum_in[block].T.astype(BF16))


def scale_kernel(channels, squares_ref, scaled_ref, scale_ref, signal_ref):
    scale = lax.rsqrt(jnp.sum(squares_ref[...], axis=0, keepdims=True) / channels + EPS)
    scale_ref[...] = scale
    signal_ref[...] = (scaled_ref[...].astype(F32) * scale).astype(BF16)


def matmul(left, right):
    return jnp.dot(left, right, preferred_element_type=F32)


def convolve_kernel(packed_ref, scale_ref, first_ref, last_ref, twist_ref, dft_ref, out_ref):
    if len(packed_ref.shape) == 4:
        flat = (out_ref.shape[0], out_ref.shape[1])
        signal = (packed_ref[:, 4].astype(F32) * scale_ref[...][:, None, :]).astype(BF16).reshape(flat)
    else:
        signal = (packed_ref[4].astype(F32) * scale_ref[...]).astype(BF16)
    mixed = matmul(first_ref[...], signal)
    half = mixed.shape[0] // 2
    real, imag = mixed[:half], mixed[half:]
    cos_twist, sin_twist = twist_ref[0], twist_ref[1]
    turned_real = (real * cos_twist + imag * sin_twist).astype(BF16)
    turned_imag = (imag * cos_twist - real * sin_twist).astype(BF16)
    cos_dft, sin_dft = dft_ref[0], dft_ref[1]
    real = matmul(turned_real, cos_dft) + matmul(turned_imag, sin_dft)
    imag = matmul(turned_imag, cos_dft) - matmul(turned_real, sin_dft)
    if len(packed_ref.shape) == 4:
        response_real = packed_ref[:, 0:2].reshape(half, -1).astype(F32)
        response_imag = packed_ref[:, 2:4].reshape(half, -1).astype(F32)
    else:
        response_real = packed_ref[0:2].reshape(half, -1).astype(F32)
        response_imag = packed_ref[2:4].reshape(half, -1).astype(F32)
    product_real = (real * response_real - imag * response_imag).astype(BF16)
    product_imag = (real * response_imag + imag * response_real).astype(BF16)
    real = matmul(product_real, cos_dft) - matmul(product_imag, sin_dft)
    imag = matmul(product_imag, cos_dft) + matmul(product_real, sin_dft)
    turned_real = (real * cos_twist - imag * sin_twist).astype(BF16)
    turned_imag = (imag * cos_twist + real * sin_twist).astype(BF16)
    out_ref[...] = (matmul(last_ref[:, :half], turned_real) + matmul(last_ref[:, half:], turned_imag)).astype(BF16)


def finish_kernel(conv_ref, signal_ref, skip_ref, post_ref, out_ref):
    turned = conv_ref[...].astype(F32) + skip_ref[...] * signal_ref[...].astype(F32)
    out_ref[...] = (post_ref[...].astype(F32) * turned.T).astype(BF16)


def call(kernel, out_shape, flops, moved, *operands, **options):
    return pl.pallas_call(
        kernel,
        out_shape=out_shape,
        compiler_params=pltpu.CompilerParams(vmem_limit_bytes=VMEM_LIMIT),
        cost_estimate=pl.CostEstimate(flops=flops, bytes_accessed=moved, transcendentals=0),
        **options,
    )(*operands)


def exchange(value):
    return lax.all_to_all(value, "seq", split_axis=0, concat_axis=0, tiled=True)


def local(features, pre_gate, post_gate, norm_gain, skip_weight, spectrum):
    rows, wide = features.shape
    places = lax.axis_size("seq")
    groups = lax.axis_size("chan")
    channels = wide * groups
    width = wide // places
    direct = width % 16 == 0
    first, last, twist, dft = tables(places, rows, width)
    packed_shape = (places, 5, width, rows) if direct else (5, wide, rows)
    squares, scaled, packed = call(
        prepare_kernel,
        (
            jax.ShapeDtypeStruct((1, rows), F32),
            jax.ShapeDtypeStruct((wide, rows), BF16),
            jax.ShapeDtypeStruct(packed_shape, BF16),
        ),
        10 * rows * wide,
        32 * rows * wide,
        features,
        pre_gate,
        norm_gain[None, :],
        spectrum,
        in_specs=[
            pl.BlockSpec(memory_space=pltpu.HBM),
            pl.BlockSpec(memory_space=pltpu.VMEM),
            pl.BlockSpec(memory_space=pltpu.VMEM),
            pl.BlockSpec(memory_space=pltpu.HBM),
        ],
        scratch_shapes=[
            pltpu.VMEM(features.shape, BF16),
            pltpu.VMEM(spectrum.shape, F32),
            pltpu.SemaphoreType.DMA((5,)),
        ],
    )
    if not direct:
        packed = packed.reshape(5, places, width, rows).transpose(1, 0, 2, 3)
    gathered = exchange(packed)
    group_squares = lax.all_gather(squares, "chan", axis=0, tiled=True)
    scale, signal = call(
        functools.partial(scale_kernel, channels),
        (jax.ShapeDtypeStruct((1, rows), F32), jax.ShapeDtypeStruct((wide, rows), BF16)),
        10 * rows * wide,
        6 * rows * wide,
        group_squares,
        scaled,
    )
    scales = lax.all_gather(scale, "seq", axis=0, tiled=True)
    if not direct:
        scales = jnp.repeat(scales, width, axis=0)
        response = gathered[:, :4].reshape(places, 2, 2, width, rows).transpose(1, 0, 2, 3, 4)
        gathered = jnp.concatenate([response.reshape(4, wide, rows), gathered[:, 4].reshape(1, wide, rows)])
    conv = call(
        convolve_kernel,
        jax.ShapeDtypeStruct((wide, rows), BF16),
        16 * (2 * wide) * rows * rows,
        40 * rows * wide,
        gathered,
        scales,
        first,
        last,
        twist,
        dft,
    )
    conv = exchange(conv.reshape(places, width, rows)).reshape(wide, rows)
    return call(
        finish_kernel,
        jax.ShapeDtypeStruct((rows, wide), BF16),
        10 * rows * wide,
        10 * rows * wide,
        conv,
        signal,
        skip_weight[:, None],
        post_gate,
    )


def solution(mesh):
    return jax.shard_map(
        local,
        mesh=mesh,
        in_specs=(
            P("seq", "chan"),
            P("seq", "chan"),
            P("seq", "chan"),
            P("chan"),
            P("chan"),
            P(None, "seq", None, "chan"),
        ),
        out_specs=P("seq", "chan"),
        check_vma=False,
    )
```

```python
import functools
import math

import jax
import jax.numpy as jnp
import numpy as np
from jax import lax
from jax.experimental import pallas as pl
from jax.experimental.pallas import tpu as pltpu
from jax.sharding import PartitionSpec as P

EPS = 1e-06
BF16 = jnp.bfloat16
F32 = jnp.float32
VMEM_LIMIT = 48 * 1024 * 1024


def reverse_bits(index, levels):
    return sum((index >> bit & 1) << levels - 1 - bit for bit in range(levels))


@functools.lru_cache(maxsize=None)
def tables(places, rows, width):
    levels = places.bit_length() - 1
    stride = 2 * places
    bins = stride * rows
    residues = np.array([2 * reverse_bits(place, levels) + parity for place in range(places) for parity in range(2)])
    angle = 2.0 * np.pi * ((residues[:, None] * np.arange(places)[None, :]) % stride) / stride
    same = np.eye(width)
    first = np.concatenate([np.kron(np.cos(angle), same), np.kron(-np.sin(angle), same)])
    last = first.T / bins
    angle = 2.0 * np.pi * ((residues[:, None] * np.arange(rows)[None, :]) % bins) / bins
    twist = np.stack([np.repeat(np.cos(angle), width, axis=0), np.repeat(np.sin(angle), width, axis=0)])
    series = np.arange(rows)
    angle = 2.0 * np.pi * ((series[:, None] * series[None, :]) % rows) / rows
    dft = np.stack([np.cos(angle), np.sin(angle)])
    return (
        first.astype(jnp.bfloat16),
        last.astype(jnp.bfloat16),
        twist.astype(np.float32),
        dft.astype(jnp.bfloat16),
    )


def prepare_kernel(features_ref, spectrum_ref, squares_ref, moved_ref, features_in, spectrum_in, sems):
    blocks = [(part, parity) for part in range(2) for parity in range(2)]
    copies = [pltpu.make_async_copy(features_ref, features_in, sems.at[4])]
    for slot, block in enumerate(blocks):
        copies.append(pltpu.make_async_copy(spectrum_ref.at[block], spectrum_in.at[block], sems.at[slot]))
    for copy in copies:
        copy.start()
    copies[0].wait()
    turned = features_in[...].astype(F32).T
    squares_ref[...] = jnp.sum(turned * turned, axis=0, keepdims=True)
    for slot, (part, parity) in enumerate(blocks):
        copies[1 + slot].wait()
        turned = spectrum_in[part, parity].T.astype(BF16)
        if len(moved_ref.shape) == 5:
            moved_ref[:, part, parity] = turned.reshape(moved_ref.shape[0], moved_ref.shape[3], moved_ref.shape[4])
        else:
            moved_ref[part, parity] = turned


def signal_kernel(channels, features_ref, pre_ref, gain_ref, squares_ref, signal_ref, *part_refs):
    total = jnp.sum(squares_ref[...], axis=0, keepdims=True)
    scale = lax.rsqrt(total / channels + EPS)
    scaled = features_ref[...].astype(F32) * gain_ref[...] * pre_ref[...].astype(F32)
    signal_ref[...] = (scaled.T * scale).astype(BF16)
    place = lax.axis_index("seq")
    for apart, part_ref in enumerate(part_refs, 1):
        width = part_ref.shape[0]
        part_ref[...] = signal_ref[pl.ds(pl.multiple_of((place ^ apart) * width, width), width), :]


def matmul(left, right):
    return jnp.dot(left, right, preferred_element_type=F32)


def convolve_kernel(signal_ref, spectrum_ref, first_ref, last_ref, twist_ref, dft_ref, *refs):
    part_refs, out_ref = refs[:-2], refs[-2]
    if part_refs:
        joined = refs[-1]
        place = lax.axis_index("seq")
        width = part_refs[0].shape[0]
        own = pl.ds(pl.multiple_of(place * width, width), width)
        joined[own, :] = signal_ref[own, :]
        for apart, part_ref in enumerate(part_refs, 1):
            joined[pl.ds(pl.multiple_of((place ^ apart) * width, width), width), :] = part_ref[...]
        signal = joined[...]
    else:
        signal = signal_ref[...]
    mixed = matmul(first_ref[...], signal)
    half = mixed.shape[0] // 2
    real, imag = mixed[:half], mixed[half:]
    cos_twist, sin_twist = twist_ref[0], twist_ref[1]
    turned_real = (real * cos_twist + imag * sin_twist).astype(BF16)
    turned_imag = (imag * cos_twist - real * sin_twist).astype(BF16)
    cos_dft, sin_dft = dft_ref[0], dft_ref[1]
    real = matmul(turned_real, cos_dft) + matmul(turned_imag, sin_dft)
    imag = matmul(turned_imag, cos_dft) - matmul(turned_real, sin_dft)
    if len(spectrum_ref.shape) == 5:
        response_real = spectrum_ref[:, 0].reshape(half, -1).astype(F32)
        response_imag = spectrum_ref[:, 1].reshape(half, -1).astype(F32)
    else:
        response_real = spectrum_ref[0].astype(F32)
        response_imag = spectrum_ref[1].astype(F32)
    product_real = (real * response_real - imag * response_imag).astype(BF16)
    product_imag = (real * response_imag + imag * response_real).astype(BF16)
    real = matmul(product_real, cos_dft) - matmul(product_imag, sin_dft)
    imag = matmul(product_imag, cos_dft) + matmul(product_real, sin_dft)
    turned_real = (real * cos_twist - imag * sin_twist).astype(BF16)
    turned_imag = (imag * cos_twist + real * sin_twist).astype(BF16)
    out_ref[...] = (matmul(last_ref[:, :half], turned_real) + matmul(last_ref[:, half:], turned_imag)).astype(BF16)


def finish_kernel(conv_ref, signal_ref, skip_ref, post_ref, out_ref):
    turned = conv_ref[...].astype(F32) + skip_ref[...] * signal_ref[...].astype(F32)
    out_ref[...] = (post_ref[...].astype(F32) * turned.T).astype(BF16)


def call(kernel, out_shape, flops, moved, *operands, **options):
    return pl.pallas_call(
        kernel,
        out_shape=out_shape,
        compiler_params=pltpu.CompilerParams(vmem_limit_bytes=VMEM_LIMIT),
        cost_estimate=pl.CostEstimate(flops=flops, bytes_accessed=moved, transcendentals=0),
        **options,
    )(*operands)


def exchange(value):
    return lax.all_to_all(value, "seq", split_axis=0, concat_axis=0, tiled=True)


def swap(value, apart):
    return lax.ppermute(value, "seq", [(place, place ^ apart) for place in range(lax.axis_size("seq"))])


def local(features, pre_gate, post_gate, norm_gain, skip_weight, spectrum):
    rows, wide = features.shape
    places = lax.axis_size("seq")
    groups = lax.axis_size("chan")
    channels = wide * groups
    width = wide // places
    direct = width % 16 == 0
    first, last, twist, dft = tables(places, rows, width)
    moved_shape = (places, 2, 2, width, rows) if direct else (2, 2, wide, rows)
    squares, moved = call(
        prepare_kernel,
        (
            jax.ShapeDtypeStruct((1, rows), F32),
            jax.ShapeDtypeStruct(moved_shape, BF16),
        ),
        10 * rows * wide,
        26 * rows * wide,
        features,
        spectrum,
        in_specs=[pl.BlockSpec(memory_space=pl.ANY)] * 2,
        scratch_shapes=[
            pltpu.VMEM(features.shape, BF16),
            pltpu.VMEM(spectrum.shape, F32),
            pltpu.SemaphoreType.DMA((5,)),
        ],
    )
    if not direct:
        moved = moved.reshape(2, 2, places, width, rows).transpose(2, 0, 1, 3, 4)
    response = exchange(moved)
    group_squares = lax.all_gather(squares, "chan", axis=0, tiled=True)
    apart = range(1, places if direct else 1)
    signal, *parts = call(
        functools.partial(signal_kernel, channels),
        [jax.ShapeDtypeStruct((wide, rows), BF16)] + [jax.ShapeDtypeStruct((width, rows), BF16) for _ in apart],
        10 * rows * wide,
        6 * rows * wide,
        features,
        pre_gate,
        norm_gain[None, :],
        group_squares,
    )
    parts = [swap(part, step) for step, part in zip(apart, parts)]
    gathered = signal
    if not direct:
        gathered = exchange(signal.reshape(places, width, rows)).reshape(wide, rows)
        response = response.transpose(1, 0, 2, 3, 4).reshape(2, 2 * wide, rows)
    conv = call(
        convolve_kernel,
        jax.ShapeDtypeStruct((wide, rows), BF16),
        16 * (2 * wide) * rows * rows,
        40 * rows * wide,
        gathered,
        response,
        first,
        last,
        twist,
        dft,
        *parts,
        scratch_shapes=[pltpu.VMEM((wide, rows), BF16)],
    )
    conv = exchange(conv.reshape(places, width, rows)).reshape(wide, rows)
    return call(
        finish_kernel,
        jax.ShapeDtypeStruct((rows, wide), BF16),
        10 * rows * wide,
        10 * rows * wide,
        conv,
        signal,
        skip_weight[:, None],
        post_gate,
    )


def solution(mesh):
    return jax.shard_map(
        local,
        mesh=mesh,
        in_specs=(
            P("seq", "chan"),
            P("seq", "chan"),
            P("seq", "chan"),
            P("chan"),
            P("chan"),
            P(None, "seq", None, "chan"),
        ),
        out_specs=P("seq", "chan"),
        check_vma=False,
    )
```

```python
import functools
import math

import jax
import jax.numpy as jnp
import numpy as np
from jax import lax
from jax.experimental import pallas as pl
from jax.experimental.pallas import tpu as pltpu
from jax.sharding import PartitionSpec as P

EPS = 1e-06
BF16 = jnp.bfloat16
F32 = jnp.float32
VMEM_LIMIT = 48 * 1024 * 1024


def reverse_bits(index, levels):
    return sum((index >> bit & 1) << levels - 1 - bit for bit in range(levels))


@functools.lru_cache(maxsize=None)
def tables(places, rows, width):
    levels = places.bit_length() - 1
    stride = 2 * places
    bins = stride * rows
    residues = np.array([2 * reverse_bits(place, levels) + parity for place in range(places) for parity in range(2)])
    angle = 2.0 * np.pi * ((residues[:, None] * np.arange(places)[None, :]) % stride) / stride
    same = np.eye(width)
    first = np.concatenate([np.kron(np.cos(angle), same), np.kron(-np.sin(angle), same)])
    last = first.T / bins
    angle = 2.0 * np.pi * ((residues[:, None] * np.arange(rows)[None, :]) % bins) / bins
    twist = np.stack([np.cos(angle), np.sin(angle)])
    series = np.arange(rows)
    angle = 2.0 * np.pi * ((series[:, None] * series[None, :]) % rows) / rows
    dft = np.stack([np.cos(angle), np.sin(angle)])
    return (
        first.astype(jnp.bfloat16),
        last.astype(jnp.bfloat16),
        twist.astype(np.float32),
        dft.astype(jnp.bfloat16),
    )


def squares_kernel(features_ref, squares_ref):
    turned = features_ref[...].astype(F32).T
    squares_ref[...] = jnp.sum(turned * turned, axis=0, keepdims=True)


def turn_kernel(spectrum_ref, packed_ref):
    for part in range(2):
        for parity in range(2):
            turned = spectrum_ref[part, parity].T.astype(BF16)
            if len(packed_ref.shape) == 4:
                shape = (packed_ref.shape[0], packed_ref.shape[2], packed_ref.shape[3])
                packed_ref[:, 2 * part + parity] = turned.reshape(shape)
            else:
                packed_ref[2 * part + parity] = turned


def signal_kernel(channels, groups, features_ref, pre_ref, gain_ref, packed_ref, *refs):
    square_refs, (out_ref, signal_ref, ready, sem) = refs[:groups], refs[groups:]
    del packed_ref
    total = square_refs[0][...]
    for square_ref in square_refs[1:]:
        total = total + square_ref[...]
    scale = lax.rsqrt(total / channels + EPS)
    scaled = features_ref[...].astype(F32) * gain_ref[...] * pre_ref[...].astype(F32)
    signal = (scaled.T * scale).astype(BF16)
    signal_ref[...] = signal
    ready[...] = signal.reshape(ready.shape)
    target = out_ref.at[:, 4] if len(out_ref.shape) == 4 else out_ref.at[4]
    copy = pltpu.make_async_copy(ready, target, sem)
    copy.start()
    copy.wait()


def matmul(left, right):
    return jnp.dot(left, right, preferred_element_type=F32)


def twisted(value, factor):
    parts = factor.shape[0]
    if value.shape[0] == parts:
        return value * factor
    return (value.reshape(parts, -1, value.shape[1]) * factor[:, None, :]).reshape(value.shape)


def convolve_kernel(packed_ref, first_ref, last_ref, twist_ref, dft_ref, out_ref):
    half = first_ref.shape[0] // 2
    if len(packed_ref.shape) == 4:
        signal = packed_ref[:, 4].reshape(out_ref.shape)
        response_real = packed_ref[:, 0:2].reshape(half, -1).astype(F32)
        response_imag = packed_ref[:, 2:4].reshape(half, -1).astype(F32)
    else:
        signal = packed_ref[4]
        response_real = packed_ref[0:2].reshape(half, -1).astype(F32)
        response_imag = packed_ref[2:4].reshape(half, -1).astype(F32)
    mixed = matmul(first_ref[...], signal)
    real, imag = mixed[:half], mixed[half:]
    cos_twist, sin_twist = twist_ref[0], twist_ref[1]
    turned_real = (twisted(real, cos_twist) + twisted(imag, sin_twist)).astype(BF16)
    turned_imag = (twisted(imag, cos_twist) - twisted(real, sin_twist)).astype(BF16)
    cos_dft, sin_dft = dft_ref[0], dft_ref[1]
    real = matmul(turned_real, cos_dft) + matmul(turned_imag, sin_dft)
    imag = matmul(turned_imag, cos_dft) - matmul(turned_real, sin_dft)
    product_real = (real * response_real - imag * response_imag).astype(BF16)
    product_imag = (real * response_imag + imag * response_real).astype(BF16)
    real = matmul(product_real, cos_dft) - matmul(product_imag, sin_dft)
    imag = matmul(product_imag, cos_dft) + matmul(product_real, sin_dft)
    turned_real = (twisted(real, cos_twist) - twisted(imag, sin_twist)).astype(BF16)
    turned_imag = (twisted(imag, cos_twist) + twisted(real, sin_twist)).astype(BF16)
    out_ref[...] = (matmul(last_ref[:, :half], turned_real) + matmul(last_ref[:, half:], turned_imag)).astype(BF16)


def finish_kernel(conv_ref, signal_ref, skip_ref, post_ref, out_ref):
    turned = conv_ref[...].astype(F32) + skip_ref[...] * signal_ref[...].astype(F32)
    out_ref[...] = (post_ref[...].astype(F32) * turned.T).astype(BF16)


def call(kernel, out_shape, flops, moved, *operands, **options):
    return pl.pallas_call(
        kernel,
        out_shape=out_shape,
        compiler_params=pltpu.CompilerParams(vmem_limit_bytes=VMEM_LIMIT),
        cost_estimate=pl.CostEstimate(flops=flops, bytes_accessed=moved, transcendentals=0),
        **options,
    )(*operands)


def exchange(value):
    return lax.all_to_all(value, "seq", split_axis=0, concat_axis=0, tiled=True)


def swap(value, axis, apart):
    return lax.ppermute(value, axis, [(place, place ^ apart) for place in range(lax.axis_size(axis))])


def local(features, pre_gate, post_gate, norm_gain, skip_weight, spectrum):
    rows, wide = features.shape
    places = lax.axis_size("seq")
    groups = lax.axis_size("chan")
    channels = wide * groups
    width = wide // places
    direct = width % 16 == 0
    first, last, twist, dft = tables(places, rows, width)
    if not direct:
        twist = np.repeat(twist, width, axis=1)
    cells = rows * wide
    squares = call(squares_kernel, jax.ShapeDtypeStruct((1, rows), F32), 4 * cells, 2 * cells, features)
    others = [swap(squares, "chan", apart) for apart in range(1, groups)]
    packed_shape = (places, 5, width, rows) if direct else (5, wide, rows)
    packed = call(turn_kernel, jax.ShapeDtypeStruct(packed_shape, BF16), 4 * cells, 24 * cells, spectrum)
    vmem, anywhere = pl.BlockSpec(memory_space=pltpu.VMEM), pl.BlockSpec(memory_space=pl.ANY)
    packed, signal = call(
        functools.partial(signal_kernel, channels, groups),
        (jax.ShapeDtypeStruct(packed_shape, BF16), jax.ShapeDtypeStruct((wide, rows), BF16)),
        10 * cells,
        8 * cells,
        features,
        pre_gate,
        norm_gain[None, :],
        packed,
        squares,
        *others,
        in_specs=[vmem] * 3 + [anywhere] + [vmem] * groups,
        out_specs=(anywhere, vmem),
        scratch_shapes=[
            pltpu.VMEM((places, width, rows) if direct else (wide, rows), BF16),
            pltpu.SemaphoreType.DMA(()),
        ],
        input_output_aliases={3: 0},
    )
    if not direct:
        packed = packed.reshape(5, places, width, rows).transpose(1, 0, 2, 3)
    gathered = exchange(packed)
    if not direct:
        response = gathered[:, :4].reshape(places, 2, 2, width, rows).transpose(1, 0, 2, 3, 4)
        gathered = jnp.concatenate([response.reshape(4, wide, rows), gathered[:, 4].reshape(1, wide, rows)])
    conv = call(
        convolve_kernel,
        jax.ShapeDtypeStruct((wide, rows), BF16),
        32 * cells * rows,
        20 * cells,
        gathered,
        first,
        last,
        twist,
        dft,
    )
    conv = exchange(conv.reshape(places, width, rows)).reshape(wide, rows)
    return call(
        finish_kernel,
        jax.ShapeDtypeStruct((rows, wide), BF16),
        10 * cells,
        8 * cells,
        conv,
        signal,
        skip_weight[:, None],
        post_gate,
    )


def solution(mesh):
    return jax.shard_map(
        local,
        mesh=mesh,
        in_specs=(
            P("seq", "chan"),
            P("seq", "chan"),
            P("seq", "chan"),
            P("chan"),
            P("chan"),
            P(None, "seq", None, "chan"),
        ),
        out_specs=P("seq", "chan"),
        check_vma=False,
    )
```

```python
import functools
import math

import jax
import jax.numpy as jnp
import numpy as np
from jax import lax
from jax.experimental import pallas as pl
from jax.experimental.pallas import tpu as pltpu
from jax.sharding import PartitionSpec as P

EPS = 1e-06
BF16 = jnp.bfloat16
F32 = jnp.float32
VMEM_LIMIT = 48 * 1024 * 1024
GROUP = 4
TURNS = (0, 2, 1, 3)


def reverse_bits(index, levels):
    return sum((index >> bit & 1) << levels - 1 - bit for bit in range(levels))


@functools.lru_cache(maxsize=None)
def tables(places, rows):
    halves = places // GROUP
    levels = halves.bit_length() - 1
    stride = 2 * places
    bins = stride * rows
    rest = np.array([[2 * reverse_bits(half, levels) + parity for parity in range(2)] for half in range(halves)])
    angle = 2.0 * np.pi * ((rest[:, :, None] * np.arange(places)) % stride) / stride
    factor = np.stack([np.cos(angle), np.sin(angle), np.cos(angle) / bins, np.sin(angle) / bins], axis=-1)
    residue = places // 2 * np.array(TURNS)[None, :, None] + rest[:, None, :]
    angle = 2.0 * np.pi * ((residue.reshape(halves, 2 * GROUP, 1) * np.arange(rows)) % bins) / bins
    twist = np.stack([np.cos(angle), np.sin(angle)], axis=1)
    series = np.arange(rows)
    angle = 2.0 * np.pi * ((series[:, None] * series[None, :]) % rows) / rows
    dft = np.concatenate([np.cos(angle), np.sin(angle)])
    return factor.reshape(-1).astype(np.float32), twist.astype(np.float32), dft.astype(jnp.bfloat16)


def squares_kernel(features_ref, squares_ref):
    turned = features_ref[...].astype(F32).T
    squares_ref[...] = jnp.sum(turned * turned, axis=0, keepdims=True)


def turn_kernel(spectrum_ref, turned_ref):
    split = (turned_ref.shape[0], turned_ref.shape[3], turned_ref.shape[4])
    for part in range(2):
        for parity in range(2):
            turned_ref[:, part, parity] = spectrum_ref[part, parity].T.astype(BF16).reshape(split)


def signal_kernel(channels, features_ref, pre_ref, gain_ref, turned_ref, *refs):
    del turned_ref
    square_refs, signal_ref, part_refs = refs[: -1 - GROUP], refs[-1 - GROUP], refs[-GROUP:]
    total = square_refs[0][...]
    for square_ref in square_refs[1:]:
        total = total + square_ref[...]
    scale = lax.rsqrt(total / channels + EPS)
    scaled = features_ref[...].astype(F32) * gain_ref[...] * pre_ref[...].astype(F32)
    signal_ref[...] = (scaled.T * scale).astype(BF16)
    low = lax.axis_index("seq") % GROUP
    width = part_refs[0].shape[1]
    for apart, part_ref in enumerate(part_refs):
        part_ref[0] = signal_ref[pl.ds(pl.multiple_of((low ^ apart) * width, width), width), :]


def pieces(refs):
    return [ref.at[at] for ref in refs for at in range(ref.shape[0])]


def convolve_kernel(spectrum_ref, factor_ref, twist_ref, dft_ref, *refs):
    signal_refs, out_refs, (joined, left, right) = refs[: len(refs) // 2 - 1], refs[len(refs) // 2 - 1 : -3], refs[-3:]
    places, width, rows = joined.shape
    half_rows = left.shape[0] // 2
    place = lax.axis_index("seq")
    half = place // GROUP
    for apart, piece in enumerate(pieces(signal_refs)):
        joined[place ^ apart] = piece[...]
    tall, wide = 16, 256

    def factor(parity, at, which):
        return factor_ref[((half * 2 + parity) * places + at) * 4 + which]

    def tiles():
        for parity in range(2):
            for top in range(0, width, tall):
                for begin in range(0, rows, wide):
                    yield parity, top, pl.ds(begin, wide), begin

    def twists(turn, parity, lanes):
        at = pl.ds(2 * turn + parity, 1)
        return twist_ref[half, 0, at, lanes], twist_ref[half, 1, at, lanes]

    for parity, top, lanes, begin in tiles():
        real, imag = [0.0] * 4, [0.0] * 4
        for at in range(places):
            piece = joined[at, pl.ds(top, tall), lanes].astype(F32)
            real[at % 4] = real[at % 4] + factor(parity, at, 0) * piece
            imag[at % 4] = imag[at % 4] - factor(parity, at, 1) * piece
        even_real, even_imag = real[0] + real[2], imag[0] + imag[2]
        odd_real, odd_imag = real[1] + real[3], imag[1] + imag[3]
        even_gap_real, even_gap_imag = real[0] - real[2], imag[0] - imag[2]
        odd_gap_real, odd_gap_imag = real[1] - real[3], imag[1] - imag[3]
        turned = [
            (even_real + odd_real, even_imag + odd_imag),
            (even_real - odd_real, even_imag - odd_imag),
            (even_gap_real + odd_gap_imag, even_gap_imag - odd_gap_real),
            (even_gap_real - odd_gap_imag, even_gap_imag + odd_gap_real),
        ]
        for turn, (real, imag) in enumerate(turned):
            cos_twist, sin_twist = twists(turn, parity, lanes)
            twisted_real = (real * cos_twist + imag * sin_twist).astype(BF16)
            twisted_imag = (imag * cos_twist - real * sin_twist).astype(BF16)
            at = (2 * turn + parity) * width + top
            left[pl.ds(at, tall), lanes] = twisted_real
            left[pl.ds(at, tall), pl.ds(rows + begin, wide)] = twisted_imag
            left[pl.ds(half_rows + at, tall), lanes] = twisted_imag
            left[pl.ds(half_rows + at, tall), pl.ds(rows + begin, wide)] = -twisted_real
    right[...] = jnp.dot(left[...], dft_ref[...], preferred_element_type=F32)
    block = 2 * width
    for turn in range(GROUP):
        over, under = pl.ds(turn * block, block), pl.ds(half_rows + turn * block, block)
        real, imag = right[over, :], right[under, :]
        response_real = spectrum_ref[turn, 0].reshape(block, rows).astype(F32)
        response_imag = spectrum_ref[turn, 1].reshape(block, rows).astype(F32)
        product_real = (real * response_real - imag * response_imag).astype(BF16)
        product_imag = (real * response_imag + imag * response_real).astype(BF16)
        left[over, pl.ds(0, rows)] = product_real
        left[over, pl.ds(rows, rows)] = -product_imag
        left[under, pl.ds(0, rows)] = product_imag
        left[under, pl.ds(rows, rows)] = product_real
    right[...] = jnp.dot(left[...], dft_ref[...], preferred_element_type=F32)
    for top in range(0, width, tall):
        for begin in range(0, rows, wide):
            lanes = pl.ds(begin, wide)
            sums = [0.0] * places
            for parity in range(2):
                turned = []
                for turn in range(GROUP):
                    at = (2 * turn + parity) * width + top
                    real, imag = right[pl.ds(at, tall), lanes], right[pl.ds(half_rows + at, tall), lanes]
                    cos_twist, sin_twist = twists(turn, parity, lanes)
                    turned.append((real * cos_twist - imag * sin_twist, imag * cos_twist + real * sin_twist))
                (real0, imag0), (real2, imag2), (real1, imag1), (real3, imag3) = turned
                even_real, even_imag = real0 + real2, imag0 + imag2
                odd_real, odd_imag = real1 + real3, imag1 + imag3
                even_gap_real, even_gap_imag = real0 - real2, imag0 - imag2
                odd_gap_real, odd_gap_imag = real1 - real3, imag1 - imag3
                back = [
                    (even_real + odd_real, even_imag + odd_imag),
                    (even_gap_real - odd_gap_imag, even_gap_imag + odd_gap_real),
                    (even_real - odd_real, even_imag - odd_imag),
                    (even_gap_real + odd_gap_imag, even_gap_imag - odd_gap_real),
                ]
                for at in range(places):
                    real, imag = back[at % 4]
                    sums[at] = sums[at] + factor(parity, at, 2) * real - factor(parity, at, 3) * imag
            for at in range(places):
                joined[at, pl.ds(top, tall), lanes] = sums[at].astype(BF16)
    for apart, piece in enumerate(pieces(out_refs)):
        piece[...] = joined[place ^ apart]


def finish_kernel(signal_ref, skip_ref, post_ref, *refs):
    conv_refs, out_ref, total = refs[:-2], refs[-2], refs[-1]
    low = lax.axis_index("seq") % GROUP
    views = pieces(conv_refs)
    width = views[0].shape[0]
    for apart in range(GROUP):
        over = pl.ds(pl.multiple_of((low ^ apart) * width, width), width)
        summed = skip_ref[over, :] * signal_ref[over, :].astype(F32)
        for view in views[apart::GROUP]:
            summed = summed + view[...].astype(F32)
        total[over, :] = summed
    out_ref[...] = (post_ref[...].astype(F32) * total[...].T).astype(BF16)


def call(kernel, out_shape, flops, moved, *operands, **options):
    return pl.pallas_call(
        kernel,
        out_shape=out_shape,
        compiler_params=pltpu.CompilerParams(vmem_limit_bytes=VMEM_LIMIT),
        cost_estimate=pl.CostEstimate(flops=flops, bytes_accessed=moved, transcendentals=0),
        **options,
    )(*operands)


def swap(value, axis, apart):
    return lax.ppermute(value, axis, [(place, place ^ apart) for place in range(lax.axis_size(axis))])


def exchange(parts):
    places = lax.axis_size("seq")
    if len(parts) > 1:
        order = sorted(range(1, places), key=lambda apart: -apart)
        taken = {apart: swap(parts[apart], "seq", apart) for apart in order}
        return [parts[0]] + [taken[apart] for apart in range(1, places)]
    order = lax.axis_index("seq") ^ jnp.arange(places)
    moved = lax.all_to_all(jnp.take(parts[0], order, axis=0), "seq", split_axis=0, concat_axis=0, tiled=True)
    return [jnp.take(moved, order, axis=0)]


def local(features, pre_gate, post_gate, norm_gain, skip_weight, spectrum):
    rows, wide = features.shape
    places = lax.axis_size("seq")
    groups = lax.axis_size("chan")
    width = wide // GROUP
    cells = rows * wide
    few = places <= 8
    factor, twist, dft = tables(places, rows)
    shape = jax.ShapeDtypeStruct
    vmem, smem = pl.BlockSpec(memory_space=pltpu.VMEM), pl.BlockSpec(memory_space=pltpu.SMEM)
    squares = call(squares_kernel, shape((1, rows), F32), 4 * cells, 2 * cells, features)
    others = [swap(squares, "chan", apart) for apart in range(1, groups)]
    response = call(turn_kernel, shape((GROUP, 2, 2, width, rows), BF16), 4 * cells, 24 * cells, spectrum)
    near = [list(range(begin, begin + GROUP)) for begin in range(0, places, GROUP)]
    moved = lax.all_to_all(response, "seq", split_axis=0, concat_axis=0, tiled=True, axis_index_groups=near)
    signal, *parts = call(
        functools.partial(signal_kernel, wide * groups),
        [shape((wide, rows), BF16)] + [shape((1, width, rows), BF16)] * GROUP,
        10 * cells,
        8 * cells,
        features,
        pre_gate,
        norm_gain[None, :],
        response,
        squares,
        *others,
        in_specs=[vmem] * 3 + [pl.BlockSpec(memory_space=pl.ANY)] + [vmem] * groups,
    )
    parts = parts * (places // GROUP)
    gathered = exchange(parts if few else [jnp.concatenate(parts)])
    piece_shapes = [shape((1, width, rows), BF16)] * places if few else [shape((places, width, rows), BF16)]
    conv = call(
        convolve_kernel,
        piece_shapes,
        32 * cells * rows,
        20 * cells,
        moved,
        factor,
        twist,
        dft,
        *gathered,
        in_specs=[vmem, smem] + [vmem] * (2 + len(gathered)),
        scratch_shapes=[
            pltpu.VMEM((places, width, rows), BF16),
            pltpu.VMEM((4 * wide, 2 * rows), BF16),
            pltpu.VMEM((4 * wide, rows), F32),
        ],
    )
    conv = exchange(conv)
    return call(
        finish_kernel,
        shape((rows, wide), BF16),
        10 * cells,
        8 * cells,
        signal,
        skip_weight[:, None],
        post_gate,
        *conv,
        scratch_shapes=[pltpu.VMEM((wide, rows), F32)],
    )


def solution(mesh):
    return jax.shard_map(
        local,
        mesh=mesh,
        in_specs=(
            P("seq", "chan"),
            P("seq", "chan"),
            P("seq", "chan"),
            P("chan"),
            P("chan"),
            P(None, "seq", None, "chan"),
        ),
        out_specs=P("seq", "chan"),
        check_vma=False,
    )
```

```python
import functools
import math

import jax
import jax.numpy as jnp
import numpy as np
from jax import lax
from jax.experimental import pallas as pl
from jax.experimental.pallas import tpu as pltpu
from jax.sharding import PartitionSpec as P

EPS = 1e-06
BF16 = jnp.bfloat16
F32 = jnp.float32
VMEM_LIMIT = 48 * 1024 * 1024
GROUP = 4
TURNS = (0, 2, 1, 3)


def reverse_bits(index, levels):
    return sum((index >> bit & 1) << levels - 1 - bit for bit in range(levels))


@functools.lru_cache(maxsize=None)
def tables(places, rows):
    halves = places // GROUP
    levels = halves.bit_length() - 1
    stride = 2 * places
    bins = stride * rows
    rest = np.array([[2 * reverse_bits(half, levels) + parity for parity in range(2)] for half in range(halves)])
    angle = 2.0 * np.pi * ((rest[:, :, None] * np.arange(places)) % stride) / stride
    factor = np.stack([np.cos(angle), np.sin(angle), np.cos(angle) / bins, np.sin(angle) / bins], axis=-1)
    residue = places // 2 * np.array(TURNS)[None, :, None] + rest[:, None, :]
    angle = 2.0 * np.pi * ((residue.reshape(halves, 2 * GROUP, 1) * np.arange(rows)) % bins) / bins
    twist = np.stack([np.cos(angle), np.sin(angle)], axis=1)
    series = np.arange(rows)
    angle = 2.0 * np.pi * ((series[:, None] * series[None, :]) % rows) / rows
    dft = np.concatenate([np.cos(angle), np.sin(angle)])
    return factor.reshape(-1).astype(np.float32), twist.astype(np.float32), dft.astype(jnp.bfloat16)


def squares_kernel(features_ref, squares_ref):
    turned = features_ref[...].astype(F32).T
    squares_ref[...] = jnp.sum(turned * turned, axis=0, keepdims=True)


def turn_kernel(spectrum_ref, *refs):
    part_refs, turned = refs[:-1], refs[-1]
    low = lax.axis_index("seq") % GROUP
    width = turned.shape[0] // GROUP
    for part in range(2):
        for parity in range(2):
            turned[...] = spectrum_ref[part, parity].T.astype(BF16)
            for apart in range(GROUP):
                chosen = turned[pl.ds(pl.multiple_of((low ^ apart) * width, width), width), :]
                part_refs[parity * GROUP + apart][part] = chosen


def signal_kernel(channels, features_ref, pre_ref, gain_ref, skip_ref, *refs):
    square_refs, (out_ref, direct_ref) = refs[GROUP - 1 : -2], refs[-2:]
    total = square_refs[0][...]
    for square_ref in square_refs[1:]:
        total = total + square_ref[...]
    scale = lax.rsqrt(total / channels + EPS)
    scaled = features_ref[...].astype(F32) * gain_ref[...] * pre_ref[...].astype(F32)
    signal = (scaled.T * scale).astype(BF16)
    for half in range(out_ref.shape[0]):
        out_ref[half] = signal
    direct_ref[...] = skip_ref[...].reshape(-1, 1) * signal.astype(F32)


def convolve_kernel(signal_ref, factor_ref, twist_ref, dft_ref, *refs):
    spectrum_refs, (out_ref, left, right) = refs[: 2 * GROUP], refs[2 * GROUP :]
    places, width, rows = signal_ref.shape
    half_rows = left.shape[0] // 2
    place = lax.axis_index("seq")
    half, low = place // GROUP, place % GROUP
    tall, wide = 16, 256

    def factor(parity, at, which):
        return factor_ref[((half * 2 + parity) * places + at) * 4 + which]

    def tiles():
        for parity in range(2):
            for top in range(0, width, tall):
                for begin in range(0, rows, wide):
                    yield parity, top, pl.ds(begin, wide), begin

    def twists(turn, parity, lanes):
        at = pl.ds(2 * turn + parity, 1)
        return twist_ref[half, 0, at, lanes], twist_ref[half, 1, at, lanes]

    for parity, top, lanes, begin in tiles():
        real, imag = [0.0] * 4, [0.0] * 4
        for at in range(places):
            piece = signal_ref[at, pl.ds(top, tall), lanes].astype(F32)
            real[at % 4] = real[at % 4] + factor(parity, at, 0) * piece
            imag[at % 4] = imag[at % 4] - factor(parity, at, 1) * piece
        even_real, even_imag = real[0] + real[2], imag[0] + imag[2]
        odd_real, odd_imag = real[1] + real[3], imag[1] + imag[3]
        even_gap_real, even_gap_imag = real[0] - real[2], imag[0] - imag[2]
        odd_gap_real, odd_gap_imag = real[1] - real[3], imag[1] - imag[3]
        turned = [
            (even_real + odd_real, even_imag + odd_imag),
            (even_real - odd_real, even_imag - odd_imag),
            (even_gap_real + odd_gap_imag, even_gap_imag - odd_gap_real),
            (even_gap_real - odd_gap_imag, even_gap_imag + odd_gap_real),
        ]
        for turn, (real, imag) in enumerate(turned):
            cos_twist, sin_twist = twists(turn, parity, lanes)
            twisted_real = (real * cos_twist + imag * sin_twist).astype(BF16)
            twisted_imag = (imag * cos_twist - real * sin_twist).astype(BF16)
            at = (2 * turn + parity) * width + top
            left[pl.ds(at, tall), lanes] = twisted_real
            left[pl.ds(at, tall), pl.ds(rows + begin, wide)] = twisted_imag
            left[pl.ds(half_rows + at, tall), lanes] = twisted_imag
            left[pl.ds(half_rows + at, tall), pl.ds(rows + begin, wide)] = -twisted_real
    right[...] = jnp.dot(left[...], dft_ref[...], preferred_element_type=F32)
    for which, spectrum_ref in enumerate(spectrum_refs):
        parity, apart = which // GROUP, which % GROUP
        at = pl.multiple_of(((low ^ apart) * 2 + parity) * width, width)
        over, under = pl.ds(at, width), pl.ds(half_rows + at, width)
        real, imag = right[over, :], right[under, :]
        response_real = spectrum_ref[0].astype(F32)
        response_imag = spectrum_ref[1].astype(F32)
        product_real = (real * response_real - imag * response_imag).astype(BF16)
        product_imag = (real * response_imag + imag * response_real).astype(BF16)
        left[over, pl.ds(0, rows)] = product_real
        left[over, pl.ds(rows, rows)] = -product_imag
        left[under, pl.ds(0, rows)] = product_imag
        left[under, pl.ds(rows, rows)] = product_real
    right[...] = jnp.dot(left[...], dft_ref[...], preferred_element_type=F32)
    for top in range(0, width, tall):
        for begin in range(0, rows, wide):
            lanes = pl.ds(begin, wide)
            sums = [0.0] * places
            for parity in range(2):
                turned = []
                for turn in range(GROUP):
                    at = (2 * turn + parity) * width + top
                    real, imag = right[pl.ds(at, tall), lanes], right[pl.ds(half_rows + at, tall), lanes]
                    cos_twist, sin_twist = twists(turn, parity, lanes)
                    turned.append((real * cos_twist - imag * sin_twist, imag * cos_twist + real * sin_twist))
                (real0, imag0), (real2, imag2), (real1, imag1), (real3, imag3) = turned
                even_real, even_imag = real0 + real2, imag0 + imag2
                odd_real, odd_imag = real1 + real3, imag1 + imag3
                even_gap_real, even_gap_imag = real0 - real2, imag0 - imag2
                odd_gap_real, odd_gap_imag = real1 - real3, imag1 - imag3
                back = [
                    (even_real + odd_real, even_imag + odd_imag),
                    (even_gap_real - odd_gap_imag, even_gap_imag + odd_gap_real),
                    (even_real - odd_real, even_imag - odd_imag),
                    (even_gap_real + odd_gap_imag, even_gap_imag - odd_gap_real),
                ]
                for at in range(places):
                    real, imag = back[at % 4]
                    sums[at] = sums[at] + factor(parity, at, 2) * real - factor(parity, at, 3) * imag
            for at in range(places):
                out_ref[at, pl.ds(top, tall), lanes] = sums[at].astype(BF16)


def finish_kernel(conv_ref, direct_ref, post_ref, out_ref):
    turned = direct_ref[...]
    for half in range(conv_ref.shape[0]):
        turned = turned + conv_ref[half].astype(F32)
    out_ref[...] = (post_ref[...].astype(F32) * turned.T).astype(BF16)


def call(kernel, out_shape, flops, moved, *operands, **options):
    return pl.pallas_call(
        kernel,
        out_shape=out_shape,
        compiler_params=pltpu.CompilerParams(vmem_limit_bytes=VMEM_LIMIT),
        cost_estimate=pl.CostEstimate(flops=flops, bytes_accessed=moved, transcendentals=0),
        **options,
    )(*operands)


def exchange(value):
    return lax.all_to_all(value, "seq", split_axis=0, concat_axis=0, tiled=True)


def swap(value, axis, apart):
    return lax.ppermute(value, axis, [(place, place ^ apart) for place in range(lax.axis_size(axis))])


def local(features, pre_gate, post_gate, norm_gain, skip_weight, spectrum):
    rows, wide = features.shape
    places = lax.axis_size("seq")
    groups = lax.axis_size("chan")
    halves = places // GROUP
    width = wide // GROUP
    cells = rows * wide
    factor, twist, dft = tables(places, rows)
    shape = jax.ShapeDtypeStruct
    vmem, smem = pl.BlockSpec(memory_space=pltpu.VMEM), pl.BlockSpec(memory_space=pltpu.SMEM)
    squares = call(squares_kernel, shape((1, rows), F32), 4 * cells, 2 * cells, features)
    others = [swap(squares, "chan", apart) for apart in range(1, groups)]
    response = call(
        turn_kernel,
        [shape((2, width, rows), BF16)] * (2 * GROUP),
        4 * cells,
        24 * cells,
        spectrum,
        scratch_shapes=[pltpu.VMEM((wide, rows), BF16)],
    )
    even = [response[0]] + [swap(response[apart], "seq", apart) for apart in range(1, GROUP)]
    odd = [response[GROUP]] + [swap(response[GROUP + apart], "seq", apart) for apart in range(1, GROUP)]
    anywhere = pl.BlockSpec(memory_space=pl.ANY)
    signal, direct = call(
        functools.partial(signal_kernel, wide * groups),
        (shape((halves, wide, rows), BF16), shape((wide, rows), F32)),
        10 * cells,
        8 * cells,
        features,
        pre_gate,
        norm_gain[None, :],
        skip_weight[None, :],
        *even[1:],
        squares,
        *others,
        in_specs=[vmem] * 4 + [anywhere] * (GROUP - 1) + [vmem] * groups,
    )
    gathered = exchange(signal.reshape(places, width, rows))
    conv = call(
        convolve_kernel,
        shape((places, width, rows), BF16),
        32 * cells * rows,
        20 * cells,
        gathered,
        factor,
        twist,
        dft,
        *even,
        *odd,
        in_specs=[vmem, smem] + [vmem] * (2 + 2 * GROUP),
        scratch_shapes=[pltpu.VMEM((4 * wide, 2 * rows), BF16), pltpu.VMEM((4 * wide, rows), F32)],
    )
    conv = exchange(conv).reshape(halves, wide, rows)
    return call(
        finish_kernel,
        shape((rows, wide), BF16),
        10 * cells,
        8 * cells,
        conv,
        direct,
        post_gate,
    )


def solution(mesh):
    return jax.shard_map(
        local,
        mesh=mesh,
        in_specs=(
            P("seq", "chan"),
            P("seq", "chan"),
            P("seq", "chan"),
            P("chan"),
            P("chan"),
            P(None, "seq", None, "chan"),
        ),
        out_specs=P("seq", "chan"),
        check_vma=False,
    )
```

```python
import functools

import jax
import jax.numpy as jnp
import numpy as np
from jax import lax
from jax.experimental import pallas as pl
from jax.experimental.pallas import tpu as pltpu
from jax.sharding import PartitionSpec as P

EPS = 1e-06
BF16 = jnp.bfloat16
F32 = jnp.float32
VMEM_LIMIT = 48 * 1024 * 1024
WHOLE_VMEM = 63 * 1024 * 1024 + 512 * 1024


def reverse_bits(index, levels):
    return sum((index >> bit & 1) << levels - 1 - bit for bit in range(levels))


@functools.lru_cache(maxsize=None)
def tables(places, rows, width):
    levels = places.bit_length() - 1
    stride = 2 * places
    bins = stride * rows
    residues = np.array([2 * reverse_bits(place, levels) + parity for place in range(places) for parity in range(2)])
    angle = 2.0 * np.pi * ((residues[:, None] * np.arange(places)[None, :]) % stride) / stride
    same = np.eye(width)
    first = np.concatenate([np.kron(np.cos(angle), same), np.kron(-np.sin(angle), same)])
    last = first.T / bins
    angle = 2.0 * np.pi * ((residues[:, None] * np.arange(rows)[None, :]) % bins) / bins
    twist = np.stack([np.cos(angle), np.sin(angle)])
    series = np.arange(rows)
    angle = 2.0 * np.pi * ((series[:, None] * series[None, :]) % rows) / rows
    dft = np.concatenate([np.cos(angle), np.sin(angle)])
    return (
        first.astype(jnp.bfloat16),
        last.astype(jnp.bfloat16),
        twist.astype(np.float32),
        dft.astype(jnp.bfloat16),
    )


def prepare_kernel(
    features_ref,
    pre_ref,
    gain_ref,
    spectrum_ref,
    squares_ref,
    scaled_ref,
    packed_ref,
    features_in,
    pre_in,
    gain_in,
    spectrum_in,
    ready,
    in_sems,
    out_sems,
):
    blocks = [(part, parity) for part in range(2) for parity in range(2)]
    pairs = [(features_ref, features_in), (pre_ref, pre_in), (gain_ref, gain_in)]
    pairs += [(spectrum_ref.at[block], spectrum_in.at[block]) for block in blocks]
    arriving = [pltpu.make_async_copy(*pair, in_sems.at[slot]) for slot, pair in enumerate(pairs)]
    for copy in arriving:
        copy.start()

    def leave(slot, turned):
        ready[slot] = turned.reshape(ready.shape[1:])
        target = packed_ref.at[:, slot] if len(packed_ref.shape) == 4 else packed_ref.at[slot]
        copy = pltpu.make_async_copy(ready.at[slot], target, out_sems.at[slot])
        copy.start()
        return copy

    for copy in arriving[:3]:
        copy.wait()
    features = features_in[...].astype(F32)
    scaled = (features * gain_in[...] * pre_in[...].astype(F32)).T.astype(BF16)
    scaled_ref[...] = scaled
    leaving = [leave(4, scaled)]
    turned = features.T
    squares_ref[...] = jnp.sum(turned * turned, axis=0, keepdims=True)
    for slot, block in enumerate(blocks):
        arriving[3 + slot].wait()
        leaving.append(leave(slot, spectrum_in[block].T.astype(BF16)))
    for copy in leaving:
        copy.wait()


def scale_kernel(channels, scaled_ref, skip_ref, *refs):
    square_refs, (scale_ref, direct_ref) = refs[:-2], refs[-2:]
    total = square_refs[0][...]
    for square_ref in square_refs[1:]:
        total = total + square_ref[...]
    scale = lax.rsqrt(total / channels + EPS)
    scale_ref[...] = scale
    signal = (scaled_ref[...].astype(F32) * scale).astype(BF16)
    direct_ref[...] = skip_ref[...].reshape(-1, 1) * signal.astype(F32)


def matmul(left, right):
    return jnp.dot(left, right, preferred_element_type=F32)


def twisted(value, factor):
    parts = factor.shape[0]
    if value.shape[0] == parts:
        return value * factor
    return (value.reshape(parts, -1, value.shape[1]) * factor[:, None, :]).reshape(value.shape)


def convolve_kernel(packed_ref, first_ref, last_ref, twist_ref, dft_ref, *refs):
    scale_refs, (out_ref, scales, left, right) = refs[:-4], refs[-4:]
    wide, rows = out_ref.shape
    half = 2 * wide
    piled = len(packed_ref.shape) == 4
    if piled:
        place = lax.axis_index("seq")
        apart = 0
        for scale_ref in scale_refs:
            for at in range(scale_ref.shape[0]):
                scales[place ^ apart] = scale_ref[pl.ds(at, 1), :]
                apart += 1
    span = 256
    for begin in range(0, rows, span):
        lanes, later = pl.ds(begin, span), pl.ds(rows + begin, span)
        if piled:
            signal = packed_ref[:, 4, :, lanes].astype(F32) * scales[:, :, lanes]
            signal = signal.astype(BF16).reshape(wide, span)
        else:
            signal = (packed_ref[4, :, lanes].astype(F32) * scale_refs[0][:, lanes]).astype(BF16)
        mixed = matmul(first_ref[...], signal)
        real, imag = mixed[:half], mixed[half:]
        cos_twist, sin_twist = twist_ref[0, :, lanes], twist_ref[1, :, lanes]
        turned_real = (twisted(real, cos_twist) + twisted(imag, sin_twist)).astype(BF16)
        turned_imag = (twisted(imag, cos_twist) - twisted(real, sin_twist)).astype(BF16)
        left[pl.ds(0, half), lanes] = turned_real
        left[pl.ds(0, half), later] = turned_imag
        left[pl.ds(half, half), lanes] = turned_imag
        left[pl.ds(half, half), later] = -turned_real
    for begin in range(0, rows, span):
        lanes, later = pl.ds(begin, span), pl.ds(rows + begin, span)
        mixed = matmul(left[...], dft_ref[:, lanes])
        real, imag = mixed[:half], mixed[half:]
        if piled:
            response_real = packed_ref[:, 0:2, :, lanes].reshape(half, span).astype(F32)
            response_imag = packed_ref[:, 2:4, :, lanes].reshape(half, span).astype(F32)
        else:
            response_real = packed_ref[0:2, :, lanes].reshape(half, span).astype(F32)
            response_imag = packed_ref[2:4, :, lanes].reshape(half, span).astype(F32)
        product_real = (real * response_real - imag * response_imag).astype(BF16)
        product_imag = (real * response_imag + imag * response_real).astype(BF16)
        right[pl.ds(0, half), lanes] = product_real
        right[pl.ds(0, half), later] = -product_imag
        right[pl.ds(half, half), lanes] = product_imag
        right[pl.ds(half, half), later] = product_real
    for begin in range(0, rows, span):
        lanes = pl.ds(begin, span)
        mixed = matmul(right[...], dft_ref[:, lanes])
        real, imag = mixed[:half], mixed[half:]
        cos_twist, sin_twist = twist_ref[0, :, lanes], twist_ref[1, :, lanes]
        turned_real = (twisted(real, cos_twist) - twisted(imag, sin_twist)).astype(BF16)
        turned_imag = (twisted(imag, cos_twist) + twisted(real, sin_twist)).astype(BF16)
        both = jnp.concatenate([turned_real, turned_imag], axis=0)
        out_ref[:, lanes] = matmul(last_ref[...], both).astype(BF16)


def finish_kernel(conv_ref, direct_ref, post_ref, out_ref):
    turned = conv_ref[...].astype(F32) + direct_ref[...]
    out_ref[...] = (post_ref[...].astype(F32) * turned.T).astype(BF16)


def call(kernel, out_shape, flops, moved, *operands, limit=VMEM_LIMIT, **options):
    return pl.pallas_call(
        kernel,
        out_shape=out_shape,
        compiler_params=pltpu.CompilerParams(vmem_limit_bytes=limit),
        cost_estimate=pl.CostEstimate(flops=flops, bytes_accessed=moved, transcendentals=0),
        **options,
    )(*operands)


def exchange(value):
    return lax.all_to_all(value, "seq", split_axis=0, concat_axis=0, tiled=True)


def swap(value, axis, apart):
    return lax.ppermute(value, axis, [(place, place ^ apart) for place in range(lax.axis_size(axis))])


def local(features, pre_gate, post_gate, norm_gain, skip_weight, spectrum):
    rows, wide = features.shape
    places = lax.axis_size("seq")
    groups = lax.axis_size("chan")
    width = wide // places
    piled = width % 16 == 0
    first, last, twist, dft = tables(places, rows, width)
    if not piled:
        twist = np.repeat(twist, width, axis=1)
    cells = rows * wide
    shape = jax.ShapeDtypeStruct
    vmem, anywhere = pl.BlockSpec(memory_space=pltpu.VMEM), pl.BlockSpec(memory_space=pl.ANY)
    squares, scaled, packed = call(
        prepare_kernel,
        (
            shape((1, rows), F32),
            shape((wide, rows), BF16),
            shape((places, 5, width, rows) if piled else (5, wide, rows), BF16),
        ),
        10 * cells,
        32 * cells,
        features,
        pre_gate,
        norm_gain[None, :],
        spectrum,
        limit=WHOLE_VMEM,
        in_specs=[anywhere] * 4,
        out_specs=(vmem, vmem, anywhere),
        scratch_shapes=[
            pltpu.VMEM(features.shape, BF16),
            pltpu.VMEM(pre_gate.shape, BF16),
            pltpu.VMEM((1, wide), F32),
            pltpu.VMEM(spectrum.shape, F32),
            pltpu.VMEM((5, places, width, rows) if piled else (5, wide, rows), BF16),
            pltpu.SemaphoreType.DMA((7,)),
            pltpu.SemaphoreType.DMA((5,)),
        ],
    )
    if not piled:
        packed = packed.reshape(5, places, width, rows).transpose(1, 0, 2, 3)
    gathered = exchange(packed)
    others = [swap(squares, "chan", apart) for apart in range(1, groups)]
    scale, direct = call(
        functools.partial(scale_kernel, wide * groups),
        (shape((1, rows), F32), shape((wide, rows), F32)),
        10 * cells,
        6 * cells,
        scaled,
        skip_weight[None, :],
        squares,
        *others,
    )
    if piled:
        scales, apart = [scale], 1
        while apart < places:
            known = jnp.concatenate(scales) if apart > 1 else scale
            scales.append(swap(known, "seq", apart))
            apart *= 2
    else:
        scales = [jnp.repeat(lax.all_gather(scale, "seq", axis=0, tiled=True), width, axis=0)]
        response = gathered[:, :4].reshape(places, 2, 2, width, rows).transpose(1, 0, 2, 3, 4)
        gathered = jnp.concatenate([response.reshape(4, wide, rows), gathered[:, 4].reshape(1, wide, rows)])
    conv = call(
        convolve_kernel,
        shape((wide, rows), BF16),
        32 * cells * rows,
        20 * cells,
        gathered,
        first,
        last,
        twist,
        dft,
        *scales,
        scratch_shapes=[
            pltpu.VMEM((places, 1, rows), F32),
            pltpu.VMEM((4 * wide, 2 * rows), BF16),
            pltpu.VMEM((4 * wide, 2 * rows), BF16),
        ],
    )
    conv = exchange(conv.reshape(places, width, rows)).reshape(wide, rows)
    return call(finish_kernel, shape((rows, wide), BF16), 10 * cells, 8 * cells, conv, direct, post_gate)


def solution(mesh):
    return jax.shard_map(
        local,
        mesh=mesh,
        in_specs=(
            P("seq", "chan"),
            P("seq", "chan"),
            P("seq", "chan"),
            P("chan"),
            P("chan"),
            P(None, "seq", None, "chan"),
        ),
        out_specs=P("seq", "chan"),
        check_vma=False,
    )
```

```python
import functools

import jax
import jax.numpy as jnp
import numpy as np
from jax import lax
from jax.experimental import pallas as pl
from jax.experimental.pallas import tpu as pltpu
from jax.sharding import PartitionSpec as P

EPS = 1e-06
BF16 = jnp.bfloat16
F32 = jnp.float32
VMEM_LIMIT = 48 * 1024 * 1024
WHOLE_VMEM = 63 * 1024 * 1024 + 512 * 1024


def reverse_bits(index, levels):
    return sum((index >> bit & 1) << levels - 1 - bit for bit in range(levels))


@functools.lru_cache(maxsize=None)
def tables(places, rows, width):
    levels = places.bit_length() - 1
    stride = 2 * places
    bins = stride * rows
    residues = np.array([2 * reverse_bits(place, levels) + parity for place in range(places) for parity in range(2)])
    angle = 2.0 * np.pi * ((residues[:, None] * np.arange(places)[None, :]) % stride) / stride
    same = np.eye(width)
    first = np.concatenate([np.kron(np.cos(angle), same), np.kron(-np.sin(angle), same)])
    last = first.T / bins
    angle = 2.0 * np.pi * ((residues[:, None] * np.arange(rows)[None, :]) % bins) / bins
    twist = np.stack([np.cos(angle), np.sin(angle)])
    series = np.arange(rows)
    angle = 2.0 * np.pi * ((series[:, None] * series[None, :]) % rows) / rows
    dft = np.concatenate([np.cos(angle), np.sin(angle)])
    return (
        first.astype(jnp.bfloat16),
        last.astype(jnp.bfloat16),
        twist.astype(np.float32),
        dft.astype(jnp.bfloat16),
    )


def hops(places):
    known, apart = [0], places // 2
    steps = [[0]]
    while apart > 0:
        steps.append([apart ^ step for step in known])
        known = known + steps[-1]
        apart //= 2
    return steps


def prepare_kernel(
    features_ref,
    pre_ref,
    gain_ref,
    spectrum_ref,
    squares_ref,
    scaled_ref,
    packed_ref,
    features_in,
    pre_in,
    gain_in,
    spectrum_in,
    squares_out,
    scaled_out,
    packed_out,
    in_sems,
    out_sems,
):
    blocks = [(part, parity) for part in range(2) for parity in range(2)]
    pairs = [(features_ref, features_in), (pre_ref, pre_in), (gain_ref, gain_in)]
    pairs += [(spectrum_ref.at[block], spectrum_in.at[block]) for block in blocks]
    arriving = [pltpu.make_async_copy(*pair, in_sems.at[slot]) for slot, pair in enumerate(pairs)]
    for copy in arriving:
        copy.start()
    leaving = []

    def leave(source, target):
        copy = pltpu.make_async_copy(source, target, out_sems.at[len(leaving)])
        copy.start()
        leaving.append(copy)

    def pack(slot, turned):
        packed_out[slot] = turned.reshape(packed_out.shape[1:])
        leave(packed_out.at[slot], packed_ref.at[:, slot] if len(packed_ref.shape) == 4 else packed_ref.at[slot])

    for copy in arriving[:3]:
        copy.wait()
    features = features_in[...].astype(F32)
    scaled = (features * gain_in[...] * pre_in[...].astype(F32)).T.astype(BF16)
    scaled_out[...] = scaled
    leave(scaled_out, scaled_ref)
    pack(4, scaled)
    turned = features.T
    squares_out[...] = jnp.sum(turned * turned, axis=0, keepdims=True)
    leave(squares_out, squares_ref)
    for slot, block in enumerate(blocks):
        arriving[3 + slot].wait()
        pack(slot, spectrum_in[block].T.astype(BF16))
    for copy in leaving:
        copy.wait()


def scale_kernel(channels, *refs):
    square_refs, scale_ref = refs[:-1], refs[-1]
    total = square_refs[0][...]
    for square_ref in square_refs[1:]:
        total = total + square_ref[...]
    scale_ref[...] = lax.rsqrt(total / channels + EPS)


def matmul(left, right):
    return jnp.dot(left, right, preferred_element_type=F32)


def twisted(value, factor):
    parts = factor.shape[0]
    if value.shape[0] == parts:
        return value * factor
    return (value.reshape(parts, -1, value.shape[1]) * factor[:, None, :]).reshape(value.shape)


def convolve_kernel(packed_ref, first_ref, last_ref, twist_ref, dft_ref, *refs):
    scale_refs, (out_ref, scales, left, right) = refs[:-4], refs[-4:]
    wide, rows = out_ref.shape
    half = 2 * wide
    piled = len(packed_ref.shape) == 4
    if piled:
        place = lax.axis_index("seq")
        for scale_ref, steps in zip(scale_refs, hops(scales.shape[0])):
            for at, step in enumerate(steps):
                scales[place ^ step] = scale_ref[pl.ds(at, 1), :]
    span = 256
    for begin in range(0, rows, span):
        lanes, later = pl.ds(begin, span), pl.ds(rows + begin, span)
        if piled:
            signal = packed_ref[:, 4, :, lanes].astype(F32) * scales[:, :, lanes]
            signal = signal.astype(BF16).reshape(wide, span)
        else:
            signal = (packed_ref[4, :, lanes].astype(F32) * scale_refs[0][:, lanes]).astype(BF16)
        mixed = matmul(first_ref[...], signal)
        real, imag = mixed[:half], mixed[half:]
        cos_twist, sin_twist = twist_ref[0, :, lanes], twist_ref[1, :, lanes]
        turned_real = (twisted(real, cos_twist) + twisted(imag, sin_twist)).astype(BF16)
        turned_imag = (twisted(imag, cos_twist) - twisted(real, sin_twist)).astype(BF16)
        left[pl.ds(0, half), lanes] = turned_real
        left[pl.ds(0, half), later] = turned_imag
        left[pl.ds(half, half), lanes] = turned_imag
        left[pl.ds(half, half), later] = -turned_real
    for begin in range(0, rows, span):
        lanes, later = pl.ds(begin, span), pl.ds(rows + begin, span)
        mixed = matmul(left[...], dft_ref[:, lanes])
        real, imag = mixed[:half], mixed[half:]
        if piled:
            response_real = packed_ref[:, 0:2, :, lanes].reshape(half, span).astype(F32)
            response_imag = packed_ref[:, 2:4, :, lanes].reshape(half, span).astype(F32)
        else:
            response_real = packed_ref[0:2, :, lanes].reshape(half, span).astype(F32)
            response_imag = packed_ref[2:4, :, lanes].reshape(half, span).astype(F32)
        product_real = (real * response_real - imag * response_imag).astype(BF16)
        product_imag = (real * response_imag + imag * response_real).astype(BF16)
        right[pl.ds(0, half), lanes] = product_real
        right[pl.ds(0, half), later] = -product_imag
        right[pl.ds(half, half), lanes] = product_imag
        right[pl.ds(half, half), later] = product_real
    for begin in range(0, rows, span):
        lanes = pl.ds(begin, span)
        mixed = matmul(right[...], dft_ref[:, lanes])
        real, imag = mixed[:half], mixed[half:]
        cos_twist, sin_twist = twist_ref[0, :, lanes], twist_ref[1, :, lanes]
        turned_real = (twisted(real, cos_twist) - twisted(imag, sin_twist)).astype(BF16)
        turned_imag = (twisted(imag, cos_twist) + twisted(real, sin_twist)).astype(BF16)
        both = jnp.concatenate([turned_real, turned_imag], axis=0)
        out_ref[:, lanes] = matmul(last_ref[...], both).astype(BF16)


def finish_kernel(conv_ref, scaled_ref, scale_ref, skip_ref, post_ref, out_ref):
    signal = (scaled_ref[...].astype(F32) * scale_ref[...]).astype(BF16)
    turned = conv_ref[...].astype(F32) + skip_ref[...].reshape(-1, 1) * signal.astype(F32)
    out_ref[...] = (post_ref[...].astype(F32) * turned.T).astype(BF16)


def call(kernel, out_shape, flops, moved, *operands, limit=VMEM_LIMIT, **options):
    return pl.pallas_call(
        kernel,
        out_shape=out_shape,
        compiler_params=pltpu.CompilerParams(vmem_limit_bytes=limit),
        cost_estimate=pl.CostEstimate(flops=flops, bytes_accessed=moved, transcendentals=0),
        **options,
    )(*operands)


def exchange(value):
    return lax.all_to_all(value, "seq", split_axis=0, concat_axis=0, tiled=True)


def swap(value, axis, apart):
    return lax.ppermute(value, axis, [(place, place ^ apart) for place in range(lax.axis_size(axis))])


def local(features, pre_gate, post_gate, norm_gain, skip_weight, spectrum):
    rows, wide = features.shape
    places = lax.axis_size("seq")
    groups = lax.axis_size("chan")
    width = wide // places
    piled = width % 16 == 0
    first, last, twist, dft = tables(places, rows, width)
    if not piled:
        twist = np.repeat(twist, width, axis=1)
    cells = rows * wide
    shape = jax.ShapeDtypeStruct
    vmem, anywhere = pl.BlockSpec(memory_space=pltpu.VMEM), pl.BlockSpec(memory_space=pl.ANY)
    squares, scaled, packed = call(
        prepare_kernel,
        (
            shape((1, rows), F32),
            shape((wide, rows), BF16),
            shape((places, 5, width, rows) if piled else (5, wide, rows), BF16),
        ),
        10 * cells,
        32 * cells,
        features,
        pre_gate,
        norm_gain[None, :],
        spectrum,
        limit=WHOLE_VMEM,
        in_specs=[anywhere] * 4,
        out_specs=(anywhere, anywhere, anywhere),
        scratch_shapes=[
            pltpu.VMEM(features.shape, BF16),
            pltpu.VMEM(pre_gate.shape, BF16),
            pltpu.VMEM((1, wide), F32),
            pltpu.VMEM(spectrum.shape, F32),
            pltpu.VMEM((1, rows), F32),
            pltpu.VMEM((wide, rows), BF16),
            pltpu.VMEM((5, places, width, rows) if piled else (5, wide, rows), BF16),
            pltpu.SemaphoreType.DMA((7,)),
            pltpu.SemaphoreType.DMA((7,)),
        ],
    )
    if not piled:
        packed = packed.reshape(5, places, width, rows).transpose(1, 0, 2, 3)
    gathered = exchange(packed)
    others = [swap(squares, "chan", apart) for apart in range(1, groups)]
    scale = call(
        functools.partial(scale_kernel, wide * groups), shape((1, rows), F32), 8 * rows, 32 * rows, squares, *others
    )
    if piled:
        scales, apart = [scale], places // 2
        while apart > 0:
            known = jnp.concatenate(scales) if len(scales) > 1 else scale
            scales.append(swap(known, "seq", apart))
            apart //= 2
    else:
        scales = [jnp.repeat(lax.all_gather(scale, "seq", axis=0, tiled=True), width, axis=0)]
        response = gathered[:, :4].reshape(places, 2, 2, width, rows).transpose(1, 0, 2, 3, 4)
        gathered = jnp.concatenate([response.reshape(4, wide, rows), gathered[:, 4].reshape(1, wide, rows)])
    conv = call(
        convolve_kernel,
        shape((wide, rows), BF16),
        32 * cells * rows,
        20 * cells,
        gathered,
        first,
        last,
        twist,
        dft,
        *scales,
        scratch_shapes=[
            pltpu.VMEM((places, 1, rows), F32),
            pltpu.VMEM((4 * wide, 2 * rows), BF16),
            pltpu.VMEM((4 * wide, 2 * rows), BF16),
        ],
    )
    conv = exchange(conv.reshape(places, width, rows)).reshape(wide, rows)
    return call(finish_kernel, shape((rows, wide), BF16), 10 * cells, 8 * cells, conv, scaled, scale, skip_weight[None, :], post_gate)


def solution(mesh):
    return jax.shard_map(
        local,
        mesh=mesh,
        in_specs=(
            P("seq", "chan"),
            P("seq", "chan"),
            P("seq", "chan"),
            P("chan"),
            P("chan"),
            P(None, "seq", None, "chan"),
        ),
        out_specs=P("seq", "chan"),
        check_vma=False,
    )
```

```python
import functools

import jax
import jax.numpy as jnp
import numpy as np
from jax import lax
from jax.experimental import pallas as pl
from jax.experimental.pallas import tpu as pltpu
from jax.sharding import PartitionSpec as P

EPS = 1e-06
BF16 = jnp.bfloat16
F32 = jnp.float32
VMEM_LIMIT = 48 * 1024 * 1024
WHOLE_VMEM = 63 * 1024 * 1024 + 512 * 1024


def rank_of(place, places):
    return place * 2 % places + place // (places // 2)


def place_of(rank, places):
    return rank // 2 + rank % 2 * (places // 2)


def reverse_bits(index, levels):
    return sum((index >> bit & 1) << levels - 1 - bit for bit in range(levels))


@functools.lru_cache(maxsize=None)
def tables(places, rows, width):
    levels = places.bit_length() - 1
    stride = 2 * places
    bins = stride * rows
    order = np.array([place_of(rank, places) for rank in range(places)])
    residues = np.array([2 * reverse_bits(place, levels) + parity for place in order for parity in range(2)])
    angle = 2.0 * np.pi * ((residues[:, None] * order[None, :]) % stride) / stride
    same = np.eye(width)
    first = np.concatenate([np.kron(np.cos(angle), same), np.kron(-np.sin(angle), same)])
    last = first.T / bins
    angle = 2.0 * np.pi * ((residues[:, None] * np.arange(rows)[None, :]) % bins) / bins
    twist = np.stack([np.cos(angle), np.sin(angle)])
    series = np.arange(rows)
    angle = 2.0 * np.pi * ((series[:, None] * series[None, :]) % rows) / rows
    dft = np.concatenate([np.cos(angle), np.sin(angle)])
    return (
        first.astype(jnp.bfloat16),
        last.astype(jnp.bfloat16),
        twist.astype(np.float32),
        dft.astype(jnp.bfloat16),
    )


def hops(places):
    known, apart = [0], 1
    steps = [[0]]
    while apart < places:
        steps.append([apart ^ step for step in known])
        known = known + steps[-1]
        apart *= 2
    return steps


def prepare_kernel(
    features_ref,
    pre_ref,
    gain_ref,
    spectrum_ref,
    squares_ref,
    scaled_ref,
    packed_ref,
    features_in,
    pre_in,
    gain_in,
    spectrum_in,
    squares_out,
    scaled_out,
    packed_out,
    in_sems,
    out_sems,
):
    blocks = [(part, parity) for part in range(2) for parity in range(2)]
    pairs = [(features_ref, features_in), (pre_ref, pre_in), (gain_ref, gain_in)]
    pairs += [(spectrum_ref.at[block], spectrum_in.at[block]) for block in blocks]
    arriving = [pltpu.make_async_copy(*pair, in_sems.at[slot]) for slot, pair in enumerate(pairs)]
    for copy in arriving:
        copy.start()
    leaving = []

    def leave(source, target):
        copy = pltpu.make_async_copy(source, target, out_sems.at[len(leaving)])
        copy.start()
        leaving.append(copy)

    def pack(slot, turned):
        if len(packed_ref.shape) == 4:
            places, width = packed_out.shape[1:3]
            for rank in range(places):
                begin = place_of(rank, places) * width
                packed_out[slot, rank] = turned[begin : begin + width]
            leave(packed_out.at[slot], packed_ref.at[:, slot])
        else:
            packed_out[slot] = turned
            leave(packed_out.at[slot], packed_ref.at[slot])

    for copy in arriving[:3]:
        copy.wait()
    features = features_in[...].astype(F32)
    scaled = (features * gain_in[...] * pre_in[...].astype(F32)).T.astype(BF16)
    scaled_out[...] = scaled
    leave(scaled_out, scaled_ref)
    pack(4, scaled)
    turned = features.T
    squares_out[...] = jnp.sum(turned * turned, axis=0, keepdims=True)
    leave(squares_out, squares_ref)
    for slot, block in enumerate(blocks):
        arriving[3 + slot].wait()
        pack(slot, spectrum_in[block].T.astype(BF16))
    for copy in leaving:
        copy.wait()


def scale_kernel(channels, *refs):
    square_refs, scale_ref = refs[:-1], refs[-1]
    total = square_refs[0][...]
    for square_ref in square_refs[1:]:
        total = total + square_ref[...]
    scale_ref[...] = lax.rsqrt(total / channels + EPS)


def matmul(left, right):
    return jnp.dot(left, right, preferred_element_type=F32)


def twisted(value, factor):
    parts = factor.shape[0]
    if value.shape[0] == parts:
        return value * factor
    return (value.reshape(parts, -1, value.shape[1]) * factor[:, None, :]).reshape(value.shape)


def convolve_kernel(packed_ref, first_ref, last_ref, twist_ref, dft_ref, *refs):
    scale_refs, (out_ref, scales, left, right) = refs[:-4], refs[-4:]
    wide, rows = out_ref.shape
    half = 2 * wide
    piled = len(packed_ref.shape) == 4
    if piled:
        place = lax.axis_index("seq")
        for scale_ref, steps in zip(scale_refs, hops(scales.shape[0])):
            for at, step in enumerate(steps):
                scales[rank_of(place ^ step, scales.shape[0])] = scale_ref[pl.ds(at, 1), :]
    span = 256
    for begin in range(0, rows, span):
        lanes, later = pl.ds(begin, span), pl.ds(rows + begin, span)
        if piled:
            signal = packed_ref[:, 4, :, lanes].astype(F32) * scales[:, :, lanes]
            signal = signal.astype(BF16).reshape(wide, span)
        else:
            signal = (packed_ref[4, :, lanes].astype(F32) * scale_refs[0][:, lanes]).astype(BF16)
        mixed = matmul(first_ref[...], signal)
        real, imag = mixed[:half], mixed[half:]
        cos_twist, sin_twist = twist_ref[0, :, lanes], twist_ref[1, :, lanes]
        turned_real = (twisted(real, cos_twist) + twisted(imag, sin_twist)).astype(BF16)
        turned_imag = (twisted(imag, cos_twist) - twisted(real, sin_twist)).astype(BF16)
        left[pl.ds(0, half), lanes] = turned_real
        left[pl.ds(0, half), later] = turned_imag
        left[pl.ds(half, half), lanes] = turned_imag
        left[pl.ds(half, half), later] = -turned_real
    for begin in range(0, rows, span):
        lanes, later = pl.ds(begin, span), pl.ds(rows + begin, span)
        mixed = matmul(left[...], dft_ref[:, lanes])
        real, imag = mixed[:half], mixed[half:]
        if piled:
            response_real = packed_ref[:, 0:2, :, lanes].reshape(half, span).astype(F32)
            response_imag = packed_ref[:, 2:4, :, lanes].reshape(half, span).astype(F32)
        else:
            response_real = packed_ref[0:2, :, lanes].reshape(half, span).astype(F32)
            response_imag = packed_ref[2:4, :, lanes].reshape(half, span).astype(F32)
        product_real = (real * response_real - imag * response_imag).astype(BF16)
        product_imag = (real * response_imag + imag * response_real).astype(BF16)
        right[pl.ds(0, half), lanes] = product_real
        right[pl.ds(0, half), later] = -product_imag
        right[pl.ds(half, half), lanes] = product_imag
        right[pl.ds(half, half), later] = product_real
    for begin in range(0, rows, span):
        lanes = pl.ds(begin, span)
        mixed = matmul(right[...], dft_ref[:, lanes])
        real, imag = mixed[:half], mixed[half:]
        cos_twist, sin_twist = twist_ref[0, :, lanes], twist_ref[1, :, lanes]
        turned_real = (twisted(real, cos_twist) - twisted(imag, sin_twist)).astype(BF16)
        turned_imag = (twisted(imag, cos_twist) + twisted(real, sin_twist)).astype(BF16)
        both = jnp.concatenate([turned_real, turned_imag], axis=0)
        out_ref[:, lanes] = matmul(last_ref[...], both).astype(BF16)


def finish_kernel(conv_ref, scaled_ref, scale_ref, skip_ref, post_ref, out_ref):
    signal = (scaled_ref[...].astype(F32) * scale_ref[...]).astype(BF16)
    conv = conv_ref[...]
    if len(conv_ref.shape) == 3:
        places = conv_ref.shape[0]
        conv = jnp.concatenate([conv_ref[rank_of(place, places)] for place in range(places)])
    turned = conv.astype(F32) + skip_ref[...].reshape(-1, 1) * signal.astype(F32)
    out_ref[...] = (post_ref[...].astype(F32) * turned.T).astype(BF16)


def call(kernel, out_shape, flops, moved, *operands, limit=VMEM_LIMIT, **options):
    return pl.pallas_call(
        kernel,
        out_shape=out_shape,
        compiler_params=pltpu.CompilerParams(vmem_limit_bytes=limit),
        cost_estimate=pl.CostEstimate(flops=flops, bytes_accessed=moved, transcendentals=0),
        **options,
    )(*operands)


def exchange(value):
    places = lax.axis_size("seq")
    ranks = [[place_of(rank, places) for rank in range(places)]]
    return lax.all_to_all(value, "seq", split_axis=0, concat_axis=0, tiled=True, axis_index_groups=ranks)


def swap(value, axis, apart):
    return lax.ppermute(value, axis, [(place, place ^ apart) for place in range(lax.axis_size(axis))])


def local(features, pre_gate, post_gate, norm_gain, skip_weight, spectrum):
    rows, wide = features.shape
    places = lax.axis_size("seq")
    groups = lax.axis_size("chan")
    width = wide // places
    piled = width % 16 == 0
    first, last, twist, dft = tables(places, rows, width)
    if not piled:
        twist = np.repeat(twist, width, axis=1)
    cells = rows * wide
    shape = jax.ShapeDtypeStruct
    vmem, anywhere = pl.BlockSpec(memory_space=pltpu.VMEM), pl.BlockSpec(memory_space=pl.ANY)
    squares, scaled, packed = call(
        prepare_kernel,
        (
            shape((1, rows), F32),
            shape((wide, rows), BF16),
            shape((places, 5, width, rows) if piled else (5, wide, rows), BF16),
        ),
        10 * cells,
        32 * cells,
        features,
        pre_gate,
        norm_gain[None, :],
        spectrum,
        limit=WHOLE_VMEM,
        in_specs=[anywhere] * 4,
        out_specs=(anywhere, anywhere, anywhere),
        scratch_shapes=[
            pltpu.VMEM(features.shape, BF16),
            pltpu.VMEM(pre_gate.shape, BF16),
            pltpu.VMEM((1, wide), F32),
            pltpu.VMEM(spectrum.shape, F32),
            pltpu.VMEM((1, rows), F32),
            pltpu.VMEM((wide, rows), BF16),
            pltpu.VMEM((5, places, width, rows) if piled else (5, wide, rows), BF16),
            pltpu.SemaphoreType.DMA((7,)),
            pltpu.SemaphoreType.DMA((7,)),
        ],
    )
    if not piled:
        order = np.array([place_of(rank, places) for rank in range(places)])
        packed = packed.reshape(5, places, width, rows).transpose(1, 0, 2, 3)[order]
    gathered = exchange(packed)
    others = [swap(squares, "chan", apart) for apart in range(1, groups)]
    scale = call(
        functools.partial(scale_kernel, wide * groups), shape((1, rows), F32), 8 * rows, 32 * rows, squares, *others
    )
    if piled:
        scales, apart = [scale], 1
        while apart < places:
            known = jnp.concatenate(scales) if len(scales) > 1 else scale
            scales.append(swap(known, "seq", apart))
            apart *= 2
    else:
        scales = [jnp.repeat(lax.all_gather(scale, "seq", axis=0, tiled=True)[order], width, axis=0)]
        response = gathered[:, :4].reshape(places, 2, 2, width, rows).transpose(1, 0, 2, 3, 4)
        gathered = jnp.concatenate([response.reshape(4, wide, rows), gathered[:, 4].reshape(1, wide, rows)])
    conv = call(
        convolve_kernel,
        shape((wide, rows), BF16),
        32 * cells * rows,
        20 * cells,
        gathered,
        first,
        last,
        twist,
        dft,
        *scales,
        scratch_shapes=[
            pltpu.VMEM((places, 1, rows), F32),
            pltpu.VMEM((4 * wide, 2 * rows), BF16),
            pltpu.VMEM((4 * wide, 2 * rows), BF16),
        ],
    )
    conv = exchange(conv.reshape(places, width, rows))
    if not piled:
        conv = conv[np.array([rank_of(place, places) for place in range(places)])].reshape(wide, rows)
    return call(finish_kernel, shape((rows, wide), BF16), 10 * cells, 8 * cells, conv, scaled, scale, skip_weight[None, :], post_gate)


def solution(mesh):
    return jax.shard_map(
        local,
        mesh=mesh,
        in_specs=(
            P("seq", "chan"),
            P("seq", "chan"),
            P("seq", "chan"),
            P("chan"),
            P("chan"),
            P(None, "seq", None, "chan"),
        ),
        out_specs=P("seq", "chan"),
        check_vma=False,
    )
```

```python
import functools

import jax
import jax.numpy as jnp
import numpy as np
from jax import lax
from jax.experimental import pallas as pl
from jax.experimental.pallas import tpu as pltpu
from jax.sharding import PartitionSpec as P

EPS = 1e-06
BF16 = jnp.bfloat16
F32 = jnp.float32
VMEM_LIMIT = 48 * 1024 * 1024
WHOLE_VMEM = 63 * 1024 * 1024 + 512 * 1024


def rank_of(place, places):
    return place * 2 % places + place // (places // 2)


def place_of(rank, places):
    return rank // 2 + rank % 2 * (places // 2)


def reverse_bits(index, levels):
    return sum((index >> bit & 1) << levels - 1 - bit for bit in range(levels))


@functools.lru_cache(maxsize=None)
def tables(places, rows, width):
    levels = places.bit_length() - 1
    stride = 2 * places
    bins = stride * rows
    order = np.array([place_of(rank, places) for rank in range(places)])
    residues = np.array([2 * reverse_bits(place, levels) + parity for place in order for parity in range(2)])
    angle = 2.0 * np.pi * ((residues[:, None] * order[None, :]) % stride) / stride
    same = np.eye(width)
    first = np.concatenate([np.kron(np.cos(angle), same), np.kron(-np.sin(angle), same)])
    last = first.T / bins
    angle = 2.0 * np.pi * ((residues[:, None] * np.arange(rows)[None, :]) % bins) / bins
    twist = np.stack([np.cos(angle), np.sin(angle)])
    series = np.arange(rows)
    angle = 2.0 * np.pi * ((series[:, None] * series[None, :]) % rows) / rows
    dft = np.concatenate([np.cos(angle), np.sin(angle)])
    return (
        first.astype(jnp.bfloat16),
        last.astype(jnp.bfloat16),
        twist.astype(np.float32),
        dft.astype(jnp.bfloat16),
    )


def pair_rows(places):
    levels = places.bit_length() - 1

    def holder(residue):
        return rank_of(reverse_bits(residue // 2, levels), places), residue % 2

    mirrors = [None if residue % places == 0 else holder(2 * places - residue) for residue in range(places + 1)]
    return [holder(residue) for residue in range(places + 1)], mirrors


@functools.lru_cache(maxsize=None)
def folded_tables(places, rows, width):
    stride = 2 * places
    bins = stride * rows
    order = np.array([place_of(rank, places) for rank in range(places)])
    residues = np.arange(places + 1)
    angle = 2.0 * np.pi * ((residues[:, None] * order[None, :]) % stride) / stride
    same = np.eye(width)
    first = np.concatenate([np.kron(np.cos(angle), same), np.kron(-np.sin(angle), same)])
    last = first.T / bins
    angle = 2.0 * np.pi * ((residues[:, None] * np.arange(rows)[None, :]) % bins) / bins
    twist = np.stack([np.cos(angle), np.sin(angle)])
    reverse = np.eye(rows)[::-1]
    return first.astype(jnp.bfloat16), last.astype(jnp.bfloat16), twist.astype(np.float32), reverse.astype(jnp.bfloat16)


def hops(places):
    known, apart = [0], 1
    steps = [[0]]
    while apart < places:
        steps.append([apart ^ step for step in known])
        known = known + steps[-1]
        apart *= 2
    return steps


def prepare_kernel(
    features_ref,
    pre_ref,
    gain_ref,
    spectrum_ref,
    squares_ref,
    scaled_ref,
    packed_ref,
    features_in,
    pre_in,
    gain_in,
    spectrum_in,
    squares_out,
    scaled_out,
    packed_out,
    in_sems,
    out_sems,
):
    blocks = [(part, parity) for part in range(2) for parity in range(2)]
    pairs = [(features_ref, features_in), (pre_ref, pre_in), (gain_ref, gain_in)]
    pairs += [(spectrum_ref.at[block], spectrum_in.at[block]) for block in blocks]
    arriving = [pltpu.make_async_copy(*pair, in_sems.at[slot]) for slot, pair in enumerate(pairs)]
    for copy in arriving:
        copy.start()
    leaving = []

    def leave(source, target):
        copy = pltpu.make_async_copy(source, target, out_sems.at[len(leaving)])
        copy.start()
        leaving.append(copy)

    def pack(slot, turned):
        if len(packed_ref.shape) == 4:
            places, width = packed_out.shape[1:3]
            for rank in range(places):
                begin = place_of(rank, places) * width
                packed_out[slot, rank] = turned[begin : begin + width]
            leave(packed_out.at[slot], packed_ref.at[:, slot])
        else:
            packed_out[slot] = turned
            leave(packed_out.at[slot], packed_ref.at[slot])

    for copy in arriving[:3]:
        copy.wait()
    features = features_in[...].astype(F32)
    scaled = (features * gain_in[...] * pre_in[...].astype(F32)).T.astype(BF16)
    scaled_out[...] = scaled
    leave(scaled_out, scaled_ref)
    pack(4, scaled)
    turned = features.T
    squares_out[...] = jnp.sum(turned * turned, axis=0, keepdims=True)
    leave(squares_out, squares_ref)
    for slot, block in enumerate(blocks):
        arriving[3 + slot].wait()
        pack(slot, spectrum_in[block].T.astype(BF16))
    for copy in leaving:
        copy.wait()


def scale_kernel(channels, *refs):
    square_refs, scale_ref = refs[:-1], refs[-1]
    total = square_refs[0][...]
    for square_ref in square_refs[1:]:
        total = total + square_ref[...]
    scale_ref[...] = lax.rsqrt(total / channels + EPS)


def matmul(left, right):
    return jnp.dot(left, right, preferred_element_type=F32)


def twisted(value, factor):
    return (value.reshape(factor.shape[0], -1, value.shape[1]) * factor[:, None, :]).reshape(value.shape)


def folded_kernel(packed_ref, first_ref, last_ref, twist_ref, reverse_ref, dft_ref, *refs):
    scale_refs, (out_ref, scales, left, right, mirror) = refs[:-5], refs[-5:]
    wide, rows = out_ref.shape
    places, width = scales.shape[0], wide // scales.shape[0]
    half = first_ref.shape[0] // 2
    place = lax.axis_index("seq")
    for scale_ref, steps in zip(scale_refs, hops(places)):
        for at, step in enumerate(steps):
            scales[rank_of(place ^ step, places)] = scale_ref[pl.ds(at, 1), :]
    direct, mirrors = pair_rows(places)
    for row, holder in enumerate(mirrors[1:places]):
        for part in range(2):
            mirror[part, pl.ds(row * width, width), :] = packed_ref[holder[0], 2 * part + holder[1]]
    span = 256
    for begin in range(0, rows, span):
        lanes, later = pl.ds(begin, span), pl.ds(rows + begin, span)
        signal = packed_ref[:, 4, :, lanes].astype(F32) * scales[:, :, lanes]
        mixed = matmul(first_ref[...], signal.astype(BF16).reshape(wide, span))
        real, imag = mixed[:half], mixed[half:]
        cos_twist, sin_twist = twist_ref[0, :, lanes], twist_ref[1, :, lanes]
        turned_real = (twisted(real, cos_twist) + twisted(imag, sin_twist)).astype(BF16)
        turned_imag = (twisted(imag, cos_twist) - twisted(real, sin_twist)).astype(BF16)
        left[pl.ds(0, half), lanes] = turned_real
        left[pl.ds(0, half), later] = turned_imag
        left[pl.ds(half, half), lanes] = turned_imag
        left[pl.ds(half, half), later] = -turned_real
    for begin in range(0, rows, span):
        lanes, later = pl.ds(begin, span), pl.ds(rows + begin, span)
        mirrored_real = matmul(mirror[0], reverse_ref[:, lanes])
        mirrored_imag = matmul(mirror[1], reverse_ref[:, lanes])
        mixed = matmul(left[...], dft_ref[:, lanes])
        for residue, holder in enumerate(direct):
            over, under = pl.ds(residue * width, width), pl.ds(half + residue * width, width)
            real = mixed[residue * width : (residue + 1) * width]
            imag = mixed[half + residue * width : half + (residue + 1) * width]
            response_real = packed_ref[holder[0], holder[1], :, lanes].astype(F32)
            response_imag = packed_ref[holder[0], 2 + holder[1], :, lanes].astype(F32)
            if mirrors[residue] is not None:
                response_real = response_real + mirrored_real[(residue - 1) * width : residue * width]
                response_imag = response_imag - mirrored_imag[(residue - 1) * width : residue * width]
            product_real = (real * response_real - imag * response_imag).astype(BF16)
            product_imag = (real * response_imag + imag * response_real).astype(BF16)
            right[over, lanes] = product_real
            right[over, later] = -product_imag
            right[under, lanes] = product_imag
            right[under, later] = product_real
    for begin in range(0, rows, span):
        lanes = pl.ds(begin, span)
        mixed = matmul(right[...], dft_ref[:, lanes])
        real, imag = mixed[:half], mixed[half:]
        cos_twist, sin_twist = twist_ref[0, :, lanes], twist_ref[1, :, lanes]
        turned_real = (twisted(real, cos_twist) - twisted(imag, sin_twist)).astype(BF16)
        turned_imag = (twisted(imag, cos_twist) + twisted(real, sin_twist)).astype(BF16)
        both = jnp.concatenate([turned_real, turned_imag], axis=0)
        out_ref[:, lanes] = matmul(last_ref[...], both).astype(BF16)


def convolve_kernel(packed_ref, first_ref, last_ref, twist_ref, dft_ref, scale_ref, out_ref, left, right):
    wide, rows = out_ref.shape
    half = 2 * wide
    signal = (packed_ref[4].astype(F32) * scale_ref[...]).astype(BF16)
    mixed = matmul(first_ref[...], signal)
    real, imag = mixed[:half], mixed[half:]
    cos_twist, sin_twist = twist_ref[0], twist_ref[1]
    turned_real = (real * cos_twist + imag * sin_twist).astype(BF16)
    turned_imag = (imag * cos_twist - real * sin_twist).astype(BF16)
    left[pl.ds(0, half), pl.ds(0, rows)] = turned_real
    left[pl.ds(0, half), pl.ds(rows, rows)] = turned_imag
    left[pl.ds(half, half), pl.ds(0, rows)] = turned_imag
    left[pl.ds(half, half), pl.ds(rows, rows)] = -turned_real
    mixed = matmul(left[...], dft_ref[...])
    real, imag = mixed[:half], mixed[half:]
    response_real = packed_ref[0:2].reshape(half, rows).astype(F32)
    response_imag = packed_ref[2:4].reshape(half, rows).astype(F32)
    product_real = (real * response_real - imag * response_imag).astype(BF16)
    product_imag = (real * response_imag + imag * response_real).astype(BF16)
    right[pl.ds(0, half), pl.ds(0, rows)] = product_real
    right[pl.ds(0, half), pl.ds(rows, rows)] = -product_imag
    right[pl.ds(half, half), pl.ds(0, rows)] = product_imag
    right[pl.ds(half, half), pl.ds(rows, rows)] = product_real
    mixed = matmul(right[...], dft_ref[...])
    real, imag = mixed[:half], mixed[half:]
    turned_real = (real * cos_twist - imag * sin_twist).astype(BF16)
    turned_imag = (imag * cos_twist + real * sin_twist).astype(BF16)
    both = jnp.concatenate([turned_real, turned_imag], axis=0)
    out_ref[...] = matmul(last_ref[...], both).astype(BF16)


def direct_kernel(scaled_ref, scale_ref, skip_ref, direct_ref):
    signal = (scaled_ref[...].astype(F32) * scale_ref[...]).astype(BF16)
    direct_ref[...] = skip_ref[...].reshape(-1, 1) * signal.astype(F32)


def finish_kernel(conv_ref, direct_ref, post_ref, out_ref):
    conv = conv_ref[...]
    if len(conv_ref.shape) == 3:
        places = conv_ref.shape[0]
        conv = jnp.concatenate([conv_ref[rank_of(place, places)] for place in range(places)])
    turned = conv.astype(F32) + direct_ref[...]
    out_ref[...] = (post_ref[...].astype(F32) * turned.T).astype(BF16)


def call(kernel, out_shape, flops, moved, *operands, limit=VMEM_LIMIT, **options):
    return pl.pallas_call(
        kernel,
        out_shape=out_shape,
        compiler_params=pltpu.CompilerParams(vmem_limit_bytes=limit),
        cost_estimate=pl.CostEstimate(flops=flops, bytes_accessed=moved, transcendentals=0),
        **options,
    )(*operands)


def exchange(value):
    places = lax.axis_size("seq")
    ranks = [[place_of(rank, places) for rank in range(places)]]
    return lax.all_to_all(value, "seq", split_axis=0, concat_axis=0, tiled=True, axis_index_groups=ranks)


def swap(value, axis, apart):
    return lax.ppermute(value, axis, [(place, place ^ apart) for place in range(lax.axis_size(axis))])


def local(features, pre_gate, post_gate, norm_gain, skip_weight, spectrum):
    rows, wide = features.shape
    places = lax.axis_size("seq")
    groups = lax.axis_size("chan")
    width = wide // places
    piled = width % 16 == 0
    first, last, twist, dft = tables(places, rows, width)
    cells = rows * wide
    shape = jax.ShapeDtypeStruct
    vmem, anywhere = pl.BlockSpec(memory_space=pltpu.VMEM), pl.BlockSpec(memory_space=pl.ANY)
    squares, scaled, packed = call(
        prepare_kernel,
        (
            shape((1, rows), F32),
            shape((wide, rows), BF16),
            shape((places, 5, width, rows) if piled else (5, wide, rows), BF16),
        ),
        10 * cells,
        32 * cells,
        features,
        pre_gate,
        norm_gain[None, :],
        spectrum,
        limit=WHOLE_VMEM,
        in_specs=[anywhere] * 4,
        out_specs=(anywhere, anywhere, anywhere),
        scratch_shapes=[
            pltpu.VMEM(features.shape, BF16),
            pltpu.VMEM(pre_gate.shape, BF16),
            pltpu.VMEM((1, wide), F32),
            pltpu.VMEM(spectrum.shape, F32),
            pltpu.VMEM((1, rows), F32),
            pltpu.VMEM((wide, rows), BF16),
            pltpu.VMEM((5, places, width, rows) if piled else (5, wide, rows), BF16),
            pltpu.SemaphoreType.DMA((7,)),
            pltpu.SemaphoreType.DMA((7,)),
        ],
    )
    if not piled:
        order = np.array([place_of(rank, places) for rank in range(places)])
        packed = packed.reshape(5, places, width, rows).transpose(1, 0, 2, 3)[order]
    gathered = exchange(packed)
    others = [swap(squares, "chan", apart) for apart in range(1, groups)]
    scale = call(
        functools.partial(scale_kernel, wide * groups), shape((1, rows), F32), 8 * rows, 32 * rows, squares, *others
    )
    direct = call(
        direct_kernel, shape((wide, rows), F32), 4 * cells, 8 * cells, scaled, scale, skip_weight[None, :]
    )
    if piled:
        scales, apart = [scale], 1
        while apart < places:
            known = jnp.concatenate(scales) if len(scales) > 1 else scale
            scales.append(swap(known, "seq", apart))
            apart *= 2
    else:
        scales = [jnp.repeat(lax.all_gather(scale, "seq", axis=0, tiled=True)[order], width, axis=0)]
        response = gathered[:, :4].reshape(places, 2, 2, width, rows).transpose(1, 0, 2, 3, 4)
        gathered = jnp.concatenate([response.reshape(4, wide, rows), gathered[:, 4].reshape(1, wide, rows)])
    if piled:
        first, last, twist, reverse = folded_tables(places, rows, width)
        constants = [first, last, twist, reverse, dft]
        half = first.shape[0] // 2
        scratch = [
            pltpu.VMEM((places, 1, rows), F32),
            pltpu.VMEM((2 * half, 2 * rows), BF16),
            pltpu.VMEM((2 * half, 2 * rows), BF16),
            pltpu.VMEM((2, half - 2 * width, rows), BF16),
        ]
    else:
        constants = [first, last, np.repeat(twist, width, axis=1), dft]
        scratch = [pltpu.VMEM((4 * wide, 2 * rows), BF16)] * 2
    conv = call(
        folded_kernel if piled else convolve_kernel,
        shape((wide, rows), BF16),
        20 * cells * rows,
        20 * cells,
        gathered,
        *constants,
        *scales,
        scratch_shapes=scratch,
    )
    conv = exchange(conv.reshape(places, width, rows))
    if not piled:
        conv = conv[np.array([rank_of(place, places) for place in range(places)])].reshape(wide, rows)
    return call(finish_kernel, shape((rows, wide), BF16), 10 * cells, 8 * cells, conv, direct, post_gate)


def solution(mesh):
    return jax.shard_map(
        local,
        mesh=mesh,
        in_specs=(
            P("seq", "chan"),
            P("seq", "chan"),
            P("seq", "chan"),
            P("chan"),
            P("chan"),
            P(None, "seq", None, "chan"),
        ),
        out_specs=P("seq", "chan"),
        check_vma=False,
    )
```

```python
import functools

import jax
import jax.numpy as jnp
import numpy as np
from jax import lax
from jax.experimental import pallas as pl
from jax.experimental.pallas import tpu as pltpu
from jax.sharding import PartitionSpec as P

EPS = 1e-06
BF16 = jnp.bfloat16
F32 = jnp.float32
VMEM_LIMIT = 48 * 1024 * 1024
WHOLE_VMEM = 63 * 1024 * 1024 + 512 * 1024


def rank_of(place, places):
    return place * 2 % places + place // (places // 2)


def place_of(rank, places):
    return rank // 2 + rank % 2 * (places // 2)


def reverse_bits(index, levels):
    return sum((index >> bit & 1) << levels - 1 - bit for bit in range(levels))


@functools.lru_cache(maxsize=None)
def tables(places, rows, width):
    levels = places.bit_length() - 1
    stride = 2 * places
    bins = stride * rows
    order = np.array([place_of(rank, places) for rank in range(places)])
    residues = np.array([2 * reverse_bits(place, levels) + parity for place in order for parity in range(2)])
    angle = 2.0 * np.pi * ((residues[:, None] * order[None, :]) % stride) / stride
    same = np.eye(width)
    first = np.concatenate([np.kron(np.cos(angle), same), np.kron(-np.sin(angle), same)])
    last = first.T / bins
    angle = 2.0 * np.pi * ((residues[:, None] * np.arange(rows)[None, :]) % bins) / bins
    twist = np.repeat(np.stack([np.cos(angle), np.sin(angle)]), width, axis=1)
    series = np.arange(rows)
    angle = 2.0 * np.pi * ((series[:, None] * series[None, :]) % rows) / rows
    dft = np.concatenate([np.cos(angle), np.sin(angle)])
    return (
        first.astype(jnp.bfloat16),
        last.astype(jnp.bfloat16),
        twist.astype(np.float32),
        dft.astype(jnp.bfloat16),
    )


def pair_rows(places):
    levels = places.bit_length() - 1

    def holder(residue):
        return rank_of(reverse_bits(residue // 2, levels), places), residue % 2

    mirrors = [None if residue % places == 0 else holder(2 * places - residue) for residue in range(places + 1)]
    return [holder(residue) for residue in range(places + 1)], mirrors


@functools.lru_cache(maxsize=None)
def folded_tables(places, rows, width):
    stride = 2 * places
    bins = stride * rows
    order = np.array([place_of(rank, places) for rank in range(places)])
    residues = np.arange(places + 1)
    angle = 2.0 * np.pi * ((residues[:, None] * order[None, :]) % stride) / stride
    same = np.eye(width)
    first = np.concatenate([np.kron(np.cos(angle), same), np.kron(-np.sin(angle), same)])
    last = first.T / bins
    angle = 2.0 * np.pi * ((residues[:, None] * np.arange(rows)[None, :]) % bins) / bins
    twist = np.stack([np.cos(angle), np.sin(angle)])
    block = rows // 4
    series = np.arange(block)
    angle = 2.0 * np.pi * ((np.arange(4)[:, None] * series[None, :]) % rows) / rows
    spin = np.stack([np.cos(angle), np.sin(angle)])
    angle = 2.0 * np.pi * ((series[:, None] * series[None, :]) % block) / block
    cos, sin = np.cos(angle), np.sin(angle)
    there = np.block([[cos, -sin], [sin, cos]])
    back = np.block([[cos, sin], [-sin, cos]])
    reverse = np.eye(block)[::-1]
    return (
        first.astype(jnp.bfloat16),
        last.astype(jnp.bfloat16),
        twist.astype(np.float32),
        spin.astype(np.float32),
        np.stack([there, back]).astype(jnp.bfloat16),
        reverse.astype(jnp.bfloat16),
    )


def hops(places):
    known, apart = [0], 1
    steps = [[0]]
    while apart < places:
        steps.append([apart ^ step for step in known])
        known = known + steps[-1]
        apart *= 2
    return steps


def prepare_kernel(
    features_ref,
    pre_ref,
    gain_ref,
    skip_ref,
    spectrum_ref,
    squares_ref,
    skipped_ref,
    packed_ref,
    features_in,
    pre_in,
    gain_in,
    skip_in,
    spectrum_in,
    squares_out,
    skipped_out,
    packed_out,
    in_sems,
    out_sems,
):
    blocks = [(part, parity) for part in range(2) for parity in range(2)]
    pairs = [(features_ref, features_in), (pre_ref, pre_in), (gain_ref, gain_in), (skip_ref, skip_in)]
    pairs += [(spectrum_ref.at[block], spectrum_in.at[block]) for block in blocks]
    arriving = [pltpu.make_async_copy(*pair, in_sems.at[slot]) for slot, pair in enumerate(pairs)]
    for copy in arriving:
        copy.start()
    leaving = []

    def leave(source, target):
        copy = pltpu.make_async_copy(source, target, out_sems.at[len(leaving)])
        copy.start()
        leaving.append(copy)

    def pack(slot, turned):
        if len(packed_ref.shape) == 4:
            places, width = packed_out.shape[1:3]
            for rank in range(places):
                begin = place_of(rank, places) * width
                packed_out[slot, rank] = turned[begin : begin + width]
            leave(packed_out.at[slot], packed_ref.at[:, slot])
        else:
            packed_out[slot] = turned
            leave(packed_out.at[slot], packed_ref.at[slot])

    for copy in arriving[:4]:
        copy.wait()
    features = features_in[...].astype(F32)
    scaled = (features * gain_in[...] * pre_in[...].astype(F32)).T
    pack(4, scaled.astype(BF16))
    skipped_out[...] = scaled * skip_in[...].reshape(-1, 1)
    leave(skipped_out, skipped_ref)
    turned = features.T
    squares_out[...] = jnp.sum(turned * turned, axis=0, keepdims=True)
    leave(squares_out, squares_ref)
    for slot, block in enumerate(blocks):
        arriving[4 + slot].wait()
        if len(packed_ref.shape) == 4:
            quarter = spectrum_in.shape[2] // 4
            rows = [spectrum_in[(*block, pl.ds(turn, quarter, stride=4), slice(None))] for turn in range(4)]
            pack(slot, jnp.concatenate([row.T for row in rows], axis=1).astype(BF16))
        else:
            pack(slot, spectrum_in[block].T.astype(BF16))
    for copy in leaving:
        copy.wait()


def scale_kernel(channels, *refs):
    square_refs, scale_ref = refs[:-1], refs[-1]
    total = square_refs[0][...]
    for square_ref in square_refs[1:]:
        total = total + square_ref[...]
    scale_ref[...] = lax.rsqrt(total / channels + EPS)


def matmul(left, right):
    return jnp.dot(left, right, preferred_element_type=F32)


def butterfly(values, direction):
    (real0, imag0), (real1, imag1), (real2, imag2), (real3, imag3) = values
    even, odd = (real0 + real2, imag0 + imag2), (real1 + real3, imag1 + imag3)
    even_gap, odd_gap = (real0 - real2, imag0 - imag2), (real1 - real3, imag1 - imag3)
    lower = (even_gap[0] + odd_gap[1], even_gap[1] - odd_gap[0])
    upper = (even_gap[0] - odd_gap[1], even_gap[1] + odd_gap[0])
    total, gap = (even[0] + odd[0], even[1] + odd[1]), (even[0] - odd[0], even[1] - odd[1])
    return [total, lower, gap, upper] if direction > 0 else [total, upper, gap, lower]


def folded_kernel(packed_ref, first_ref, last_ref, twist_ref, spin_ref, dft_ref, reverse_ref, *refs):
    scale_refs, (out_ref, scales, mirror, mixed, work, both) = refs[:-6], refs[-6:]
    wide, rows = out_ref.shape
    places, width = scales.shape[0], wide // scales.shape[0]
    half, block = first_ref.shape[0] // 2, rows // 4
    inner = half - 2 * width
    place = lax.axis_index("seq")
    for scale_ref, steps in zip(scale_refs, hops(places)):
        for at, step in enumerate(steps):
            scales[rank_of(place ^ step, places)] = scale_ref[pl.ds(at, 1), :]
    direct, mirrors = pair_rows(places)
    quarters = [pl.ds(turn * block, block) for turn in range(4)]
    signal = (packed_ref[:, 4].astype(F32) * scales[...]).astype(BF16).reshape(wide, rows)
    mixed[...] = matmul(first_ref[...], signal)
    for residue in range(places + 1):
        over, under = pl.ds(residue * width, width), pl.ds(half + residue * width, width)
        values = []
        for lanes in quarters:
            real, imag = mixed[over, lanes], mixed[under, lanes]
            cos, sin = twist_ref[0, pl.ds(residue, 1), lanes], twist_ref[1, pl.ds(residue, 1), lanes]
            values.append((real * cos + imag * sin, imag * cos - real * sin))
        for turn, (real, imag) in enumerate(butterfly(values, 1)):
            if turn > 0:
                cos, sin = spin_ref[0, pl.ds(turn, 1), :], spin_ref[1, pl.ds(turn, 1), :]
                real, imag = real * cos + imag * sin, imag * cos - real * sin
            at = pl.ds(turn * half + residue * width, width)
            work[at, pl.ds(0, block)] = real.astype(BF16)
            work[at, pl.ds(block, block)] = imag.astype(BF16)
    for row, holder in enumerate(mirrors[1:places]):
        for part in range(2):
            for turn in range(4):
                at = pl.ds((part * 4 + 3 - turn) * inner + row * width, width)
                mirror[at, :] = packed_ref[holder[0], 2 * part + holder[1], :, quarters[turn]]
    reversed_bins = matmul(mirror[...], reverse_ref[...])
    spectral = matmul(work[...], dft_ref[0])
    for turn in range(4):
        for residue, holder in enumerate(direct):
            at = turn * half + residue * width
            real, imag = spectral[at : at + width, :block], spectral[at : at + width, block:]
            response_real = packed_ref[holder[0], holder[1], :, quarters[turn]].astype(F32)
            response_imag = packed_ref[holder[0], 2 + holder[1], :, quarters[turn]].astype(F32)
            if mirrors[residue] is not None:
                begin = turn * inner + (residue - 1) * width
                response_real = response_real + reversed_bins[begin : begin + width]
                begin = begin + 4 * inner
                response_imag = response_imag - reversed_bins[begin : begin + width]
            work[pl.ds(at, width), pl.ds(0, block)] = (real * response_real - imag * response_imag).astype(BF16)
            work[pl.ds(at, width), pl.ds(block, block)] = (real * response_imag + imag * response_real).astype(BF16)
    restored = matmul(work[...], dft_ref[1])
    for residue in range(places + 1):
        values = []
        for turn in range(4):
            at = turn * half + residue * width
            real, imag = restored[at : at + width, :block], restored[at : at + width, block:]
            if turn > 0:
                cos, sin = spin_ref[0, pl.ds(turn, 1), :], spin_ref[1, pl.ds(turn, 1), :]
                real, imag = real * cos - imag * sin, imag * cos + real * sin
            values.append((real, imag))
        for lanes, (real, imag) in zip(quarters, butterfly(values, -1)):
            cos, sin = twist_ref[0, pl.ds(residue, 1), lanes], twist_ref[1, pl.ds(residue, 1), lanes]
            both[pl.ds(residue * width, width), lanes] = (real * cos - imag * sin).astype(BF16)
            both[pl.ds(half + residue * width, width), lanes] = (imag * cos + real * sin).astype(BF16)
    out_ref[...] = matmul(last_ref[...], both[...]).astype(BF16)


def convolve_kernel(packed_ref, first_ref, last_ref, twist_ref, dft_ref, scale_ref, out_ref, left, right):
    wide, rows = out_ref.shape
    half = 2 * wide
    signal = (packed_ref[4].astype(F32) * scale_ref[...]).astype(BF16)
    mixed = matmul(first_ref[...], signal)
    real, imag = mixed[:half], mixed[half:]
    cos_twist, sin_twist = twist_ref[0], twist_ref[1]
    turned_real = (real * cos_twist + imag * sin_twist).astype(BF16)
    turned_imag = (imag * cos_twist - real * sin_twist).astype(BF16)
    left[pl.ds(0, half), pl.ds(0, rows)] = turned_real
    left[pl.ds(0, half), pl.ds(rows, rows)] = turned_imag
    left[pl.ds(half, half), pl.ds(0, rows)] = turned_imag
    left[pl.ds(half, half), pl.ds(rows, rows)] = -turned_real
    mixed = matmul(left[...], dft_ref[...])
    real, imag = mixed[:half], mixed[half:]
    response_real = packed_ref[0:2].reshape(half, rows).astype(F32)
    response_imag = packed_ref[2:4].reshape(half, rows).astype(F32)
    product_real = (real * response_real - imag * response_imag).astype(BF16)
    product_imag = (real * response_imag + imag * response_real).astype(BF16)
    right[pl.ds(0, half), pl.ds(0, rows)] = product_real
    right[pl.ds(0, half), pl.ds(rows, rows)] = -product_imag
    right[pl.ds(half, half), pl.ds(0, rows)] = product_imag
    right[pl.ds(half, half), pl.ds(rows, rows)] = product_real
    mixed = matmul(right[...], dft_ref[...])
    real, imag = mixed[:half], mixed[half:]
    turned_real = (real * cos_twist - imag * sin_twist).astype(BF16)
    turned_imag = (imag * cos_twist + real * sin_twist).astype(BF16)
    both = jnp.concatenate([turned_real, turned_imag], axis=0)
    out_ref[...] = matmul(last_ref[...], both).astype(BF16)


def finish_kernel(conv_ref, skipped_ref, scale_ref, post_ref, out_ref):
    conv = conv_ref[...]
    if len(conv_ref.shape) == 3:
        places = conv_ref.shape[0]
        conv = jnp.concatenate([conv_ref[rank_of(place, places)] for place in range(places)])
    turned = conv.astype(F32) + skipped_ref[...] * scale_ref[...]
    out_ref[...] = (post_ref[...].astype(F32) * turned.T).astype(BF16)


def call(kernel, out_shape, flops, moved, *operands, limit=VMEM_LIMIT, **options):
    return pl.pallas_call(
        kernel,
        out_shape=out_shape,
        compiler_params=pltpu.CompilerParams(vmem_limit_bytes=limit),
        cost_estimate=pl.CostEstimate(flops=flops, bytes_accessed=moved, transcendentals=0),
        **options,
    )(*operands)


def exchange(value):
    places = lax.axis_size("seq")
    ranks = [[place_of(rank, places) for rank in range(places)]]
    return lax.all_to_all(value, "seq", split_axis=0, concat_axis=0, tiled=True, axis_index_groups=ranks)


def swap(value, axis, apart):
    return lax.ppermute(value, axis, [(place, place ^ apart) for place in range(lax.axis_size(axis))])


def local(features, pre_gate, post_gate, norm_gain, skip_weight, spectrum):
    rows, wide = features.shape
    places = lax.axis_size("seq")
    groups = lax.axis_size("chan")
    width = wide // places
    piled = width % 16 == 0
    cells = rows * wide
    shape = jax.ShapeDtypeStruct
    vmem, anywhere = pl.BlockSpec(memory_space=pltpu.VMEM), pl.BlockSpec(memory_space=pl.ANY)
    squares, skipped, packed = call(
        prepare_kernel,
        (
            shape((1, rows), F32),
            shape((wide, rows), F32),
            shape((places, 5, width, rows) if piled else (5, wide, rows), BF16),
        ),
        10 * cells,
        32 * cells,
        features,
        pre_gate,
        norm_gain[None, :],
        skip_weight[None, :],
        spectrum,
        limit=WHOLE_VMEM,
        in_specs=[anywhere] * 5,
        out_specs=(anywhere, anywhere, anywhere),
        scratch_shapes=[
            pltpu.VMEM(features.shape, BF16),
            pltpu.VMEM(pre_gate.shape, BF16),
            pltpu.VMEM((1, wide), F32),
            pltpu.VMEM((1, wide), F32),
            pltpu.VMEM(spectrum.shape, F32),
            pltpu.VMEM((1, rows), F32),
            pltpu.VMEM((wide, rows), F32),
            pltpu.VMEM((5, places, width, rows) if piled else (5, wide, rows), BF16),
            pltpu.SemaphoreType.DMA((8,)),
            pltpu.SemaphoreType.DMA((7,)),
        ],
    )
    if not piled:
        order = np.array([place_of(rank, places) for rank in range(places)])
        packed = packed.reshape(5, places, width, rows).transpose(1, 0, 2, 3)[order]
    gathered = exchange(packed)
    others = [swap(squares, "chan", apart) for apart in range(1, groups)]
    scale = call(
        functools.partial(scale_kernel, wide * groups), shape((1, rows), F32), 8 * rows, 32 * rows, squares, *others
    )
    if piled:
        scales, apart = [scale], 1
        while apart < places:
            known = jnp.concatenate(scales) if len(scales) > 1 else scale
            scales.append(swap(known, "seq", apart))
            apart *= 2
    else:
        scales = [jnp.repeat(lax.all_gather(scale, "seq", axis=0, tiled=True)[order], width, axis=0)]
        response = gathered[:, :4].reshape(places, 2, 2, width, rows).transpose(1, 0, 2, 3, 4)
        gathered = jnp.concatenate([response.reshape(4, wide, rows), gathered[:, 4].reshape(1, wide, rows)])
    if piled:
        constants = folded_tables(places, rows, width)
        half = constants[0].shape[0] // 2
        scratch = [
            pltpu.VMEM((places, 1, rows), F32),
            pltpu.VMEM((8 * (half - 2 * width), rows // 4), BF16),
            pltpu.VMEM((2 * half, rows), F32),
            pltpu.VMEM((4 * half, rows // 2), BF16),
            pltpu.VMEM((2 * half, rows), BF16),
        ]
    else:
        constants = tables(places, rows, width)
        scratch = [pltpu.VMEM((4 * wide, 2 * rows), BF16)] * 2
    conv = call(
        folded_kernel if piled else convolve_kernel,
        shape((wide, rows), BF16),
        20 * cells * rows,
        20 * cells,
        gathered,
        *constants,
        *scales,
        scratch_shapes=scratch,
    )
    conv = exchange(conv.reshape(places, width, rows))
    if not piled:
        conv = conv[np.array([rank_of(place, places) for place in range(places)])].reshape(wide, rows)
    return call(finish_kernel, shape((rows, wide), BF16), 10 * cells, 8 * cells, conv, skipped, scale, post_gate)


def solution(mesh):
    return jax.shard_map(
        local,
        mesh=mesh,
        in_specs=(
            P("seq", "chan"),
            P("seq", "chan"),
            P("seq", "chan"),
            P("chan"),
            P("chan"),
            P(None, "seq", None, "chan"),
        ),
        out_specs=P("seq", "chan"),
        check_vma=False,
    )
```

```python
import functools

import jax
import jax.numpy as jnp
import numpy as np
from jax import lax
from jax.experimental import pallas as pl
from jax.experimental.pallas import tpu as pltpu
from jax.sharding import PartitionSpec as P

EPS = 1e-06
BF16 = jnp.bfloat16
F32 = jnp.float32
VMEM_LIMIT = 48 * 1024 * 1024
WHOLE_VMEM = 63 * 1024 * 1024 + 512 * 1024


def reverse_bits(index, levels):
    return sum((index >> bit & 1) << levels - 1 - bit for bit in range(levels))


@functools.lru_cache(maxsize=None)
def tables(places, rows, width):
    levels = places.bit_length() - 1
    stride = 2 * places
    bins = stride * rows
    residues = np.array([2 * reverse_bits(place, levels) + parity for place in range(places) for parity in range(2)])
    angle = 2.0 * np.pi * ((residues[:, None] * np.arange(places)[None, :]) % stride) / stride
    same = np.eye(width)
    first = np.concatenate([np.kron(np.cos(angle), same), np.kron(-np.sin(angle), same)])
    last = first.T / bins
    angle = 2.0 * np.pi * ((residues[:, None] * np.arange(rows)[None, :]) % bins) / bins
    twist = np.repeat(np.stack([np.cos(angle), np.sin(angle)]), width, axis=1)
    series = np.arange(rows)
    angle = 2.0 * np.pi * ((series[:, None] * series[None, :]) % rows) / rows
    dft = np.concatenate([np.cos(angle), np.sin(angle)])
    return (
        first.astype(jnp.bfloat16),
        last.astype(jnp.bfloat16),
        twist.astype(np.float32),
        dft.astype(jnp.bfloat16),
    )


def pair_rows(places):
    levels = places.bit_length() - 1

    def holder(residue):
        return reverse_bits(residue // 2, levels), residue % 2

    mirrors = [None if residue % places == 0 else holder(2 * places - residue) for residue in range(places + 1)]
    return [holder(residue) for residue in range(places + 1)], mirrors


@functools.lru_cache(maxsize=None)
def folded_tables(places, rows, width):
    stride = 2 * places
    bins = stride * rows
    residues = np.arange(places + 1)
    angle = 2.0 * np.pi * ((residues[:, None] * np.arange(places)[None, :]) % stride) / stride
    same = np.eye(width)
    first = np.concatenate([np.kron(np.cos(angle), same), np.kron(-np.sin(angle), same)])
    last = first.T / bins
    angle = 2.0 * np.pi * ((residues[:, None] * np.arange(rows)[None, :]) % bins) / bins
    twist = np.stack([np.cos(angle), np.sin(angle)])
    block = rows // 4
    series = np.arange(block)
    angle = 2.0 * np.pi * ((np.arange(4)[:, None] * series[None, :]) % rows) / rows
    spin = np.stack([np.cos(angle), np.sin(angle)])
    angle = 2.0 * np.pi * ((series[:, None] * series[None, :]) % block) / block
    cos, sin = np.cos(angle), np.sin(angle)
    there = np.block([[cos, -sin], [sin, cos]])
    back = np.block([[cos, sin], [-sin, cos]])
    reverse = np.eye(block)[::-1]
    return (
        first.astype(jnp.bfloat16),
        last.astype(jnp.bfloat16),
        twist.astype(np.float32),
        spin.astype(np.float32),
        np.stack([there, back]).astype(jnp.bfloat16),
        reverse.astype(jnp.bfloat16),
    )


def hops(places):
    known, apart = [0], 1
    steps = [[0]]
    while apart < places:
        steps.append([apart ^ step for step in known])
        known = known + steps[-1]
        apart *= 2
    return steps


def prepare_kernel(
    features_ref,
    pre_ref,
    gain_ref,
    skip_ref,
    spectrum_ref,
    squares_ref,
    skipped_ref,
    packed_ref,
    features_in,
    pre_in,
    gain_in,
    skip_in,
    spectrum_in,
    squares_out,
    skipped_out,
    packed_out,
    in_sems,
    out_sems,
):
    blocks = [(part, parity) for part in range(2) for parity in range(2)]
    pairs = [(features_ref, features_in), (pre_ref, pre_in), (gain_ref, gain_in), (skip_ref, skip_in)]
    pairs += [(spectrum_ref.at[block], spectrum_in.at[block]) for block in blocks]
    arriving = [pltpu.make_async_copy(*pair, in_sems.at[slot]) for slot, pair in enumerate(pairs)]
    for copy in arriving:
        copy.start()
    leaving = []

    def leave(source, target):
        copy = pltpu.make_async_copy(source, target, out_sems.at[len(leaving)])
        copy.start()
        leaving.append(copy)

    def pack(slot, turned):
        if len(packed_ref.shape) == 4:
            packed_out[slot] = turned.reshape(packed_out.shape[1:])
            leave(packed_out.at[slot], packed_ref.at[:, slot])
        else:
            packed_out[slot] = turned
            leave(packed_out.at[slot], packed_ref.at[slot])

    for copy in arriving[:4]:
        copy.wait()
    features = features_in[...].astype(F32)
    scaled = (features * gain_in[...] * pre_in[...].astype(F32)).T
    pack(4, scaled.astype(BF16))
    skipped_out[...] = scaled * skip_in[...].reshape(-1, 1)
    leave(skipped_out, skipped_ref)
    turned = features.T
    squares_out[...] = jnp.sum(turned * turned, axis=0, keepdims=True)
    leave(squares_out, squares_ref)
    for slot, block in enumerate(blocks):
        arriving[4 + slot].wait()
        if len(packed_ref.shape) == 4:
            quarter = spectrum_in.shape[2] // 4
            rows = [spectrum_in[(*block, pl.ds(turn, quarter, stride=4), slice(None))] for turn in range(4)]
            pack(slot, jnp.concatenate([row.T for row in rows], axis=1).astype(BF16))
        else:
            pack(slot, spectrum_in[block].T.astype(BF16))
    for copy in leaving:
        copy.wait()


def scale_kernel(channels, *refs):
    square_refs, scale_ref = refs[:-1], refs[-1]
    total = square_refs[0][...]
    for square_ref in square_refs[1:]:
        total = total + square_ref[...]
    scale_ref[...] = lax.rsqrt(total / channels + EPS)


def matmul(left, right):
    return jnp.dot(left, right, preferred_element_type=F32)


def butterfly(values, direction):
    (real0, imag0), (real1, imag1), (real2, imag2), (real3, imag3) = values
    even, odd = (real0 + real2, imag0 + imag2), (real1 + real3, imag1 + imag3)
    even_gap, odd_gap = (real0 - real2, imag0 - imag2), (real1 - real3, imag1 - imag3)
    lower = (even_gap[0] + odd_gap[1], even_gap[1] - odd_gap[0])
    upper = (even_gap[0] - odd_gap[1], even_gap[1] + odd_gap[0])
    total, gap = (even[0] + odd[0], even[1] + odd[1]), (even[0] - odd[0], even[1] - odd[1])
    return [total, lower, gap, upper] if direction > 0 else [total, upper, gap, lower]


def folded_kernel(packed_ref, first_ref, last_ref, twist_ref, spin_ref, dft_ref, reverse_ref, *refs):
    scale_refs, (out_ref, scales, mirror, mixed, work, both) = refs[:-6], refs[-6:]
    wide, rows = out_ref.shape
    places, width = scales.shape[0], wide // scales.shape[0]
    half, block = first_ref.shape[0] // 2, rows // 4
    inner = half - 2 * width
    place = lax.axis_index("seq")
    for scale_ref, steps in zip(scale_refs, hops(places)):
        for at, step in enumerate(steps):
            scales[place ^ step] = scale_ref[pl.ds(at, 1), :]
    direct, mirrors = pair_rows(places)
    quarters = [pl.ds(turn * block, block) for turn in range(4)]
    signal = (packed_ref[:, 4].astype(F32) * scales[...]).astype(BF16).reshape(wide, rows)
    mixed[...] = matmul(first_ref[...], signal)
    for residue in range(places + 1):
        over, under = pl.ds(residue * width, width), pl.ds(half + residue * width, width)
        values = []
        for lanes in quarters:
            real, imag = mixed[over, lanes], mixed[under, lanes]
            cos, sin = twist_ref[0, pl.ds(residue, 1), lanes], twist_ref[1, pl.ds(residue, 1), lanes]
            values.append((real * cos + imag * sin, imag * cos - real * sin))
        for turn, (real, imag) in enumerate(butterfly(values, 1)):
            if turn > 0:
                cos, sin = spin_ref[0, pl.ds(turn, 1), :], spin_ref[1, pl.ds(turn, 1), :]
                real, imag = real * cos + imag * sin, imag * cos - real * sin
            at = pl.ds(turn * half + residue * width, width)
            work[at, pl.ds(0, block)] = real.astype(BF16)
            work[at, pl.ds(block, block)] = imag.astype(BF16)
    for row, holder in enumerate(mirrors[1:places]):
        for part in range(2):
            for turn in range(4):
                at = pl.ds((part * 4 + 3 - turn) * inner + row * width, width)
                mirror[at, :] = packed_ref[holder[0], 2 * part + holder[1], :, quarters[turn]]
    reversed_bins = matmul(mirror[...], reverse_ref[...])
    spectral = matmul(work[...], dft_ref[0])
    for turn in range(4):
        for residue, holder in enumerate(direct):
            at = turn * half + residue * width
            real, imag = spectral[at : at + width, :block], spectral[at : at + width, block:]
            response_real = packed_ref[holder[0], holder[1], :, quarters[turn]].astype(F32)
            response_imag = packed_ref[holder[0], 2 + holder[1], :, quarters[turn]].astype(F32)
            if mirrors[residue] is not None:
                begin = turn * inner + (residue - 1) * width
                response_real = response_real + reversed_bins[begin : begin + width]
                begin = begin + 4 * inner
                response_imag = response_imag - reversed_bins[begin : begin + width]
            work[pl.ds(at, width), pl.ds(0, block)] = (real * response_real - imag * response_imag).astype(BF16)
            work[pl.ds(at, width), pl.ds(block, block)] = (real * response_imag + imag * response_real).astype(BF16)
    restored = matmul(work[...], dft_ref[1])
    for residue in range(places + 1):
        values = []
        for turn in range(4):
            at = turn * half + residue * width
            real, imag = restored[at : at + width, :block], restored[at : at + width, block:]
            if turn > 0:
                cos, sin = spin_ref[0, pl.ds(turn, 1), :], spin_ref[1, pl.ds(turn, 1), :]
                real, imag = real * cos - imag * sin, imag * cos + real * sin
            values.append((real, imag))
        for lanes, (real, imag) in zip(quarters, butterfly(values, -1)):
            cos, sin = twist_ref[0, pl.ds(residue, 1), lanes], twist_ref[1, pl.ds(residue, 1), lanes]
            both[pl.ds(residue * width, width), lanes] = (real * cos - imag * sin).astype(BF16)
            both[pl.ds(half + residue * width, width), lanes] = (imag * cos + real * sin).astype(BF16)
    out_ref[...] = matmul(last_ref[...], both[...]).astype(BF16)


def convolve_kernel(packed_ref, first_ref, last_ref, twist_ref, dft_ref, scale_ref, out_ref, left, right):
    wide, rows = out_ref.shape
    half = 2 * wide
    signal = (packed_ref[4].astype(F32) * scale_ref[...]).astype(BF16)
    mixed = matmul(first_ref[...], signal)
    real, imag = mixed[:half], mixed[half:]
    cos_twist, sin_twist = twist_ref[0], twist_ref[1]
    turned_real = (real * cos_twist + imag * sin_twist).astype(BF16)
    turned_imag = (imag * cos_twist - real * sin_twist).astype(BF16)
    left[pl.ds(0, half), pl.ds(0, rows)] = turned_real
    left[pl.ds(0, half), pl.ds(rows, rows)] = turned_imag
    left[pl.ds(half, half), pl.ds(0, rows)] = turned_imag
    left[pl.ds(half, half), pl.ds(rows, rows)] = -turned_real
    mixed = matmul(left[...], dft_ref[...])
    real, imag = mixed[:half], mixed[half:]
    response_real = packed_ref[0:2].reshape(half, rows).astype(F32)
    response_imag = packed_ref[2:4].reshape(half, rows).astype(F32)
    product_real = (real * response_real - imag * response_imag).astype(BF16)
    product_imag = (real * response_imag + imag * response_real).astype(BF16)
    right[pl.ds(0, half), pl.ds(0, rows)] = product_real
    right[pl.ds(0, half), pl.ds(rows, rows)] = -product_imag
    right[pl.ds(half, half), pl.ds(0, rows)] = product_imag
    right[pl.ds(half, half), pl.ds(rows, rows)] = product_real
    mixed = matmul(right[...], dft_ref[...])
    real, imag = mixed[:half], mixed[half:]
    turned_real = (real * cos_twist - imag * sin_twist).astype(BF16)
    turned_imag = (imag * cos_twist + real * sin_twist).astype(BF16)
    both = jnp.concatenate([turned_real, turned_imag], axis=0)
    out_ref[...] = matmul(last_ref[...], both).astype(BF16)


def finish_kernel(conv_ref, skipped_ref, scale_ref, post_ref, out_ref):
    turned = conv_ref[...].astype(F32) + skipped_ref[...] * scale_ref[...]
    out_ref[...] = (post_ref[...].astype(F32) * turned.T).astype(BF16)


def call(kernel, out_shape, flops, moved, *operands, limit=VMEM_LIMIT, **options):
    return pl.pallas_call(
        kernel,
        out_shape=out_shape,
        compiler_params=pltpu.CompilerParams(vmem_limit_bytes=limit),
        cost_estimate=pl.CostEstimate(flops=flops, bytes_accessed=moved, transcendentals=0),
        **options,
    )(*operands)


def exchange(value):
    return lax.all_to_all(value, "seq", split_axis=0, concat_axis=0, tiled=True)


def swap(value, axis, apart):
    return lax.ppermute(value, axis, [(place, place ^ apart) for place in range(lax.axis_size(axis))])


def local(features, pre_gate, post_gate, norm_gain, skip_weight, spectrum):
    rows, wide = features.shape
    places = lax.axis_size("seq")
    groups = lax.axis_size("chan")
    width = wide // places
    piled = width % 16 == 0
    cells = rows * wide
    shape = jax.ShapeDtypeStruct
    vmem, anywhere = pl.BlockSpec(memory_space=pltpu.VMEM), pl.BlockSpec(memory_space=pl.ANY)
    squares, skipped, packed = call(
        prepare_kernel,
        (
            shape((1, rows), F32),
            shape((wide, rows), F32),
            shape((places, 5, width, rows) if piled else (5, wide, rows), BF16),
        ),
        10 * cells,
        32 * cells,
        features,
        pre_gate,
        norm_gain[None, :],
        skip_weight[None, :],
        spectrum,
        limit=WHOLE_VMEM,
        in_specs=[anywhere] * 5,
        out_specs=(anywhere, anywhere, anywhere),
        scratch_shapes=[
            pltpu.VMEM(features.shape, BF16),
            pltpu.VMEM(pre_gate.shape, BF16),
            pltpu.VMEM((1, wide), F32),
            pltpu.VMEM((1, wide), F32),
            pltpu.VMEM(spectrum.shape, F32),
            pltpu.VMEM((1, rows), F32),
            pltpu.VMEM((wide, rows), F32),
            pltpu.VMEM((5, places, width, rows) if piled else (5, wide, rows), BF16),
            pltpu.SemaphoreType.DMA((8,)),
            pltpu.SemaphoreType.DMA((7,)),
        ],
    )
    if not piled:
        packed = packed.reshape(5, places, width, rows).transpose(1, 0, 2, 3)
    gathered = exchange(packed)
    others = [swap(squares, "chan", apart) for apart in range(1, groups)]
    scale = call(
        functools.partial(scale_kernel, wide * groups), shape((1, rows), F32), 8 * rows, 32 * rows, squares, *others
    )
    if piled:
        scales, apart = [scale], 1
        while apart < places:
            known = jnp.concatenate(scales) if len(scales) > 1 else scale
            scales.append(swap(known, "seq", apart))
            apart *= 2
    else:
        scales = [jnp.repeat(lax.all_gather(scale, "seq", axis=0, tiled=True), width, axis=0)]
        response = gathered[:, :4].reshape(places, 2, 2, width, rows).transpose(1, 0, 2, 3, 4)
        gathered = jnp.concatenate([response.reshape(4, wide, rows), gathered[:, 4].reshape(1, wide, rows)])
    if piled:
        constants = folded_tables(places, rows, width)
        half = constants[0].shape[0] // 2
        scratch = [
            pltpu.VMEM((places, 1, rows), F32),
            pltpu.VMEM((8 * (half - 2 * width), rows // 4), BF16),
            pltpu.VMEM((2 * half, rows), F32),
            pltpu.VMEM((4 * half, rows // 2), BF16),
            pltpu.VMEM((2 * half, rows), BF16),
        ]
    else:
        constants = tables(places, rows, width)
        scratch = [pltpu.VMEM((4 * wide, 2 * rows), BF16)] * 2
    conv = call(
        folded_kernel if piled else convolve_kernel,
        shape((wide, rows), BF16),
        20 * cells * rows,
        20 * cells,
        gathered,
        *constants,
        *scales,
        scratch_shapes=scratch,
    )
    conv = exchange(conv.reshape(places, width, rows)).reshape(wide, rows)
    return call(finish_kernel, shape((rows, wide), BF16), 10 * cells, 8 * cells, conv, skipped, scale, post_gate)


def solution(mesh):
    return jax.shard_map(
        local,
        mesh=mesh,
        in_specs=(
            P("seq", "chan"),
            P("seq", "chan"),
            P("seq", "chan"),
            P("chan"),
            P("chan"),
            P(None, "seq", None, "chan"),
        ),
        out_specs=P("seq", "chan"),
        check_vma=False,
    )
```

```python
import functools

import jax
import jax.numpy as jnp
import numpy as np
from jax import lax
from jax.experimental import pallas as pl
from jax.experimental.pallas import tpu as pltpu
from jax.sharding import PartitionSpec as P

EPS = 1e-06
BF16 = jnp.bfloat16
F32 = jnp.float32
VMEM_LIMIT = 48 * 1024 * 1024
WHOLE_VMEM = 63 * 1024 * 1024 + 512 * 1024


def reverse_bits(index, levels):
    return sum((index >> bit & 1) << levels - 1 - bit for bit in range(levels))


@functools.lru_cache(maxsize=None)
def tables(places, rows, width):
    levels = places.bit_length() - 1
    stride = 2 * places
    bins = stride * rows
    residues = np.array([2 * reverse_bits(place, levels) + parity for place in range(places) for parity in range(2)])
    angle = 2.0 * np.pi * ((residues[:, None] * np.arange(places)[None, :]) % stride) / stride
    same = np.eye(width)
    first = np.concatenate([np.kron(np.cos(angle), same), np.kron(-np.sin(angle), same)])
    last = first.T / bins
    angle = 2.0 * np.pi * ((residues[:, None] * np.arange(rows)[None, :]) % bins) / bins
    twist = np.repeat(np.stack([np.cos(angle), np.sin(angle)]), width, axis=1)
    series = np.arange(rows)
    angle = 2.0 * np.pi * ((series[:, None] * series[None, :]) % rows) / rows
    dft = np.concatenate([np.cos(angle), np.sin(angle)])
    return (
        first.astype(jnp.bfloat16),
        last.astype(jnp.bfloat16),
        twist.astype(np.float32),
        dft.astype(jnp.bfloat16),
    )


def pair_rows(places):
    levels = places.bit_length() - 1

    def holder(residue):
        return reverse_bits(residue // 2, levels), residue % 2

    mirrors = [None if residue % places == 0 else holder(2 * places - residue) for residue in range(places + 1)]
    return [holder(residue) for residue in range(places + 1)], mirrors


@functools.lru_cache(maxsize=None)
def folded_tables(places, rows, width):
    stride = 2 * places
    bins = stride * rows
    residues = np.arange(places + 1)
    angle = 2.0 * np.pi * ((residues[:, None] * np.arange(places)[None, :]) % stride) / stride
    same = np.eye(width)
    first = np.concatenate([np.kron(np.cos(angle), same), np.kron(-np.sin(angle), same)])
    last = first.T / bins
    angle = 2.0 * np.pi * ((residues[:, None] * np.arange(rows)[None, :]) % bins) / bins
    twist = np.stack([np.cos(angle), np.sin(angle)])
    block = rows // 4
    series = np.arange(block)
    angle = 2.0 * np.pi * ((np.arange(4)[:, None] * series[None, :]) % rows) / rows
    spin = np.stack([np.cos(angle), np.sin(angle)])
    angle = 2.0 * np.pi * ((series[:, None] * series[None, :]) % block) / block
    cos, sin = np.cos(angle), np.sin(angle)
    there = np.block([[cos, -sin], [sin, cos]])
    back = np.block([[cos, sin], [-sin, cos]])
    reverse = np.eye(block)[::-1]
    return (
        first.astype(jnp.bfloat16),
        last.astype(jnp.bfloat16),
        twist.astype(np.float32),
        spin.astype(np.float32),
        np.stack([there, back]).astype(jnp.bfloat16),
        reverse.astype(jnp.bfloat16),
    )


def hops(places):
    known, apart = [0, places // 2], 1
    steps = [known]
    while apart < places // 2:
        steps.append([apart ^ step for step in known])
        known = known + steps[-1]
        apart *= 2
    return steps


def squares_kernel(features_ref, squares_ref):
    turned = features_ref[...].astype(F32).T
    squares_ref[...] = jnp.sum(turned * turned, axis=0, keepdims=True)


def prepare_kernel(
    features_ref,
    pre_ref,
    gain_ref,
    skip_ref,
    spectrum_ref,
    skipped_ref,
    packed_ref,
    features_in,
    pre_in,
    gain_in,
    skip_in,
    spectrum_in,
    skipped_out,
    packed_out,
    in_sems,
    out_sems,
):
    blocks = [(part, parity) for part in range(2) for parity in range(2)]
    pairs = [(features_ref, features_in), (pre_ref, pre_in), (gain_ref, gain_in), (skip_ref, skip_in)]
    pairs += [(spectrum_ref.at[block], spectrum_in.at[block]) for block in blocks]
    arriving = [pltpu.make_async_copy(*pair, in_sems.at[slot]) for slot, pair in enumerate(pairs)]
    for copy in arriving:
        copy.start()
    leaving = []

    def leave(source, target):
        copy = pltpu.make_async_copy(source, target, out_sems.at[len(leaving)])
        copy.start()
        leaving.append(copy)

    def pack(slot, turned):
        if len(packed_ref.shape) == 4:
            packed_out[slot] = turned.reshape(packed_out.shape[1:])
            leave(packed_out.at[slot], packed_ref.at[:, slot])
        else:
            packed_out[slot] = turned
            leave(packed_out.at[slot], packed_ref.at[slot])

    for copy in arriving[:4]:
        copy.wait()
    features = features_in[...].astype(F32)
    scaled = (features * gain_in[...] * pre_in[...].astype(F32)).T
    pack(4, scaled.astype(BF16))
    skipped_out[...] = scaled * skip_in[...].reshape(-1, 1)
    leave(skipped_out, skipped_ref)
    for slot, block in enumerate(blocks):
        arriving[4 + slot].wait()
        if len(packed_ref.shape) == 4:
            quarter = spectrum_in.shape[2] // 4
            rows = [spectrum_in[(*block, pl.ds(turn, quarter, stride=4), slice(None))] for turn in range(4)]
            pack(slot, jnp.concatenate([row.T for row in rows], axis=1).astype(BF16))
        else:
            pack(slot, spectrum_in[block].T.astype(BF16))
    for copy in leaving:
        copy.wait()


def join_kernel(packed_ref, own_ref, far_ref, out_ref, squares_ref):
    del packed_ref, out_ref
    squares_ref[pl.ds(0, 1), :] = own_ref[...]
    squares_ref[pl.ds(1, 1), :] = far_ref[...]


def scale_kernel(channels, *refs):
    square_refs, scale_ref = refs[:-1], refs[-1]
    total = square_refs[0][...]
    for square_ref in square_refs[1:]:
        total = total + square_ref[...]
    scale_ref[...] = lax.rsqrt(total / channels + EPS)


def matmul(left, right):
    return jnp.dot(left, right, preferred_element_type=F32)


def butterfly(values, direction):
    (real0, imag0), (real1, imag1), (real2, imag2), (real3, imag3) = values
    even, odd = (real0 + real2, imag0 + imag2), (real1 + real3, imag1 + imag3)
    even_gap, odd_gap = (real0 - real2, imag0 - imag2), (real1 - real3, imag1 - imag3)
    lower = (even_gap[0] + odd_gap[1], even_gap[1] - odd_gap[0])
    upper = (even_gap[0] - odd_gap[1], even_gap[1] + odd_gap[0])
    total, gap = (even[0] + odd[0], even[1] + odd[1]), (even[0] - odd[0], even[1] - odd[1])
    return [total, lower, gap, upper] if direction > 0 else [total, upper, gap, lower]


def folded_kernel(packed_ref, first_ref, last_ref, twist_ref, spin_ref, dft_ref, reverse_ref, *refs):
    scale_refs, (out_ref, scales, mirror, mixed, work, both) = refs[:-6], refs[-6:]
    wide, rows = out_ref.shape
    places, width = scales.shape[0], wide // scales.shape[0]
    half, block = first_ref.shape[0] // 2, rows // 4
    inner = half - 2 * width
    place = lax.axis_index("seq")
    for scale_ref, steps in zip(scale_refs, hops(places)):
        for at, step in enumerate(steps):
            scales[place ^ step] = scale_ref[pl.ds(at, 1), :]
    direct, mirrors = pair_rows(places)
    quarters = [pl.ds(turn * block, block) for turn in range(4)]
    signal = (packed_ref[:, 4].astype(F32) * scales[...]).astype(BF16).reshape(wide, rows)
    mixed[...] = matmul(first_ref[...], signal)
    for residue in range(places + 1):
        over, under = pl.ds(residue * width, width), pl.ds(half + residue * width, width)
        values = []
        for lanes in quarters:
            real, imag = mixed[over, lanes], mixed[under, lanes]
            cos, sin = twist_ref[0, pl.ds(residue, 1), lanes], twist_ref[1, pl.ds(residue, 1), lanes]
            values.append((real * cos + imag * sin, imag * cos - real * sin))
        for turn, (real, imag) in enumerate(butterfly(values, 1)):
            if turn > 0:
                cos, sin = spin_ref[0, pl.ds(turn, 1), :], spin_ref[1, pl.ds(turn, 1), :]
                real, imag = real * cos + imag * sin, imag * cos - real * sin
            at = pl.ds(turn * half + residue * width, width)
            work[at, pl.ds(0, block)] = real.astype(BF16)
            work[at, pl.ds(block, block)] = imag.astype(BF16)
    for row, holder in enumerate(mirrors[1:places]):
        for part in range(2):
            for turn in range(4):
                at = pl.ds((part * 4 + 3 - turn) * inner + row * width, width)
                mirror[at, :] = packed_ref[holder[0], 2 * part + holder[1], :, quarters[turn]]
    reversed_bins = matmul(mirror[...], reverse_ref[...])
    spectral = matmul(work[...], dft_ref[0])
    for turn in range(4):
        for residue, holder in enumerate(direct):
            at = turn * half + residue * width
            real, imag = spectral[at : at + width, :block], spectral[at : at + width, block:]
            response_real = packed_ref[holder[0], holder[1], :, quarters[turn]].astype(F32)
            response_imag = packed_ref[holder[0], 2 + holder[1], :, quarters[turn]].astype(F32)
            if mirrors[residue] is not None:
                begin = turn * inner + (residue - 1) * width
                response_real = response_real + reversed_bins[begin : begin + width]
                begin = begin + 4 * inner
                response_imag = response_imag - reversed_bins[begin : begin + width]
            work[pl.ds(at, width), pl.ds(0, block)] = (real * response_real - imag * response_imag).astype(BF16)
            work[pl.ds(at, width), pl.ds(block, block)] = (real * response_imag + imag * response_real).astype(BF16)
    restored = matmul(work[...], dft_ref[1])
    for residue in range(places + 1):
        values = []
        for turn in range(4):
            at = turn * half + residue * width
            real, imag = restored[at : at + width, :block], restored[at : at + width, block:]
            if turn > 0:
                cos, sin = spin_ref[0, pl.ds(turn, 1), :], spin_ref[1, pl.ds(turn, 1), :]
                real, imag = real * cos - imag * sin, imag * cos + real * sin
            values.append((real, imag))
        for lanes, (real, imag) in zip(quarters, butterfly(values, -1)):
            cos, sin = twist_ref[0, pl.ds(residue, 1), lanes], twist_ref[1, pl.ds(residue, 1), lanes]
            both[pl.ds(residue * width, width), lanes] = (real * cos - imag * sin).astype(BF16)
            both[pl.ds(half + residue * width, width), lanes] = (imag * cos + real * sin).astype(BF16)
    out_ref[...] = matmul(last_ref[...], both[...]).astype(BF16)


def convolve_kernel(packed_ref, first_ref, last_ref, twist_ref, dft_ref, scale_ref, out_ref, left, right):
    wide, rows = out_ref.shape
    half = 2 * wide
    signal = (packed_ref[4].astype(F32) * scale_ref[...]).astype(BF16)
    mixed = matmul(first_ref[...], signal)
    real, imag = mixed[:half], mixed[half:]
    cos_twist, sin_twist = twist_ref[0], twist_ref[1]
    turned_real = (real * cos_twist + imag * sin_twist).astype(BF16)
    turned_imag = (imag * cos_twist - real * sin_twist).astype(BF16)
    left[pl.ds(0, half), pl.ds(0, rows)] = turned_real
    left[pl.ds(0, half), pl.ds(rows, rows)] = turned_imag
    left[pl.ds(half, half), pl.ds(0, rows)] = turned_imag
    left[pl.ds(half, half), pl.ds(rows, rows)] = -turned_real
    mixed = matmul(left[...], dft_ref[...])
    real, imag = mixed[:half], mixed[half:]
    response_real = packed_ref[0:2].reshape(half, rows).astype(F32)
    response_imag = packed_ref[2:4].reshape(half, rows).astype(F32)
    product_real = (real * response_real - imag * response_imag).astype(BF16)
    product_imag = (real * response_imag + imag * response_real).astype(BF16)
    right[pl.ds(0, half), pl.ds(0, rows)] = product_real
    right[pl.ds(0, half), pl.ds(rows, rows)] = -product_imag
    right[pl.ds(half, half), pl.ds(0, rows)] = product_imag
    right[pl.ds(half, half), pl.ds(rows, rows)] = product_real
    mixed = matmul(right[...], dft_ref[...])
    real, imag = mixed[:half], mixed[half:]
    turned_real = (real * cos_twist - imag * sin_twist).astype(BF16)
    turned_imag = (imag * cos_twist + real * sin_twist).astype(BF16)
    both = jnp.concatenate([turned_real, turned_imag], axis=0)
    out_ref[...] = matmul(last_ref[...], both).astype(BF16)


def finish_kernel(conv_ref, skipped_ref, scale_ref, post_ref, out_ref):
    turned = conv_ref[...].astype(F32) + skipped_ref[...] * scale_ref[pl.ds(0, 1), :]
    out_ref[...] = (post_ref[...].astype(F32) * turned.T).astype(BF16)


def call(kernel, out_shape, flops, moved, *operands, limit=VMEM_LIMIT, **options):
    return pl.pallas_call(
        kernel,
        out_shape=out_shape,
        compiler_params=pltpu.CompilerParams(vmem_limit_bytes=limit),
        cost_estimate=pl.CostEstimate(flops=flops, bytes_accessed=moved, transcendentals=0),
        **options,
    )(*operands)


def exchange(value):
    return lax.all_to_all(value, "seq", split_axis=0, concat_axis=0, tiled=True)


def swap(value, axis, apart):
    return lax.ppermute(value, axis, [(place, place ^ apart) for place in range(lax.axis_size(axis))])


def local(features, pre_gate, post_gate, norm_gain, skip_weight, spectrum):
    rows, wide = features.shape
    places = lax.axis_size("seq")
    groups = lax.axis_size("chan")
    width = wide // places
    piled = width % 16 == 0
    cells = rows * wide
    shape = jax.ShapeDtypeStruct
    vmem, anywhere = pl.BlockSpec(memory_space=pltpu.VMEM), pl.BlockSpec(memory_space=pl.ANY)
    squares = call(squares_kernel, shape((1, rows), F32), 4 * cells, 2 * cells, features)
    far = swap(squares, "seq", places // 2)
    skipped, packed = call(
        prepare_kernel,
        (
            shape((wide, rows), F32),
            shape((places, 5, width, rows) if piled else (5, wide, rows), BF16),
        ),
        10 * cells,
        32 * cells,
        features,
        pre_gate,
        norm_gain[None, :],
        skip_weight[None, :],
        spectrum,
        limit=WHOLE_VMEM,
        in_specs=[anywhere] * 5,
        out_specs=(anywhere, anywhere),
        scratch_shapes=[
            pltpu.VMEM(features.shape, BF16),
            pltpu.VMEM(pre_gate.shape, BF16),
            pltpu.VMEM((1, wide), F32),
            pltpu.VMEM((1, wide), F32),
            pltpu.VMEM(spectrum.shape, F32),
            pltpu.VMEM((wide, rows), F32),
            pltpu.VMEM((5, places, width, rows) if piled else (5, wide, rows), BF16),
            pltpu.SemaphoreType.DMA((8,)),
            pltpu.SemaphoreType.DMA((6,)),
        ],
    )
    packed, squares = call(
        join_kernel,
        (shape(packed.shape, BF16), shape((2, rows), F32)),
        rows,
        16 * rows,
        packed,
        squares,
        far,
        in_specs=[anywhere, vmem, vmem],
        out_specs=(anywhere, vmem),
        input_output_aliases={0: 0},
    )
    if not piled:
        packed = packed.reshape(5, places, width, rows).transpose(1, 0, 2, 3)
    gathered = exchange(packed)
    others = [swap(squares, "chan", apart) for apart in range(1, groups)]
    scale = call(
        functools.partial(scale_kernel, wide * groups), shape((2, rows), F32), 16 * rows, 64 * rows, squares, *others
    )
    if piled:
        scales, apart = [scale], 1
        while apart < places // 2:
            known = jnp.concatenate(scales) if len(scales) > 1 else scale
            scales.append(swap(known, "seq", apart))
            apart *= 2
    else:
        scales = [jnp.repeat(lax.all_gather(scale[:1], "seq", axis=0, tiled=True), width, axis=0)]
        response = gathered[:, :4].reshape(places, 2, 2, width, rows).transpose(1, 0, 2, 3, 4)
        gathered = jnp.concatenate([response.reshape(4, wide, rows), gathered[:, 4].reshape(1, wide, rows)])
    if piled:
        constants = folded_tables(places, rows, width)
        half = constants[0].shape[0] // 2
        scratch = [
            pltpu.VMEM((places, 1, rows), F32),
            pltpu.VMEM((8 * (half - 2 * width), rows // 4), BF16),
            pltpu.VMEM((2 * half, rows), F32),
            pltpu.VMEM((4 * half, rows // 2), BF16),
            pltpu.VMEM((2 * half, rows), BF16),
        ]
    else:
        constants = tables(places, rows, width)
        scratch = [pltpu.VMEM((4 * wide, 2 * rows), BF16)] * 2
    conv = call(
        folded_kernel if piled else convolve_kernel,
        shape((wide, rows), BF16),
        20 * cells * rows,
        20 * cells,
        gathered,
        *constants,
        *scales,
        scratch_shapes=scratch,
    )
    conv = exchange(conv.reshape(places, width, rows)).reshape(wide, rows)
    return call(finish_kernel, shape((rows, wide), BF16), 10 * cells, 8 * cells, conv, skipped, scale, post_gate)


def solution(mesh):
    return jax.shard_map(
        local,
        mesh=mesh,
        in_specs=(
            P("seq", "chan"),
            P("seq", "chan"),
            P("seq", "chan"),
            P("chan"),
            P("chan"),
            P(None, "seq", None, "chan"),
        ),
        out_specs=P("seq", "chan"),
        check_vma=False,
    )
```

```python
import functools

import jax
import jax.numpy as jnp
import numpy as np
from jax import lax
from jax.experimental import pallas as pl
from jax.experimental.pallas import tpu as pltpu
from jax.sharding import PartitionSpec as P

EPS = 1e-06
BF16 = jnp.bfloat16
F32 = jnp.float32
VMEM_LIMIT = 48 * 1024 * 1024
WHOLE_VMEM = 63 * 1024 * 1024 + 512 * 1024


def reverse_bits(index, levels):
    return sum((index >> bit & 1) << levels - 1 - bit for bit in range(levels))


@functools.lru_cache(maxsize=None)
def tables(places, rows, width):
    levels = places.bit_length() - 1
    stride = 2 * places
    bins = stride * rows
    residues = np.array([2 * reverse_bits(place, levels) + parity for place in range(places) for parity in range(2)])
    angle = 2.0 * np.pi * ((residues[:, None] * np.arange(places)[None, :]) % stride) / stride
    same = np.eye(width)
    first = np.concatenate([np.kron(np.cos(angle), same), np.kron(-np.sin(angle), same)])
    last = first.T / bins
    angle = 2.0 * np.pi * ((residues[:, None] * np.arange(rows)[None, :]) % bins) / bins
    twist = np.repeat(np.stack([np.cos(angle), np.sin(angle)]), width, axis=1)
    series = np.arange(rows)
    angle = 2.0 * np.pi * ((series[:, None] * series[None, :]) % rows) / rows
    dft = np.concatenate([np.cos(angle), np.sin(angle)])
    return (
        first.astype(jnp.bfloat16),
        last.astype(jnp.bfloat16),
        twist.astype(np.float32),
        dft.astype(jnp.bfloat16),
    )


def pair_rows(places):
    levels = places.bit_length() - 1

    def holder(residue):
        return reverse_bits(residue // 2, levels), residue % 2

    mirrors = [None if residue % places == 0 else holder(2 * places - residue) for residue in range(places + 1)]
    return [holder(residue) for residue in range(places + 1)], mirrors


@functools.lru_cache(maxsize=None)
def folded_tables(places, rows, width):
    stride = 2 * places
    bins = stride * rows
    residues = np.arange(places + 1)
    angle = 2.0 * np.pi * ((residues[:, None] * np.arange(places)[None, :]) % stride) / stride
    same = np.eye(width)
    first = np.concatenate([np.kron(np.cos(angle), same), np.kron(-np.sin(angle), same)])
    last = first.T / bins
    angle = 2.0 * np.pi * ((residues[:, None] * np.arange(rows)[None, :]) % bins) / bins
    twist = np.stack([np.cos(angle), np.sin(angle)])
    block = rows // 4
    series = np.arange(block)
    angle = 2.0 * np.pi * ((np.arange(4)[:, None] * series[None, :]) % rows) / rows
    spin = np.stack([np.cos(angle), np.sin(angle)])
    angle = 2.0 * np.pi * ((series[:, None] * series[None, :]) % block) / block
    cos, sin = np.cos(angle), np.sin(angle)
    there = np.block([[cos, -sin], [sin, cos]])
    back = np.block([[cos, sin], [-sin, cos]])
    reverse = np.eye(block)[::-1]
    return (
        first.astype(jnp.bfloat16),
        last.astype(jnp.bfloat16),
        twist.astype(np.float32),
        spin.astype(np.float32),
        np.stack([there, back]).astype(jnp.bfloat16),
        reverse.astype(jnp.bfloat16),
    )


def hops(places):
    return [[apart, apart + 1] for apart in range(0, places, 2)]


def prepare_kernel(
    features_ref,
    pre_ref,
    gain_ref,
    skip_ref,
    spectrum_ref,
    squares_ref,
    skipped_ref,
    packed_ref,
    features_in,
    pre_in,
    gain_in,
    skip_in,
    spectrum_in,
    squares_out,
    skipped_out,
    packed_out,
    in_sems,
    out_sems,
):
    blocks = [(part, parity) for part in range(2) for parity in range(2)]
    pairs = [(features_ref, features_in), (pre_ref, pre_in), (gain_ref, gain_in), (skip_ref, skip_in)]
    pairs += [(spectrum_ref.at[block], spectrum_in.at[block]) for block in blocks]
    arriving = [pltpu.make_async_copy(*pair, in_sems.at[slot]) for slot, pair in enumerate(pairs)]
    for copy in arriving:
        copy.start()
    leaving = []

    def leave(source, target):
        copy = pltpu.make_async_copy(source, target, out_sems.at[len(leaving)])
        copy.start()
        leaving.append(copy)

    def pack(slot, turned):
        if len(packed_ref.shape) == 4:
            packed_out[slot] = turned.reshape(packed_out.shape[1:])
            leave(packed_out.at[slot], packed_ref.at[:, slot])
        else:
            packed_out[slot] = turned
            leave(packed_out.at[slot], packed_ref.at[slot])

    for copy in arriving[:4]:
        copy.wait()
    features = features_in[...].astype(F32)
    scaled = (features * gain_in[...] * pre_in[...].astype(F32)).T
    pack(4, scaled.astype(BF16))
    skipped_out[...] = (scaled * skip_in[...].reshape(-1, 1)).astype(BF16)
    leave(skipped_out, skipped_ref)
    turned = features.T
    squares_out[...] = jnp.sum(turned * turned, axis=0, keepdims=True)
    leave(squares_out, squares_ref)
    for slot, block in enumerate(blocks):
        arriving[4 + slot].wait()
        if len(packed_ref.shape) == 4:
            quarter = spectrum_in.shape[2] // 4
            rows = [spectrum_in[(*block, pl.ds(turn, quarter, stride=4), slice(None))] for turn in range(4)]
            pack(slot, jnp.concatenate([row.T for row in rows], axis=1).astype(BF16))
        else:
            pack(slot, spectrum_in[block].T.astype(BF16))
    for copy in leaving:
        copy.wait()


def scale_kernel(channels, *refs):
    square_refs, scale_ref = refs[:-1], refs[-1]
    total = square_refs[0][...]
    for square_ref in square_refs[1:]:
        total = total + square_ref[...]
    scale_ref[...] = lax.rsqrt(total / channels + EPS)


def matmul(left, right):
    return jnp.dot(left, right, preferred_element_type=F32)


def butterfly(values, direction):
    (real0, imag0), (real1, imag1), (real2, imag2), (real3, imag3) = values
    even, odd = (real0 + real2, imag0 + imag2), (real1 + real3, imag1 + imag3)
    even_gap, odd_gap = (real0 - real2, imag0 - imag2), (real1 - real3, imag1 - imag3)
    lower = (even_gap[0] + odd_gap[1], even_gap[1] - odd_gap[0])
    upper = (even_gap[0] - odd_gap[1], even_gap[1] + odd_gap[0])
    total, gap = (even[0] + odd[0], even[1] + odd[1]), (even[0] - odd[0], even[1] - odd[1])
    return [total, lower, gap, upper] if direction > 0 else [total, upper, gap, lower]


def folded_kernel(packed_ref, first_ref, last_ref, twist_ref, spin_ref, dft_ref, reverse_ref, *refs):
    scale_refs, (out_ref, scales, mirror, mixed, work, both) = refs[:-6], refs[-6:]
    wide, rows = out_ref.shape
    places, width = scales.shape[0], wide // scales.shape[0]
    half, block = first_ref.shape[0] // 2, rows // 4
    inner = half - 2 * width
    place = lax.axis_index("seq")
    for scale_ref, steps in zip(scale_refs, hops(places)):
        for at, step in enumerate(steps):
            scales[place ^ step] = scale_ref[pl.ds(at, 1), :]
    direct, mirrors = pair_rows(places)
    quarters = [pl.ds(turn * block, block) for turn in range(4)]
    signal = (packed_ref[:, 4].astype(F32) * scales[...]).astype(BF16).reshape(wide, rows)
    mixed[...] = matmul(first_ref[...], signal)
    for residue in range(places + 1):
        over, under = pl.ds(residue * width, width), pl.ds(half + residue * width, width)
        values = []
        for lanes in quarters:
            real, imag = mixed[over, lanes], mixed[under, lanes]
            cos, sin = twist_ref[0, pl.ds(residue, 1), lanes], twist_ref[1, pl.ds(residue, 1), lanes]
            values.append((real * cos + imag * sin, imag * cos - real * sin))
        for turn, (real, imag) in enumerate(butterfly(values, 1)):
            if turn > 0:
                cos, sin = spin_ref[0, pl.ds(turn, 1), :], spin_ref[1, pl.ds(turn, 1), :]
                real, imag = real * cos + imag * sin, imag * cos - real * sin
            at = pl.ds(turn * half + residue * width, width)
            work[at, pl.ds(0, block)] = real.astype(BF16)
            work[at, pl.ds(block, block)] = imag.astype(BF16)
    for row, holder in enumerate(mirrors[1:places]):
        for part in range(2):
            for turn in range(4):
                at = pl.ds((part * 4 + 3 - turn) * inner + row * width, width)
                mirror[at, :] = packed_ref[holder[0], 2 * part + holder[1], :, quarters[turn]]
    reversed_bins = matmul(mirror[...], reverse_ref[...])
    spectral = matmul(work[...], dft_ref[0])
    for turn in range(4):
        for residue, holder in enumerate(direct):
            at = turn * half + residue * width
            real, imag = spectral[at : at + width, :block], spectral[at : at + width, block:]
            response_real = packed_ref[holder[0], holder[1], :, quarters[turn]].astype(F32)
            response_imag = packed_ref[holder[0], 2 + holder[1], :, quarters[turn]].astype(F32)
            if mirrors[residue] is not None:
                begin = turn * inner + (residue - 1) * width
                response_real = response_real + reversed_bins[begin : begin + width]
                begin = begin + 4 * inner
                response_imag = response_imag - reversed_bins[begin : begin + width]
            work[pl.ds(at, width), pl.ds(0, block)] = (real * response_real - imag * response_imag).astype(BF16)
            work[pl.ds(at, width), pl.ds(block, block)] = (real * response_imag + imag * response_real).astype(BF16)
    restored = matmul(work[...], dft_ref[1])
    for residue in range(places + 1):
        values = []
        for turn in range(4):
            at = turn * half + residue * width
            real, imag = restored[at : at + width, :block], restored[at : at + width, block:]
            if turn > 0:
                cos, sin = spin_ref[0, pl.ds(turn, 1), :], spin_ref[1, pl.ds(turn, 1), :]
                real, imag = real * cos - imag * sin, imag * cos + real * sin
            values.append((real, imag))
        for lanes, (real, imag) in zip(quarters, butterfly(values, -1)):
            cos, sin = twist_ref[0, pl.ds(residue, 1), lanes], twist_ref[1, pl.ds(residue, 1), lanes]
            both[pl.ds(residue * width, width), lanes] = (real * cos - imag * sin).astype(BF16)
            both[pl.ds(half + residue * width, width), lanes] = (imag * cos + real * sin).astype(BF16)
    out_ref[...] = matmul(last_ref[...], both[...]).astype(BF16)


def convolve_kernel(packed_ref, first_ref, last_ref, twist_ref, dft_ref, scale_ref, out_ref, left, right):
    wide, rows = out_ref.shape
    half = 2 * wide
    signal = (packed_ref[4].astype(F32) * scale_ref[...]).astype(BF16)
    mixed = matmul(first_ref[...], signal)
    real, imag = mixed[:half], mixed[half:]
    cos_twist, sin_twist = twist_ref[0], twist_ref[1]
    turned_real = (real * cos_twist + imag * sin_twist).astype(BF16)
    turned_imag = (imag * cos_twist - real * sin_twist).astype(BF16)
    left[pl.ds(0, half), pl.ds(0, rows)] = turned_real
    left[pl.ds(0, half), pl.ds(rows, rows)] = turned_imag
    left[pl.ds(half, half), pl.ds(0, rows)] = turned_imag
    left[pl.ds(half, half), pl.ds(rows, rows)] = -turned_real
    mixed = matmul(left[...], dft_ref[...])
    real, imag = mixed[:half], mixed[half:]
    response_real = packed_ref[0:2].reshape(half, rows).astype(F32)
    response_imag = packed_ref[2:4].reshape(half, rows).astype(F32)
    product_real = (real * response_real - imag * response_imag).astype(BF16)
    product_imag = (real * response_imag + imag * response_real).astype(BF16)
    right[pl.ds(0, half), pl.ds(0, rows)] = product_real
    right[pl.ds(0, half), pl.ds(rows, rows)] = -product_imag
    right[pl.ds(half, half), pl.ds(0, rows)] = product_imag
    right[pl.ds(half, half), pl.ds(rows, rows)] = product_real
    mixed = matmul(right[...], dft_ref[...])
    real, imag = mixed[:half], mixed[half:]
    turned_real = (real * cos_twist - imag * sin_twist).astype(BF16)
    turned_imag = (imag * cos_twist + real * sin_twist).astype(BF16)
    both = jnp.concatenate([turned_real, turned_imag], axis=0)
    out_ref[...] = matmul(last_ref[...], both).astype(BF16)


def finish_kernel(conv_ref, skipped_ref, scale_ref, post_ref, out_ref):
    turned = conv_ref[...].astype(F32) + skipped_ref[...].astype(F32) * scale_ref[...]
    out_ref[...] = (post_ref[...].astype(F32) * turned.T).astype(BF16)


def call(kernel, out_shape, flops, moved, *operands, limit=VMEM_LIMIT, **options):
    return pl.pallas_call(
        kernel,
        out_shape=out_shape,
        compiler_params=pltpu.CompilerParams(vmem_limit_bytes=limit),
        cost_estimate=pl.CostEstimate(flops=flops, bytes_accessed=moved, transcendentals=0),
        **options,
    )(*operands)


def exchange(value):
    return lax.all_to_all(value, "seq", split_axis=0, concat_axis=0, tiled=True)


def swap(value, axis, apart):
    return lax.ppermute(value, axis, [(place, place ^ apart) for place in range(lax.axis_size(axis))])


def local(features, pre_gate, post_gate, norm_gain, skip_weight, spectrum):
    rows, wide = features.shape
    places = lax.axis_size("seq")
    groups = lax.axis_size("chan")
    width = wide // places
    piled = width % 16 == 0
    cells = rows * wide
    shape = jax.ShapeDtypeStruct
    vmem, anywhere = pl.BlockSpec(memory_space=pltpu.VMEM), pl.BlockSpec(memory_space=pl.ANY)
    squares, skipped, packed = call(
        prepare_kernel,
        (
            shape((1, rows), F32),
            shape((wide, rows), BF16),
            shape((places, 5, width, rows) if piled else (5, wide, rows), BF16),
        ),
        10 * cells,
        32 * cells,
        features,
        pre_gate,
        norm_gain[None, :],
        skip_weight[None, :],
        spectrum,
        limit=WHOLE_VMEM,
        in_specs=[anywhere] * 5,
        out_specs=(anywhere, anywhere, anywhere),
        scratch_shapes=[
            pltpu.VMEM(features.shape, BF16),
            pltpu.VMEM(pre_gate.shape, BF16),
            pltpu.VMEM((1, wide), F32),
            pltpu.VMEM((1, wide), F32),
            pltpu.VMEM(spectrum.shape, F32),
            pltpu.VMEM((1, rows), F32),
            pltpu.VMEM((wide, rows), BF16),
            pltpu.VMEM((5, places, width, rows) if piled else (5, wide, rows), BF16),
            pltpu.SemaphoreType.DMA((8,)),
            pltpu.SemaphoreType.DMA((7,)),
        ],
    )
    if not piled:
        packed = packed.reshape(5, places, width, rows).transpose(1, 0, 2, 3)
    gathered = exchange(packed)
    others = [swap(squares, "chan", apart) for apart in range(1, groups)]
    scale = call(
        functools.partial(scale_kernel, wide * groups), shape((1, rows), F32), 8 * rows, 32 * rows, squares, *others
    )
    if piled:
        near = jnp.concatenate([scale, swap(scale, "seq", 1)])
        scales = [near] + [swap(near, "seq", steps[0]) for steps in hops(places)[1:]]
    else:
        scales = [jnp.repeat(lax.all_gather(scale, "seq", axis=0, tiled=True), width, axis=0)]
        response = gathered[:, :4].reshape(places, 2, 2, width, rows).transpose(1, 0, 2, 3, 4)
        gathered = jnp.concatenate([response.reshape(4, wide, rows), gathered[:, 4].reshape(1, wide, rows)])
    if piled:
        constants = folded_tables(places, rows, width)
        half = constants[0].shape[0] // 2
        scratch = [
            pltpu.VMEM((places, 1, rows), F32),
            pltpu.VMEM((8 * (half - 2 * width), rows // 4), BF16),
            pltpu.VMEM((2 * half, rows), F32),
            pltpu.VMEM((4 * half, rows // 2), BF16),
            pltpu.VMEM((2 * half, rows), BF16),
        ]
    else:
        constants = tables(places, rows, width)
        scratch = [pltpu.VMEM((4 * wide, 2 * rows), BF16)] * 2
    conv = call(
        folded_kernel if piled else convolve_kernel,
        shape((wide, rows), BF16),
        20 * cells * rows,
        20 * cells,
        gathered,
        *constants,
        *scales,
        scratch_shapes=scratch,
    )
    conv = exchange(conv.reshape(places, width, rows)).reshape(wide, rows)
    return call(finish_kernel, shape((rows, wide), BF16), 10 * cells, 8 * cells, conv, skipped, scale, post_gate)


def solution(mesh):
    return jax.shard_map(
        local,
        mesh=mesh,
        in_specs=(
            P("seq", "chan"),
            P("seq", "chan"),
            P("seq", "chan"),
            P("chan"),
            P("chan"),
            P(None, "seq", None, "chan"),
        ),
        out_specs=P("seq", "chan"),
        check_vma=False,
    )
```

```python
import functools

import jax
import jax.numpy as jnp
import numpy as np
from jax import lax
from jax.experimental import pallas as pl
from jax.experimental.pallas import tpu as pltpu
from jax.sharding import PartitionSpec as P

EPS = 1e-06
BF16 = jnp.bfloat16
F32 = jnp.float32
VMEM_LIMIT = 48 * 1024 * 1024
WHOLE_VMEM = 63 * 1024 * 1024 + 512 * 1024


def reverse_bits(index, levels):
    return sum((index >> bit & 1) << levels - 1 - bit for bit in range(levels))


@functools.lru_cache(maxsize=None)
def tables(places, rows, width):
    levels = places.bit_length() - 1
    stride = 2 * places
    bins = stride * rows
    residues = np.array([2 * reverse_bits(place, levels) + parity for place in range(places) for parity in range(2)])
    angle = 2.0 * np.pi * ((residues[:, None] * np.arange(places)[None, :]) % stride) / stride
    same = np.eye(width)
    first = np.concatenate([np.kron(np.cos(angle), same), np.kron(-np.sin(angle), same)])
    last = first.T / bins
    angle = 2.0 * np.pi * ((residues[:, None] * np.arange(rows)[None, :]) % bins) / bins
    twist = np.repeat(np.stack([np.cos(angle), np.sin(angle)]), width, axis=1)
    series = np.arange(rows)
    angle = 2.0 * np.pi * ((series[:, None] * series[None, :]) % rows) / rows
    dft = np.concatenate([np.cos(angle), np.sin(angle)])
    return (
        first.astype(jnp.bfloat16),
        last.astype(jnp.bfloat16),
        twist.astype(np.float32),
        dft.astype(jnp.bfloat16),
    )


def pair_rows(places):
    levels = places.bit_length() - 1

    def holder(residue):
        return reverse_bits(residue // 2, levels), residue % 2

    mirrors = [None if residue % places == 0 else holder(2 * places - residue) for residue in range(places + 1)]
    return [holder(residue) for residue in range(places + 1)], mirrors


@functools.lru_cache(maxsize=None)
def folded_tables(places, rows, width):
    stride = 2 * places
    bins = stride * rows
    residues = np.arange(places + 1)
    angle = 2.0 * np.pi * ((residues[:, None] * np.arange(places)[None, :]) % stride) / stride
    same = np.eye(width)
    first = np.concatenate([np.kron(np.cos(angle), same), np.kron(-np.sin(angle), same)])
    last = first.T / bins
    angle = 2.0 * np.pi * ((residues[:, None] * np.arange(rows)[None, :]) % bins) / bins
    twist = np.stack([np.cos(angle), np.sin(angle)])
    block = rows // 4
    series = np.arange(block)
    angle = 2.0 * np.pi * ((np.arange(4)[:, None] * series[None, :]) % rows) / rows
    spin = np.stack([np.cos(angle), np.sin(angle)])
    angle = 2.0 * np.pi * ((series[:, None] * series[None, :]) % block) / block
    cos, sin = np.cos(angle), np.sin(angle)
    there = np.block([[cos, -sin], [sin, cos]])
    back = np.block([[cos, sin], [-sin, cos]])
    reverse = np.eye(block)[::-1]
    return (
        first.astype(jnp.bfloat16),
        last.astype(jnp.bfloat16),
        twist.astype(np.float32),
        spin.astype(np.float32),
        np.stack([there, back]).astype(jnp.bfloat16),
        reverse.astype(jnp.bfloat16),
    )


def hops(places):
    return [[apart, apart + 1] for apart in range(0, places, 2)]


def prepare_kernel(
    features_ref,
    pre_ref,
    gain_ref,
    skip_ref,
    spectrum_ref,
    squares_ref,
    skipped_ref,
    packed_ref,
    features_in,
    pre_in,
    gain_in,
    skip_in,
    spectrum_in,
    squares_out,
    skipped_out,
    packed_out,
    in_sems,
    out_sems,
):
    blocks = [(part, parity) for part in range(2) for parity in range(2)]
    pairs = [(features_ref, features_in), (pre_ref, pre_in), (gain_ref, gain_in), (skip_ref, skip_in)]
    pairs += [(spectrum_ref.at[block], spectrum_in.at[block]) for block in blocks]
    arriving = [pltpu.make_async_copy(*pair, in_sems.at[slot]) for slot, pair in enumerate(pairs)]
    for copy in arriving:
        copy.start()
    leaving = []

    def leave(source, target):
        copy = pltpu.make_async_copy(source, target, out_sems.at[len(leaving)])
        copy.start()
        leaving.append(copy)

    def pack(slot, turned):
        if len(packed_ref.shape) == 4:
            packed_out[slot] = turned.reshape(packed_out.shape[1:])
            leave(packed_out.at[slot], packed_ref.at[:, slot])
        else:
            packed_out[slot] = turned
            leave(packed_out.at[slot], packed_ref.at[slot])

    for copy in arriving[:4]:
        copy.wait()
    features = features_in[...].astype(F32)
    scaled = features * gain_in[...] * pre_in[...].astype(F32)
    pack(4, scaled.astype(BF16).T)
    skipped_out[...] = (scaled * skip_in[...]).astype(BF16).T
    leave(skipped_out, skipped_ref)
    turned = features_in[...].T.astype(F32)
    squares_out[...] = jnp.sum(turned * turned, axis=0, keepdims=True)
    leave(squares_out, squares_ref)
    for slot, block in enumerate(blocks):
        arriving[4 + slot].wait()
        if len(packed_ref.shape) == 4:
            quarter = spectrum_in.shape[2] // 4
            rows = [spectrum_in[(*block, pl.ds(turn, quarter, stride=4), slice(None))] for turn in range(4)]
            pack(slot, jnp.concatenate([row.astype(BF16).T for row in rows], axis=1))
        else:
            pack(slot, spectrum_in[block].astype(BF16).T)
    for copy in leaving:
        copy.wait()


def scale_kernel(channels, *refs):
    square_refs, scale_ref = refs[:-1], refs[-1]
    total = square_refs[0][...]
    for square_ref in square_refs[1:]:
        total = total + square_ref[...]
    scale_ref[...] = lax.rsqrt(total / channels + EPS)


def matmul(left, right):
    return jnp.dot(left, right, preferred_element_type=F32)


def butterfly(values, direction):
    (real0, imag0), (real1, imag1), (real2, imag2), (real3, imag3) = values
    even, odd = (real0 + real2, imag0 + imag2), (real1 + real3, imag1 + imag3)
    even_gap, odd_gap = (real0 - real2, imag0 - imag2), (real1 - real3, imag1 - imag3)
    lower = (even_gap[0] + odd_gap[1], even_gap[1] - odd_gap[0])
    upper = (even_gap[0] - odd_gap[1], even_gap[1] + odd_gap[0])
    total, gap = (even[0] + odd[0], even[1] + odd[1]), (even[0] - odd[0], even[1] - odd[1])
    return [total, lower, gap, upper] if direction > 0 else [total, upper, gap, lower]


def folded_kernel(packed_ref, first_ref, last_ref, twist_ref, spin_ref, dft_ref, reverse_ref, *refs):
    scale_refs, (out_ref, scales, mirror, mixed, work, both) = refs[:-6], refs[-6:]
    wide, rows = out_ref.shape
    places, width = scales.shape[0], wide // scales.shape[0]
    half, block = first_ref.shape[0] // 2, rows // 4
    inner = half - 2 * width
    place = lax.axis_index("seq")
    for scale_ref, steps in zip(scale_refs, hops(places)):
        for at, step in enumerate(steps):
            scales[place ^ step] = scale_ref[pl.ds(at, 1), :]
    direct, mirrors = pair_rows(places)
    quarters = [pl.ds(turn * block, block) for turn in range(4)]
    signal = (packed_ref[:, 4].astype(F32) * scales[...]).astype(BF16).reshape(wide, rows)
    mixed[...] = matmul(first_ref[...], signal)
    for residue in range(places + 1):
        over, under = pl.ds(residue * width, width), pl.ds(half + residue * width, width)
        values = []
        for lanes in quarters:
            real, imag = mixed[over, lanes], mixed[under, lanes]
            cos, sin = twist_ref[0, pl.ds(residue, 1), lanes], twist_ref[1, pl.ds(residue, 1), lanes]
            values.append((real * cos + imag * sin, imag * cos - real * sin))
        for turn, (real, imag) in enumerate(butterfly(values, 1)):
            if turn > 0:
                cos, sin = spin_ref[0, pl.ds(turn, 1), :], spin_ref[1, pl.ds(turn, 1), :]
                real, imag = real * cos + imag * sin, imag * cos - real * sin
            at = pl.ds(turn * half + residue * width, width)
            work[at, pl.ds(0, block)] = real.astype(BF16)
            work[at, pl.ds(block, block)] = imag.astype(BF16)
    for row, holder in enumerate(mirrors[1:places]):
        for part in range(2):
            for turn in range(4):
                at = pl.ds((part * 4 + 3 - turn) * inner + row * width, width)
                mirror[at, :] = packed_ref[holder[0], 2 * part + holder[1], :, quarters[turn]]
    reversed_bins = matmul(mirror[...], reverse_ref[...])
    spectral = matmul(work[...], dft_ref[0])
    for turn in range(4):
        for residue, holder in enumerate(direct):
            at = turn * half + residue * width
            real, imag = spectral[at : at + width, :block], spectral[at : at + width, block:]
            response_real = packed_ref[holder[0], holder[1], :, quarters[turn]].astype(F32)
            response_imag = packed_ref[holder[0], 2 + holder[1], :, quarters[turn]].astype(F32)
            if mirrors[residue] is not None:
                begin = turn * inner + (residue - 1) * width
                response_real = response_real + reversed_bins[begin : begin + width]
                begin = begin + 4 * inner
                response_imag = response_imag - reversed_bins[begin : begin + width]
            work[pl.ds(at, width), pl.ds(0, block)] = (real * response_real - imag * response_imag).astype(BF16)
            work[pl.ds(at, width), pl.ds(block, block)] = (real * response_imag + imag * response_real).astype(BF16)
    restored = matmul(work[...], dft_ref[1])
    for residue in range(places + 1):
        values = []
        for turn in range(4):
            at = turn * half + residue * width
            real, imag = restored[at : at + width, :block], restored[at : at + width, block:]
            if turn > 0:
                cos, sin = spin_ref[0, pl.ds(turn, 1), :], spin_ref[1, pl.ds(turn, 1), :]
                real, imag = real * cos - imag * sin, imag * cos + real * sin
            values.append((real, imag))
        for lanes, (real, imag) in zip(quarters, butterfly(values, -1)):
            cos, sin = twist_ref[0, pl.ds(residue, 1), lanes], twist_ref[1, pl.ds(residue, 1), lanes]
            both[pl.ds(residue * width, width), lanes] = (real * cos - imag * sin).astype(BF16)
            both[pl.ds(half + residue * width, width), lanes] = (imag * cos + real * sin).astype(BF16)
    out_ref[...] = matmul(last_ref[...], both[...]).astype(BF16)


def convolve_kernel(packed_ref, first_ref, last_ref, twist_ref, dft_ref, scale_ref, out_ref, left, right):
    wide, rows = out_ref.shape
    half = 2 * wide
    signal = (packed_ref[4].astype(F32) * scale_ref[...]).astype(BF16)
    mixed = matmul(first_ref[...], signal)
    real, imag = mixed[:half], mixed[half:]
    cos_twist, sin_twist = twist_ref[0], twist_ref[1]
    turned_real = (real * cos_twist + imag * sin_twist).astype(BF16)
    turned_imag = (imag * cos_twist - real * sin_twist).astype(BF16)
    left[pl.ds(0, half), pl.ds(0, rows)] = turned_real
    left[pl.ds(0, half), pl.ds(rows, rows)] = turned_imag
    left[pl.ds(half, half), pl.ds(0, rows)] = turned_imag
    left[pl.ds(half, half), pl.ds(rows, rows)] = -turned_real
    mixed = matmul(left[...], dft_ref[...])
    real, imag = mixed[:half], mixed[half:]
    response_real = packed_ref[0:2].reshape(half, rows).astype(F32)
    response_imag = packed_ref[2:4].reshape(half, rows).astype(F32)
    product_real = (real * response_real - imag * response_imag).astype(BF16)
    product_imag = (real * response_imag + imag * response_real).astype(BF16)
    right[pl.ds(0, half), pl.ds(0, rows)] = product_real
    right[pl.ds(0, half), pl.ds(rows, rows)] = -product_imag
    right[pl.ds(half, half), pl.ds(0, rows)] = product_imag
    right[pl.ds(half, half), pl.ds(rows, rows)] = product_real
    mixed = matmul(right[...], dft_ref[...])
    real, imag = mixed[:half], mixed[half:]
    turned_real = (real * cos_twist - imag * sin_twist).astype(BF16)
    turned_imag = (imag * cos_twist + real * sin_twist).astype(BF16)
    both = jnp.concatenate([turned_real, turned_imag], axis=0)
    out_ref[...] = matmul(last_ref[...], both).astype(BF16)


def finish_kernel(conv_ref, skipped_ref, scale_ref, post_ref, out_ref):
    turned = conv_ref[...].astype(F32) + skipped_ref[...].astype(F32) * scale_ref[...]
    out_ref[...] = (post_ref[...].astype(F32) * turned.T).astype(BF16)


def call(kernel, out_shape, flops, moved, *operands, limit=VMEM_LIMIT, **options):
    return pl.pallas_call(
        kernel,
        out_shape=out_shape,
        compiler_params=pltpu.CompilerParams(vmem_limit_bytes=limit),
        cost_estimate=pl.CostEstimate(flops=flops, bytes_accessed=moved, transcendentals=0),
        **options,
    )(*operands)


def exchange(value):
    return lax.all_to_all(value, "seq", split_axis=0, concat_axis=0, tiled=True)


def swap(value, axis, apart):
    return lax.ppermute(value, axis, [(place, place ^ apart) for place in range(lax.axis_size(axis))])


def local(features, pre_gate, post_gate, norm_gain, skip_weight, spectrum):
    rows, wide = features.shape
    places = lax.axis_size("seq")
    groups = lax.axis_size("chan")
    width = wide // places
    piled = width % 16 == 0
    cells = rows * wide
    shape = jax.ShapeDtypeStruct
    vmem, anywhere = pl.BlockSpec(memory_space=pltpu.VMEM), pl.BlockSpec(memory_space=pl.ANY)
    squares, skipped, packed = call(
        prepare_kernel,
        (
            shape((1, rows), F32),
            shape((wide, rows), BF16),
            shape((places, 5, width, rows) if piled else (5, wide, rows), BF16),
        ),
        10 * cells,
        32 * cells,
        features,
        pre_gate,
        norm_gain[None, :],
        skip_weight[None, :],
        spectrum,
        limit=WHOLE_VMEM,
        in_specs=[anywhere] * 5,
        out_specs=(anywhere, anywhere, anywhere),
        scratch_shapes=[
            pltpu.VMEM(features.shape, BF16),
            pltpu.VMEM(pre_gate.shape, BF16),
            pltpu.VMEM((1, wide), F32),
            pltpu.VMEM((1, wide), F32),
            pltpu.VMEM(spectrum.shape, F32),
            pltpu.VMEM((1, rows), F32),
            pltpu.VMEM((wide, rows), BF16),
            pltpu.VMEM((5, places, width, rows) if piled else (5, wide, rows), BF16),
            pltpu.SemaphoreType.DMA((8,)),
            pltpu.SemaphoreType.DMA((7,)),
        ],
    )
    if not piled:
        packed = packed.reshape(5, places, width, rows).transpose(1, 0, 2, 3)
    gathered = exchange(packed)
    others = [swap(squares, "chan", apart) for apart in range(1, groups)]
    scale = call(
        functools.partial(scale_kernel, wide * groups), shape((1, rows), F32), 8 * rows, 32 * rows, squares, *others
    )
    if piled:
        near = jnp.concatenate([scale, swap(scale, "seq", 1)])
        scales = [near] + [swap(near, "seq", steps[0]) for steps in hops(places)[1:]]
    else:
        scales = [jnp.repeat(lax.all_gather(scale, "seq", axis=0, tiled=True), width, axis=0)]
        response = gathered[:, :4].reshape(places, 2, 2, width, rows).transpose(1, 0, 2, 3, 4)
        gathered = jnp.concatenate([response.reshape(4, wide, rows), gathered[:, 4].reshape(1, wide, rows)])
    if piled:
        constants = folded_tables(places, rows, width)
        half = constants[0].shape[0] // 2
        scratch = [
            pltpu.VMEM((places, 1, rows), F32),
            pltpu.VMEM((8 * (half - 2 * width), rows // 4), BF16),
            pltpu.VMEM((2 * half, rows), F32),
            pltpu.VMEM((4 * half, rows // 2), BF16),
            pltpu.VMEM((2 * half, rows), BF16),
        ]
    else:
        constants = tables(places, rows, width)
        scratch = [pltpu.VMEM((4 * wide, 2 * rows), BF16)] * 2
    conv = call(
        folded_kernel if piled else convolve_kernel,
        shape((wide, rows), BF16),
        20 * cells * rows,
        20 * cells,
        gathered,
        *constants,
        *scales,
        scratch_shapes=scratch,
    )
    conv = exchange(conv.reshape(places, width, rows)).reshape(wide, rows)
    return call(finish_kernel, shape((rows, wide), BF16), 10 * cells, 8 * cells, conv, skipped, scale, post_gate)


def solution(mesh):
    return jax.shard_map(
        local,
        mesh=mesh,
        in_specs=(
            P("seq", "chan"),
            P("seq", "chan"),
            P("seq", "chan"),
            P("chan"),
            P("chan"),
            P(None, "seq", None, "chan"),
        ),
        out_specs=P("seq", "chan"),
        check_vma=False,
    )
```

```python
import functools

import jax
import jax.numpy as jnp
import numpy as np
from jax import lax
from jax.experimental import pallas as pl
from jax.experimental.pallas import tpu as pltpu
from jax.sharding import PartitionSpec as P

EPS = 1e-06
BF16 = jnp.bfloat16
F32 = jnp.float32
VMEM_LIMIT = 48 * 1024 * 1024
WHOLE_VMEM = 63 * 1024 * 1024 + 512 * 1024


def order_of(places):
    return (0, 2, 6, 4, 1, 5, 3, 7) if places == 8 else tuple(range(places))


def reverse_bits(index, levels):
    return sum((index >> bit & 1) << levels - 1 - bit for bit in range(levels))


@functools.lru_cache(maxsize=None)
def tables(places, rows, width):
    levels = places.bit_length() - 1
    stride = 2 * places
    bins = stride * rows
    residues = np.array([2 * reverse_bits(place, levels) + parity for place in range(places) for parity in range(2)])
    angle = 2.0 * np.pi * ((residues[:, None] * np.arange(places)[None, :]) % stride) / stride
    same = np.eye(width)
    first = np.concatenate([np.kron(np.cos(angle), same), np.kron(-np.sin(angle), same)])
    last = first.T / bins
    angle = 2.0 * np.pi * ((residues[:, None] * np.arange(rows)[None, :]) % bins) / bins
    twist = np.repeat(np.stack([np.cos(angle), np.sin(angle)]), width, axis=1)
    series = np.arange(rows)
    angle = 2.0 * np.pi * ((series[:, None] * series[None, :]) % rows) / rows
    dft = np.concatenate([np.cos(angle), np.sin(angle)])
    return (
        first.astype(jnp.bfloat16),
        last.astype(jnp.bfloat16),
        twist.astype(np.float32),
        dft.astype(jnp.bfloat16),
    )


def pair_rows(places):
    levels = places.bit_length() - 1

    def holder(residue):
        return order_of(places).index(reverse_bits(residue // 2, levels)), residue % 2

    mirrors = [None if residue % places == 0 else holder(2 * places - residue) for residue in range(places + 1)]
    return [holder(residue) for residue in range(places + 1)], mirrors


@functools.lru_cache(maxsize=None)
def folded_tables(places, rows, width):
    stride = 2 * places
    bins = stride * rows
    residues = np.arange(places + 1)
    angle = 2.0 * np.pi * ((residues[:, None] * np.arange(places)[None, :]) % stride) / stride
    same = np.eye(width)
    first = np.concatenate([np.kron(np.cos(angle), same), np.kron(-np.sin(angle), same)])
    last = first.T / bins
    angle = 2.0 * np.pi * ((residues[:, None] * np.arange(rows)[None, :]) % bins) / bins
    twist = np.stack([np.cos(angle), np.sin(angle)])
    block = rows // 4
    series = np.arange(block)
    angle = 2.0 * np.pi * ((np.arange(4)[:, None] * series[None, :]) % rows) / rows
    spin = np.stack([np.cos(angle), np.sin(angle)])
    angle = 2.0 * np.pi * ((series[:, None] * series[None, :]) % block) / block
    cos, sin = np.cos(angle), np.sin(angle)
    there = np.block([[cos, -sin], [sin, cos]])
    back = np.block([[cos, sin], [-sin, cos]])
    reverse = np.eye(block)[::-1]
    return (
        first.astype(jnp.bfloat16),
        last.astype(jnp.bfloat16),
        twist.astype(np.float32),
        spin.astype(np.float32),
        np.stack([there, back]).astype(jnp.bfloat16),
        reverse.astype(jnp.bfloat16),
    )


def hops(places):
    return [[apart, apart + 1] for apart in range(0, places, 2)]


def prepare_kernel(
    features_ref,
    pre_ref,
    gain_ref,
    skip_ref,
    spectrum_ref,
    squares_ref,
    skipped_ref,
    packed_ref,
    features_in,
    pre_in,
    gain_in,
    skip_in,
    spectrum_in,
    squares_out,
    skipped_out,
    packed_out,
    in_sems,
    out_sems,
):
    blocks = [(part, parity) for part in range(2) for parity in range(2)]
    pairs = [(features_ref, features_in), (pre_ref, pre_in), (gain_ref, gain_in), (skip_ref, skip_in)]
    pairs += [(spectrum_ref.at[block], spectrum_in.at[block]) for block in blocks]
    arriving = [pltpu.make_async_copy(*pair, in_sems.at[slot]) for slot, pair in enumerate(pairs)]
    for copy in arriving:
        copy.start()
    leaving = []

    def leave(source, target):
        copy = pltpu.make_async_copy(source, target, out_sems.at[len(leaving)])
        copy.start()
        leaving.append(copy)

    def pack(slot, turned):
        if len(packed_ref.shape) == 4:
            places, width = packed_out.shape[1:3]
            for rank, place in enumerate(order_of(places)):
                packed_out[slot, rank] = turned[place * width : (place + 1) * width]
            leave(packed_out.at[slot], packed_ref.at[:, slot])
        else:
            packed_out[slot] = turned
            leave(packed_out.at[slot], packed_ref.at[slot])

    for copy in arriving[:4]:
        copy.wait()
    features = features_in[...].astype(F32)
    scaled = features * gain_in[...] * pre_in[...].astype(F32)
    pack(4, scaled.astype(BF16).T)
    skipped_out[...] = (scaled * skip_in[...]).astype(BF16).T
    leave(skipped_out, skipped_ref)
    turned = features_in[...].T.astype(F32)
    squares_out[...] = jnp.sum(turned * turned, axis=0, keepdims=True)
    leave(squares_out, squares_ref)
    for slot, block in enumerate(blocks):
        arriving[4 + slot].wait()
        if len(packed_ref.shape) == 4:
            quarter = spectrum_in.shape[2] // 4
            rows = [spectrum_in[(*block, pl.ds(turn, quarter, stride=4), slice(None))] for turn in range(4)]
            pack(slot, jnp.concatenate([row.astype(BF16).T for row in rows], axis=1))
        else:
            pack(slot, spectrum_in[block].astype(BF16).T)
    for copy in leaving:
        copy.wait()


def scale_kernel(channels, *refs):
    square_refs, scale_ref = refs[:-1], refs[-1]
    total = square_refs[0][...]
    for square_ref in square_refs[1:]:
        total = total + square_ref[...]
    scale_ref[...] = lax.rsqrt(total / channels + EPS)


def matmul(left, right):
    return jnp.dot(left, right, preferred_element_type=F32)


def butterfly(values, direction):
    (real0, imag0), (real1, imag1), (real2, imag2), (real3, imag3) = values
    even, odd = (real0 + real2, imag0 + imag2), (real1 + real3, imag1 + imag3)
    even_gap, odd_gap = (real0 - real2, imag0 - imag2), (real1 - real3, imag1 - imag3)
    lower = (even_gap[0] + odd_gap[1], even_gap[1] - odd_gap[0])
    upper = (even_gap[0] - odd_gap[1], even_gap[1] + odd_gap[0])
    total, gap = (even[0] + odd[0], even[1] + odd[1]), (even[0] - odd[0], even[1] - odd[1])
    return [total, lower, gap, upper] if direction > 0 else [total, upper, gap, lower]


def folded_kernel(packed_ref, first_ref, last_ref, twist_ref, spin_ref, dft_ref, reverse_ref, *refs):
    scale_refs, (out_ref, scales, signal, mirror, mixed, work, both) = refs[:-7], refs[-7:]
    wide, rows = out_ref.shape
    places, width = scales.shape[0], wide // scales.shape[0]
    half, block = first_ref.shape[0] // 2, rows // 4
    inner = half - 2 * width
    place = lax.axis_index("seq")
    for scale_ref, steps in zip(scale_refs, hops(places)):
        for at, step in enumerate(steps):
            scales[place ^ step] = scale_ref[pl.ds(at, 1), :]
    direct, mirrors = pair_rows(places)
    quarters = [pl.ds(turn * block, block) for turn in range(4)]
    order = order_of(places)
    for rank, at in enumerate(order):
        signal[pl.ds(at * width, width), :] = (packed_ref[rank, 4].astype(F32) * scales[at]).astype(BF16)
    mixed[...] = matmul(first_ref[...], signal[...])
    for residue in range(places + 1):
        over, under = pl.ds(residue * width, width), pl.ds(half + residue * width, width)
        values = []
        for lanes in quarters:
            real, imag = mixed[over, lanes], mixed[under, lanes]
            cos, sin = twist_ref[0, pl.ds(residue, 1), lanes], twist_ref[1, pl.ds(residue, 1), lanes]
            values.append((real * cos + imag * sin, imag * cos - real * sin))
        for turn, (real, imag) in enumerate(butterfly(values, 1)):
            if turn > 0:
                cos, sin = spin_ref[0, pl.ds(turn, 1), :], spin_ref[1, pl.ds(turn, 1), :]
                real, imag = real * cos + imag * sin, imag * cos - real * sin
            at = pl.ds(turn * half + residue * width, width)
            work[at, pl.ds(0, block)] = real.astype(BF16)
            work[at, pl.ds(block, block)] = imag.astype(BF16)
    for row, holder in enumerate(mirrors[1:places]):
        for part in range(2):
            for turn in range(4):
                at = pl.ds((part * 4 + 3 - turn) * inner + row * width, width)
                mirror[at, :] = packed_ref[holder[0], 2 * part + holder[1], :, quarters[turn]]
    reversed_bins = matmul(mirror[...], reverse_ref[...])
    spectral = matmul(work[...], dft_ref[0])
    for turn in range(4):
        for residue, holder in enumerate(direct):
            at = turn * half + residue * width
            real, imag = spectral[at : at + width, :block], spectral[at : at + width, block:]
            response_real = packed_ref[holder[0], holder[1], :, quarters[turn]].astype(F32)
            response_imag = packed_ref[holder[0], 2 + holder[1], :, quarters[turn]].astype(F32)
            if mirrors[residue] is not None:
                begin = turn * inner + (residue - 1) * width
                response_real = response_real + reversed_bins[begin : begin + width]
                begin = begin + 4 * inner
                response_imag = response_imag - reversed_bins[begin : begin + width]
            work[pl.ds(at, width), pl.ds(0, block)] = (real * response_real - imag * response_imag).astype(BF16)
            work[pl.ds(at, width), pl.ds(block, block)] = (real * response_imag + imag * response_real).astype(BF16)
    restored = matmul(work[...], dft_ref[1])
    for residue in range(places + 1):
        values = []
        for turn in range(4):
            at = turn * half + residue * width
            real, imag = restored[at : at + width, :block], restored[at : at + width, block:]
            if turn > 0:
                cos, sin = spin_ref[0, pl.ds(turn, 1), :], spin_ref[1, pl.ds(turn, 1), :]
                real, imag = real * cos - imag * sin, imag * cos + real * sin
            values.append((real, imag))
        for lanes, (real, imag) in zip(quarters, butterfly(values, -1)):
            cos, sin = twist_ref[0, pl.ds(residue, 1), lanes], twist_ref[1, pl.ds(residue, 1), lanes]
            both[pl.ds(residue * width, width), lanes] = (real * cos - imag * sin).astype(BF16)
            both[pl.ds(half + residue * width, width), lanes] = (imag * cos + real * sin).astype(BF16)
    result = matmul(last_ref[...], both[...]).astype(BF16)
    for rank, at in enumerate(order):
        out_ref[pl.ds(rank * width, width), :] = result[at * width : (at + 1) * width]


def convolve_kernel(packed_ref, first_ref, last_ref, twist_ref, dft_ref, scale_ref, out_ref, left, right):
    wide, rows = out_ref.shape
    half = 2 * wide
    signal = (packed_ref[4].astype(F32) * scale_ref[...]).astype(BF16)
    mixed = matmul(first_ref[...], signal)
    real, imag = mixed[:half], mixed[half:]
    cos_twist, sin_twist = twist_ref[0], twist_ref[1]
    turned_real = (real * cos_twist + imag * sin_twist).astype(BF16)
    turned_imag = (imag * cos_twist - real * sin_twist).astype(BF16)
    left[pl.ds(0, half), pl.ds(0, rows)] = turned_real
    left[pl.ds(0, half), pl.ds(rows, rows)] = turned_imag
    left[pl.ds(half, half), pl.ds(0, rows)] = turned_imag
    left[pl.ds(half, half), pl.ds(rows, rows)] = -turned_real
    mixed = matmul(left[...], dft_ref[...])
    real, imag = mixed[:half], mixed[half:]
    response_real = packed_ref[0:2].reshape(half, rows).astype(F32)
    response_imag = packed_ref[2:4].reshape(half, rows).astype(F32)
    product_real = (real * response_real - imag * response_imag).astype(BF16)
    product_imag = (real * response_imag + imag * response_real).astype(BF16)
    right[pl.ds(0, half), pl.ds(0, rows)] = product_real
    right[pl.ds(0, half), pl.ds(rows, rows)] = -product_imag
    right[pl.ds(half, half), pl.ds(0, rows)] = product_imag
    right[pl.ds(half, half), pl.ds(rows, rows)] = product_real
    mixed = matmul(right[...], dft_ref[...])
    real, imag = mixed[:half], mixed[half:]
    turned_real = (real * cos_twist - imag * sin_twist).astype(BF16)
    turned_imag = (imag * cos_twist + real * sin_twist).astype(BF16)
    both = jnp.concatenate([turned_real, turned_imag], axis=0)
    out_ref[...] = matmul(last_ref[...], both).astype(BF16)


def finish_kernel(conv_ref, skipped_ref, scale_ref, post_ref, out_ref):
    conv = conv_ref[...]
    if len(conv_ref.shape) == 3:
        order = order_of(conv_ref.shape[0])
        conv = jnp.concatenate([conv_ref[order.index(place)] for place in range(len(order))])
    turned = conv.astype(F32) + skipped_ref[...].astype(F32) * scale_ref[...]
    out_ref[...] = (post_ref[...].astype(F32) * turned.T).astype(BF16)


def call(kernel, out_shape, flops, moved, *operands, limit=VMEM_LIMIT, **options):
    return pl.pallas_call(
        kernel,
        out_shape=out_shape,
        compiler_params=pltpu.CompilerParams(vmem_limit_bytes=limit),
        cost_estimate=pl.CostEstimate(flops=flops, bytes_accessed=moved, transcendentals=0),
        **options,
    )(*operands)


def exchange(value):
    ranks = [list(order_of(lax.axis_size("seq")))]
    return lax.all_to_all(value, "seq", split_axis=0, concat_axis=0, tiled=True, axis_index_groups=ranks)


def swap(value, axis, apart):
    return lax.ppermute(value, axis, [(place, place ^ apart) for place in range(lax.axis_size(axis))])


def local(features, pre_gate, post_gate, norm_gain, skip_weight, spectrum):
    rows, wide = features.shape
    places = lax.axis_size("seq")
    groups = lax.axis_size("chan")
    width = wide // places
    piled = width % 16 == 0
    cells = rows * wide
    shape = jax.ShapeDtypeStruct
    vmem, anywhere = pl.BlockSpec(memory_space=pltpu.VMEM), pl.BlockSpec(memory_space=pl.ANY)
    squares, skipped, packed = call(
        prepare_kernel,
        (
            shape((1, rows), F32),
            shape((wide, rows), BF16),
            shape((places, 5, width, rows) if piled else (5, wide, rows), BF16),
        ),
        10 * cells,
        32 * cells,
        features,
        pre_gate,
        norm_gain[None, :],
        skip_weight[None, :],
        spectrum,
        limit=WHOLE_VMEM,
        in_specs=[anywhere] * 5,
        out_specs=(anywhere, anywhere, anywhere),
        scratch_shapes=[
            pltpu.VMEM(features.shape, BF16),
            pltpu.VMEM(pre_gate.shape, BF16),
            pltpu.VMEM((1, wide), F32),
            pltpu.VMEM((1, wide), F32),
            pltpu.VMEM(spectrum.shape, F32),
            pltpu.VMEM((1, rows), F32),
            pltpu.VMEM((wide, rows), BF16),
            pltpu.VMEM((5, places, width, rows) if piled else (5, wide, rows), BF16),
            pltpu.SemaphoreType.DMA((8,)),
            pltpu.SemaphoreType.DMA((7,)),
        ],
    )
    if not piled:
        packed = packed.reshape(5, places, width, rows).transpose(1, 0, 2, 3)
    gathered = exchange(packed)
    others = [swap(squares, "chan", apart) for apart in range(1, groups)]
    scale = call(
        functools.partial(scale_kernel, wide * groups), shape((1, rows), F32), 8 * rows, 32 * rows, squares, *others
    )
    if piled:
        near = jnp.concatenate([scale, swap(scale, "seq", 1)])
        scales = [near] + [swap(near, "seq", steps[0]) for steps in hops(places)[1:]]
    else:
        scales = [jnp.repeat(lax.all_gather(scale, "seq", axis=0, tiled=True), width, axis=0)]
        response = gathered[:, :4].reshape(places, 2, 2, width, rows).transpose(1, 0, 2, 3, 4)
        gathered = jnp.concatenate([response.reshape(4, wide, rows), gathered[:, 4].reshape(1, wide, rows)])
    if piled:
        constants = folded_tables(places, rows, width)
        half = constants[0].shape[0] // 2
        scratch = [
            pltpu.VMEM((places, 1, rows), F32),
            pltpu.VMEM((wide, rows), BF16),
            pltpu.VMEM((8 * (half - 2 * width), rows // 4), BF16),
            pltpu.VMEM((2 * half, rows), F32),
            pltpu.VMEM((4 * half, rows // 2), BF16),
            pltpu.VMEM((2 * half, rows), BF16),
        ]
    else:
        constants = tables(places, rows, width)
        scratch = [pltpu.VMEM((4 * wide, 2 * rows), BF16)] * 2
    conv = call(
        folded_kernel if piled else convolve_kernel,
        shape((wide, rows), BF16),
        20 * cells * rows,
        20 * cells,
        gathered,
        *constants,
        *scales,
        scratch_shapes=scratch,
    )
    conv = exchange(conv.reshape(places, width, rows))
    if not piled:
        conv = conv.reshape(wide, rows)
    return call(finish_kernel, shape((rows, wide), BF16), 10 * cells, 8 * cells, conv, skipped, scale, post_gate)


def solution(mesh):
    return jax.shard_map(
        local,
        mesh=mesh,
        in_specs=(
            P("seq", "chan"),
            P("seq", "chan"),
            P("seq", "chan"),
            P("chan"),
            P("chan"),
            P(None, "seq", None, "chan"),
        ),
        out_specs=P("seq", "chan"),
        check_vma=False,
    )
```

```python
import functools

import jax
import jax.numpy as jnp
import numpy as np
from jax import lax
from jax.experimental import pallas as pl
from jax.experimental.pallas import tpu as pltpu
from jax.sharding import PartitionSpec as P

EPS = 1e-06
BF16 = jnp.bfloat16
F32 = jnp.float32
TAIL = 16
VMEM_LIMIT = 48 * 1024 * 1024
WHOLE_VMEM = 63 * 1024 * 1024 + 512 * 1024


def order_of(places):
    return (0, 2, 6, 4, 1, 5, 3, 7) if places == 8 else tuple(range(places))


def reverse_bits(index, levels):
    return sum((index >> bit & 1) << levels - 1 - bit for bit in range(levels))


@functools.lru_cache(maxsize=None)
def tables(places, rows, width):
    levels = places.bit_length() - 1
    stride = 2 * places
    bins = stride * rows
    residues = np.array([2 * reverse_bits(place, levels) + parity for place in range(places) for parity in range(2)])
    angle = 2.0 * np.pi * ((residues[:, None] * np.arange(places)[None, :]) % stride) / stride
    same = np.eye(width)
    first = np.concatenate([np.kron(np.cos(angle), same), np.kron(-np.sin(angle), same)])
    last = first.T / bins
    angle = 2.0 * np.pi * ((residues[:, None] * np.arange(rows)[None, :]) % bins) / bins
    twist = np.repeat(np.stack([np.cos(angle), np.sin(angle)]), width, axis=1)
    series = np.arange(rows)
    angle = 2.0 * np.pi * ((series[:, None] * series[None, :]) % rows) / rows
    dft = np.concatenate([np.cos(angle), np.sin(angle)])
    return (
        first.astype(jnp.bfloat16),
        last.astype(jnp.bfloat16),
        twist.astype(np.float32),
        dft.astype(jnp.bfloat16),
    )


def pair_rows(places):
    levels = places.bit_length() - 1

    def holder(residue):
        return order_of(places).index(reverse_bits(residue // 2, levels)), residue % 2

    mirrors = [None if residue % places == 0 else holder(2 * places - residue) for residue in range(places + 1)]
    return [holder(residue) for residue in range(places + 1)], mirrors


@functools.lru_cache(maxsize=None)
def folded_tables(places, rows, width):
    stride = 2 * places
    bins = stride * rows
    residues = np.arange(places + 1)
    angle = 2.0 * np.pi * ((residues[:, None] * np.arange(places)[None, :]) % stride) / stride
    same = np.eye(width)
    first = np.concatenate([np.kron(np.cos(angle), same), np.kron(-np.sin(angle), same)])
    last = first.T / bins
    angle = 2.0 * np.pi * ((residues[:, None] * np.arange(rows)[None, :]) % bins) / bins
    twist = np.stack([np.cos(angle), np.sin(angle)])
    block = rows // 4
    series = np.arange(block)
    angle = 2.0 * np.pi * ((np.arange(4)[:, None] * series[None, :]) % rows) / rows
    spin = np.stack([np.cos(angle), np.sin(angle)])
    angle = 2.0 * np.pi * ((series[:, None] * series[None, :]) % block) / block
    cos, sin = np.cos(angle), np.sin(angle)
    there = np.block([[cos, -sin], [sin, cos]])
    back = np.block([[cos, sin], [-sin, cos]])
    reverse = np.eye(block)[::-1]
    return (
        first.astype(jnp.bfloat16),
        last.astype(jnp.bfloat16),
        twist.astype(np.float32),
        spin.astype(np.float32),
        np.stack([there, back]).astype(jnp.bfloat16),
        reverse.astype(jnp.bfloat16),
    )


def prepare_kernel(
    features_ref,
    pre_ref,
    gain_ref,
    skip_ref,
    spectrum_ref,
    skipped_ref,
    scaled_ref,
    packed_ref,
    features_in,
    pre_in,
    gain_in,
    skip_in,
    spectrum_in,
    skipped_out,
    scaled_out,
    packed_out,
    in_sems,
    out_sems,
):
    blocks = [(part, parity) for part in range(2) for parity in range(2)]
    pairs = [(features_ref, features_in), (pre_ref, pre_in), (gain_ref, gain_in), (skip_ref, skip_in)]
    pairs += [(spectrum_ref.at[block], spectrum_in.at[block]) for block in blocks]
    arriving = [pltpu.make_async_copy(*pair, in_sems.at[slot]) for slot, pair in enumerate(pairs)]
    for copy in arriving:
        copy.start()
    leaving = []

    def leave(source, target):
        copy = pltpu.make_async_copy(source, target, out_sems.at[len(leaving)])
        copy.start()
        leaving.append(copy)

    def pack(slot, turned):
        if len(packed_ref.shape) == 4:
            places, width = packed_out.shape[1:3]
            for rank, place in enumerate(order_of(places)):
                packed_out[slot, rank] = turned[place * width : (place + 1) * width]
            leave(packed_out.at[slot], packed_ref.at[:, slot])
        else:
            packed_out[slot] = turned
            leave(packed_out.at[slot], packed_ref.at[slot])

    for copy in arriving[:4]:
        copy.wait()
    features = features_in[...].astype(F32)
    scaled = features * gain_in[...] * pre_in[...].astype(F32)
    wide = scaled.shape[1]
    scaled_out[pl.ds(0, wide), :] = scaled.astype(BF16).T
    turned = features_in[...].T.astype(F32)
    squares = jnp.sum(turned * turned, axis=0, keepdims=True)
    high = squares.astype(BF16).astype(F32)
    row = lax.broadcasted_iota(jnp.int32, (TAIL, squares.shape[1]), 0)
    tail = jnp.where(row == 0, high, jnp.where(row == 1, squares - high, 0.0))
    scaled_out[pl.ds(wide, TAIL), :] = tail.astype(BF16)
    leave(scaled_out, scaled_ref)
    skipped_out[...] = (scaled * skip_in[...]).astype(BF16).T
    leave(skipped_out, skipped_ref)
    for slot, block in enumerate(blocks):
        arriving[4 + slot].wait()
        if len(packed_ref.shape) == 4:
            quarter = spectrum_in.shape[2] // 4
            rows = [spectrum_in[(*block, pl.ds(turn, quarter, stride=4), slice(None))] for turn in range(4)]
            pack(slot, jnp.concatenate([row.astype(BF16).T for row in rows], axis=1))
        else:
            pack(slot, spectrum_in[block].astype(BF16).T)
    for copy in leaving:
        copy.wait()


def split_kernel(gathered_ref, squares_ref, own_ref, tail, sems):
    places, width = own_ref.shape[:2]
    wide = gathered_ref.shape[1] - TAIL
    begin = pl.multiple_of(lax.axis_index("seq") * width, width)
    first = pltpu.make_async_copy(gathered_ref.at[:, pl.ds(wide, TAIL), :], tail, sems.at[0])
    second = pltpu.make_async_copy(gathered_ref.at[:, pl.ds(begin, width), :], own_ref, sems.at[1])
    first.start()
    second.start()
    first.wait()
    squares_ref[...] = tail[:, 0, :].astype(F32) + tail[:, 1, :].astype(F32)
    second.wait()


def scale_kernel(channels, *refs):
    square_refs, scale_ref = refs[:-1], refs[-1]
    total = square_refs[0][...]
    for square_ref in square_refs[1:]:
        total = total + square_ref[...]
    scale_ref[...] = lax.rsqrt(total / channels + EPS)


def matmul(left, right):
    return jnp.dot(left, right, preferred_element_type=F32)


def butterfly(values, direction):
    (real0, imag0), (real1, imag1), (real2, imag2), (real3, imag3) = values
    even, odd = (real0 + real2, imag0 + imag2), (real1 + real3, imag1 + imag3)
    even_gap, odd_gap = (real0 - real2, imag0 - imag2), (real1 - real3, imag1 - imag3)
    lower = (even_gap[0] + odd_gap[1], even_gap[1] - odd_gap[0])
    upper = (even_gap[0] - odd_gap[1], even_gap[1] + odd_gap[0])
    total, gap = (even[0] + odd[0], even[1] + odd[1]), (even[0] - odd[0], even[1] - odd[1])
    return [total, lower, gap, upper] if direction > 0 else [total, upper, gap, lower]


def folded_kernel(
    own_ref,
    scale_ref,
    packed_ref,
    first_ref,
    last_ref,
    twist_ref,
    spin_ref,
    dft_ref,
    reverse_ref,
    out_ref,
    signal,
    mirror,
    mixed,
    work,
    both,
):
    wide, rows = out_ref.shape
    places, width = own_ref.shape[:2]
    half, block = first_ref.shape[0] // 2, rows // 4
    inner = half - 2 * width
    direct, mirrors = pair_rows(places)
    quarters = [pl.ds(turn * block, block) for turn in range(4)]
    order = order_of(places)
    for at in range(places):
        scaled = own_ref[at].astype(F32) * scale_ref[pl.ds(at, 1), :]
        signal[pl.ds(at * width, width), :] = scaled.astype(BF16)
    mixed[...] = matmul(first_ref[...], signal[...])
    for residue in range(places + 1):
        over, under = pl.ds(residue * width, width), pl.ds(half + residue * width, width)
        values = []
        for lanes in quarters:
            real, imag = mixed[over, lanes], mixed[under, lanes]
            cos, sin = twist_ref[0, pl.ds(residue, 1), lanes], twist_ref[1, pl.ds(residue, 1), lanes]
            values.append((real * cos + imag * sin, imag * cos - real * sin))
        for turn, (real, imag) in enumerate(butterfly(values, 1)):
            if turn > 0:
                cos, sin = spin_ref[0, pl.ds(turn, 1), :], spin_ref[1, pl.ds(turn, 1), :]
                real, imag = real * cos + imag * sin, imag * cos - real * sin
            at = pl.ds(turn * half + residue * width, width)
            work[at, pl.ds(0, block)] = real.astype(BF16)
            work[at, pl.ds(block, block)] = imag.astype(BF16)
    for row, holder in enumerate(mirrors[1:places]):
        for part in range(2):
            for turn in range(4):
                at = pl.ds((part * 4 + 3 - turn) * inner + row * width, width)
                mirror[at, :] = packed_ref[holder[0], 2 * part + holder[1], :, quarters[turn]]
    reversed_bins = matmul(mirror[...], reverse_ref[...])
    spectral = matmul(work[...], dft_ref[0])
    for turn in range(4):
        for residue, holder in enumerate(direct):
            at = turn * half + residue * width
            real, imag = spectral[at : at + width, :block], spectral[at : at + width, block:]
            response_real = packed_ref[holder[0], holder[1], :, quarters[turn]].astype(F32)
            response_imag = packed_ref[holder[0], 2 + holder[1], :, quarters[turn]].astype(F32)
            if mirrors[residue] is not None:
                begin = turn * inner + (residue - 1) * width
                response_real = response_real + reversed_bins[begin : begin + width]
                begin = begin + 4 * inner
                response_imag = response_imag - reversed_bins[begin : begin + width]
            work[pl.ds(at, width), pl.ds(0, block)] = (real * response_real - imag * response_imag).astype(BF16)
            work[pl.ds(at, width), pl.ds(block, block)] = (real * response_imag + imag * response_real).astype(BF16)
    restored = matmul(work[...], dft_ref[1])
    for residue in range(places + 1):
        values = []
        for turn in range(4):
            at = turn * half + residue * width
            real, imag = restored[at : at + width, :block], restored[at : at + width, block:]
            if turn > 0:
                cos, sin = spin_ref[0, pl.ds(turn, 1), :], spin_ref[1, pl.ds(turn, 1), :]
                real, imag = real * cos - imag * sin, imag * cos + real * sin
            values.append((real, imag))
        for lanes, (real, imag) in zip(quarters, butterfly(values, -1)):
            cos, sin = twist_ref[0, pl.ds(residue, 1), lanes], twist_ref[1, pl.ds(residue, 1), lanes]
            both[pl.ds(residue * width, width), lanes] = (real * cos - imag * sin).astype(BF16)
            both[pl.ds(half + residue * width, width), lanes] = (imag * cos + real * sin).astype(BF16)
    result = matmul(last_ref[...], both[...]).astype(BF16)
    for rank, at in enumerate(order):
        out_ref[pl.ds(rank * width, width), :] = result[at * width : (at + 1) * width]


def convolve_kernel(own_ref, scale_ref, packed_ref, first_ref, last_ref, twist_ref, dft_ref, out_ref, left, right):
    wide, rows = out_ref.shape
    half = 2 * wide
    signal = (own_ref[...].astype(F32) * scale_ref[...]).astype(BF16)
    mixed = matmul(first_ref[...], signal)
    real, imag = mixed[:half], mixed[half:]
    cos_twist, sin_twist = twist_ref[0], twist_ref[1]
    turned_real = (real * cos_twist + imag * sin_twist).astype(BF16)
    turned_imag = (imag * cos_twist - real * sin_twist).astype(BF16)
    left[pl.ds(0, half), pl.ds(0, rows)] = turned_real
    left[pl.ds(0, half), pl.ds(rows, rows)] = turned_imag
    left[pl.ds(half, half), pl.ds(0, rows)] = turned_imag
    left[pl.ds(half, half), pl.ds(rows, rows)] = -turned_real
    mixed = matmul(left[...], dft_ref[...])
    real, imag = mixed[:half], mixed[half:]
    response_real = packed_ref[0:2].reshape(half, rows).astype(F32)
    response_imag = packed_ref[2:4].reshape(half, rows).astype(F32)
    product_real = (real * response_real - imag * response_imag).astype(BF16)
    product_imag = (real * response_imag + imag * response_real).astype(BF16)
    right[pl.ds(0, half), pl.ds(0, rows)] = product_real
    right[pl.ds(0, half), pl.ds(rows, rows)] = -product_imag
    right[pl.ds(half, half), pl.ds(0, rows)] = product_imag
    right[pl.ds(half, half), pl.ds(rows, rows)] = product_real
    mixed = matmul(right[...], dft_ref[...])
    real, imag = mixed[:half], mixed[half:]
    turned_real = (real * cos_twist - imag * sin_twist).astype(BF16)
    turned_imag = (imag * cos_twist + real * sin_twist).astype(BF16)
    both = jnp.concatenate([turned_real, turned_imag], axis=0)
    out_ref[...] = matmul(last_ref[...], both).astype(BF16)


def finish_kernel(conv_ref, skipped_ref, scale_ref, post_ref, out_ref):
    conv = conv_ref[...]
    if len(conv_ref.shape) == 3:
        order = order_of(conv_ref.shape[0])
        conv = jnp.concatenate([conv_ref[order.index(place)] for place in range(len(order))])
    turned = conv.astype(F32) + skipped_ref[...].astype(F32) * scale_ref[pl.ds(lax.axis_index("seq"), 1), :]
    out_ref[...] = (post_ref[...].astype(F32) * turned.T).astype(BF16)


def call(kernel, out_shape, flops, moved, *operands, limit=VMEM_LIMIT, **options):
    return pl.pallas_call(
        kernel,
        out_shape=out_shape,
        compiler_params=pltpu.CompilerParams(vmem_limit_bytes=limit),
        cost_estimate=pl.CostEstimate(flops=flops, bytes_accessed=moved, transcendentals=0),
        **options,
    )(*operands)


def exchange(value):
    ranks = [list(order_of(lax.axis_size("seq")))]
    return lax.all_to_all(value, "seq", split_axis=0, concat_axis=0, tiled=True, axis_index_groups=ranks)


def swap(value, axis, apart):
    return lax.ppermute(value, axis, [(place, place ^ apart) for place in range(lax.axis_size(axis))])


def local(features, pre_gate, post_gate, norm_gain, skip_weight, spectrum):
    rows, wide = features.shape
    places = lax.axis_size("seq")
    groups = lax.axis_size("chan")
    width = wide // places
    piled = width % 16 == 0
    cells = rows * wide
    shape = jax.ShapeDtypeStruct
    vmem, anywhere = pl.BlockSpec(memory_space=pltpu.VMEM), pl.BlockSpec(memory_space=pl.ANY)
    skipped, scaled, packed = call(
        prepare_kernel,
        (
            shape((wide, rows), BF16),
            shape((wide + TAIL, rows), BF16),
            shape((places, 4, width, rows) if piled else (4, wide, rows), BF16),
        ),
        10 * cells,
        32 * cells,
        features,
        pre_gate,
        norm_gain[None, :],
        skip_weight[None, :],
        spectrum,
        limit=WHOLE_VMEM,
        in_specs=[anywhere] * 5,
        out_specs=(anywhere, anywhere, anywhere),
        scratch_shapes=[
            pltpu.VMEM(features.shape, BF16),
            pltpu.VMEM(pre_gate.shape, BF16),
            pltpu.VMEM((1, wide), F32),
            pltpu.VMEM((1, wide), F32),
            pltpu.VMEM(spectrum.shape, F32),
            pltpu.VMEM((wide, rows), BF16),
            pltpu.VMEM((wide + TAIL, rows), BF16),
            pltpu.VMEM((4, places, width, rows) if piled else (4, wide, rows), BF16),
            pltpu.SemaphoreType.DMA((8,)),
            pltpu.SemaphoreType.DMA((6,)),
        ],
    )
    signals = lax.all_gather(scaled, "seq", axis=0)
    if not piled:
        packed = packed.reshape(4, places, width, rows).transpose(1, 0, 2, 3)
    response = exchange(packed)
    if piled:
        squares, own = call(
            split_kernel,
            (shape((places, rows), F32), shape((places, width, rows), BF16)),
            2 * cells,
            4 * cells,
            signals,
            in_specs=[anywhere],
            scratch_shapes=[pltpu.VMEM((places, TAIL, rows), BF16), pltpu.SemaphoreType.DMA((2,))],
        )
    else:
        squares = signals[:, wide].astype(F32) + signals[:, wide + 1].astype(F32)
        own = lax.dynamic_slice_in_dim(signals, lax.axis_index("seq") * width, width, axis=1).reshape(wide, rows)
        response = response.reshape(places, 2, 2, width, rows).transpose(1, 0, 2, 3, 4).reshape(4, wide, rows)
    others = [swap(squares, "chan", apart) for apart in range(1, groups)]
    scale = call(
        functools.partial(scale_kernel, wide * groups),
        shape((places, rows), F32),
        8 * places * rows,
        20 * places * rows,
        squares,
        *others,
    )
    if piled:
        constants = folded_tables(places, rows, width)
        half = constants[0].shape[0] // 2
        scratch = [
            pltpu.VMEM((wide, rows), BF16),
            pltpu.VMEM((8 * (half - 2 * width), rows // 4), BF16),
            pltpu.VMEM((2 * half, rows), F32),
            pltpu.VMEM((4 * half, rows // 2), BF16),
            pltpu.VMEM((2 * half, rows), BF16),
        ]
    else:
        constants = tables(places, rows, width)
        scratch = [pltpu.VMEM((4 * wide, 2 * rows), BF16)] * 2
    conv = call(
        folded_kernel if piled else convolve_kernel,
        shape((wide, rows), BF16),
        20 * cells * rows,
        20 * cells,
        own,
        scale if piled else jnp.repeat(scale, width, axis=0),
        response,
        *constants,
        scratch_shapes=scratch,
    )
    conv = exchange(conv.reshape(places, width, rows))
    if not piled:
        conv = conv.reshape(wide, rows)
    return call(finish_kernel, shape((rows, wide), BF16), 10 * cells, 8 * cells, conv, skipped, scale, post_gate)


def solution(mesh):
    return jax.shard_map(
        local,
        mesh=mesh,
        in_specs=(
            P("seq", "chan"),
            P("seq", "chan"),
            P("seq", "chan"),
            P("chan"),
            P("chan"),
            P(None, "seq", None, "chan"),
        ),
        out_specs=P("seq", "chan"),
        check_vma=False,
    )
```

```python
import functools

import jax
import jax.numpy as jnp
import numpy as np
from jax import lax
from jax.experimental import pallas as pl
from jax.experimental.pallas import tpu as pltpu
from jax.sharding import PartitionSpec as P

EPS = 1e-06
BF16 = jnp.bfloat16
F32 = jnp.float32
VMEM_LIMIT = 48 * 1024 * 1024
WHOLE_VMEM = 63 * 1024 * 1024 + 512 * 1024


def order_of(places):
    return (0, 3, 4, 7, 1, 2, 5, 6) if places == 8 else tuple(range(places))


def reverse_bits(index, levels):
    return sum((index >> bit & 1) << levels - 1 - bit for bit in range(levels))


@functools.lru_cache(maxsize=None)
def tables(places, rows, width):
    levels = places.bit_length() - 1
    stride = 2 * places
    bins = stride * rows
    residues = np.array([2 * reverse_bits(place, levels) + parity for place in range(places) for parity in range(2)])
    angle = 2.0 * np.pi * ((residues[:, None] * np.arange(places)[None, :]) % stride) / stride
    same = np.eye(width)
    first = np.concatenate([np.kron(np.cos(angle), same), np.kron(-np.sin(angle), same)])
    last = first.T / bins
    angle = 2.0 * np.pi * ((residues[:, None] * np.arange(rows)[None, :]) % bins) / bins
    twist = np.repeat(np.stack([np.cos(angle), np.sin(angle)]), width, axis=1)
    series = np.arange(rows)
    angle = 2.0 * np.pi * ((series[:, None] * series[None, :]) % rows) / rows
    dft = np.concatenate([np.cos(angle), np.sin(angle)])
    return (
        first.astype(jnp.bfloat16),
        last.astype(jnp.bfloat16),
        twist.astype(np.float32),
        dft.astype(jnp.bfloat16),
    )


def pair_rows(places):
    levels = places.bit_length() - 1

    def holder(residue):
        return order_of(places).index(reverse_bits(residue // 2, levels)), residue % 2

    mirrors = [None if residue % places == 0 else holder(2 * places - residue) for residue in range(places + 1)]
    return [holder(residue) for residue in range(places + 1)], mirrors


@functools.lru_cache(maxsize=None)
def folded_tables(places, rows, width):
    stride = 2 * places
    bins = stride * rows
    residues = np.arange(places + 1)
    angle = 2.0 * np.pi * ((residues[:, None] * np.arange(places)[None, :]) % stride) / stride
    parts = np.stack([np.cos(angle), -np.sin(angle)], axis=1)
    first = np.kron(parts.reshape(-1, places), np.eye(width))
    last = first.T / bins
    angle = 2.0 * np.pi * ((residues[:, None] * np.arange(rows)[None, :]) % bins) / bins
    twist = np.stack([np.cos(angle), np.sin(angle)])
    block = rows // 4
    series = np.arange(block)
    angle = 2.0 * np.pi * ((np.arange(4)[:, None] * series[None, :]) % rows) / rows
    spin = np.stack([np.cos(angle), np.sin(angle)])
    angle = 2.0 * np.pi * ((series[:, None] * series[None, :]) % block) / block
    cos, sin = np.cos(angle), np.sin(angle)
    there = np.block([[cos, -sin], [sin, cos]])
    back = np.block([[cos, sin], [-sin, cos]])
    reverse = np.eye(block)[::-1]
    return (
        first.astype(jnp.bfloat16),
        last.astype(jnp.bfloat16),
        twist.astype(np.float32),
        spin.astype(np.float32),
        np.stack([there, back]).astype(jnp.bfloat16),
        reverse.astype(jnp.bfloat16),
    )


def hops(places):
    return [[apart, apart + 1] for apart in range(0, places, 2)]


def prepare_kernel(
    features_ref,
    pre_ref,
    gain_ref,
    skip_ref,
    spectrum_ref,
    squares_ref,
    skipped_ref,
    packed_ref,
    features_in,
    pre_in,
    gain_in,
    skip_in,
    spectrum_in,
    squares_out,
    skipped_out,
    packed_out,
    in_sems,
    out_sems,
):
    blocks = [(part, parity) for part in range(2) for parity in range(2)]
    pairs = [(features_ref, features_in), (pre_ref, pre_in), (gain_ref, gain_in), (skip_ref, skip_in)]
    pairs += [(spectrum_ref.at[block], spectrum_in.at[block]) for block in blocks]
    arriving = [pltpu.make_async_copy(*pair, in_sems.at[slot]) for slot, pair in enumerate(pairs)]
    for copy in arriving:
        copy.start()
    leaving = []

    def leave(source, target):
        copy = pltpu.make_async_copy(source, target, out_sems.at[len(leaving)])
        copy.start()
        leaving.append(copy)

    def pack(slot, turned):
        if len(packed_ref.shape) == 4:
            places, width = packed_out.shape[1:3]
            for rank, place in enumerate(order_of(places)):
                packed_out[slot, rank] = turned[place * width : (place + 1) * width]
            leave(packed_out.at[slot], packed_ref.at[:, slot])
        else:
            packed_out[slot] = turned
            leave(packed_out.at[slot], packed_ref.at[slot])

    for copy in arriving[:4]:
        copy.wait()
    features = features_in[...].astype(F32)
    scaled = features * gain_in[...] * pre_in[...].astype(F32)
    pack(4, scaled.astype(BF16).T)
    skipped_out[...] = (scaled * skip_in[...]).astype(BF16).T
    leave(skipped_out, skipped_ref)
    turned = features_in[...].T.astype(F32)
    squares_out[...] = jnp.sum(turned * turned, axis=0, keepdims=True)
    leave(squares_out, squares_ref)
    for slot, block in enumerate(blocks):
        arriving[4 + slot].wait()
        if len(packed_ref.shape) == 4:
            quarter = spectrum_in.shape[2] // 4
            rows = [spectrum_in[(*block, pl.ds(turn, quarter, stride=4), slice(None))] for turn in range(4)]
            pack(slot, jnp.concatenate([row.astype(BF16).T for row in rows], axis=1))
        else:
            pack(slot, spectrum_in[block].astype(BF16).T)
    for copy in leaving:
        copy.wait()


def scale_kernel(channels, *refs):
    square_refs, scale_ref = refs[:-1], refs[-1]
    total = square_refs[0][...]
    for square_ref in square_refs[1:]:
        total = total + square_ref[...]
    scale_ref[...] = lax.rsqrt(total / channels + EPS)


def matmul(left, right):
    return jnp.dot(left, right, preferred_element_type=F32)


def butterfly(values, direction):
    (real0, imag0), (real1, imag1), (real2, imag2), (real3, imag3) = values
    even, odd = (real0 + real2, imag0 + imag2), (real1 + real3, imag1 + imag3)
    even_gap, odd_gap = (real0 - real2, imag0 - imag2), (real1 - real3, imag1 - imag3)
    lower = (even_gap[0] + odd_gap[1], even_gap[1] - odd_gap[0])
    upper = (even_gap[0] - odd_gap[1], even_gap[1] + odd_gap[0])
    total, gap = (even[0] + odd[0], even[1] + odd[1]), (even[0] - odd[0], even[1] - odd[1])
    return [total, lower, gap, upper] if direction > 0 else [total, upper, gap, lower]


def folded_kernel(packed_ref, first_ref, last_ref, twist_ref, spin_ref, dft_ref, reverse_ref, *refs):
    scale_refs, (out_ref, scales, signal, mirror, forward, backward, both) = refs[:-7], refs[-7:]
    wide, rows = out_ref.shape
    places, width = scales.shape[0], wide // scales.shape[0]
    block, inner = rows // 4, mirror.shape[0] // 8
    order = order_of(places)
    direct, mirrors = pair_rows(places)
    quarters = [pl.ds(turn * block, block) for turn in range(4)]
    groups = [range(begin, min(begin + 3, places + 1)) for begin in range(0, places + 1, 3)]
    for row, holder in enumerate(mirrors[1:places]):
        for part in range(2):
            for turn in range(4):
                at = pl.ds((part * 4 + 3 - turn) * inner + row * width, width)
                mirror[at, :] = packed_ref[holder[0], 2 * part + holder[1], :, quarters[turn]]
    reversed_bins = matmul(mirror[...], reverse_ref[...])
    place = lax.axis_index("seq")
    for scale_ref, steps in zip(scale_refs, hops(places)):
        for at, step in enumerate(steps):
            scales[place ^ step] = scale_ref[pl.ds(at, 1), :]
    for rank, at in enumerate(order):
        signal[pl.ds(at * width, width), :] = (packed_ref[rank, 4].astype(F32) * scales[at]).astype(BF16)
    spectral = []
    for group in groups:
        begin = group[0] * width
        mixed = matmul(first_ref[pl.ds(2 * begin, 2 * len(group) * width), :], signal[...])
        for at, residue in enumerate(group):
            over, under = mixed[2 * at * width : (2 * at + 1) * width], mixed[(2 * at + 1) * width : (2 * at + 2) * width]
            values = []
            for turn in range(4):
                real, imag = (part[:, turn * block : (turn + 1) * block] for part in (over, under))
                cos, sin = (twist_ref[part, pl.ds(residue, 1), quarters[turn]] for part in range(2))
                values.append((real * cos + imag * sin, imag * cos - real * sin))
            for turn, (real, imag) in enumerate(butterfly(values, 1)):
                if turn > 0:
                    cos, sin = spin_ref[0, pl.ds(turn, 1), :], spin_ref[1, pl.ds(turn, 1), :]
                    real, imag = real * cos + imag * sin, imag * cos - real * sin
                row = pl.ds(4 * begin + (turn * len(group) + at) * width, width)
                forward[row, pl.ds(0, block)] = real.astype(BF16)
                forward[row, pl.ds(block, block)] = imag.astype(BF16)
        spectral.append(matmul(forward[pl.ds(4 * begin, 4 * len(group) * width), :], dft_ref[0]))
    restored = []
    for group, values in zip(groups, spectral):
        begin = group[0] * width
        for turn in range(4):
            for at, residue in enumerate(group):
                row = (turn * len(group) + at) * width
                real, imag = values[row : row + width, :block], values[row : row + width, block:]
                holder = direct[residue]
                response_real = packed_ref[holder[0], holder[1], :, quarters[turn]].astype(F32)
                response_imag = packed_ref[holder[0], 2 + holder[1], :, quarters[turn]].astype(F32)
                if mirrors[residue] is not None:
                    other = turn * inner + (residue - 1) * width
                    response_real = response_real + reversed_bins[other : other + width]
                    other = other + 4 * inner
                    response_imag = response_imag - reversed_bins[other : other + width]
                target = pl.ds(4 * begin + row, width)
                backward[target, pl.ds(0, block)] = (real * response_real - imag * response_imag).astype(BF16)
                backward[target, pl.ds(block, block)] = (real * response_imag + imag * response_real).astype(BF16)
        restored.append(matmul(backward[pl.ds(4 * begin, 4 * len(group) * width), :], dft_ref[1]))
    for group, turned in zip(groups, restored):
        for at, residue in enumerate(group):
            values = []
            for turn in range(4):
                row = (turn * len(group) + at) * width
                real, imag = turned[row : row + width, :block], turned[row : row + width, block:]
                if turn > 0:
                    cos, sin = spin_ref[0, pl.ds(turn, 1), :], spin_ref[1, pl.ds(turn, 1), :]
                    real, imag = real * cos - imag * sin, imag * cos + real * sin
                values.append((real, imag))
            for lanes, (real, imag) in zip(quarters, butterfly(values, -1)):
                cos, sin = twist_ref[0, pl.ds(residue, 1), lanes], twist_ref[1, pl.ds(residue, 1), lanes]
                both[pl.ds(2 * residue * width, width), lanes] = (real * cos - imag * sin).astype(BF16)
                both[pl.ds((2 * residue + 1) * width, width), lanes] = (imag * cos + real * sin).astype(BF16)
    result = matmul(last_ref[...], both[...]).astype(BF16)
    for rank, at in enumerate(order):
        out_ref[pl.ds(rank * width, width), :] = result[at * width : (at + 1) * width]


def convolve_kernel(packed_ref, first_ref, last_ref, twist_ref, dft_ref, scale_ref, out_ref, left, right):
    wide, rows = out_ref.shape
    half = 2 * wide
    signal = (packed_ref[4].astype(F32) * scale_ref[...]).astype(BF16)
    mixed = matmul(first_ref[...], signal)
    real, imag = mixed[:half], mixed[half:]
    cos_twist, sin_twist = twist_ref[0], twist_ref[1]
    turned_real = (real * cos_twist + imag * sin_twist).astype(BF16)
    turned_imag = (imag * cos_twist - real * sin_twist).astype(BF16)
    left[pl.ds(0, half), pl.ds(0, rows)] = turned_real
    left[pl.ds(0, half), pl.ds(rows, rows)] = turned_imag
    left[pl.ds(half, half), pl.ds(0, rows)] = turned_imag
    left[pl.ds(half, half), pl.ds(rows, rows)] = -turned_real
    mixed = matmul(left[...], dft_ref[...])
    real, imag = mixed[:half], mixed[half:]
    response_real = packed_ref[0:2].reshape(half, rows).astype(F32)
    response_imag = packed_ref[2:4].reshape(half, rows).astype(F32)
    product_real = (real * response_real - imag * response_imag).astype(BF16)
    product_imag = (real * response_imag + imag * response_real).astype(BF16)
    right[pl.ds(0, half), pl.ds(0, rows)] = product_real
    right[pl.ds(0, half), pl.ds(rows, rows)] = -product_imag
    right[pl.ds(half, half), pl.ds(0, rows)] = product_imag
    right[pl.ds(half, half), pl.ds(rows, rows)] = product_real
    mixed = matmul(right[...], dft_ref[...])
    real, imag = mixed[:half], mixed[half:]
    turned_real = (real * cos_twist - imag * sin_twist).astype(BF16)
    turned_imag = (imag * cos_twist + real * sin_twist).astype(BF16)
    both = jnp.concatenate([turned_real, turned_imag], axis=0)
    out_ref[...] = matmul(last_ref[...], both).astype(BF16)


def finish_kernel(conv_ref, skipped_ref, scale_ref, post_ref, out_ref):
    conv = conv_ref[...]
    if len(conv_ref.shape) == 3:
        order = order_of(conv_ref.shape[0])
        conv = jnp.concatenate([conv_ref[order.index(place)] for place in range(len(order))])
    turned = conv.astype(F32) + skipped_ref[...].astype(F32) * scale_ref[...]
    out_ref[...] = (post_ref[...].astype(F32) * turned.T).astype(BF16)


def call(kernel, out_shape, flops, moved, *operands, limit=VMEM_LIMIT, **options):
    return pl.pallas_call(
        kernel,
        out_shape=out_shape,
        compiler_params=pltpu.CompilerParams(vmem_limit_bytes=limit),
        cost_estimate=pl.CostEstimate(flops=flops, bytes_accessed=moved, transcendentals=0),
        **options,
    )(*operands)


def exchange(value):
    ranks = [list(order_of(lax.axis_size("seq")))]
    return lax.all_to_all(value, "seq", split_axis=0, concat_axis=0, tiled=True, axis_index_groups=ranks)


def swap(value, axis, apart):
    return lax.ppermute(value, axis, [(place, place ^ apart) for place in range(lax.axis_size(axis))])


def local(features, pre_gate, post_gate, norm_gain, skip_weight, spectrum):
    rows, wide = features.shape
    places = lax.axis_size("seq")
    groups = lax.axis_size("chan")
    width = wide // places
    piled = width % 16 == 0
    cells = rows * wide
    shape = jax.ShapeDtypeStruct
    vmem, anywhere = pl.BlockSpec(memory_space=pltpu.VMEM), pl.BlockSpec(memory_space=pl.ANY)
    squares, skipped, packed = call(
        prepare_kernel,
        (
            shape((1, rows), F32),
            shape((wide, rows), BF16),
            shape((places, 5, width, rows) if piled else (5, wide, rows), BF16),
        ),
        10 * cells,
        32 * cells,
        features,
        pre_gate,
        norm_gain[None, :],
        skip_weight[None, :],
        spectrum,
        limit=WHOLE_VMEM,
        in_specs=[anywhere] * 5,
        out_specs=(anywhere, anywhere, anywhere),
        scratch_shapes=[
            pltpu.VMEM(features.shape, BF16),
            pltpu.VMEM(pre_gate.shape, BF16),
            pltpu.VMEM((1, wide), F32),
            pltpu.VMEM((1, wide), F32),
            pltpu.VMEM(spectrum.shape, F32),
            pltpu.VMEM((1, rows), F32),
            pltpu.VMEM((wide, rows), BF16),
            pltpu.VMEM((5, places, width, rows) if piled else (5, wide, rows), BF16),
            pltpu.SemaphoreType.DMA((8,)),
            pltpu.SemaphoreType.DMA((7,)),
        ],
    )
    if not piled:
        packed = packed.reshape(5, places, width, rows).transpose(1, 0, 2, 3)
    gathered = exchange(packed)
    others = [swap(squares, "chan", apart) for apart in range(1, groups)]
    scale = call(
        functools.partial(scale_kernel, wide * groups), shape((1, rows), F32), 8 * rows, 32 * rows, squares, *others
    )
    if piled:
        near = jnp.concatenate([scale, swap(scale, "seq", 1)])
        scales = [near] + [swap(near, "seq", steps[0]) for steps in hops(places)[1:]]
    else:
        scales = [jnp.repeat(lax.all_gather(scale, "seq", axis=0, tiled=True), width, axis=0)]
        response = gathered[:, :4].reshape(places, 2, 2, width, rows).transpose(1, 0, 2, 3, 4)
        gathered = jnp.concatenate([response.reshape(4, wide, rows), gathered[:, 4].reshape(1, wide, rows)])
    if piled:
        constants = folded_tables(places, rows, width)
        half = constants[0].shape[0] // 2
        scratch = [
            pltpu.VMEM((places, 1, rows), F32),
            pltpu.VMEM((wide, rows), BF16),
            pltpu.VMEM((8 * (half - 2 * width), rows // 4), BF16),
            pltpu.VMEM((4 * half, rows // 2), BF16),
            pltpu.VMEM((4 * half, rows // 2), BF16),
            pltpu.VMEM((2 * half, rows), BF16),
        ]
    else:
        constants = tables(places, rows, width)
        scratch = [pltpu.VMEM((4 * wide, 2 * rows), BF16)] * 2
    conv = call(
        folded_kernel if piled else convolve_kernel,
        shape((wide, rows), BF16),
        20 * cells * rows,
        20 * cells,
        gathered,
        *constants,
        *scales,
        scratch_shapes=scratch,
    )
    conv = exchange(conv.reshape(places, width, rows))
    if not piled:
        conv = conv.reshape(wide, rows)
    return call(finish_kernel, shape((rows, wide), BF16), 10 * cells, 8 * cells, conv, skipped, scale, post_gate)


def solution(mesh):
    return jax.shard_map(
        local,
        mesh=mesh,
        in_specs=(
            P("seq", "chan"),
            P("seq", "chan"),
            P("seq", "chan"),
            P("chan"),
            P("chan"),
            P(None, "seq", None, "chan"),
        ),
        out_specs=P("seq", "chan"),
        check_vma=False,
    )
```

```python
import functools

import jax
import jax.numpy as jnp
import numpy as np
from jax import lax
from jax.experimental import pallas as pl
from jax.experimental.pallas import tpu as pltpu
from jax.sharding import PartitionSpec as P

EPS = 1e-06
BF16 = jnp.bfloat16
F32 = jnp.float32
VMEM_LIMIT = 48 * 1024 * 1024
WHOLE_VMEM = 63 * 1024 * 1024 + 512 * 1024


def order_of(places):
    return (0, 2, 6, 4, 1, 5, 3, 7) if places == 8 else tuple(range(places))


def reverse_bits(index, levels):
    return sum((index >> bit & 1) << levels - 1 - bit for bit in range(levels))


@functools.lru_cache(maxsize=None)
def tables(places, rows, width):
    levels = places.bit_length() - 1
    stride = 2 * places
    bins = stride * rows
    residues = np.array([2 * reverse_bits(place, levels) + parity for place in range(places) for parity in range(2)])
    angle = 2.0 * np.pi * ((residues[:, None] * np.arange(places)[None, :]) % stride) / stride
    same = np.eye(width)
    first = np.concatenate([np.kron(np.cos(angle), same), np.kron(-np.sin(angle), same)])
    last = first.T / bins
    angle = 2.0 * np.pi * ((residues[:, None] * np.arange(rows)[None, :]) % bins) / bins
    twist = np.repeat(np.stack([np.cos(angle), np.sin(angle)]), width, axis=1)
    series = np.arange(rows)
    angle = 2.0 * np.pi * ((series[:, None] * series[None, :]) % rows) / rows
    dft = np.concatenate([np.cos(angle), np.sin(angle)])
    return (
        first.astype(jnp.bfloat16),
        last.astype(jnp.bfloat16),
        twist.astype(np.float32),
        dft.astype(jnp.bfloat16),
    )


def pair_rows(places):
    levels = places.bit_length() - 1

    def holder(residue):
        return order_of(places).index(reverse_bits(residue // 2, levels)), residue % 2

    mirrors = [None if residue % places == 0 else holder(2 * places - residue) for residue in range(places + 1)]
    return [holder(residue) for residue in range(places + 1)], mirrors


@functools.lru_cache(maxsize=None)
def folded_tables(places, rows, width):
    stride = 2 * places
    bins = stride * rows
    residues = np.arange(places + 1)
    angle = 2.0 * np.pi * ((residues[:, None] * np.arange(places)[None, :]) % stride) / stride
    parts = np.stack([np.cos(angle), -np.sin(angle)], axis=1)
    first = np.kron(parts.reshape(-1, places), np.eye(width))
    last = first.T / bins
    angle = 2.0 * np.pi * ((residues[:, None] * np.arange(rows)[None, :]) % bins) / bins
    twist = np.stack([np.cos(angle), np.sin(angle)])
    block = rows // 4
    series = np.arange(block)
    angle = 2.0 * np.pi * ((np.arange(4)[:, None] * series[None, :]) % rows) / rows
    spin = np.stack([np.cos(angle), np.sin(angle)])
    angle = 2.0 * np.pi * ((series[:, None] * series[None, :]) % block) / block
    cos, sin = np.cos(angle), np.sin(angle)
    there = np.block([[cos, -sin], [sin, cos]])
    back = np.block([[cos, sin], [-sin, cos]])
    reverse = np.eye(block)[::-1]
    return (
        first.astype(jnp.bfloat16),
        last.astype(jnp.bfloat16),
        twist.astype(np.float32),
        spin.astype(np.float32),
        np.stack([there, back]).astype(jnp.bfloat16),
        reverse.astype(jnp.bfloat16),
    )


def hops(places):
    return [[apart, apart + 1] for apart in range(0, places, 2)]


def prepare_kernel(
    features_ref,
    pre_ref,
    gain_ref,
    skip_ref,
    spectrum_ref,
    squares_ref,
    skipped_ref,
    packed_ref,
    features_in,
    pre_in,
    gain_in,
    skip_in,
    spectrum_in,
    squares_out,
    skipped_out,
    packed_out,
    in_sems,
    out_sems,
):
    blocks = [(part, parity) for part in range(2) for parity in range(2)]
    pairs = [(features_ref, features_in), (pre_ref, pre_in), (gain_ref, gain_in), (skip_ref, skip_in)]
    pairs += [(spectrum_ref.at[block], spectrum_in.at[block]) for block in blocks]
    arriving = [pltpu.make_async_copy(*pair, in_sems.at[slot]) for slot, pair in enumerate(pairs)]
    for copy in arriving:
        copy.start()
    leaving = []

    def leave(source, target):
        copy = pltpu.make_async_copy(source, target, out_sems.at[len(leaving)])
        copy.start()
        leaving.append(copy)

    def pack(slot, turned):
        if len(packed_ref.shape) == 4:
            places, width = packed_out.shape[1:3]
            for rank, place in enumerate(order_of(places)):
                packed_out[slot, rank] = turned[place * width : (place + 1) * width]
            leave(packed_out.at[slot], packed_ref.at[:, slot])
        else:
            packed_out[slot] = turned
            leave(packed_out.at[slot], packed_ref.at[slot])

    for copy in arriving[:4]:
        copy.wait()
    features = features_in[...].astype(F32)
    scaled = features * gain_in[...] * pre_in[...].astype(F32)
    pack(4, scaled.astype(BF16).T)
    skipped_out[...] = (scaled * skip_in[...]).astype(BF16).T
    leave(skipped_out, skipped_ref)
    turned = features_in[...].T.astype(F32)
    squares_out[...] = jnp.sum(turned * turned, axis=0, keepdims=True)
    leave(squares_out, squares_ref)
    for slot, block in enumerate(blocks):
        arriving[4 + slot].wait()
        if len(packed_ref.shape) == 4:
            quarter = spectrum_in.shape[2] // 4
            rows = [spectrum_in[(*block, pl.ds(turn, quarter, stride=4), slice(None))] for turn in range(4)]
            pack(slot, jnp.concatenate([row.astype(BF16).T for row in rows], axis=1))
        else:
            pack(slot, spectrum_in[block].astype(BF16).T)
    for copy in leaving:
        copy.wait()


def scale_kernel(channels, *refs):
    square_refs, scale_ref = refs[:-1], refs[-1]
    total = square_refs[0][...]
    for square_ref in square_refs[1:]:
        total = total + square_ref[...]
    scale_ref[...] = lax.rsqrt(total / channels + EPS)


def matmul(left, right):
    return jnp.dot(left, right, preferred_element_type=F32)


def butterfly(values, direction):
    (real0, imag0), (real1, imag1), (real2, imag2), (real3, imag3) = values
    even, odd = (real0 + real2, imag0 + imag2), (real1 + real3, imag1 + imag3)
    even_gap, odd_gap = (real0 - real2, imag0 - imag2), (real1 - real3, imag1 - imag3)
    lower = (even_gap[0] + odd_gap[1], even_gap[1] - odd_gap[0])
    upper = (even_gap[0] - odd_gap[1], even_gap[1] + odd_gap[0])
    total, gap = (even[0] + odd[0], even[1] + odd[1]), (even[0] - odd[0], even[1] - odd[1])
    return [total, lower, gap, upper] if direction > 0 else [total, upper, gap, lower]


def folded_kernel(packed_ref, first_ref, last_ref, twist_ref, spin_ref, dft_ref, reverse_ref, *refs):
    scale_refs, (out_ref, scales, signal, mirror, forward, backward, both) = refs[:-7], refs[-7:]
    wide, rows = out_ref.shape
    places, width = scales.shape[0], wide // scales.shape[0]
    block, inner = rows // 4, mirror.shape[0] // 8
    order = order_of(places)
    direct, mirrors = pair_rows(places)
    quarters = [pl.ds(turn * block, block) for turn in range(4)]
    groups = [range(begin, min(begin + 3, places + 1)) for begin in range(0, places + 1, 3)]
    for row, holder in enumerate(mirrors[1:places]):
        for part in range(2):
            for turn in range(4):
                at = pl.ds((part * 4 + 3 - turn) * inner + row * width, width)
                mirror[at, :] = packed_ref[holder[0], 2 * part + holder[1], :, quarters[turn]]
    reversed_bins = matmul(mirror[...], reverse_ref[...])
    place = lax.axis_index("seq")
    for scale_ref, steps in zip(scale_refs, hops(places)):
        for at, step in enumerate(steps):
            scales[place ^ step] = scale_ref[pl.ds(at, 1), :]
    for rank, at in enumerate(order):
        signal[pl.ds(at * width, width), :] = (packed_ref[rank, 4].astype(F32) * scales[at]).astype(BF16)
    spectral = []
    for group in groups:
        begin = group[0] * width
        mixed = matmul(first_ref[pl.ds(2 * begin, 2 * len(group) * width), :], signal[...])
        for at, residue in enumerate(group):
            over, under = mixed[2 * at * width : (2 * at + 1) * width], mixed[(2 * at + 1) * width : (2 * at + 2) * width]
            values = []
            for turn in range(4):
                real, imag = (part[:, turn * block : (turn + 1) * block] for part in (over, under))
                cos, sin = (twist_ref[part, pl.ds(residue, 1), quarters[turn]] for part in range(2))
                values.append((real * cos + imag * sin, imag * cos - real * sin))
            for turn, (real, imag) in enumerate(butterfly(values, 1)):
                if turn > 0:
                    cos, sin = spin_ref[0, pl.ds(turn, 1), :], spin_ref[1, pl.ds(turn, 1), :]
                    real, imag = real * cos + imag * sin, imag * cos - real * sin
                row = pl.ds(4 * begin + (turn * len(group) + at) * width, width)
                forward[row, pl.ds(0, block)] = real.astype(BF16)
                forward[row, pl.ds(block, block)] = imag.astype(BF16)
        spectral.append(matmul(forward[pl.ds(4 * begin, 4 * len(group) * width), :], dft_ref[0]))
    restored = []
    for group, values in zip(groups, spectral):
        begin = group[0] * width
        for turn in range(4):
            for at, residue in enumerate(group):
                row = (turn * len(group) + at) * width
                real, imag = values[row : row + width, :block], values[row : row + width, block:]
                holder = direct[residue]
                response_real = packed_ref[holder[0], holder[1], :, quarters[turn]].astype(F32)
                response_imag = packed_ref[holder[0], 2 + holder[1], :, quarters[turn]].astype(F32)
                if mirrors[residue] is not None:
                    other = turn * inner + (residue - 1) * width
                    response_real = response_real + reversed_bins[other : other + width]
                    other = other + 4 * inner
                    response_imag = response_imag - reversed_bins[other : other + width]
                target = pl.ds(4 * begin + row, width)
                backward[target, pl.ds(0, block)] = (real * response_real - imag * response_imag).astype(BF16)
                backward[target, pl.ds(block, block)] = (real * response_imag + imag * response_real).astype(BF16)
        restored.append(matmul(backward[pl.ds(4 * begin, 4 * len(group) * width), :], dft_ref[1]))
    for group, turned in zip(groups, restored):
        for at, residue in enumerate(group):
            values = []
            for turn in range(4):
                row = (turn * len(group) + at) * width
                real, imag = turned[row : row + width, :block], turned[row : row + width, block:]
                if turn > 0:
                    cos, sin = spin_ref[0, pl.ds(turn, 1), :], spin_ref[1, pl.ds(turn, 1), :]
                    real, imag = real * cos - imag * sin, imag * cos + real * sin
                values.append((real, imag))
            for lanes, (real, imag) in zip(quarters, butterfly(values, -1)):
                cos, sin = twist_ref[0, pl.ds(residue, 1), lanes], twist_ref[1, pl.ds(residue, 1), lanes]
                both[pl.ds(2 * residue * width, width), lanes] = (real * cos - imag * sin).astype(BF16)
                both[pl.ds((2 * residue + 1) * width, width), lanes] = (imag * cos + real * sin).astype(BF16)
    result = matmul(last_ref[...], both[...]).astype(BF16)
    for rank, at in enumerate(order):
        out_ref[pl.ds(rank * width, width), :] = result[at * width : (at + 1) * width]


def convolve_kernel(packed_ref, first_ref, last_ref, twist_ref, dft_ref, scale_ref, out_ref, left, right):
    wide, rows = out_ref.shape
    half = 2 * wide
    signal = (packed_ref[4].astype(F32) * scale_ref[...]).astype(BF16)
    mixed = matmul(first_ref[...], signal)
    real, imag = mixed[:half], mixed[half:]
    cos_twist, sin_twist = twist_ref[0], twist_ref[1]
    turned_real = (real * cos_twist + imag * sin_twist).astype(BF16)
    turned_imag = (imag * cos_twist - real * sin_twist).astype(BF16)
    left[pl.ds(0, half), pl.ds(0, rows)] = turned_real
    left[pl.ds(0, half), pl.ds(rows, rows)] = turned_imag
    left[pl.ds(half, half), pl.ds(0, rows)] = turned_imag
    left[pl.ds(half, half), pl.ds(rows, rows)] = -turned_real
    mixed = matmul(left[...], dft_ref[...])
    real, imag = mixed[:half], mixed[half:]
    response_real = packed_ref[0:2].reshape(half, rows).astype(F32)
    response_imag = packed_ref[2:4].reshape(half, rows).astype(F32)
    product_real = (real * response_real - imag * response_imag).astype(BF16)
    product_imag = (real * response_imag + imag * response_real).astype(BF16)
    right[pl.ds(0, half), pl.ds(0, rows)] = product_real
    right[pl.ds(0, half), pl.ds(rows, rows)] = -product_imag
    right[pl.ds(half, half), pl.ds(0, rows)] = product_imag
    right[pl.ds(half, half), pl.ds(rows, rows)] = product_real
    mixed = matmul(right[...], dft_ref[...])
    real, imag = mixed[:half], mixed[half:]
    turned_real = (real * cos_twist - imag * sin_twist).astype(BF16)
    turned_imag = (imag * cos_twist + real * sin_twist).astype(BF16)
    both = jnp.concatenate([turned_real, turned_imag], axis=0)
    out_ref[...] = matmul(last_ref[...], both).astype(BF16)


def finish_kernel(conv_ref, skipped_ref, scale_ref, post_ref, out_ref):
    conv = conv_ref[...]
    if len(conv_ref.shape) == 3:
        order = order_of(conv_ref.shape[0])
        conv = jnp.concatenate([conv_ref[order.index(place)] for place in range(len(order))])
    turned = conv.astype(F32) + skipped_ref[...].astype(F32) * scale_ref[...]
    out_ref[...] = (post_ref[...].astype(F32) * turned.T).astype(BF16)


def call(kernel, out_shape, flops, moved, *operands, limit=VMEM_LIMIT, **options):
    return pl.pallas_call(
        kernel,
        out_shape=out_shape,
        compiler_params=pltpu.CompilerParams(vmem_limit_bytes=limit),
        cost_estimate=pl.CostEstimate(flops=flops, bytes_accessed=moved, transcendentals=0),
        **options,
    )(*operands)


def exchange(value):
    ranks = [list(order_of(lax.axis_size("seq")))]
    return lax.all_to_all(value, "seq", split_axis=0, concat_axis=0, tiled=True, axis_index_groups=ranks)


def swap(value, axis, apart):
    return lax.ppermute(value, axis, [(place, place ^ apart) for place in range(lax.axis_size(axis))])


def local(features, pre_gate, post_gate, norm_gain, skip_weight, spectrum):
    rows, wide = features.shape
    places = lax.axis_size("seq")
    groups = lax.axis_size("chan")
    width = wide // places
    piled = width % 16 == 0
    cells = rows * wide
    shape = jax.ShapeDtypeStruct
    vmem, anywhere = pl.BlockSpec(memory_space=pltpu.VMEM), pl.BlockSpec(memory_space=pl.ANY)
    squares, skipped, packed = call(
        prepare_kernel,
        (
            shape((1, rows), F32),
            shape((wide, rows), BF16),
            shape((places, 5, width, rows) if piled else (5, wide, rows), BF16),
        ),
        10 * cells,
        32 * cells,
        features,
        pre_gate,
        norm_gain[None, :],
        skip_weight[None, :],
        spectrum,
        limit=WHOLE_VMEM,
        in_specs=[anywhere] * 5,
        out_specs=(anywhere, anywhere, anywhere),
        scratch_shapes=[
            pltpu.VMEM(features.shape, BF16),
            pltpu.VMEM(pre_gate.shape, BF16),
            pltpu.VMEM((1, wide), F32),
            pltpu.VMEM((1, wide), F32),
            pltpu.VMEM(spectrum.shape, F32),
            pltpu.VMEM((1, rows), F32),
            pltpu.VMEM((wide, rows), BF16),
            pltpu.VMEM((5, places, width, rows) if piled else (5, wide, rows), BF16),
            pltpu.SemaphoreType.DMA((8,)),
            pltpu.SemaphoreType.DMA((7,)),
        ],
    )
    if not piled:
        packed = packed.reshape(5, places, width, rows).transpose(1, 0, 2, 3)
    gathered = exchange(packed)
    others = [swap(squares, "chan", apart) for apart in range(1, groups)]
    scale = call(
        functools.partial(scale_kernel, wide * groups), shape((1, rows), F32), 8 * rows, 32 * rows, squares, *others
    )
    if piled:
        near = jnp.concatenate([scale, swap(scale, "seq", 1)])
        scales = [near] + [swap(near, "seq", steps[0]) for steps in hops(places)[1:]]
    else:
        scales = [jnp.repeat(lax.all_gather(scale, "seq", axis=0, tiled=True), width, axis=0)]
        response = gathered[:, :4].reshape(places, 2, 2, width, rows).transpose(1, 0, 2, 3, 4)
        gathered = jnp.concatenate([response.reshape(4, wide, rows), gathered[:, 4].reshape(1, wide, rows)])
    if piled:
        constants = folded_tables(places, rows, width)
        half = constants[0].shape[0] // 2
        scratch = [
            pltpu.VMEM((places, 1, rows), F32),
            pltpu.VMEM((wide, rows), BF16),
            pltpu.VMEM((8 * (half - 2 * width), rows // 4), BF16),
            pltpu.VMEM((4 * half, rows // 2), BF16),
            pltpu.VMEM((4 * half, rows // 2), BF16),
            pltpu.VMEM((2 * half, rows), BF16),
        ]
    else:
        constants = tables(places, rows, width)
        scratch = [pltpu.VMEM((4 * wide, 2 * rows), BF16)] * 2
    conv = call(
        folded_kernel if piled else convolve_kernel,
        shape((wide, rows), BF16),
        20 * cells * rows,
        20 * cells,
        gathered,
        *constants,
        *scales,
        scratch_shapes=scratch,
    )
    conv = exchange(conv.reshape(places, width, rows))
    if not piled:
        conv = conv.reshape(wide, rows)
    return call(finish_kernel, shape((rows, wide), BF16), 10 * cells, 8 * cells, conv, skipped, scale, post_gate)


def solution(mesh):
    return jax.shard_map(
        local,
        mesh=mesh,
        in_specs=(
            P("seq", "chan"),
            P("seq", "chan"),
            P("seq", "chan"),
            P("chan"),
            P("chan"),
            P(None, "seq", None, "chan"),
        ),
        out_specs=P("seq", "chan"),
        check_vma=False,
    )
```

```python
import functools

import jax
import jax.numpy as jnp
import numpy as np
from jax import lax
from jax.experimental import pallas as pl
from jax.experimental.pallas import tpu as pltpu
from jax.sharding import PartitionSpec as P

EPS = 1e-06
BF16 = jnp.bfloat16
F32 = jnp.float32
VMEM_LIMIT = 48 * 1024 * 1024
WHOLE_VMEM = 63 * 1024 * 1024 + 512 * 1024


def order_of(places):
    return (7, 5, 1, 3, 6, 2, 4, 0) if places == 8 else tuple(range(places))


def reverse_bits(index, levels):
    return sum((index >> bit & 1) << levels - 1 - bit for bit in range(levels))


@functools.lru_cache(maxsize=None)
def tables(places, rows, width):
    levels = places.bit_length() - 1
    stride = 2 * places
    bins = stride * rows
    residues = np.array([2 * reverse_bits(place, levels) + parity for place in range(places) for parity in range(2)])
    angle = 2.0 * np.pi * ((residues[:, None] * np.arange(places)[None, :]) % stride) / stride
    same = np.eye(width)
    first = np.concatenate([np.kron(np.cos(angle), same), np.kron(-np.sin(angle), same)])
    last = first.T / bins
    angle = 2.0 * np.pi * ((residues[:, None] * np.arange(rows)[None, :]) % bins) / bins
    twist = np.repeat(np.stack([np.cos(angle), np.sin(angle)]), width, axis=1)
    series = np.arange(rows)
    angle = 2.0 * np.pi * ((series[:, None] * series[None, :]) % rows) / rows
    dft = np.concatenate([np.cos(angle), np.sin(angle)])
    return (
        first.astype(jnp.bfloat16),
        last.astype(jnp.bfloat16),
        twist.astype(np.float32),
        dft.astype(jnp.bfloat16),
    )


def pair_rows(places):
    levels = places.bit_length() - 1

    def holder(residue):
        return order_of(places).index(reverse_bits(residue // 2, levels)), residue % 2

    mirrors = [None if residue % places == 0 else holder(2 * places - residue) for residue in range(places + 1)]
    return [holder(residue) for residue in range(places + 1)], mirrors


@functools.lru_cache(maxsize=None)
def folded_tables(places, rows, width):
    stride = 2 * places
    bins = stride * rows
    residues = np.arange(places + 1)
    angle = 2.0 * np.pi * ((residues[:, None] * np.arange(places)[None, :]) % stride) / stride
    parts = np.stack([np.cos(angle), -np.sin(angle)], axis=1)
    first = np.kron(parts.reshape(-1, places), np.eye(width))
    last = first.T / bins
    angle = 2.0 * np.pi * ((residues[:, None] * np.arange(rows)[None, :]) % bins) / bins
    twist = np.stack([np.cos(angle), np.sin(angle)])
    block = rows // 4
    series = np.arange(block)
    angle = 2.0 * np.pi * ((np.arange(4)[:, None] * series[None, :]) % rows) / rows
    spin = np.stack([np.cos(angle), np.sin(angle)])
    angle = 2.0 * np.pi * ((series[:, None] * series[None, :]) % block) / block
    cos, sin = np.cos(angle), np.sin(angle)
    there = np.block([[cos, -sin], [sin, cos]])
    back = np.block([[cos, sin], [-sin, cos]])
    reverse = np.eye(block)[::-1]
    return (
        first.astype(jnp.bfloat16),
        last.astype(jnp.bfloat16),
        twist.astype(np.float32),
        spin.astype(np.float32),
        np.stack([there, back]).astype(jnp.bfloat16),
        reverse.astype(jnp.bfloat16),
    )


def hops(places):
    return [[apart, apart + 1] for apart in range(0, places, 2)]


def prepare_kernel(
    features_ref,
    pre_ref,
    gain_ref,
    skip_ref,
    spectrum_ref,
    squares_ref,
    skipped_ref,
    packed_ref,
    features_in,
    pre_in,
    gain_in,
    skip_in,
    spectrum_in,
    squares_out,
    skipped_out,
    packed_out,
    in_sems,
    out_sems,
):
    blocks = [(part, parity) for part in range(2) for parity in range(2)]
    pairs = [(features_ref, features_in), (pre_ref, pre_in), (gain_ref, gain_in), (skip_ref, skip_in)]
    pairs += [(spectrum_ref.at[block], spectrum_in.at[block]) for block in blocks]
    arriving = [pltpu.make_async_copy(*pair, in_sems.at[slot]) for slot, pair in enumerate(pairs)]
    for copy in arriving:
        copy.start()
    leaving = []

    def leave(source, target):
        copy = pltpu.make_async_copy(source, target, out_sems.at[len(leaving)])
        copy.start()
        leaving.append(copy)

    def pack(slot, turned):
        if len(packed_ref.shape) == 4:
            places, width = packed_out.shape[1:3]
            for rank, place in enumerate(order_of(places)):
                packed_out[slot, rank] = turned[place * width : (place + 1) * width]
            leave(packed_out.at[slot], packed_ref.at[:, slot])
        else:
            packed_out[slot] = turned
            leave(packed_out.at[slot], packed_ref.at[slot])

    for copy in arriving[:4]:
        copy.wait()
    features = features_in[...].astype(F32)
    scaled = features * gain_in[...] * pre_in[...].astype(F32)
    pack(4, scaled.astype(BF16).T)
    skipped_out[...] = (scaled * skip_in[...]).astype(BF16).T
    leave(skipped_out, skipped_ref)
    turned = features_in[...].T.astype(F32)
    squares_out[...] = jnp.sum(turned * turned, axis=0, keepdims=True)
    leave(squares_out, squares_ref)
    for slot, block in enumerate(blocks):
        arriving[4 + slot].wait()
        if len(packed_ref.shape) == 4:
            quarter = spectrum_in.shape[2] // 4
            rows = [spectrum_in[(*block, pl.ds(turn, quarter, stride=4), slice(None))] for turn in range(4)]
            pack(slot, jnp.concatenate([row.astype(BF16).T for row in rows], axis=1))
        else:
            pack(slot, spectrum_in[block].astype(BF16).T)
    for copy in leaving:
        copy.wait()


def scale_kernel(channels, *refs):
    square_refs, scale_ref = refs[:-1], refs[-1]
    total = square_refs[0][...]
    for square_ref in square_refs[1:]:
        total = total + square_ref[...]
    scale_ref[...] = lax.rsqrt(total / channels + EPS)


def matmul(left, right):
    return jnp.dot(left, right, preferred_element_type=F32)


def butterfly(values, direction):
    (real0, imag0), (real1, imag1), (real2, imag2), (real3, imag3) = values
    even, odd = (real0 + real2, imag0 + imag2), (real1 + real3, imag1 + imag3)
    even_gap, odd_gap = (real0 - real2, imag0 - imag2), (real1 - real3, imag1 - imag3)
    lower = (even_gap[0] + odd_gap[1], even_gap[1] - odd_gap[0])
    upper = (even_gap[0] - odd_gap[1], even_gap[1] + odd_gap[0])
    total, gap = (even[0] + odd[0], even[1] + odd[1]), (even[0] - odd[0], even[1] - odd[1])
    return [total, lower, gap, upper] if direction > 0 else [total, upper, gap, lower]


def folded_kernel(packed_ref, first_ref, last_ref, twist_ref, spin_ref, dft_ref, reverse_ref, *refs):
    scale_refs, (out_ref, scales, signal, mirror, forward, backward, both) = refs[:-7], refs[-7:]
    wide, rows = out_ref.shape
    places, width = scales.shape[0], wide // scales.shape[0]
    block, inner = rows // 4, mirror.shape[0] // 8
    order = order_of(places)
    direct, mirrors = pair_rows(places)
    quarters = [pl.ds(turn * block, block) for turn in range(4)]
    groups = [range(begin, min(begin + 3, places + 1)) for begin in range(0, places + 1, 3)]
    for row, holder in enumerate(mirrors[1:places]):
        for part in range(2):
            for turn in range(4):
                at = pl.ds((part * 4 + 3 - turn) * inner + row * width, width)
                mirror[at, :] = packed_ref[holder[0], 2 * part + holder[1], :, quarters[turn]]
    reversed_bins = matmul(mirror[...], reverse_ref[...])
    place = lax.axis_index("seq")
    for scale_ref, steps in zip(scale_refs, hops(places)):
        for at, step in enumerate(steps):
            scales[place ^ step] = scale_ref[pl.ds(at, 1), :]
    for rank, at in enumerate(order):
        signal[pl.ds(at * width, width), :] = (packed_ref[rank, 4].astype(F32) * scales[at]).astype(BF16)
    spectral = []
    for group in groups:
        begin = group[0] * width
        mixed = matmul(first_ref[pl.ds(2 * begin, 2 * len(group) * width), :], signal[...])
        for at, residue in enumerate(group):
            over, under = mixed[2 * at * width : (2 * at + 1) * width], mixed[(2 * at + 1) * width : (2 * at + 2) * width]
            values = []
            for turn in range(4):
                real, imag = (part[:, turn * block : (turn + 1) * block] for part in (over, under))
                cos, sin = (twist_ref[part, pl.ds(residue, 1), quarters[turn]] for part in range(2))
                values.append((real * cos + imag * sin, imag * cos - real * sin))
            for turn, (real, imag) in enumerate(butterfly(values, 1)):
                if turn > 0:
                    cos, sin = spin_ref[0, pl.ds(turn, 1), :], spin_ref[1, pl.ds(turn, 1), :]
                    real, imag = real * cos + imag * sin, imag * cos - real * sin
                row = pl.ds(4 * begin + (turn * len(group) + at) * width, width)
                forward[row, pl.ds(0, block)] = real.astype(BF16)
                forward[row, pl.ds(block, block)] = imag.astype(BF16)
        spectral.append(matmul(forward[pl.ds(4 * begin, 4 * len(group) * width), :], dft_ref[0]))
    restored = []
    for group, values in zip(groups, spectral):
        begin = group[0] * width
        for turn in range(4):
            for at, residue in enumerate(group):
                row = (turn * len(group) + at) * width
                real, imag = values[row : row + width, :block], values[row : row + width, block:]
                holder = direct[residue]
                response_real = packed_ref[holder[0], holder[1], :, quarters[turn]].astype(F32)
                response_imag = packed_ref[holder[0], 2 + holder[1], :, quarters[turn]].astype(F32)
                if mirrors[residue] is not None:
                    other = turn * inner + (residue - 1) * width
                    response_real = response_real + reversed_bins[other : other + width]
                    other = other + 4 * inner
                    response_imag = response_imag - reversed_bins[other : other + width]
                target = pl.ds(4 * begin + row, width)
                backward[target, pl.ds(0, block)] = (real * response_real - imag * response_imag).astype(BF16)
                backward[target, pl.ds(block, block)] = (real * response_imag + imag * response_real).astype(BF16)
        restored.append(matmul(backward[pl.ds(4 * begin, 4 * len(group) * width), :], dft_ref[1]))
    for group, turned in zip(groups, restored):
        for at, residue in enumerate(group):
            values = []
            for turn in range(4):
                row = (turn * len(group) + at) * width
                real, imag = turned[row : row + width, :block], turned[row : row + width, block:]
                if turn > 0:
                    cos, sin = spin_ref[0, pl.ds(turn, 1), :], spin_ref[1, pl.ds(turn, 1), :]
                    real, imag = real * cos - imag * sin, imag * cos + real * sin
                values.append((real, imag))
            for lanes, (real, imag) in zip(quarters, butterfly(values, -1)):
                cos, sin = twist_ref[0, pl.ds(residue, 1), lanes], twist_ref[1, pl.ds(residue, 1), lanes]
                both[pl.ds(2 * residue * width, width), lanes] = (real * cos - imag * sin).astype(BF16)
                both[pl.ds((2 * residue + 1) * width, width), lanes] = (imag * cos + real * sin).astype(BF16)
    result = matmul(last_ref[...], both[...]).astype(BF16)
    for rank, at in enumerate(order):
        out_ref[pl.ds(rank * width, width), :] = result[at * width : (at + 1) * width]


def convolve_kernel(packed_ref, first_ref, last_ref, twist_ref, dft_ref, scale_ref, out_ref, left, right):
    wide, rows = out_ref.shape
    half = 2 * wide
    signal = (packed_ref[4].astype(F32) * scale_ref[...]).astype(BF16)
    mixed = matmul(first_ref[...], signal)
    real, imag = mixed[:half], mixed[half:]
    cos_twist, sin_twist = twist_ref[0], twist_ref[1]
    turned_real = (real * cos_twist + imag * sin_twist).astype(BF16)
    turned_imag = (imag * cos_twist - real * sin_twist).astype(BF16)
    left[pl.ds(0, half), pl.ds(0, rows)] = turned_real
    left[pl.ds(0, half), pl.ds(rows, rows)] = turned_imag
    left[pl.ds(half, half), pl.ds(0, rows)] = turned_imag
    left[pl.ds(half, half), pl.ds(rows, rows)] = -turned_real
    mixed = matmul(left[...], dft_ref[...])
    real, imag = mixed[:half], mixed[half:]
    response_real = packed_ref[0:2].reshape(half, rows).astype(F32)
    response_imag = packed_ref[2:4].reshape(half, rows).astype(F32)
    product_real = (real * response_real - imag * response_imag).astype(BF16)
    product_imag = (real * response_imag + imag * response_real).astype(BF16)
    right[pl.ds(0, half), pl.ds(0, rows)] = product_real
    right[pl.ds(0, half), pl.ds(rows, rows)] = -product_imag
    right[pl.ds(half, half), pl.ds(0, rows)] = product_imag
    right[pl.ds(half, half), pl.ds(rows, rows)] = product_real
    mixed = matmul(right[...], dft_ref[...])
    real, imag = mixed[:half], mixed[half:]
    turned_real = (real * cos_twist - imag * sin_twist).astype(BF16)
    turned_imag = (imag * cos_twist + real * sin_twist).astype(BF16)
    both = jnp.concatenate([turned_real, turned_imag], axis=0)
    out_ref[...] = matmul(last_ref[...], both).astype(BF16)


def finish_kernel(conv_ref, skipped_ref, scale_ref, post_ref, out_ref):
    conv = conv_ref[...]
    if len(conv_ref.shape) == 3:
        order = order_of(conv_ref.shape[0])
        conv = jnp.concatenate([conv_ref[order.index(place)] for place in range(len(order))])
    turned = conv.astype(F32) + skipped_ref[...].astype(F32) * scale_ref[...]
    out_ref[...] = (post_ref[...].astype(F32) * turned.T).astype(BF16)


def call(kernel, out_shape, flops, moved, *operands, limit=VMEM_LIMIT, **options):
    return pl.pallas_call(
        kernel,
        out_shape=out_shape,
        compiler_params=pltpu.CompilerParams(vmem_limit_bytes=limit),
        cost_estimate=pl.CostEstimate(flops=flops, bytes_accessed=moved, transcendentals=0),
        **options,
    )(*operands)


def exchange(value):
    ranks = [list(order_of(lax.axis_size("seq")))]
    return lax.all_to_all(value, "seq", split_axis=0, concat_axis=0, tiled=True, axis_index_groups=ranks)


def swap(value, axis, apart):
    return lax.ppermute(value, axis, [(place, place ^ apart) for place in range(lax.axis_size(axis))])


def local(features, pre_gate, post_gate, norm_gain, skip_weight, spectrum):
    rows, wide = features.shape
    places = lax.axis_size("seq")
    groups = lax.axis_size("chan")
    width = wide // places
    piled = width % 16 == 0
    cells = rows * wide
    shape = jax.ShapeDtypeStruct
    vmem, anywhere = pl.BlockSpec(memory_space=pltpu.VMEM), pl.BlockSpec(memory_space=pl.ANY)
    squares, skipped, packed = call(
        prepare_kernel,
        (
            shape((1, rows), F32),
            shape((wide, rows), BF16),
            shape((places, 5, width, rows) if piled else (5, wide, rows), BF16),
        ),
        10 * cells,
        32 * cells,
        features,
        pre_gate,
        norm_gain[None, :],
        skip_weight[None, :],
        spectrum,
        limit=WHOLE_VMEM,
        in_specs=[anywhere] * 5,
        out_specs=(anywhere, anywhere, anywhere),
        scratch_shapes=[
            pltpu.VMEM(features.shape, BF16),
            pltpu.VMEM(pre_gate.shape, BF16),
            pltpu.VMEM((1, wide), F32),
            pltpu.VMEM((1, wide), F32),
            pltpu.VMEM(spectrum.shape, F32),
            pltpu.VMEM((1, rows), F32),
            pltpu.VMEM((wide, rows), BF16),
            pltpu.VMEM((5, places, width, rows) if piled else (5, wide, rows), BF16),
            pltpu.SemaphoreType.DMA((8,)),
            pltpu.SemaphoreType.DMA((7,)),
        ],
    )
    if not piled:
        packed = packed.reshape(5, places, width, rows).transpose(1, 0, 2, 3)
    gathered = exchange(packed)
    others = [swap(squares, "chan", apart) for apart in range(1, groups)]
    scale = call(
        functools.partial(scale_kernel, wide * groups), shape((1, rows), F32), 8 * rows, 32 * rows, squares, *others
    )
    if piled:
        near = jnp.concatenate([scale, swap(scale, "seq", 1)])
        scales = [near] + [swap(near, "seq", steps[0]) for steps in hops(places)[1:]]
    else:
        scales = [jnp.repeat(lax.all_gather(scale, "seq", axis=0, tiled=True), width, axis=0)]
        response = gathered[:, :4].reshape(places, 2, 2, width, rows).transpose(1, 0, 2, 3, 4)
        gathered = jnp.concatenate([response.reshape(4, wide, rows), gathered[:, 4].reshape(1, wide, rows)])
    if piled:
        constants = folded_tables(places, rows, width)
        half = constants[0].shape[0] // 2
        scratch = [
            pltpu.VMEM((places, 1, rows), F32),
            pltpu.VMEM((wide, rows), BF16),
            pltpu.VMEM((8 * (half - 2 * width), rows // 4), BF16),
            pltpu.VMEM((4 * half, rows // 2), BF16),
            pltpu.VMEM((4 * half, rows // 2), BF16),
            pltpu.VMEM((2 * half, rows), BF16),
        ]
    else:
        constants = tables(places, rows, width)
        scratch = [pltpu.VMEM((4 * wide, 2 * rows), BF16)] * 2
    conv = call(
        folded_kernel if piled else convolve_kernel,
        shape((wide, rows), BF16),
        20 * cells * rows,
        20 * cells,
        gathered,
        *constants,
        *scales,
        scratch_shapes=scratch,
    )
    conv = exchange(conv.reshape(places, width, rows))
    if not piled:
        conv = conv.reshape(wide, rows)
    return call(finish_kernel, shape((rows, wide), BF16), 10 * cells, 8 * cells, conv, skipped, scale, post_gate)


def solution(mesh):
    return jax.shard_map(
        local,
        mesh=mesh,
        in_specs=(
            P("seq", "chan"),
            P("seq", "chan"),
            P("seq", "chan"),
            P("chan"),
            P("chan"),
            P(None, "seq", None, "chan"),
        ),
        out_specs=P("seq", "chan"),
        check_vma=False,
    )
```

```python
import functools

import jax
import jax.numpy as jnp
import numpy as np
from jax import lax
from jax.experimental import pallas as pl
from jax.experimental.pallas import tpu as pltpu
from jax.sharding import PartitionSpec as P

EPS = 1e-06
BF16 = jnp.bfloat16
F32 = jnp.float32
VMEM_LIMIT = 48 * 1024 * 1024
WHOLE_VMEM = 63 * 1024 * 1024 + 512 * 1024


def order_of(places):
    return (1, 3, 6, 2, 4, 0, 7, 5) if places == 8 else tuple(range(places))


def reverse_bits(index, levels):
    return sum((index >> bit & 1) << levels - 1 - bit for bit in range(levels))


@functools.lru_cache(maxsize=None)
def tables(places, rows, width):
    levels = places.bit_length() - 1
    stride = 2 * places
    bins = stride * rows
    residues = np.array([2 * reverse_bits(place, levels) + parity for place in range(places) for parity in range(2)])
    angle = 2.0 * np.pi * ((residues[:, None] * np.arange(places)[None, :]) % stride) / stride
    same = np.eye(width)
    first = np.concatenate([np.kron(np.cos(angle), same), np.kron(-np.sin(angle), same)])
    last = first.T / bins
    angle = 2.0 * np.pi * ((residues[:, None] * np.arange(rows)[None, :]) % bins) / bins
    twist = np.repeat(np.stack([np.cos(angle), np.sin(angle)]), width, axis=1)
    series = np.arange(rows)
    angle = 2.0 * np.pi * ((series[:, None] * series[None, :]) % rows) / rows
    dft = np.concatenate([np.cos(angle), np.sin(angle)])
    return (
        first.astype(jnp.bfloat16),
        last.astype(jnp.bfloat16),
        twist.astype(np.float32),
        dft.astype(jnp.bfloat16),
    )


def pair_rows(places):
    levels = places.bit_length() - 1

    def holder(residue):
        return order_of(places).index(reverse_bits(residue // 2, levels)), residue % 2

    mirrors = [None if residue % places == 0 else holder(2 * places - residue) for residue in range(places + 1)]
    return [holder(residue) for residue in range(places + 1)], mirrors


@functools.lru_cache(maxsize=None)
def folded_tables(places, rows, width):
    stride = 2 * places
    bins = stride * rows
    residues = np.arange(places + 1)
    angle = 2.0 * np.pi * ((residues[:, None] * np.arange(places)[None, :]) % stride) / stride
    parts = np.stack([np.cos(angle), -np.sin(angle)], axis=1)
    first = np.kron(parts.reshape(-1, places), np.eye(width))
    last = first.T / bins
    angle = 2.0 * np.pi * ((residues[:, None] * np.arange(rows)[None, :]) % bins) / bins
    twist = np.stack([np.cos(angle), np.sin(angle)])
    block = rows // 4
    series = np.arange(block)
    angle = 2.0 * np.pi * ((np.arange(4)[:, None] * series[None, :]) % rows) / rows
    spin = np.stack([np.cos(angle), np.sin(angle)])
    angle = 2.0 * np.pi * ((series[:, None] * series[None, :]) % block) / block
    cos, sin = np.cos(angle), np.sin(angle)
    there = np.block([[cos, -sin], [sin, cos]])
    back = np.block([[cos, sin], [-sin, cos]])
    reverse = np.eye(block)[::-1]
    return (
        first.astype(jnp.bfloat16),
        last.astype(jnp.bfloat16),
        twist.astype(np.float32),
        spin.astype(np.float32),
        np.stack([there, back]).astype(jnp.bfloat16),
        reverse.astype(jnp.bfloat16),
    )


def hops(places):
    return [[apart, apart + 1] for apart in range(0, places, 2)]


def prepare_kernel(
    features_ref,
    pre_ref,
    gain_ref,
    skip_ref,
    spectrum_ref,
    squares_ref,
    skipped_ref,
    packed_ref,
    features_in,
    pre_in,
    gain_in,
    skip_in,
    spectrum_in,
    squares_out,
    skipped_out,
    packed_out,
    in_sems,
    out_sems,
):
    blocks = [(part, parity) for part in range(2) for parity in range(2)]
    pairs = [(features_ref, features_in), (pre_ref, pre_in), (gain_ref, gain_in), (skip_ref, skip_in)]
    pairs += [(spectrum_ref.at[block], spectrum_in.at[block]) for block in blocks]
    arriving = [pltpu.make_async_copy(*pair, in_sems.at[slot]) for slot, pair in enumerate(pairs)]
    for copy in arriving:
        copy.start()
    leaving = []

    def leave(source, target):
        copy = pltpu.make_async_copy(source, target, out_sems.at[len(leaving)])
        copy.start()
        leaving.append(copy)

    def pack(slot, turned):
        if len(packed_ref.shape) == 4:
            places, width = packed_out.shape[1:3]
            for rank, place in enumerate(order_of(places)):
                packed_out[slot, rank] = turned[place * width : (place + 1) * width]
            leave(packed_out.at[slot], packed_ref.at[:, slot])
        else:
            packed_out[slot] = turned
            leave(packed_out.at[slot], packed_ref.at[slot])

    for copy in arriving[:4]:
        copy.wait()
    features = features_in[...].astype(F32)
    scaled = features * gain_in[...] * pre_in[...].astype(F32)
    pack(4, scaled.astype(BF16).T)
    skipped_out[...] = (scaled * skip_in[...]).astype(BF16).T
    leave(skipped_out, skipped_ref)
    turned = features_in[...].T.astype(F32)
    squares_out[...] = jnp.sum(turned * turned, axis=0, keepdims=True)
    leave(squares_out, squares_ref)
    for slot, block in enumerate(blocks):
        arriving[4 + slot].wait()
        if len(packed_ref.shape) == 4:
            quarter = spectrum_in.shape[2] // 4
            rows = [spectrum_in[(*block, pl.ds(turn, quarter, stride=4), slice(None))] for turn in range(4)]
            pack(slot, jnp.concatenate([row.astype(BF16).T for row in rows], axis=1))
        else:
            pack(slot, spectrum_in[block].astype(BF16).T)
    for copy in leaving:
        copy.wait()


def scale_kernel(channels, *refs):
    square_refs, scale_ref = refs[:-1], refs[-1]
    total = square_refs[0][...]
    for square_ref in square_refs[1:]:
        total = total + square_ref[...]
    scale_ref[...] = lax.rsqrt(total / channels + EPS)


def matmul(left, right):
    return jnp.dot(left, right, preferred_element_type=F32)


def butterfly(values, direction):
    (real0, imag0), (real1, imag1), (real2, imag2), (real3, imag3) = values
    even, odd = (real0 + real2, imag0 + imag2), (real1 + real3, imag1 + imag3)
    even_gap, odd_gap = (real0 - real2, imag0 - imag2), (real1 - real3, imag1 - imag3)
    lower = (even_gap[0] + odd_gap[1], even_gap[1] - odd_gap[0])
    upper = (even_gap[0] - odd_gap[1], even_gap[1] + odd_gap[0])
    total, gap = (even[0] + odd[0], even[1] + odd[1]), (even[0] - odd[0], even[1] - odd[1])
    return [total, lower, gap, upper] if direction > 0 else [total, upper, gap, lower]


def folded_kernel(packed_ref, first_ref, last_ref, twist_ref, spin_ref, dft_ref, reverse_ref, *refs):
    scale_refs, (out_ref, scales, signal, mirror, forward, backward, both) = refs[:-7], refs[-7:]
    wide, rows = out_ref.shape
    places, width = scales.shape[0], wide // scales.shape[0]
    block, inner = rows // 4, mirror.shape[0] // 8
    order = order_of(places)
    direct, mirrors = pair_rows(places)
    quarters = [pl.ds(turn * block, block) for turn in range(4)]
    groups = [range(begin, min(begin + 3, places + 1)) for begin in range(0, places + 1, 3)]
    for row, holder in enumerate(mirrors[1:places]):
        for part in range(2):
            for turn in range(4):
                at = pl.ds((part * 4 + 3 - turn) * inner + row * width, width)
                mirror[at, :] = packed_ref[holder[0], 2 * part + holder[1], :, quarters[turn]]
    reversed_bins = matmul(mirror[...], reverse_ref[...])
    place = lax.axis_index("seq")
    for scale_ref, steps in zip(scale_refs, hops(places)):
        for at, step in enumerate(steps):
            scales[place ^ step] = scale_ref[pl.ds(at, 1), :]
    for rank, at in enumerate(order):
        signal[pl.ds(at * width, width), :] = (packed_ref[rank, 4].astype(F32) * scales[at]).astype(BF16)
    spectral = []
    for group in groups:
        begin = group[0] * width
        mixed = matmul(first_ref[pl.ds(2 * begin, 2 * len(group) * width), :], signal[...])
        for at, residue in enumerate(group):
            over, under = mixed[2 * at * width : (2 * at + 1) * width], mixed[(2 * at + 1) * width : (2 * at + 2) * width]
            values = []
            for turn in range(4):
                real, imag = (part[:, turn * block : (turn + 1) * block] for part in (over, under))
                cos, sin = (twist_ref[part, pl.ds(residue, 1), quarters[turn]] for part in range(2))
                values.append((real * cos + imag * sin, imag * cos - real * sin))
            for turn, (real, imag) in enumerate(butterfly(values, 1)):
                if turn > 0:
                    cos, sin = spin_ref[0, pl.ds(turn, 1), :], spin_ref[1, pl.ds(turn, 1), :]
                    real, imag = real * cos + imag * sin, imag * cos - real * sin
                row = pl.ds(4 * begin + (turn * len(group) + at) * width, width)
                forward[row, pl.ds(0, block)] = real.astype(BF16)
                forward[row, pl.ds(block, block)] = imag.astype(BF16)
        spectral.append(matmul(forward[pl.ds(4 * begin, 4 * len(group) * width), :], dft_ref[0]))
    restored = []
    for group, values in zip(groups, spectral):
        begin = group[0] * width
        for turn in range(4):
            for at, residue in enumerate(group):
                row = (turn * len(group) + at) * width
                real, imag = values[row : row + width, :block], values[row : row + width, block:]
                holder = direct[residue]
                response_real = packed_ref[holder[0], holder[1], :, quarters[turn]].astype(F32)
                response_imag = packed_ref[holder[0], 2 + holder[1], :, quarters[turn]].astype(F32)
                if mirrors[residue] is not None:
                    other = turn * inner + (residue - 1) * width
                    response_real = response_real + reversed_bins[other : other + width]
                    other = other + 4 * inner
                    response_imag = response_imag - reversed_bins[other : other + width]
                target = pl.ds(4 * begin + row, width)
                backward[target, pl.ds(0, block)] = (real * response_real - imag * response_imag).astype(BF16)
                backward[target, pl.ds(block, block)] = (real * response_imag + imag * response_real).astype(BF16)
        restored.append(matmul(backward[pl.ds(4 * begin, 4 * len(group) * width), :], dft_ref[1]))
    for group, turned in zip(groups, restored):
        for at, residue in enumerate(group):
            values = []
            for turn in range(4):
                row = (turn * len(group) + at) * width
                real, imag = turned[row : row + width, :block], turned[row : row + width, block:]
                if turn > 0:
                    cos, sin = spin_ref[0, pl.ds(turn, 1), :], spin_ref[1, pl.ds(turn, 1), :]
                    real, imag = real * cos - imag * sin, imag * cos + real * sin
                values.append((real, imag))
            for lanes, (real, imag) in zip(quarters, butterfly(values, -1)):
                cos, sin = twist_ref[0, pl.ds(residue, 1), lanes], twist_ref[1, pl.ds(residue, 1), lanes]
                both[pl.ds(2 * residue * width, width), lanes] = (real * cos - imag * sin).astype(BF16)
                both[pl.ds((2 * residue + 1) * width, width), lanes] = (imag * cos + real * sin).astype(BF16)
    result = matmul(last_ref[...], both[...]).astype(BF16)
    for rank, at in enumerate(order):
        out_ref[pl.ds(rank * width, width), :] = result[at * width : (at + 1) * width]


def convolve_kernel(packed_ref, first_ref, last_ref, twist_ref, dft_ref, scale_ref, out_ref, left, right):
    wide, rows = out_ref.shape
    half = 2 * wide
    signal = (packed_ref[4].astype(F32) * scale_ref[...]).astype(BF16)
    mixed = matmul(first_ref[...], signal)
    real, imag = mixed[:half], mixed[half:]
    cos_twist, sin_twist = twist_ref[0], twist_ref[1]
    turned_real = (real * cos_twist + imag * sin_twist).astype(BF16)
    turned_imag = (imag * cos_twist - real * sin_twist).astype(BF16)
    left[pl.ds(0, half), pl.ds(0, rows)] = turned_real
    left[pl.ds(0, half), pl.ds(rows, rows)] = turned_imag
    left[pl.ds(half, half), pl.ds(0, rows)] = turned_imag
    left[pl.ds(half, half), pl.ds(rows, rows)] = -turned_real
    mixed = matmul(left[...], dft_ref[...])
    real, imag = mixed[:half], mixed[half:]
    response_real = packed_ref[0:2].reshape(half, rows).astype(F32)
    response_imag = packed_ref[2:4].reshape(half, rows).astype(F32)
    product_real = (real * response_real - imag * response_imag).astype(BF16)
    product_imag = (real * response_imag + imag * response_real).astype(BF16)
    right[pl.ds(0, half), pl.ds(0, rows)] = product_real
    right[pl.ds(0, half), pl.ds(rows, rows)] = -product_imag
    right[pl.ds(half, half), pl.ds(0, rows)] = product_imag
    right[pl.ds(half, half), pl.ds(rows, rows)] = product_real
    mixed = matmul(right[...], dft_ref[...])
    real, imag = mixed[:half], mixed[half:]
    turned_real = (real * cos_twist - imag * sin_twist).astype(BF16)
    turned_imag = (imag * cos_twist + real * sin_twist).astype(BF16)
    both = jnp.concatenate([turned_real, turned_imag], axis=0)
    out_ref[...] = matmul(last_ref[...], both).astype(BF16)


def finish_kernel(conv_ref, skipped_ref, scale_ref, post_ref, out_ref):
    conv = conv_ref[...]
    if len(conv_ref.shape) == 3:
        order = order_of(conv_ref.shape[0])
        conv = jnp.concatenate([conv_ref[order.index(place)] for place in range(len(order))])
    turned = conv.astype(F32) + skipped_ref[...].astype(F32) * scale_ref[...]
    out_ref[...] = (post_ref[...].astype(F32) * turned.T).astype(BF16)


def call(kernel, out_shape, flops, moved, *operands, limit=VMEM_LIMIT, **options):
    return pl.pallas_call(
        kernel,
        out_shape=out_shape,
        compiler_params=pltpu.CompilerParams(vmem_limit_bytes=limit),
        cost_estimate=pl.CostEstimate(flops=flops, bytes_accessed=moved, transcendentals=0),
        **options,
    )(*operands)


def exchange(value):
    ranks = [list(order_of(lax.axis_size("seq")))]
    return lax.all_to_all(value, "seq", split_axis=0, concat_axis=0, tiled=True, axis_index_groups=ranks)


def swap(value, axis, apart):
    return lax.ppermute(value, axis, [(place, place ^ apart) for place in range(lax.axis_size(axis))])


def local(features, pre_gate, post_gate, norm_gain, skip_weight, spectrum):
    rows, wide = features.shape
    places = lax.axis_size("seq")
    groups = lax.axis_size("chan")
    width = wide // places
    piled = width % 16 == 0
    cells = rows * wide
    shape = jax.ShapeDtypeStruct
    vmem, anywhere = pl.BlockSpec(memory_space=pltpu.VMEM), pl.BlockSpec(memory_space=pl.ANY)
    squares, skipped, packed = call(
        prepare_kernel,
        (
            shape((1, rows), F32),
            shape((wide, rows), BF16),
            shape((places, 5, width, rows) if piled else (5, wide, rows), BF16),
        ),
        10 * cells,
        32 * cells,
        features,
        pre_gate,
        norm_gain[None, :],
        skip_weight[None, :],
        spectrum,
        limit=WHOLE_VMEM,
        in_specs=[anywhere] * 5,
        out_specs=(anywhere, anywhere, anywhere),
        scratch_shapes=[
            pltpu.VMEM(features.shape, BF16),
            pltpu.VMEM(pre_gate.shape, BF16),
            pltpu.VMEM((1, wide), F32),
            pltpu.VMEM((1, wide), F32),
            pltpu.VMEM(spectrum.shape, F32),
            pltpu.VMEM((1, rows), F32),
            pltpu.VMEM((wide, rows), BF16),
            pltpu.VMEM((5, places, width, rows) if piled else (5, wide, rows), BF16),
            pltpu.SemaphoreType.DMA((8,)),
            pltpu.SemaphoreType.DMA((7,)),
        ],
    )
    if not piled:
        packed = packed.reshape(5, places, width, rows).transpose(1, 0, 2, 3)
    gathered = exchange(packed)
    others = [swap(squares, "chan", apart) for apart in range(1, groups)]
    scale = call(
        functools.partial(scale_kernel, wide * groups), shape((1, rows), F32), 8 * rows, 32 * rows, squares, *others
    )
    if piled:
        near = jnp.concatenate([scale, swap(scale, "seq", 1)])
        scales = [near] + [swap(near, "seq", steps[0]) for steps in hops(places)[1:]]
    else:
        scales = [jnp.repeat(lax.all_gather(scale, "seq", axis=0, tiled=True), width, axis=0)]
        response = gathered[:, :4].reshape(places, 2, 2, width, rows).transpose(1, 0, 2, 3, 4)
        gathered = jnp.concatenate([response.reshape(4, wide, rows), gathered[:, 4].reshape(1, wide, rows)])
    if piled:
        constants = folded_tables(places, rows, width)
        half = constants[0].shape[0] // 2
        scratch = [
            pltpu.VMEM((places, 1, rows), F32),
            pltpu.VMEM((wide, rows), BF16),
            pltpu.VMEM((8 * (half - 2 * width), rows // 4), BF16),
            pltpu.VMEM((4 * half, rows // 2), BF16),
            pltpu.VMEM((4 * half, rows // 2), BF16),
            pltpu.VMEM((2 * half, rows), BF16),
        ]
    else:
        constants = tables(places, rows, width)
        scratch = [pltpu.VMEM((4 * wide, 2 * rows), BF16)] * 2
    conv = call(
        folded_kernel if piled else convolve_kernel,
        shape((wide, rows), BF16),
        20 * cells * rows,
        20 * cells,
        gathered,
        *constants,
        *scales,
        scratch_shapes=scratch,
    )
    conv = exchange(conv.reshape(places, width, rows))
    if not piled:
        conv = conv.reshape(wide, rows)
    return call(finish_kernel, shape((rows, wide), BF16), 10 * cells, 8 * cells, conv, skipped, scale, post_gate)


def solution(mesh):
    return jax.shard_map(
        local,
        mesh=mesh,
        in_specs=(
            P("seq", "chan"),
            P("seq", "chan"),
            P("seq", "chan"),
            P("chan"),
            P("chan"),
            P(None, "seq", None, "chan"),
        ),
        out_specs=P("seq", "chan"),
        check_vma=False,
    )
```

```python
import functools

import jax
import jax.numpy as jnp
import numpy as np
from jax import lax
from jax.experimental import pallas as pl
from jax.experimental.pallas import tpu as pltpu
from jax.sharding import PartitionSpec as P

EPS = 1e-06
BF16 = jnp.bfloat16
F32 = jnp.float32
VMEM_LIMIT = 48 * 1024 * 1024
WHOLE_VMEM = 63 * 1024 * 1024 + 512 * 1024


def order_of(places):
    return (5, 1, 3, 6, 2, 4, 0, 7) if places == 8 else tuple(range(places))


def reverse_bits(index, levels):
    return sum((index >> bit & 1) << levels - 1 - bit for bit in range(levels))


@functools.lru_cache(maxsize=None)
def tables(places, rows, width):
    levels = places.bit_length() - 1
    stride = 2 * places
    bins = stride * rows
    residues = np.array([2 * reverse_bits(place, levels) + parity for place in range(places) for parity in range(2)])
    angle = 2.0 * np.pi * ((residues[:, None] * np.arange(places)[None, :]) % stride) / stride
    same = np.eye(width)
    first = np.concatenate([np.kron(np.cos(angle), same), np.kron(-np.sin(angle), same)])
    last = first.T / bins
    angle = 2.0 * np.pi * ((residues[:, None] * np.arange(rows)[None, :]) % bins) / bins
    twist = np.repeat(np.stack([np.cos(angle), np.sin(angle)]), width, axis=1)
    series = np.arange(rows)
    angle = 2.0 * np.pi * ((series[:, None] * series[None, :]) % rows) / rows
    dft = np.concatenate([np.cos(angle), np.sin(angle)])
    return (
        first.astype(jnp.bfloat16),
        last.astype(jnp.bfloat16),
        twist.astype(np.float32),
        dft.astype(jnp.bfloat16),
    )


def pair_rows(places):
    levels = places.bit_length() - 1

    def holder(residue):
        return order_of(places).index(reverse_bits(residue // 2, levels)), residue % 2

    mirrors = [None if residue % places == 0 else holder(2 * places - residue) for residue in range(places + 1)]
    return [holder(residue) for residue in range(places + 1)], mirrors


@functools.lru_cache(maxsize=None)
def folded_tables(places, rows, width):
    stride = 2 * places
    bins = stride * rows
    residues = np.arange(places + 1)
    angle = 2.0 * np.pi * ((residues[:, None] * np.arange(places)[None, :]) % stride) / stride
    parts = np.stack([np.cos(angle), -np.sin(angle)], axis=1)
    first = np.kron(parts.reshape(-1, places), np.eye(width))
    last = first.T / bins
    angle = 2.0 * np.pi * ((residues[:, None] * np.arange(rows)[None, :]) % bins) / bins
    twist = np.stack([np.cos(angle), np.sin(angle)])
    block = rows // 4
    series = np.arange(block)
    angle = 2.0 * np.pi * ((np.arange(4)[:, None] * series[None, :]) % rows) / rows
    spin = np.stack([np.cos(angle), np.sin(angle)])
    angle = 2.0 * np.pi * ((series[:, None] * series[None, :]) % block) / block
    cos, sin = np.cos(angle), np.sin(angle)
    there = np.block([[cos, -sin], [sin, cos]])
    back = np.block([[cos, sin], [-sin, cos]])
    reverse = np.eye(block)[::-1]
    return (
        first.astype(jnp.bfloat16),
        last.astype(jnp.bfloat16),
        twist.astype(np.float32),
        spin.astype(np.float32),
        np.stack([there, back]).astype(jnp.bfloat16),
        reverse.astype(jnp.bfloat16),
    )


def hops(places):
    return [[apart, apart + 1] for apart in range(0, places, 2)]


def prepare_kernel(
    features_ref,
    pre_ref,
    gain_ref,
    skip_ref,
    spectrum_ref,
    squares_ref,
    skipped_ref,
    packed_ref,
    features_in,
    pre_in,
    gain_in,
    skip_in,
    spectrum_in,
    squares_out,
    skipped_out,
    packed_out,
    in_sems,
    out_sems,
):
    blocks = [(part, parity) for part in range(2) for parity in range(2)]
    pairs = [(features_ref, features_in), (pre_ref, pre_in), (gain_ref, gain_in), (skip_ref, skip_in)]
    pairs += [(spectrum_ref.at[block], spectrum_in.at[block]) for block in blocks]
    arriving = [pltpu.make_async_copy(*pair, in_sems.at[slot]) for slot, pair in enumerate(pairs)]
    for copy in arriving:
        copy.start()
    leaving = []

    def leave(source, target):
        copy = pltpu.make_async_copy(source, target, out_sems.at[len(leaving)])
        copy.start()
        leaving.append(copy)

    def pack(slot, turned):
        if len(packed_ref.shape) == 4:
            places, width = packed_out.shape[1:3]
            for rank, place in enumerate(order_of(places)):
                packed_out[slot, rank] = turned[place * width : (place + 1) * width]
            leave(packed_out.at[slot], packed_ref.at[:, slot])
        else:
            packed_out[slot] = turned
            leave(packed_out.at[slot], packed_ref.at[slot])

    for copy in arriving[:4]:
        copy.wait()
    features = features_in[...].astype(F32)
    scaled = features * gain_in[...] * pre_in[...].astype(F32)
    pack(4, scaled.astype(BF16).T)
    skipped_out[...] = (scaled * skip_in[...]).astype(BF16).T
    leave(skipped_out, skipped_ref)
    turned = features_in[...].T.astype(F32)
    squares_out[...] = jnp.sum(turned * turned, axis=0, keepdims=True)
    leave(squares_out, squares_ref)
    for slot, block in enumerate(blocks):
        arriving[4 + slot].wait()
        if len(packed_ref.shape) == 4:
            quarter = spectrum_in.shape[2] // 4
            rows = [spectrum_in[(*block, pl.ds(turn, quarter, stride=4), slice(None))] for turn in range(4)]
            pack(slot, jnp.concatenate([row.astype(BF16).T for row in rows], axis=1))
        else:
            pack(slot, spectrum_in[block].astype(BF16).T)
    for copy in leaving:
        copy.wait()


def scale_kernel(channels, *refs):
    square_refs, scale_ref = refs[:-1], refs[-1]
    total = square_refs[0][...]
    for square_ref in square_refs[1:]:
        total = total + square_ref[...]
    scale_ref[...] = lax.rsqrt(total / channels + EPS)


def matmul(left, right):
    return jnp.dot(left, right, preferred_element_type=F32)


def butterfly(values, direction):
    (real0, imag0), (real1, imag1), (real2, imag2), (real3, imag3) = values
    even, odd = (real0 + real2, imag0 + imag2), (real1 + real3, imag1 + imag3)
    even_gap, odd_gap = (real0 - real2, imag0 - imag2), (real1 - real3, imag1 - imag3)
    lower = (even_gap[0] + odd_gap[1], even_gap[1] - odd_gap[0])
    upper = (even_gap[0] - odd_gap[1], even_gap[1] + odd_gap[0])
    total, gap = (even[0] + odd[0], even[1] + odd[1]), (even[0] - odd[0], even[1] - odd[1])
    return [total, lower, gap, upper] if direction > 0 else [total, upper, gap, lower]


def folded_kernel(packed_ref, first_ref, last_ref, twist_ref, spin_ref, dft_ref, reverse_ref, *refs):
    scale_refs, (out_ref, scales, signal, mirror, forward, backward, both) = refs[:-7], refs[-7:]
    wide, rows = out_ref.shape
    places, width = scales.shape[0], wide // scales.shape[0]
    block, inner = rows // 4, mirror.shape[0] // 8
    order = order_of(places)
    direct, mirrors = pair_rows(places)
    quarters = [pl.ds(turn * block, block) for turn in range(4)]
    groups = [range(begin, min(begin + 3, places + 1)) for begin in range(0, places + 1, 3)]
    for row, holder in enumerate(mirrors[1:places]):
        for part in range(2):
            for turn in range(4):
                at = pl.ds((part * 4 + 3 - turn) * inner + row * width, width)
                mirror[at, :] = packed_ref[holder[0], 2 * part + holder[1], :, quarters[turn]]
    reversed_bins = matmul(mirror[...], reverse_ref[...])
    place = lax.axis_index("seq")
    for scale_ref, steps in zip(scale_refs, hops(places)):
        for at, step in enumerate(steps):
            scales[place ^ step] = scale_ref[pl.ds(at, 1), :]
    for rank, at in enumerate(order):
        signal[pl.ds(at * width, width), :] = (packed_ref[rank, 4].astype(F32) * scales[at]).astype(BF16)
    spectral = []
    for group in groups:
        begin = group[0] * width
        mixed = matmul(first_ref[pl.ds(2 * begin, 2 * len(group) * width), :], signal[...])
        for at, residue in enumerate(group):
            over, under = mixed[2 * at * width : (2 * at + 1) * width], mixed[(2 * at + 1) * width : (2 * at + 2) * width]
            values = []
            for turn in range(4):
                real, imag = (part[:, turn * block : (turn + 1) * block] for part in (over, under))
                cos, sin = (twist_ref[part, pl.ds(residue, 1), quarters[turn]] for part in range(2))
                values.append((real * cos + imag * sin, imag * cos - real * sin))
            for turn, (real, imag) in enumerate(butterfly(values, 1)):
                if turn > 0:
                    cos, sin = spin_ref[0, pl.ds(turn, 1), :], spin_ref[1, pl.ds(turn, 1), :]
                    real, imag = real * cos + imag * sin, imag * cos - real * sin
                row = pl.ds(4 * begin + (turn * len(group) + at) * width, width)
                forward[row, pl.ds(0, block)] = real.astype(BF16)
                forward[row, pl.ds(block, block)] = imag.astype(BF16)
        spectral.append(matmul(forward[pl.ds(4 * begin, 4 * len(group) * width), :], dft_ref[0]))
    restored = []
    for group, values in zip(groups, spectral):
        begin = group[0] * width
        for turn in range(4):
            for at, residue in enumerate(group):
                row = (turn * len(group) + at) * width
                real, imag = values[row : row + width, :block], values[row : row + width, block:]
                holder = direct[residue]
                response_real = packed_ref[holder[0], holder[1], :, quarters[turn]].astype(F32)
                response_imag = packed_ref[holder[0], 2 + holder[1], :, quarters[turn]].astype(F32)
                if mirrors[residue] is not None:
                    other = turn * inner + (residue - 1) * width
                    response_real = response_real + reversed_bins[other : other + width]
                    other = other + 4 * inner
                    response_imag = response_imag - reversed_bins[other : other + width]
                target = pl.ds(4 * begin + row, width)
                backward[target, pl.ds(0, block)] = (real * response_real - imag * response_imag).astype(BF16)
                backward[target, pl.ds(block, block)] = (real * response_imag + imag * response_real).astype(BF16)
        restored.append(matmul(backward[pl.ds(4 * begin, 4 * len(group) * width), :], dft_ref[1]))
    for group, turned in zip(groups, restored):
        for at, residue in enumerate(group):
            values = []
            for turn in range(4):
                row = (turn * len(group) + at) * width
                real, imag = turned[row : row + width, :block], turned[row : row + width, block:]
                if turn > 0:
                    cos, sin = spin_ref[0, pl.ds(turn, 1), :], spin_ref[1, pl.ds(turn, 1), :]
                    real, imag = real * cos - imag * sin, imag * cos + real * sin
                values.append((real, imag))
            for lanes, (real, imag) in zip(quarters, butterfly(values, -1)):
                cos, sin = twist_ref[0, pl.ds(residue, 1), lanes], twist_ref[1, pl.ds(residue, 1), lanes]
                both[pl.ds(2 * residue * width, width), lanes] = (real * cos - imag * sin).astype(BF16)
                both[pl.ds((2 * residue + 1) * width, width), lanes] = (imag * cos + real * sin).astype(BF16)
    result = matmul(last_ref[...], both[...]).astype(BF16)
    for rank, at in enumerate(order):
        out_ref[pl.ds(rank * width, width), :] = result[at * width : (at + 1) * width]


def convolve_kernel(packed_ref, first_ref, last_ref, twist_ref, dft_ref, scale_ref, out_ref, left, right):
    wide, rows = out_ref.shape
    half = 2 * wide
    signal = (packed_ref[4].astype(F32) * scale_ref[...]).astype(BF16)
    mixed = matmul(first_ref[...], signal)
    real, imag = mixed[:half], mixed[half:]
    cos_twist, sin_twist = twist_ref[0], twist_ref[1]
    turned_real = (real * cos_twist + imag * sin_twist).astype(BF16)
    turned_imag = (imag * cos_twist - real * sin_twist).astype(BF16)
    left[pl.ds(0, half), pl.ds(0, rows)] = turned_real
    left[pl.ds(0, half), pl.ds(rows, rows)] = turned_imag
    left[pl.ds(half, half), pl.ds(0, rows)] = turned_imag
    left[pl.ds(half, half), pl.ds(rows, rows)] = -turned_real
    mixed = matmul(left[...], dft_ref[...])
    real, imag = mixed[:half], mixed[half:]
    response_real = packed_ref[0:2].reshape(half, rows).astype(F32)
    response_imag = packed_ref[2:4].reshape(half, rows).astype(F32)
    product_real = (real * response_real - imag * response_imag).astype(BF16)
    product_imag = (real * response_imag + imag * response_real).astype(BF16)
    right[pl.ds(0, half), pl.ds(0, rows)] = product_real
    right[pl.ds(0, half), pl.ds(rows, rows)] = -product_imag
    right[pl.ds(half, half), pl.ds(0, rows)] = product_imag
    right[pl.ds(half, half), pl.ds(rows, rows)] = product_real
    mixed = matmul(right[...], dft_ref[...])
    real, imag = mixed[:half], mixed[half:]
    turned_real = (real * cos_twist - imag * sin_twist).astype(BF16)
    turned_imag = (imag * cos_twist + real * sin_twist).astype(BF16)
    both = jnp.concatenate([turned_real, turned_imag], axis=0)
    out_ref[...] = matmul(last_ref[...], both).astype(BF16)


def finish_kernel(conv_ref, skipped_ref, scale_ref, post_ref, out_ref):
    conv = conv_ref[...]
    if len(conv_ref.shape) == 3:
        order = order_of(conv_ref.shape[0])
        conv = jnp.concatenate([conv_ref[order.index(place)] for place in range(len(order))])
    turned = conv.astype(F32) + skipped_ref[...].astype(F32) * scale_ref[...]
    out_ref[...] = (post_ref[...].astype(F32) * turned.T).astype(BF16)


def call(kernel, out_shape, flops, moved, *operands, limit=VMEM_LIMIT, **options):
    return pl.pallas_call(
        kernel,
        out_shape=out_shape,
        compiler_params=pltpu.CompilerParams(vmem_limit_bytes=limit),
        cost_estimate=pl.CostEstimate(flops=flops, bytes_accessed=moved, transcendentals=0),
        **options,
    )(*operands)


def exchange(value):
    ranks = [list(order_of(lax.axis_size("seq")))]
    return lax.all_to_all(value, "seq", split_axis=0, concat_axis=0, tiled=True, axis_index_groups=ranks)


def swap(value, axis, apart):
    return lax.ppermute(value, axis, [(place, place ^ apart) for place in range(lax.axis_size(axis))])


def local(features, pre_gate, post_gate, norm_gain, skip_weight, spectrum):
    rows, wide = features.shape
    places = lax.axis_size("seq")
    groups = lax.axis_size("chan")
    width = wide // places
    piled = width % 16 == 0
    cells = rows * wide
    shape = jax.ShapeDtypeStruct
    vmem, anywhere = pl.BlockSpec(memory_space=pltpu.VMEM), pl.BlockSpec(memory_space=pl.ANY)
    squares, skipped, packed = call(
        prepare_kernel,
        (
            shape((1, rows), F32),
            shape((wide, rows), BF16),
            shape((places, 5, width, rows) if piled else (5, wide, rows), BF16),
        ),
        10 * cells,
        32 * cells,
        features,
        pre_gate,
        norm_gain[None, :],
        skip_weight[None, :],
        spectrum,
        limit=WHOLE_VMEM,
        in_specs=[anywhere] * 5,
        out_specs=(anywhere, anywhere, anywhere),
        scratch_shapes=[
            pltpu.VMEM(features.shape, BF16),
            pltpu.VMEM(pre_gate.shape, BF16),
            pltpu.VMEM((1, wide), F32),
            pltpu.VMEM((1, wide), F32),
            pltpu.VMEM(spectrum.shape, F32),
            pltpu.VMEM((1, rows), F32),
            pltpu.VMEM((wide, rows), BF16),
            pltpu.VMEM((5, places, width, rows) if piled else (5, wide, rows), BF16),
            pltpu.SemaphoreType.DMA((8,)),
            pltpu.SemaphoreType.DMA((7,)),
        ],
    )
    if not piled:
        packed = packed.reshape(5, places, width, rows).transpose(1, 0, 2, 3)
    gathered = exchange(packed)
    others = [swap(squares, "chan", apart) for apart in range(1, groups)]
    scale = call(
        functools.partial(scale_kernel, wide * groups), shape((1, rows), F32), 8 * rows, 32 * rows, squares, *others
    )
    if piled:
        near = jnp.concatenate([scale, swap(scale, "seq", 1)])
        scales = [near] + [swap(near, "seq", steps[0]) for steps in hops(places)[1:]]
    else:
        scales = [jnp.repeat(lax.all_gather(scale, "seq", axis=0, tiled=True), width, axis=0)]
        response = gathered[:, :4].reshape(places, 2, 2, width, rows).transpose(1, 0, 2, 3, 4)
        gathered = jnp.concatenate([response.reshape(4, wide, rows), gathered[:, 4].reshape(1, wide, rows)])
    if piled:
        constants = folded_tables(places, rows, width)
        half = constants[0].shape[0] // 2
        scratch = [
            pltpu.VMEM((places, 1, rows), F32),
            pltpu.VMEM((wide, rows), BF16),
            pltpu.VMEM((8 * (half - 2 * width), rows // 4), BF16),
            pltpu.VMEM((4 * half, rows // 2), BF16),
            pltpu.VMEM((4 * half, rows // 2), BF16),
            pltpu.VMEM((2 * half, rows), BF16),
        ]
    else:
        constants = tables(places, rows, width)
        scratch = [pltpu.VMEM((4 * wide, 2 * rows), BF16)] * 2
    conv = call(
        folded_kernel if piled else convolve_kernel,
        shape((wide, rows), BF16),
        20 * cells * rows,
        20 * cells,
        gathered,
        *constants,
        *scales,
        scratch_shapes=scratch,
    )
    conv = exchange(conv.reshape(places, width, rows))
    if not piled:
        conv = conv.reshape(wide, rows)
    return call(finish_kernel, shape((rows, wide), BF16), 10 * cells, 8 * cells, conv, skipped, scale, post_gate)


def solution(mesh):
    return jax.shard_map(
        local,
        mesh=mesh,
        in_specs=(
            P("seq", "chan"),
            P("seq", "chan"),
            P("seq", "chan"),
            P("chan"),
            P("chan"),
            P(None, "seq", None, "chan"),
        ),
        out_specs=P("seq", "chan"),
        check_vma=False,
    )
```

```python
import functools

import jax
import jax.numpy as jnp
import numpy as np
from jax import lax
from jax.experimental import pallas as pl
from jax.experimental.pallas import tpu as pltpu
from jax.sharding import PartitionSpec as P

EPS = 1e-06
BF16 = jnp.bfloat16
F32 = jnp.float32
VMEM_LIMIT = 48 * 1024 * 1024
WHOLE_VMEM = 63 * 1024 * 1024 + 512 * 1024


def order_of(places):
    return (5, 2, 1, 7, 4, 3, 0, 6) if places == 8 else tuple(range(places))


def reverse_bits(index, levels):
    return sum((index >> bit & 1) << levels - 1 - bit for bit in range(levels))


@functools.lru_cache(maxsize=None)
def tables(places, rows, width):
    levels = places.bit_length() - 1
    stride = 2 * places
    bins = stride * rows
    residues = np.array([2 * reverse_bits(place, levels) + parity for place in range(places) for parity in range(2)])
    angle = 2.0 * np.pi * ((residues[:, None] * np.arange(places)[None, :]) % stride) / stride
    same = np.eye(width)
    first = np.concatenate([np.kron(np.cos(angle), same), np.kron(-np.sin(angle), same)])
    last = first.T / bins
    angle = 2.0 * np.pi * ((residues[:, None] * np.arange(rows)[None, :]) % bins) / bins
    twist = np.repeat(np.stack([np.cos(angle), np.sin(angle)]), width, axis=1)
    series = np.arange(rows)
    angle = 2.0 * np.pi * ((series[:, None] * series[None, :]) % rows) / rows
    dft = np.concatenate([np.cos(angle), np.sin(angle)])
    return (
        first.astype(jnp.bfloat16),
        last.astype(jnp.bfloat16),
        twist.astype(np.float32),
        dft.astype(jnp.bfloat16),
    )


def pair_rows(places):
    levels = places.bit_length() - 1

    def holder(residue):
        return order_of(places).index(reverse_bits(residue // 2, levels)), residue % 2

    mirrors = [None if residue % places == 0 else holder(2 * places - residue) for residue in range(places + 1)]
    return [holder(residue) for residue in range(places + 1)], mirrors


@functools.lru_cache(maxsize=None)
def folded_tables(places, rows, width):
    stride = 2 * places
    bins = stride * rows
    residues = np.arange(places + 1)
    angle = 2.0 * np.pi * ((residues[:, None] * np.arange(places)[None, :]) % stride) / stride
    parts = np.stack([np.cos(angle), -np.sin(angle)], axis=1)
    first = np.kron(parts.reshape(-1, places), np.eye(width))
    last = first.T / bins
    angle = 2.0 * np.pi * ((residues[:, None] * np.arange(rows)[None, :]) % bins) / bins
    twist = np.stack([np.cos(angle), np.sin(angle)])
    block = rows // 4
    series = np.arange(block)
    angle = 2.0 * np.pi * ((np.arange(4)[:, None] * series[None, :]) % rows) / rows
    spin = np.stack([np.cos(angle), np.sin(angle)])
    angle = 2.0 * np.pi * ((series[:, None] * series[None, :]) % block) / block
    cos, sin = np.cos(angle), np.sin(angle)
    there = np.block([[cos, -sin], [sin, cos]])
    back = np.block([[cos, sin], [-sin, cos]])
    reverse = np.eye(block)[::-1]
    return (
        first.astype(jnp.bfloat16),
        last.astype(jnp.bfloat16),
        twist.astype(np.float32),
        spin.astype(np.float32),
        np.stack([there, back]).astype(jnp.bfloat16),
        reverse.astype(jnp.bfloat16),
    )


def hops(places):
    return [[apart, apart + 1] for apart in range(0, places, 2)]


def prepare_kernel(
    features_ref,
    pre_ref,
    gain_ref,
    skip_ref,
    spectrum_ref,
    squares_ref,
    skipped_ref,
    packed_ref,
    features_in,
    pre_in,
    gain_in,
    skip_in,
    spectrum_in,
    squares_out,
    skipped_out,
    packed_out,
    in_sems,
    out_sems,
):
    blocks = [(part, parity) for part in range(2) for parity in range(2)]
    pairs = [(features_ref, features_in), (pre_ref, pre_in), (gain_ref, gain_in), (skip_ref, skip_in)]
    pairs += [(spectrum_ref.at[block], spectrum_in.at[block]) for block in blocks]
    arriving = [pltpu.make_async_copy(*pair, in_sems.at[slot]) for slot, pair in enumerate(pairs)]
    for copy in arriving:
        copy.start()
    leaving = []

    def leave(source, target):
        copy = pltpu.make_async_copy(source, target, out_sems.at[len(leaving)])
        copy.start()
        leaving.append(copy)

    def pack(slot, turned):
        if len(packed_ref.shape) == 4:
            places, width = packed_out.shape[1:3]
            for rank, place in enumerate(order_of(places)):
                packed_out[slot, rank] = turned[place * width : (place + 1) * width]
            leave(packed_out.at[slot], packed_ref.at[:, slot])
        else:
            packed_out[slot] = turned
            leave(packed_out.at[slot], packed_ref.at[slot])

    for copy in arriving[:4]:
        copy.wait()
    features = features_in[...].astype(F32)
    scaled = features * gain_in[...] * pre_in[...].astype(F32)
    pack(4, scaled.astype(BF16).T)
    skipped_out[...] = (scaled * skip_in[...]).astype(BF16).T
    leave(skipped_out, skipped_ref)
    turned = features_in[...].T.astype(F32)
    squares_out[...] = jnp.sum(turned * turned, axis=0, keepdims=True)
    leave(squares_out, squares_ref)
    for slot, block in enumerate(blocks):
        arriving[4 + slot].wait()
        if len(packed_ref.shape) == 4:
            quarter = spectrum_in.shape[2] // 4
            rows = [spectrum_in[(*block, pl.ds(turn, quarter, stride=4), slice(None))] for turn in range(4)]
            pack(slot, jnp.concatenate([row.astype(BF16).T for row in rows], axis=1))
        else:
            pack(slot, spectrum_in[block].astype(BF16).T)
    for copy in leaving:
        copy.wait()


def scale_kernel(channels, *refs):
    square_refs, scale_ref = refs[:-1], refs[-1]
    total = square_refs[0][...]
    for square_ref in square_refs[1:]:
        total = total + square_ref[...]
    scale_ref[...] = lax.rsqrt(total / channels + EPS)


def matmul(left, right):
    return jnp.dot(left, right, preferred_element_type=F32)


def butterfly(values, direction):
    (real0, imag0), (real1, imag1), (real2, imag2), (real3, imag3) = values
    even, odd = (real0 + real2, imag0 + imag2), (real1 + real3, imag1 + imag3)
    even_gap, odd_gap = (real0 - real2, imag0 - imag2), (real1 - real3, imag1 - imag3)
    lower = (even_gap[0] + odd_gap[1], even_gap[1] - odd_gap[0])
    upper = (even_gap[0] - odd_gap[1], even_gap[1] + odd_gap[0])
    total, gap = (even[0] + odd[0], even[1] + odd[1]), (even[0] - odd[0], even[1] - odd[1])
    return [total, lower, gap, upper] if direction > 0 else [total, upper, gap, lower]


def folded_kernel(packed_ref, first_ref, last_ref, twist_ref, spin_ref, dft_ref, reverse_ref, *refs):
    scale_refs, (out_ref, scales, signal, mirror, forward, backward, both) = refs[:-7], refs[-7:]
    wide, rows = out_ref.shape
    places, width = scales.shape[0], wide // scales.shape[0]
    block, inner = rows // 4, mirror.shape[0] // 8
    order = order_of(places)
    direct, mirrors = pair_rows(places)
    quarters = [pl.ds(turn * block, block) for turn in range(4)]
    groups = [range(begin, min(begin + 3, places + 1)) for begin in range(0, places + 1, 3)]
    for row, holder in enumerate(mirrors[1:places]):
        for part in range(2):
            for turn in range(4):
                at = pl.ds((part * 4 + 3 - turn) * inner + row * width, width)
                mirror[at, :] = packed_ref[holder[0], 2 * part + holder[1], :, quarters[turn]]
    reversed_bins = matmul(mirror[...], reverse_ref[...])
    place = lax.axis_index("seq")
    for scale_ref, steps in zip(scale_refs, hops(places)):
        for at, step in enumerate(steps):
            scales[place ^ step] = scale_ref[pl.ds(at, 1), :]
    for rank, at in enumerate(order):
        signal[pl.ds(at * width, width), :] = (packed_ref[rank, 4].astype(F32) * scales[at]).astype(BF16)
    spectral = []
    for group in groups:
        begin = group[0] * width
        mixed = matmul(first_ref[pl.ds(2 * begin, 2 * len(group) * width), :], signal[...])
        for at, residue in enumerate(group):
            over, under = mixed[2 * at * width : (2 * at + 1) * width], mixed[(2 * at + 1) * width : (2 * at + 2) * width]
            values = []
            for turn in range(4):
                real, imag = (part[:, turn * block : (turn + 1) * block] for part in (over, under))
                cos, sin = (twist_ref[part, pl.ds(residue, 1), quarters[turn]] for part in range(2))
                values.append((real * cos + imag * sin, imag * cos - real * sin))
            for turn, (real, imag) in enumerate(butterfly(values, 1)):
                if turn > 0:
                    cos, sin = spin_ref[0, pl.ds(turn, 1), :], spin_ref[1, pl.ds(turn, 1), :]
                    real, imag = real * cos + imag * sin, imag * cos - real * sin
                row = pl.ds(4 * begin + (turn * len(group) + at) * width, width)
                forward[row, pl.ds(0, block)] = real.astype(BF16)
                forward[row, pl.ds(block, block)] = imag.astype(BF16)
        spectral.append(matmul(forward[pl.ds(4 * begin, 4 * len(group) * width), :], dft_ref[0]))
    restored = []
    for group, values in zip(groups, spectral):
        begin = group[0] * width
        for turn in range(4):
            for at, residue in enumerate(group):
                row = (turn * len(group) + at) * width
                real, imag = values[row : row + width, :block], values[row : row + width, block:]
                holder = direct[residue]
                response_real = packed_ref[holder[0], holder[1], :, quarters[turn]].astype(F32)
                response_imag = packed_ref[holder[0], 2 + holder[1], :, quarters[turn]].astype(F32)
                if mirrors[residue] is not None:
                    other = turn * inner + (residue - 1) * width
                    response_real = response_real + reversed_bins[other : other + width]
                    other = other + 4 * inner
                    response_imag = response_imag - reversed_bins[other : other + width]
                target = pl.ds(4 * begin + row, width)
                backward[target, pl.ds(0, block)] = (real * response_real - imag * response_imag).astype(BF16)
                backward[target, pl.ds(block, block)] = (real * response_imag + imag * response_real).astype(BF16)
        restored.append(matmul(backward[pl.ds(4 * begin, 4 * len(group) * width), :], dft_ref[1]))
    for group, turned in zip(groups, restored):
        for at, residue in enumerate(group):
            values = []
            for turn in range(4):
                row = (turn * len(group) + at) * width
                real, imag = turned[row : row + width, :block], turned[row : row + width, block:]
                if turn > 0:
                    cos, sin = spin_ref[0, pl.ds(turn, 1), :], spin_ref[1, pl.ds(turn, 1), :]
                    real, imag = real * cos - imag * sin, imag * cos + real * sin
                values.append((real, imag))
            for lanes, (real, imag) in zip(quarters, butterfly(values, -1)):
                cos, sin = twist_ref[0, pl.ds(residue, 1), lanes], twist_ref[1, pl.ds(residue, 1), lanes]
                both[pl.ds(2 * residue * width, width), lanes] = (real * cos - imag * sin).astype(BF16)
                both[pl.ds((2 * residue + 1) * width, width), lanes] = (imag * cos + real * sin).astype(BF16)
    result = matmul(last_ref[...], both[...]).astype(BF16)
    for rank, at in enumerate(order):
        out_ref[pl.ds(rank * width, width), :] = result[at * width : (at + 1) * width]


def convolve_kernel(packed_ref, first_ref, last_ref, twist_ref, dft_ref, scale_ref, out_ref, left, right):
    wide, rows = out_ref.shape
    half = 2 * wide
    signal = (packed_ref[4].astype(F32) * scale_ref[...]).astype(BF16)
    mixed = matmul(first_ref[...], signal)
    real, imag = mixed[:half], mixed[half:]
    cos_twist, sin_twist = twist_ref[0], twist_ref[1]
    turned_real = (real * cos_twist + imag * sin_twist).astype(BF16)
    turned_imag = (imag * cos_twist - real * sin_twist).astype(BF16)
    left[pl.ds(0, half), pl.ds(0, rows)] = turned_real
    left[pl.ds(0, half), pl.ds(rows, rows)] = turned_imag
    left[pl.ds(half, half), pl.ds(0, rows)] = turned_imag
    left[pl.ds(half, half), pl.ds(rows, rows)] = -turned_real
    mixed = matmul(left[...], dft_ref[...])
    real, imag = mixed[:half], mixed[half:]
    response_real = packed_ref[0:2].reshape(half, rows).astype(F32)
    response_imag = packed_ref[2:4].reshape(half, rows).astype(F32)
    product_real = (real * response_real - imag * response_imag).astype(BF16)
    product_imag = (real * response_imag + imag * response_real).astype(BF16)
    right[pl.ds(0, half), pl.ds(0, rows)] = product_real
    right[pl.ds(0, half), pl.ds(rows, rows)] = -product_imag
    right[pl.ds(half, half), pl.ds(0, rows)] = product_imag
    right[pl.ds(half, half), pl.ds(rows, rows)] = product_real
    mixed = matmul(right[...], dft_ref[...])
    real, imag = mixed[:half], mixed[half:]
    turned_real = (real * cos_twist - imag * sin_twist).astype(BF16)
    turned_imag = (imag * cos_twist + real * sin_twist).astype(BF16)
    both = jnp.concatenate([turned_real, turned_imag], axis=0)
    out_ref[...] = matmul(last_ref[...], both).astype(BF16)


def finish_kernel(conv_ref, skipped_ref, scale_ref, post_ref, out_ref):
    conv = conv_ref[...]
    if len(conv_ref.shape) == 3:
        order = order_of(conv_ref.shape[0])
        conv = jnp.concatenate([conv_ref[order.index(place)] for place in range(len(order))])
    turned = conv.astype(F32) + skipped_ref[...].astype(F32) * scale_ref[...]
    out_ref[...] = (post_ref[...].astype(F32) * turned.T).astype(BF16)


def call(kernel, out_shape, flops, moved, *operands, limit=VMEM_LIMIT, **options):
    return pl.pallas_call(
        kernel,
        out_shape=out_shape,
        compiler_params=pltpu.CompilerParams(vmem_limit_bytes=limit),
        cost_estimate=pl.CostEstimate(flops=flops, bytes_accessed=moved, transcendentals=0),
        **options,
    )(*operands)


def exchange(value):
    ranks = [list(order_of(lax.axis_size("seq")))]
    return lax.all_to_all(value, "seq", split_axis=0, concat_axis=0, tiled=True, axis_index_groups=ranks)


def swap(value, axis, apart):
    return lax.ppermute(value, axis, [(place, place ^ apart) for place in range(lax.axis_size(axis))])


def local(features, pre_gate, post_gate, norm_gain, skip_weight, spectrum):
    rows, wide = features.shape
    places = lax.axis_size("seq")
    groups = lax.axis_size("chan")
    width = wide // places
    piled = width % 16 == 0
    cells = rows * wide
    shape = jax.ShapeDtypeStruct
    vmem, anywhere = pl.BlockSpec(memory_space=pltpu.VMEM), pl.BlockSpec(memory_space=pl.ANY)
    squares, skipped, packed = call(
        prepare_kernel,
        (
            shape((1, rows), F32),
            shape((wide, rows), BF16),
            shape((places, 5, width, rows) if piled else (5, wide, rows), BF16),
        ),
        10 * cells,
        32 * cells,
        features,
        pre_gate,
        norm_gain[None, :],
        skip_weight[None, :],
        spectrum,
        limit=WHOLE_VMEM,
        in_specs=[anywhere] * 5,
        out_specs=(anywhere, anywhere, anywhere),
        scratch_shapes=[
            pltpu.VMEM(features.shape, BF16),
            pltpu.VMEM(pre_gate.shape, BF16),
            pltpu.VMEM((1, wide), F32),
            pltpu.VMEM((1, wide), F32),
            pltpu.VMEM(spectrum.shape, F32),
            pltpu.VMEM((1, rows), F32),
            pltpu.VMEM((wide, rows), BF16),
            pltpu.VMEM((5, places, width, rows) if piled else (5, wide, rows), BF16),
            pltpu.SemaphoreType.DMA((8,)),
            pltpu.SemaphoreType.DMA((7,)),
        ],
    )
    if not piled:
        packed = packed.reshape(5, places, width, rows).transpose(1, 0, 2, 3)
    gathered = exchange(packed)
    others = [swap(squares, "chan", apart) for apart in range(1, groups)]
    scale = call(
        functools.partial(scale_kernel, wide * groups), shape((1, rows), F32), 8 * rows, 32 * rows, squares, *others
    )
    if piled:
        near = jnp.concatenate([scale, swap(scale, "seq", 1)])
        scales = [near] + [swap(near, "seq", steps[0]) for steps in hops(places)[1:]]
    else:
        scales = [jnp.repeat(lax.all_gather(scale, "seq", axis=0, tiled=True), width, axis=0)]
        response = gathered[:, :4].reshape(places, 2, 2, width, rows).transpose(1, 0, 2, 3, 4)
        gathered = jnp.concatenate([response.reshape(4, wide, rows), gathered[:, 4].reshape(1, wide, rows)])
    if piled:
        constants = folded_tables(places, rows, width)
        half = constants[0].shape[0] // 2
        scratch = [
            pltpu.VMEM((places, 1, rows), F32),
            pltpu.VMEM((wide, rows), BF16),
            pltpu.VMEM((8 * (half - 2 * width), rows // 4), BF16),
            pltpu.VMEM((4 * half, rows // 2), BF16),
            pltpu.VMEM((4 * half, rows // 2), BF16),
            pltpu.VMEM((2 * half, rows), BF16),
        ]
    else:
        constants = tables(places, rows, width)
        scratch = [pltpu.VMEM((4 * wide, 2 * rows), BF16)] * 2
    conv = call(
        folded_kernel if piled else convolve_kernel,
        shape((wide, rows), BF16),
        20 * cells * rows,
        20 * cells,
        gathered,
        *constants,
        *scales,
        scratch_shapes=scratch,
    )
    conv = exchange(conv.reshape(places, width, rows))
    if not piled:
        conv = conv.reshape(wide, rows)
    return call(finish_kernel, shape((rows, wide), BF16), 10 * cells, 8 * cells, conv, skipped, scale, post_gate)


def solution(mesh):
    return jax.shard_map(
        local,
        mesh=mesh,
        in_specs=(
            P("seq", "chan"),
            P("seq", "chan"),
            P("seq", "chan"),
            P("chan"),
            P("chan"),
            P(None, "seq", None, "chan"),
        ),
        out_specs=P("seq", "chan"),
        check_vma=False,
    )
```

```python
import functools

import jax
import jax.numpy as jnp
import numpy as np
from jax import lax
from jax.experimental import pallas as pl
from jax.experimental.pallas import tpu as pltpu
from jax.sharding import PartitionSpec as P

EPS = 1e-06
BF16 = jnp.bfloat16
F32 = jnp.float32
VMEM_LIMIT = 48 * 1024 * 1024
WHOLE_VMEM = 63 * 1024 * 1024 + 512 * 1024


def order_of(places, back=False):
    if places != 8:
        return tuple(range(places))
    return (2, 1, 7, 4, 3, 0, 6, 5) if back else (5, 2, 1, 7, 4, 3, 0, 6)


def reverse_bits(index, levels):
    return sum((index >> bit & 1) << levels - 1 - bit for bit in range(levels))


@functools.lru_cache(maxsize=None)
def tables(places, rows, width):
    levels = places.bit_length() - 1
    stride = 2 * places
    bins = stride * rows
    residues = np.array([2 * reverse_bits(place, levels) + parity for place in range(places) for parity in range(2)])
    angle = 2.0 * np.pi * ((residues[:, None] * np.arange(places)[None, :]) % stride) / stride
    same = np.eye(width)
    first = np.concatenate([np.kron(np.cos(angle), same), np.kron(-np.sin(angle), same)])
    last = first.T / bins
    angle = 2.0 * np.pi * ((residues[:, None] * np.arange(rows)[None, :]) % bins) / bins
    twist = np.repeat(np.stack([np.cos(angle), np.sin(angle)]), width, axis=1)
    series = np.arange(rows)
    angle = 2.0 * np.pi * ((series[:, None] * series[None, :]) % rows) / rows
    dft = np.concatenate([np.cos(angle), np.sin(angle)])
    return (
        first.astype(jnp.bfloat16),
        last.astype(jnp.bfloat16),
        twist.astype(np.float32),
        dft.astype(jnp.bfloat16),
    )


def pair_rows(places):
    levels = places.bit_length() - 1

    def holder(residue):
        return order_of(places).index(reverse_bits(residue // 2, levels)), residue % 2

    mirrors = [None if residue % places == 0 else holder(2 * places - residue) for residue in range(places + 1)]
    return [holder(residue) for residue in range(places + 1)], mirrors


@functools.lru_cache(maxsize=None)
def folded_tables(places, rows, width):
    stride = 2 * places
    bins = stride * rows
    residues = np.arange(places + 1)
    angle = 2.0 * np.pi * ((residues[:, None] * np.arange(places)[None, :]) % stride) / stride
    parts = np.stack([np.cos(angle), -np.sin(angle)], axis=1)
    first = np.kron(parts.reshape(-1, places), np.eye(width))
    last = first.T / bins
    angle = 2.0 * np.pi * ((residues[:, None] * np.arange(rows)[None, :]) % bins) / bins
    twist = np.stack([np.cos(angle), np.sin(angle)])
    block = rows // 4
    series = np.arange(block)
    angle = 2.0 * np.pi * ((np.arange(4)[:, None] * series[None, :]) % rows) / rows
    spin = np.stack([np.cos(angle), np.sin(angle)])
    angle = 2.0 * np.pi * ((series[:, None] * series[None, :]) % block) / block
    cos, sin = np.cos(angle), np.sin(angle)
    there = np.block([[cos, -sin], [sin, cos]])
    back = np.block([[cos, sin], [-sin, cos]])
    reverse = np.eye(block)[::-1]
    return (
        first.astype(jnp.bfloat16),
        last.astype(jnp.bfloat16),
        twist.astype(np.float32),
        spin.astype(np.float32),
        np.stack([there, back]).astype(jnp.bfloat16),
        reverse.astype(jnp.bfloat16),
    )


def hops(places):
    return [[apart, apart + 1] for apart in range(0, places, 2)]


def prepare_kernel(
    features_ref,
    pre_ref,
    gain_ref,
    skip_ref,
    spectrum_ref,
    squares_ref,
    skipped_ref,
    packed_ref,
    features_in,
    pre_in,
    gain_in,
    skip_in,
    spectrum_in,
    squares_out,
    skipped_out,
    packed_out,
    in_sems,
    out_sems,
):
    blocks = [(part, parity) for part in range(2) for parity in range(2)]
    pairs = [(features_ref, features_in), (pre_ref, pre_in), (gain_ref, gain_in), (skip_ref, skip_in)]
    pairs += [(spectrum_ref.at[block], spectrum_in.at[block]) for block in blocks]
    arriving = [pltpu.make_async_copy(*pair, in_sems.at[slot]) for slot, pair in enumerate(pairs)]
    for copy in arriving:
        copy.start()
    leaving = []

    def leave(source, target):
        copy = pltpu.make_async_copy(source, target, out_sems.at[len(leaving)])
        copy.start()
        leaving.append(copy)

    def pack(slot, turned):
        if len(packed_ref.shape) == 4:
            places, width = packed_out.shape[1:3]
            for rank, place in enumerate(order_of(places)):
                packed_out[slot, rank] = turned[place * width : (place + 1) * width]
            leave(packed_out.at[slot], packed_ref.at[:, slot])
        else:
            packed_out[slot] = turned
            leave(packed_out.at[slot], packed_ref.at[slot])

    for copy in arriving[:4]:
        copy.wait()
    features = features_in[...].astype(F32)
    scaled = features * gain_in[...] * pre_in[...].astype(F32)
    pack(4, scaled.astype(BF16).T)
    skipped_out[...] = (scaled * skip_in[...]).astype(BF16).T
    leave(skipped_out, skipped_ref)
    turned = features_in[...].T.astype(F32)
    squares_out[...] = jnp.sum(turned * turned, axis=0, keepdims=True)
    leave(squares_out, squares_ref)
    for slot, block in enumerate(blocks):
        arriving[4 + slot].wait()
        if len(packed_ref.shape) == 4:
            quarter = spectrum_in.shape[2] // 4
            rows = [spectrum_in[(*block, pl.ds(turn, quarter, stride=4), slice(None))] for turn in range(4)]
            pack(slot, jnp.concatenate([row.astype(BF16).T for row in rows], axis=1))
        else:
            pack(slot, spectrum_in[block].astype(BF16).T)
    for copy in leaving:
        copy.wait()


def scale_kernel(channels, *refs):
    square_refs, scale_ref = refs[:-1], refs[-1]
    total = square_refs[0][...]
    for square_ref in square_refs[1:]:
        total = total + square_ref[...]
    scale_ref[...] = lax.rsqrt(total / channels + EPS)


def matmul(left, right):
    return jnp.dot(left, right, preferred_element_type=F32)


def butterfly(values, direction):
    (real0, imag0), (real1, imag1), (real2, imag2), (real3, imag3) = values
    even, odd = (real0 + real2, imag0 + imag2), (real1 + real3, imag1 + imag3)
    even_gap, odd_gap = (real0 - real2, imag0 - imag2), (real1 - real3, imag1 - imag3)
    lower = (even_gap[0] + odd_gap[1], even_gap[1] - odd_gap[0])
    upper = (even_gap[0] - odd_gap[1], even_gap[1] + odd_gap[0])
    total, gap = (even[0] + odd[0], even[1] + odd[1]), (even[0] - odd[0], even[1] - odd[1])
    return [total, lower, gap, upper] if direction > 0 else [total, upper, gap, lower]


def folded_kernel(packed_ref, first_ref, last_ref, twist_ref, spin_ref, dft_ref, reverse_ref, *refs):
    scale_refs, (out_ref, scales, signal, mirror, forward, backward, both) = refs[:-7], refs[-7:]
    wide, rows = out_ref.shape
    places, width = scales.shape[0], wide // scales.shape[0]
    block, inner = rows // 4, mirror.shape[0] // 8
    order = order_of(places)
    direct, mirrors = pair_rows(places)
    quarters = [pl.ds(turn * block, block) for turn in range(4)]
    groups = [range(begin, min(begin + 3, places + 1)) for begin in range(0, places + 1, 3)]
    for row, holder in enumerate(mirrors[1:places]):
        for part in range(2):
            for turn in range(4):
                at = pl.ds((part * 4 + 3 - turn) * inner + row * width, width)
                mirror[at, :] = packed_ref[holder[0], 2 * part + holder[1], :, quarters[turn]]
    reversed_bins = matmul(mirror[...], reverse_ref[...])
    place = lax.axis_index("seq")
    for scale_ref, steps in zip(scale_refs, hops(places)):
        for at, step in enumerate(steps):
            scales[place ^ step] = scale_ref[pl.ds(at, 1), :]
    for rank, at in enumerate(order):
        signal[pl.ds(at * width, width), :] = (packed_ref[rank, 4].astype(F32) * scales[at]).astype(BF16)
    spectral = []
    for group in groups:
        begin = group[0] * width
        mixed = matmul(first_ref[pl.ds(2 * begin, 2 * len(group) * width), :], signal[...])
        for at, residue in enumerate(group):
            over, under = mixed[2 * at * width : (2 * at + 1) * width], mixed[(2 * at + 1) * width : (2 * at + 2) * width]
            values = []
            for turn in range(4):
                real, imag = (part[:, turn * block : (turn + 1) * block] for part in (over, under))
                cos, sin = (twist_ref[part, pl.ds(residue, 1), quarters[turn]] for part in range(2))
                values.append((real * cos + imag * sin, imag * cos - real * sin))
            for turn, (real, imag) in enumerate(butterfly(values, 1)):
                if turn > 0:
                    cos, sin = spin_ref[0, pl.ds(turn, 1), :], spin_ref[1, pl.ds(turn, 1), :]
                    real, imag = real * cos + imag * sin, imag * cos - real * sin
                row = pl.ds(4 * begin + (turn * len(group) + at) * width, width)
                forward[row, pl.ds(0, block)] = real.astype(BF16)
                forward[row, pl.ds(block, block)] = imag.astype(BF16)
        spectral.append(matmul(forward[pl.ds(4 * begin, 4 * len(group) * width), :], dft_ref[0]))
    restored = []
    for group, values in zip(groups, spectral):
        begin = group[0] * width
        for turn in range(4):
            for at, residue in enumerate(group):
                row = (turn * len(group) + at) * width
                real, imag = values[row : row + width, :block], values[row : row + width, block:]
                holder = direct[residue]
                response_real = packed_ref[holder[0], holder[1], :, quarters[turn]].astype(F32)
                response_imag = packed_ref[holder[0], 2 + holder[1], :, quarters[turn]].astype(F32)
                if mirrors[residue] is not None:
                    other = turn * inner + (residue - 1) * width
                    response_real = response_real + reversed_bins[other : other + width]
                    other = other + 4 * inner
                    response_imag = response_imag - reversed_bins[other : other + width]
                target = pl.ds(4 * begin + row, width)
                backward[target, pl.ds(0, block)] = (real * response_real - imag * response_imag).astype(BF16)
                backward[target, pl.ds(block, block)] = (real * response_imag + imag * response_real).astype(BF16)
        restored.append(matmul(backward[pl.ds(4 * begin, 4 * len(group) * width), :], dft_ref[1]))
    for group, turned in zip(groups, restored):
        for at, residue in enumerate(group):
            values = []
            for turn in range(4):
                row = (turn * len(group) + at) * width
                real, imag = turned[row : row + width, :block], turned[row : row + width, block:]
                if turn > 0:
                    cos, sin = spin_ref[0, pl.ds(turn, 1), :], spin_ref[1, pl.ds(turn, 1), :]
                    real, imag = real * cos - imag * sin, imag * cos + real * sin
                values.append((real, imag))
            for lanes, (real, imag) in zip(quarters, butterfly(values, -1)):
                cos, sin = twist_ref[0, pl.ds(residue, 1), lanes], twist_ref[1, pl.ds(residue, 1), lanes]
                both[pl.ds(2 * residue * width, width), lanes] = (real * cos - imag * sin).astype(BF16)
                both[pl.ds((2 * residue + 1) * width, width), lanes] = (imag * cos + real * sin).astype(BF16)
    result = matmul(last_ref[...], both[...]).astype(BF16)
    for rank, at in enumerate(order_of(places, back=True)):
        out_ref[pl.ds(rank * width, width), :] = result[at * width : (at + 1) * width]


def convolve_kernel(packed_ref, first_ref, last_ref, twist_ref, dft_ref, scale_ref, out_ref, left, right):
    wide, rows = out_ref.shape
    half = 2 * wide
    signal = (packed_ref[4].astype(F32) * scale_ref[...]).astype(BF16)
    mixed = matmul(first_ref[...], signal)
    real, imag = mixed[:half], mixed[half:]
    cos_twist, sin_twist = twist_ref[0], twist_ref[1]
    turned_real = (real * cos_twist + imag * sin_twist).astype(BF16)
    turned_imag = (imag * cos_twist - real * sin_twist).astype(BF16)
    left[pl.ds(0, half), pl.ds(0, rows)] = turned_real
    left[pl.ds(0, half), pl.ds(rows, rows)] = turned_imag
    left[pl.ds(half, half), pl.ds(0, rows)] = turned_imag
    left[pl.ds(half, half), pl.ds(rows, rows)] = -turned_real
    mixed = matmul(left[...], dft_ref[...])
    real, imag = mixed[:half], mixed[half:]
    response_real = packed_ref[0:2].reshape(half, rows).astype(F32)
    response_imag = packed_ref[2:4].reshape(half, rows).astype(F32)
    product_real = (real * response_real - imag * response_imag).astype(BF16)
    product_imag = (real * response_imag + imag * response_real).astype(BF16)
    right[pl.ds(0, half), pl.ds(0, rows)] = product_real
    right[pl.ds(0, half), pl.ds(rows, rows)] = -product_imag
    right[pl.ds(half, half), pl.ds(0, rows)] = product_imag
    right[pl.ds(half, half), pl.ds(rows, rows)] = product_real
    mixed = matmul(right[...], dft_ref[...])
    real, imag = mixed[:half], mixed[half:]
    turned_real = (real * cos_twist - imag * sin_twist).astype(BF16)
    turned_imag = (imag * cos_twist + real * sin_twist).astype(BF16)
    both = jnp.concatenate([turned_real, turned_imag], axis=0)
    out_ref[...] = matmul(last_ref[...], both).astype(BF16)


def finish_kernel(conv_ref, skipped_ref, scale_ref, post_ref, out_ref):
    conv = conv_ref[...]
    if len(conv_ref.shape) == 3:
        order = order_of(conv_ref.shape[0], back=True)
        conv = jnp.concatenate([conv_ref[order.index(place)] for place in range(len(order))])
    turned = conv.astype(F32) + skipped_ref[...].astype(F32) * scale_ref[...]
    out_ref[...] = (post_ref[...].astype(F32) * turned.T).astype(BF16)


def call(kernel, out_shape, flops, moved, *operands, limit=VMEM_LIMIT, **options):
    return pl.pallas_call(
        kernel,
        out_shape=out_shape,
        compiler_params=pltpu.CompilerParams(vmem_limit_bytes=limit),
        cost_estimate=pl.CostEstimate(flops=flops, bytes_accessed=moved, transcendentals=0),
        **options,
    )(*operands)


def exchange(value, back=False):
    ranks = [list(order_of(lax.axis_size("seq"), back))]
    return lax.all_to_all(value, "seq", split_axis=0, concat_axis=0, tiled=True, axis_index_groups=ranks)


def swap(value, axis, apart):
    return lax.ppermute(value, axis, [(place, place ^ apart) for place in range(lax.axis_size(axis))])


def local(features, pre_gate, post_gate, norm_gain, skip_weight, spectrum):
    rows, wide = features.shape
    places = lax.axis_size("seq")
    groups = lax.axis_size("chan")
    width = wide // places
    piled = width % 16 == 0
    cells = rows * wide
    shape = jax.ShapeDtypeStruct
    vmem, anywhere = pl.BlockSpec(memory_space=pltpu.VMEM), pl.BlockSpec(memory_space=pl.ANY)
    squares, skipped, packed = call(
        prepare_kernel,
        (
            shape((1, rows), F32),
            shape((wide, rows), BF16),
            shape((places, 5, width, rows) if piled else (5, wide, rows), BF16),
        ),
        10 * cells,
        32 * cells,
        features,
        pre_gate,
        norm_gain[None, :],
        skip_weight[None, :],
        spectrum,
        limit=WHOLE_VMEM,
        in_specs=[anywhere] * 5,
        out_specs=(anywhere, anywhere, anywhere),
        scratch_shapes=[
            pltpu.VMEM(features.shape, BF16),
            pltpu.VMEM(pre_gate.shape, BF16),
            pltpu.VMEM((1, wide), F32),
            pltpu.VMEM((1, wide), F32),
            pltpu.VMEM(spectrum.shape, F32),
            pltpu.VMEM((1, rows), F32),
            pltpu.VMEM((wide, rows), BF16),
            pltpu.VMEM((5, places, width, rows) if piled else (5, wide, rows), BF16),
            pltpu.SemaphoreType.DMA((8,)),
            pltpu.SemaphoreType.DMA((7,)),
        ],
    )
    if not piled:
        packed = packed.reshape(5, places, width, rows).transpose(1, 0, 2, 3)
    gathered = exchange(packed)
    others = [swap(squares, "chan", apart) for apart in range(1, groups)]
    scale = call(
        functools.partial(scale_kernel, wide * groups), shape((1, rows), F32), 8 * rows, 32 * rows, squares, *others
    )
    if piled:
        near = jnp.concatenate([scale, swap(scale, "seq", 1)])
        scales = [near] + [swap(near, "seq", steps[0]) for steps in hops(places)[1:]]
    else:
        scales = [jnp.repeat(lax.all_gather(scale, "seq", axis=0, tiled=True), width, axis=0)]
        response = gathered[:, :4].reshape(places, 2, 2, width, rows).transpose(1, 0, 2, 3, 4)
        gathered = jnp.concatenate([response.reshape(4, wide, rows), gathered[:, 4].reshape(1, wide, rows)])
    if piled:
        constants = folded_tables(places, rows, width)
        half = constants[0].shape[0] // 2
        scratch = [
            pltpu.VMEM((places, 1, rows), F32),
            pltpu.VMEM((wide, rows), BF16),
            pltpu.VMEM((8 * (half - 2 * width), rows // 4), BF16),
            pltpu.VMEM((4 * half, rows // 2), BF16),
            pltpu.VMEM((4 * half, rows // 2), BF16),
            pltpu.VMEM((2 * half, rows), BF16),
        ]
    else:
        constants = tables(places, rows, width)
        scratch = [pltpu.VMEM((4 * wide, 2 * rows), BF16)] * 2
    conv = call(
        folded_kernel if piled else convolve_kernel,
        shape((wide, rows), BF16),
        20 * cells * rows,
        20 * cells,
        gathered,
        *constants,
        *scales,
        scratch_shapes=scratch,
    )
    conv = exchange(conv.reshape(places, width, rows), back=True)
    if not piled:
        conv = conv.reshape(wide, rows)
    return call(finish_kernel, shape((rows, wide), BF16), 10 * cells, 8 * cells, conv, skipped, scale, post_gate)


def solution(mesh):
    return jax.shard_map(
        local,
        mesh=mesh,
        in_specs=(
            P("seq", "chan"),
            P("seq", "chan"),
            P("seq", "chan"),
            P("chan"),
            P("chan"),
            P(None, "seq", None, "chan"),
        ),
        out_specs=P("seq", "chan"),
        check_vma=False,
    )
```

```python
import functools

import jax
import jax.numpy as jnp
import numpy as np
from jax import lax
from jax.experimental import pallas as pl
from jax.experimental.pallas import tpu as pltpu
from jax.sharding import PartitionSpec as P

EPS = 1e-06
BF16 = jnp.bfloat16
F32 = jnp.float32
VMEM_LIMIT = 48 * 1024 * 1024
WHOLE_VMEM = 63 * 1024 * 1024 + 512 * 1024


def order_of(places):
    return (4, 7, 1, 2, 5, 6, 0, 3) if places == 8 else tuple(range(places))


def reverse_bits(index, levels):
    return sum((index >> bit & 1) << levels - 1 - bit for bit in range(levels))


@functools.lru_cache(maxsize=None)
def tables(places, rows, width):
    levels = places.bit_length() - 1
    stride = 2 * places
    bins = stride * rows
    residues = np.array([2 * reverse_bits(place, levels) + parity for place in range(places) for parity in range(2)])
    angle = 2.0 * np.pi * ((residues[:, None] * np.arange(places)[None, :]) % stride) / stride
    same = np.eye(width)
    first = np.concatenate([np.kron(np.cos(angle), same), np.kron(-np.sin(angle), same)])
    last = first.T / bins
    angle = 2.0 * np.pi * ((residues[:, None] * np.arange(rows)[None, :]) % bins) / bins
    twist = np.repeat(np.stack([np.cos(angle), np.sin(angle)]), width, axis=1)
    series = np.arange(rows)
    angle = 2.0 * np.pi * ((series[:, None] * series[None, :]) % rows) / rows
    dft = np.concatenate([np.cos(angle), np.sin(angle)])
    return (
        first.astype(jnp.bfloat16),
        last.astype(jnp.bfloat16),
        twist.astype(np.float32),
        dft.astype(jnp.bfloat16),
    )


def pair_rows(places):
    levels = places.bit_length() - 1

    def holder(residue):
        return order_of(places).index(reverse_bits(residue // 2, levels)), residue % 2

    mirrors = [None if residue % places == 0 else holder(2 * places - residue) for residue in range(places + 1)]
    return [holder(residue) for residue in range(places + 1)], mirrors


@functools.lru_cache(maxsize=None)
def folded_tables(places, rows, width):
    stride = 2 * places
    bins = stride * rows
    residues = np.arange(places + 1)
    angle = 2.0 * np.pi * ((residues[:, None] * np.arange(places)[None, :]) % stride) / stride
    parts = np.stack([np.cos(angle), -np.sin(angle)], axis=1)
    first = np.kron(parts.reshape(-1, places), np.eye(width))
    last = first.T / bins
    angle = 2.0 * np.pi * ((residues[:, None] * np.arange(rows)[None, :]) % bins) / bins
    twist = np.stack([np.cos(angle), np.sin(angle)])
    block = rows // 4
    series = np.arange(block)
    angle = 2.0 * np.pi * ((np.arange(4)[:, None] * series[None, :]) % rows) / rows
    spin = np.stack([np.cos(angle), np.sin(angle)])
    angle = 2.0 * np.pi * ((series[:, None] * series[None, :]) % block) / block
    cos, sin = np.cos(angle), np.sin(angle)
    there = np.block([[cos, -sin], [sin, cos]])
    back = np.block([[cos, sin], [-sin, cos]])
    reverse = np.eye(block)[::-1]
    return (
        first.astype(jnp.bfloat16),
        last.astype(jnp.bfloat16),
        twist.astype(np.float32),
        spin.astype(np.float32),
        np.stack([there, back]).astype(jnp.bfloat16),
        reverse.astype(jnp.bfloat16),
    )


def hops(places):
    return [[apart, apart + 1] for apart in range(0, places, 2)]


def prepare_kernel(
    features_ref,
    pre_ref,
    gain_ref,
    skip_ref,
    spectrum_ref,
    squares_ref,
    skipped_ref,
    packed_ref,
    features_in,
    pre_in,
    gain_in,
    skip_in,
    spectrum_in,
    squares_out,
    skipped_out,
    packed_out,
    in_sems,
    out_sems,
):
    blocks = [(part, parity) for part in range(2) for parity in range(2)]
    pairs = [(features_ref, features_in), (pre_ref, pre_in), (gain_ref, gain_in), (skip_ref, skip_in)]
    pairs += [(spectrum_ref.at[block], spectrum_in.at[block]) for block in blocks]
    arriving = [pltpu.make_async_copy(*pair, in_sems.at[slot]) for slot, pair in enumerate(pairs)]
    for copy in arriving:
        copy.start()
    leaving = []

    def leave(source, target):
        copy = pltpu.make_async_copy(source, target, out_sems.at[len(leaving)])
        copy.start()
        leaving.append(copy)

    def pack(slot, turned):
        if len(packed_ref.shape) == 4:
            places, width = packed_out.shape[1:3]
            for rank, place in enumerate(order_of(places)):
                packed_out[slot, rank] = turned[place * width : (place + 1) * width]
            leave(packed_out.at[slot], packed_ref.at[:, slot])
        else:
            packed_out[slot] = turned
            leave(packed_out.at[slot], packed_ref.at[slot])

    for copy in arriving[:4]:
        copy.wait()
    features = features_in[...].astype(F32)
    scaled = features * gain_in[...] * pre_in[...].astype(F32)
    pack(4, scaled.astype(BF16).T)
    skipped_out[...] = (scaled * skip_in[...]).astype(BF16).T
    leave(skipped_out, skipped_ref)
    turned = features_in[...].T.astype(F32)
    squares_out[...] = jnp.sum(turned * turned, axis=0, keepdims=True)
    leave(squares_out, squares_ref)
    for slot, block in enumerate(blocks):
        arriving[4 + slot].wait()
        if len(packed_ref.shape) == 4:
            quarter = spectrum_in.shape[2] // 4
            rows = [spectrum_in[(*block, pl.ds(turn, quarter, stride=4), slice(None))] for turn in range(4)]
            pack(slot, jnp.concatenate([row.astype(BF16).T for row in rows], axis=1))
        else:
            pack(slot, spectrum_in[block].astype(BF16).T)
    for copy in leaving:
        copy.wait()


def scale_kernel(channels, *refs):
    square_refs, scale_ref = refs[:-1], refs[-1]
    total = square_refs[0][...]
    for square_ref in square_refs[1:]:
        total = total + square_ref[...]
    scale_ref[...] = lax.rsqrt(total / channels + EPS)


def matmul(left, right):
    return jnp.dot(left, right, preferred_element_type=F32)


def butterfly(values, direction):
    (real0, imag0), (real1, imag1), (real2, imag2), (real3, imag3) = values
    even, odd = (real0 + real2, imag0 + imag2), (real1 + real3, imag1 + imag3)
    even_gap, odd_gap = (real0 - real2, imag0 - imag2), (real1 - real3, imag1 - imag3)
    lower = (even_gap[0] + odd_gap[1], even_gap[1] - odd_gap[0])
    upper = (even_gap[0] - odd_gap[1], even_gap[1] + odd_gap[0])
    total, gap = (even[0] + odd[0], even[1] + odd[1]), (even[0] - odd[0], even[1] - odd[1])
    return [total, lower, gap, upper] if direction > 0 else [total, upper, gap, lower]


def folded_kernel(packed_ref, first_ref, last_ref, twist_ref, spin_ref, dft_ref, reverse_ref, *refs):
    scale_refs, (out_ref, scales, signal, mirror, forward, backward, both) = refs[:-7], refs[-7:]
    wide, rows = out_ref.shape
    places, width = scales.shape[0], wide // scales.shape[0]
    block, inner = rows // 4, mirror.shape[0] // 8
    order = order_of(places)
    direct, mirrors = pair_rows(places)
    quarters = [pl.ds(turn * block, block) for turn in range(4)]
    groups = [range(begin, min(begin + 3, places + 1)) for begin in range(0, places + 1, 3)]
    for row, holder in enumerate(mirrors[1:places]):
        for part in range(2):
            for turn in range(4):
                at = pl.ds((part * 4 + 3 - turn) * inner + row * width, width)
                mirror[at, :] = packed_ref[holder[0], 2 * part + holder[1], :, quarters[turn]]
    reversed_bins = matmul(mirror[...], reverse_ref[...])
    place = lax.axis_index("seq")
    for scale_ref, steps in zip(scale_refs, hops(places)):
        for at, step in enumerate(steps):
            scales[place ^ step] = scale_ref[pl.ds(at, 1), :]
    for rank, at in enumerate(order):
        signal[pl.ds(at * width, width), :] = (packed_ref[rank, 4].astype(F32) * scales[at]).astype(BF16)
    spectral = []
    for group in groups:
        begin = group[0] * width
        mixed = matmul(first_ref[pl.ds(2 * begin, 2 * len(group) * width), :], signal[...])
        for at, residue in enumerate(group):
            over, under = mixed[2 * at * width : (2 * at + 1) * width], mixed[(2 * at + 1) * width : (2 * at + 2) * width]
            values = []
            for turn in range(4):
                real, imag = (part[:, turn * block : (turn + 1) * block] for part in (over, under))
                cos, sin = (twist_ref[part, pl.ds(residue, 1), quarters[turn]] for part in range(2))
                values.append((real * cos + imag * sin, imag * cos - real * sin))
            for turn, (real, imag) in enumerate(butterfly(values, 1)):
                if turn > 0:
                    cos, sin = spin_ref[0, pl.ds(turn, 1), :], spin_ref[1, pl.ds(turn, 1), :]
                    real, imag = real * cos + imag * sin, imag * cos - real * sin
                row = pl.ds(4 * begin + (turn * len(group) + at) * width, width)
                forward[row, pl.ds(0, block)] = real.astype(BF16)
                forward[row, pl.ds(block, block)] = imag.astype(BF16)
        spectral.append(matmul(forward[pl.ds(4 * begin, 4 * len(group) * width), :], dft_ref[0]))
    restored = []
    for group, values in zip(groups, spectral):
        begin = group[0] * width
        for turn in range(4):
            for at, residue in enumerate(group):
                row = (turn * len(group) + at) * width
                real, imag = values[row : row + width, :block], values[row : row + width, block:]
                holder = direct[residue]
                response_real = packed_ref[holder[0], holder[1], :, quarters[turn]].astype(F32)
                response_imag = packed_ref[holder[0], 2 + holder[1], :, quarters[turn]].astype(F32)
                if mirrors[residue] is not None:
                    other = turn * inner + (residue - 1) * width
                    response_real = response_real + reversed_bins[other : other + width]
                    other = other + 4 * inner
                    response_imag = response_imag - reversed_bins[other : other + width]
                target = pl.ds(4 * begin + row, width)
                backward[target, pl.ds(0, block)] = (real * response_real - imag * response_imag).astype(BF16)
                backward[target, pl.ds(block, block)] = (real * response_imag + imag * response_real).astype(BF16)
        restored.append(matmul(backward[pl.ds(4 * begin, 4 * len(group) * width), :], dft_ref[1]))
    for group, turned in zip(groups, restored):
        for at, residue in enumerate(group):
            values = []
            for turn in range(4):
                row = (turn * len(group) + at) * width
                real, imag = turned[row : row + width, :block], turned[row : row + width, block:]
                if turn > 0:
                    cos, sin = spin_ref[0, pl.ds(turn, 1), :], spin_ref[1, pl.ds(turn, 1), :]
                    real, imag = real * cos - imag * sin, imag * cos + real * sin
                values.append((real, imag))
            for lanes, (real, imag) in zip(quarters, butterfly(values, -1)):
                cos, sin = twist_ref[0, pl.ds(residue, 1), lanes], twist_ref[1, pl.ds(residue, 1), lanes]
                both[pl.ds(2 * residue * width, width), lanes] = (real * cos - imag * sin).astype(BF16)
                both[pl.ds((2 * residue + 1) * width, width), lanes] = (imag * cos + real * sin).astype(BF16)
    result = matmul(last_ref[...], both[...]).astype(BF16)
    for rank, at in enumerate(order):
        out_ref[pl.ds(rank * width, width), :] = result[at * width : (at + 1) * width]


def convolve_kernel(packed_ref, first_ref, last_ref, twist_ref, dft_ref, scale_ref, out_ref, left, right):
    wide, rows = out_ref.shape
    half = 2 * wide
    signal = (packed_ref[4].astype(F32) * scale_ref[...]).astype(BF16)
    mixed = matmul(first_ref[...], signal)
    real, imag = mixed[:half], mixed[half:]
    cos_twist, sin_twist = twist_ref[0], twist_ref[1]
    turned_real = (real * cos_twist + imag * sin_twist).astype(BF16)
    turned_imag = (imag * cos_twist - real * sin_twist).astype(BF16)
    left[pl.ds(0, half), pl.ds(0, rows)] = turned_real
    left[pl.ds(0, half), pl.ds(rows, rows)] = turned_imag
    left[pl.ds(half, half), pl.ds(0, rows)] = turned_imag
    left[pl.ds(half, half), pl.ds(rows, rows)] = -turned_real
    mixed = matmul(left[...], dft_ref[...])
    real, imag = mixed[:half], mixed[half:]
    response_real = packed_ref[0:2].reshape(half, rows).astype(F32)
    response_imag = packed_ref[2:4].reshape(half, rows).astype(F32)
    product_real = (real * response_real - imag * response_imag).astype(BF16)
    product_imag = (real * response_imag + imag * response_real).astype(BF16)
    right[pl.ds(0, half), pl.ds(0, rows)] = product_real
    right[pl.ds(0, half), pl.ds(rows, rows)] = -product_imag
    right[pl.ds(half, half), pl.ds(0, rows)] = product_imag
    right[pl.ds(half, half), pl.ds(rows, rows)] = product_real
    mixed = matmul(right[...], dft_ref[...])
    real, imag = mixed[:half], mixed[half:]
    turned_real = (real * cos_twist - imag * sin_twist).astype(BF16)
    turned_imag = (imag * cos_twist + real * sin_twist).astype(BF16)
    both = jnp.concatenate([turned_real, turned_imag], axis=0)
    out_ref[...] = matmul(last_ref[...], both).astype(BF16)


def finish_kernel(conv_ref, skipped_ref, scale_ref, post_ref, out_ref):
    conv = conv_ref[...]
    if len(conv_ref.shape) == 3:
        order = order_of(conv_ref.shape[0])
        conv = jnp.concatenate([conv_ref[order.index(place)] for place in range(len(order))])
    turned = conv.astype(F32) + skipped_ref[...].astype(F32) * scale_ref[...]
    out_ref[...] = (post_ref[...].astype(F32) * turned.T).astype(BF16)


def call(kernel, out_shape, flops, moved, *operands, limit=VMEM_LIMIT, **options):
    return pl.pallas_call(
        kernel,
        out_shape=out_shape,
        compiler_params=pltpu.CompilerParams(vmem_limit_bytes=limit),
        cost_estimate=pl.CostEstimate(flops=flops, bytes_accessed=moved, transcendentals=0),
        **options,
    )(*operands)


def exchange(value):
    ranks = [list(order_of(lax.axis_size("seq")))]
    return lax.all_to_all(value, "seq", split_axis=0, concat_axis=0, tiled=True, axis_index_groups=ranks)


def swap(value, axis, apart):
    return lax.ppermute(value, axis, [(place, place ^ apart) for place in range(lax.axis_size(axis))])


def local(features, pre_gate, post_gate, norm_gain, skip_weight, spectrum):
    rows, wide = features.shape
    places = lax.axis_size("seq")
    groups = lax.axis_size("chan")
    width = wide // places
    piled = width % 16 == 0
    cells = rows * wide
    shape = jax.ShapeDtypeStruct
    vmem, anywhere = pl.BlockSpec(memory_space=pltpu.VMEM), pl.BlockSpec(memory_space=pl.ANY)
    squares, skipped, packed = call(
        prepare_kernel,
        (
            shape((1, rows), F32),
            shape((wide, rows), BF16),
            shape((places, 5, width, rows) if piled else (5, wide, rows), BF16),
        ),
        10 * cells,
        32 * cells,
        features,
        pre_gate,
        norm_gain[None, :],
        skip_weight[None, :],
        spectrum,
        limit=WHOLE_VMEM,
        in_specs=[anywhere] * 5,
        out_specs=(anywhere, anywhere, anywhere),
        scratch_shapes=[
            pltpu.VMEM(features.shape, BF16),
            pltpu.VMEM(pre_gate.shape, BF16),
            pltpu.VMEM((1, wide), F32),
            pltpu.VMEM((1, wide), F32),
            pltpu.VMEM(spectrum.shape, F32),
            pltpu.VMEM((1, rows), F32),
            pltpu.VMEM((wide, rows), BF16),
            pltpu.VMEM((5, places, width, rows) if piled else (5, wide, rows), BF16),
            pltpu.SemaphoreType.DMA((8,)),
            pltpu.SemaphoreType.DMA((7,)),
        ],
    )
    if not piled:
        packed = packed.reshape(5, places, width, rows).transpose(1, 0, 2, 3)
    gathered = exchange(packed)
    others = [swap(squares, "chan", apart) for apart in range(1, groups)]
    scale = call(
        functools.partial(scale_kernel, wide * groups), shape((1, rows), F32), 8 * rows, 32 * rows, squares, *others
    )
    if piled:
        near = jnp.concatenate([scale, swap(scale, "seq", 1)])
        scales = [near] + [swap(near, "seq", steps[0]) for steps in hops(places)[1:]]
    else:
        scales = [jnp.repeat(lax.all_gather(scale, "seq", axis=0, tiled=True), width, axis=0)]
        response = gathered[:, :4].reshape(places, 2, 2, width, rows).transpose(1, 0, 2, 3, 4)
        gathered = jnp.concatenate([response.reshape(4, wide, rows), gathered[:, 4].reshape(1, wide, rows)])
    if piled:
        constants = folded_tables(places, rows, width)
        half = constants[0].shape[0] // 2
        scratch = [
            pltpu.VMEM((places, 1, rows), F32),
            pltpu.VMEM((wide, rows), BF16),
            pltpu.VMEM((8 * (half - 2 * width), rows // 4), BF16),
            pltpu.VMEM((4 * half, rows // 2), BF16),
            pltpu.VMEM((4 * half, rows // 2), BF16),
            pltpu.VMEM((2 * half, rows), BF16),
        ]
    else:
        constants = tables(places, rows, width)
        scratch = [pltpu.VMEM((4 * wide, 2 * rows), BF16)] * 2
    conv = call(
        folded_kernel if piled else convolve_kernel,
        shape((wide, rows), BF16),
        20 * cells * rows,
        20 * cells,
        gathered,
        *constants,
        *scales,
        scratch_shapes=scratch,
    )
    conv = exchange(conv.reshape(places, width, rows))
    if not piled:
        conv = conv.reshape(wide, rows)
    return call(finish_kernel, shape((rows, wide), BF16), 10 * cells, 8 * cells, conv, skipped, scale, post_gate)


def solution(mesh):
    return jax.shard_map(
        local,
        mesh=mesh,
        in_specs=(
            P("seq", "chan"),
            P("seq", "chan"),
            P("seq", "chan"),
            P("chan"),
            P("chan"),
            P(None, "seq", None, "chan"),
        ),
        out_specs=P("seq", "chan"),
        check_vma=False,
    )
```

```python
import functools

import jax
import jax.numpy as jnp
import numpy as np
from jax import lax
from jax.experimental import pallas as pl
from jax.experimental.pallas import tpu as pltpu
from jax.sharding import PartitionSpec as P

EPS = 1e-06
BF16 = jnp.bfloat16
F32 = jnp.float32
VMEM_LIMIT = 48 * 1024 * 1024
WHOLE_VMEM = 63 * 1024 * 1024 + 512 * 1024


def order_of(places, back=False):
    if places != 8:
        return tuple(range(places))
    return (5, 1, 3, 6, 2, 4, 0, 7) if back else (4, 7, 1, 2, 5, 6, 0, 3)


def reverse_bits(index, levels):
    return sum((index >> bit & 1) << levels - 1 - bit for bit in range(levels))


@functools.lru_cache(maxsize=None)
def tables(places, rows, width):
    levels = places.bit_length() - 1
    stride = 2 * places
    bins = stride * rows
    residues = np.array([2 * reverse_bits(place, levels) + parity for place in range(places) for parity in range(2)])
    angle = 2.0 * np.pi * ((residues[:, None] * np.arange(places)[None, :]) % stride) / stride
    same = np.eye(width)
    first = np.concatenate([np.kron(np.cos(angle), same), np.kron(-np.sin(angle), same)])
    last = first.T / bins
    angle = 2.0 * np.pi * ((residues[:, None] * np.arange(rows)[None, :]) % bins) / bins
    twist = np.repeat(np.stack([np.cos(angle), np.sin(angle)]), width, axis=1)
    series = np.arange(rows)
    angle = 2.0 * np.pi * ((series[:, None] * series[None, :]) % rows) / rows
    dft = np.concatenate([np.cos(angle), np.sin(angle)])
    return (
        first.astype(jnp.bfloat16),
        last.astype(jnp.bfloat16),
        twist.astype(np.float32),
        dft.astype(jnp.bfloat16),
    )


def pair_rows(places):
    levels = places.bit_length() - 1

    def holder(residue):
        return order_of(places).index(reverse_bits(residue // 2, levels)), residue % 2

    mirrors = [None if residue % places == 0 else holder(2 * places - residue) for residue in range(places + 1)]
    return [holder(residue) for residue in range(places + 1)], mirrors


@functools.lru_cache(maxsize=None)
def folded_tables(places, rows, width):
    stride = 2 * places
    bins = stride * rows
    residues = np.arange(places + 1)
    angle = 2.0 * np.pi * ((residues[:, None] * np.arange(places)[None, :]) % stride) / stride
    parts = np.stack([np.cos(angle), -np.sin(angle)], axis=1)
    first = np.kron(parts.reshape(-1, places), np.eye(width))
    last = first.T / bins
    angle = 2.0 * np.pi * ((residues[:, None] * np.arange(rows)[None, :]) % bins) / bins
    twist = np.stack([np.cos(angle), np.sin(angle)])
    block = rows // 4
    series = np.arange(block)
    angle = 2.0 * np.pi * ((np.arange(4)[:, None] * series[None, :]) % rows) / rows
    spin = np.stack([np.cos(angle), np.sin(angle)])
    angle = 2.0 * np.pi * ((series[:, None] * series[None, :]) % block) / block
    cos, sin = np.cos(angle), np.sin(angle)
    there = np.block([[cos, -sin], [sin, cos]])
    back = np.block([[cos, sin], [-sin, cos]])
    reverse = np.eye(block)[::-1]
    return (
        first.astype(jnp.bfloat16),
        last.astype(jnp.bfloat16),
        twist.astype(np.float32),
        spin.astype(np.float32),
        np.stack([there, back]).astype(jnp.bfloat16),
        reverse.astype(jnp.bfloat16),
    )


def hops(places):
    return [[apart, apart + 1] for apart in range(0, places, 2)]


def prepare_kernel(
    features_ref,
    pre_ref,
    gain_ref,
    skip_ref,
    spectrum_ref,
    squares_ref,
    skipped_ref,
    packed_ref,
    features_in,
    pre_in,
    gain_in,
    skip_in,
    spectrum_in,
    squares_out,
    skipped_out,
    packed_out,
    in_sems,
    out_sems,
):
    blocks = [(part, parity) for part in range(2) for parity in range(2)]
    pairs = [(features_ref, features_in), (pre_ref, pre_in), (gain_ref, gain_in), (skip_ref, skip_in)]
    pairs += [(spectrum_ref.at[block], spectrum_in.at[block]) for block in blocks]
    arriving = [pltpu.make_async_copy(*pair, in_sems.at[slot]) for slot, pair in enumerate(pairs)]
    for copy in arriving:
        copy.start()
    leaving = []

    def leave(source, target):
        copy = pltpu.make_async_copy(source, target, out_sems.at[len(leaving)])
        copy.start()
        leaving.append(copy)

    def pack(slot, turned):
        if len(packed_ref.shape) == 4:
            places, width = packed_out.shape[1:3]
            for rank, place in enumerate(order_of(places)):
                packed_out[slot, rank] = turned[place * width : (place + 1) * width]
            leave(packed_out.at[slot], packed_ref.at[:, slot])
        else:
            packed_out[slot] = turned
            leave(packed_out.at[slot], packed_ref.at[slot])

    for copy in arriving[:4]:
        copy.wait()
    features = features_in[...].astype(F32)
    scaled = features * gain_in[...] * pre_in[...].astype(F32)
    pack(4, scaled.astype(BF16).T)
    skipped_out[...] = (scaled * skip_in[...]).astype(BF16).T
    leave(skipped_out, skipped_ref)
    turned = features_in[...].T.astype(F32)
    squares_out[...] = jnp.sum(turned * turned, axis=0, keepdims=True)
    leave(squares_out, squares_ref)
    for slot, block in enumerate(blocks):
        arriving[4 + slot].wait()
        if len(packed_ref.shape) == 4:
            quarter = spectrum_in.shape[2] // 4
            rows = [spectrum_in[(*block, pl.ds(turn, quarter, stride=4), slice(None))] for turn in range(4)]
            pack(slot, jnp.concatenate([row.astype(BF16).T for row in rows], axis=1))
        else:
            pack(slot, spectrum_in[block].astype(BF16).T)
    for copy in leaving:
        copy.wait()


def scale_kernel(channels, *refs):
    square_refs, scale_ref = refs[:-1], refs[-1]
    total = square_refs[0][...]
    for square_ref in square_refs[1:]:
        total = total + square_ref[...]
    scale_ref[...] = lax.rsqrt(total / channels + EPS)


def matmul(left, right):
    return jnp.dot(left, right, preferred_element_type=F32)


def butterfly(values, direction):
    (real0, imag0), (real1, imag1), (real2, imag2), (real3, imag3) = values
    even, odd = (real0 + real2, imag0 + imag2), (real1 + real3, imag1 + imag3)
    even_gap, odd_gap = (real0 - real2, imag0 - imag2), (real1 - real3, imag1 - imag3)
    lower = (even_gap[0] + odd_gap[1], even_gap[1] - odd_gap[0])
    upper = (even_gap[0] - odd_gap[1], even_gap[1] + odd_gap[0])
    total, gap = (even[0] + odd[0], even[1] + odd[1]), (even[0] - odd[0], even[1] - odd[1])
    return [total, lower, gap, upper] if direction > 0 else [total, upper, gap, lower]


def folded_kernel(packed_ref, first_ref, last_ref, twist_ref, spin_ref, dft_ref, reverse_ref, *refs):
    scale_refs, (out_ref, scales, signal, mirror, forward, backward, both) = refs[:-7], refs[-7:]
    wide, rows = out_ref.shape
    places, width = scales.shape[0], wide // scales.shape[0]
    block, inner = rows // 4, mirror.shape[0] // 8
    order = order_of(places)
    direct, mirrors = pair_rows(places)
    quarters = [pl.ds(turn * block, block) for turn in range(4)]
    groups = [range(begin, min(begin + 3, places + 1)) for begin in range(0, places + 1, 3)]
    for row, holder in enumerate(mirrors[1:places]):
        for part in range(2):
            for turn in range(4):
                at = pl.ds((part * 4 + 3 - turn) * inner + row * width, width)
                mirror[at, :] = packed_ref[holder[0], 2 * part + holder[1], :, quarters[turn]]
    reversed_bins = matmul(mirror[...], reverse_ref[...])
    place = lax.axis_index("seq")
    for scale_ref, steps in zip(scale_refs, hops(places)):
        for at, step in enumerate(steps):
            scales[place ^ step] = scale_ref[pl.ds(at, 1), :]
    for rank, at in enumerate(order):
        signal[pl.ds(at * width, width), :] = (packed_ref[rank, 4].astype(F32) * scales[at]).astype(BF16)
    spectral = []
    for group in groups:
        begin = group[0] * width
        mixed = matmul(first_ref[pl.ds(2 * begin, 2 * len(group) * width), :], signal[...])
        for at, residue in enumerate(group):
            over, under = mixed[2 * at * width : (2 * at + 1) * width], mixed[(2 * at + 1) * width : (2 * at + 2) * width]
            values = []
            for turn in range(4):
                real, imag = (part[:, turn * block : (turn + 1) * block] for part in (over, under))
                cos, sin = (twist_ref[part, pl.ds(residue, 1), quarters[turn]] for part in range(2))
                values.append((real * cos + imag * sin, imag * cos - real * sin))
            for turn, (real, imag) in enumerate(butterfly(values, 1)):
                if turn > 0:
                    cos, sin = spin_ref[0, pl.ds(turn, 1), :], spin_ref[1, pl.ds(turn, 1), :]
                    real, imag = real * cos + imag * sin, imag * cos - real * sin
                row = pl.ds(4 * begin + (turn * len(group) + at) * width, width)
                forward[row, pl.ds(0, block)] = real.astype(BF16)
                forward[row, pl.ds(block, block)] = imag.astype(BF16)
        spectral.append(matmul(forward[pl.ds(4 * begin, 4 * len(group) * width), :], dft_ref[0]))
    restored = []
    for group, values in zip(groups, spectral):
        begin = group[0] * width
        for turn in range(4):
            for at, residue in enumerate(group):
                row = (turn * len(group) + at) * width
                real, imag = values[row : row + width, :block], values[row : row + width, block:]
                holder = direct[residue]
                response_real = packed_ref[holder[0], holder[1], :, quarters[turn]].astype(F32)
                response_imag = packed_ref[holder[0], 2 + holder[1], :, quarters[turn]].astype(F32)
                if mirrors[residue] is not None:
                    other = turn * inner + (residue - 1) * width
                    response_real = response_real + reversed_bins[other : other + width]
                    other = other + 4 * inner
                    response_imag = response_imag - reversed_bins[other : other + width]
                target = pl.ds(4 * begin + row, width)
                backward[target, pl.ds(0, block)] = (real * response_real - imag * response_imag).astype(BF16)
                backward[target, pl.ds(block, block)] = (real * response_imag + imag * response_real).astype(BF16)
        restored.append(matmul(backward[pl.ds(4 * begin, 4 * len(group) * width), :], dft_ref[1]))
    for group, turned in zip(groups, restored):
        for at, residue in enumerate(group):
            values = []
            for turn in range(4):
                row = (turn * len(group) + at) * width
                real, imag = turned[row : row + width, :block], turned[row : row + width, block:]
                if turn > 0:
                    cos, sin = spin_ref[0, pl.ds(turn, 1), :], spin_ref[1, pl.ds(turn, 1), :]
                    real, imag = real * cos - imag * sin, imag * cos + real * sin
                values.append((real, imag))
            for lanes, (real, imag) in zip(quarters, butterfly(values, -1)):
                cos, sin = twist_ref[0, pl.ds(residue, 1), lanes], twist_ref[1, pl.ds(residue, 1), lanes]
                both[pl.ds(2 * residue * width, width), lanes] = (real * cos - imag * sin).astype(BF16)
                both[pl.ds((2 * residue + 1) * width, width), lanes] = (imag * cos + real * sin).astype(BF16)
    result = matmul(last_ref[...], both[...]).astype(BF16)
    for rank, at in enumerate(order_of(places, back=True)):
        out_ref[pl.ds(rank * width, width), :] = result[at * width : (at + 1) * width]


def convolve_kernel(packed_ref, first_ref, last_ref, twist_ref, dft_ref, scale_ref, out_ref, left, right):
    wide, rows = out_ref.shape
    half = 2 * wide
    signal = (packed_ref[4].astype(F32) * scale_ref[...]).astype(BF16)
    mixed = matmul(first_ref[...], signal)
    real, imag = mixed[:half], mixed[half:]
    cos_twist, sin_twist = twist_ref[0], twist_ref[1]
    turned_real = (real * cos_twist + imag * sin_twist).astype(BF16)
    turned_imag = (imag * cos_twist - real * sin_twist).astype(BF16)
    left[pl.ds(0, half), pl.ds(0, rows)] = turned_real
    left[pl.ds(0, half), pl.ds(rows, rows)] = turned_imag
    left[pl.ds(half, half), pl.ds(0, rows)] = turned_imag
    left[pl.ds(half, half), pl.ds(rows, rows)] = -turned_real
    mixed = matmul(left[...], dft_ref[...])
    real, imag = mixed[:half], mixed[half:]
    response_real = packed_ref[0:2].reshape(half, rows).astype(F32)
    response_imag = packed_ref[2:4].reshape(half, rows).astype(F32)
    product_real = (real * response_real - imag * response_imag).astype(BF16)
    product_imag = (real * response_imag + imag * response_real).astype(BF16)
    right[pl.ds(0, half), pl.ds(0, rows)] = product_real
    right[pl.ds(0, half), pl.ds(rows, rows)] = -product_imag
    right[pl.ds(half, half), pl.ds(0, rows)] = product_imag
    right[pl.ds(half, half), pl.ds(rows, rows)] = product_real
    mixed = matmul(right[...], dft_ref[...])
    real, imag = mixed[:half], mixed[half:]
    turned_real = (real * cos_twist - imag * sin_twist).astype(BF16)
    turned_imag = (imag * cos_twist + real * sin_twist).astype(BF16)
    both = jnp.concatenate([turned_real, turned_imag], axis=0)
    out_ref[...] = matmul(last_ref[...], both).astype(BF16)


def finish_kernel(conv_ref, skipped_ref, scale_ref, post_ref, out_ref):
    conv = conv_ref[...]
    if len(conv_ref.shape) == 3:
        order = order_of(conv_ref.shape[0], back=True)
        conv = jnp.concatenate([conv_ref[order.index(place)] for place in range(len(order))])
    turned = conv.astype(F32) + skipped_ref[...].astype(F32) * scale_ref[...]
    out_ref[...] = (post_ref[...].astype(F32) * turned.T).astype(BF16)


def call(kernel, out_shape, flops, moved, *operands, limit=VMEM_LIMIT, **options):
    return pl.pallas_call(
        kernel,
        out_shape=out_shape,
        compiler_params=pltpu.CompilerParams(vmem_limit_bytes=limit),
        cost_estimate=pl.CostEstimate(flops=flops, bytes_accessed=moved, transcendentals=0),
        **options,
    )(*operands)


def exchange(value, back=False):
    ranks = [list(order_of(lax.axis_size("seq"), back))]
    return lax.all_to_all(value, "seq", split_axis=0, concat_axis=0, tiled=True, axis_index_groups=ranks)


def swap(value, axis, apart):
    return lax.ppermute(value, axis, [(place, place ^ apart) for place in range(lax.axis_size(axis))])


def local(features, pre_gate, post_gate, norm_gain, skip_weight, spectrum):
    rows, wide = features.shape
    places = lax.axis_size("seq")
    groups = lax.axis_size("chan")
    width = wide // places
    piled = width % 16 == 0
    cells = rows * wide
    shape = jax.ShapeDtypeStruct
    vmem, anywhere = pl.BlockSpec(memory_space=pltpu.VMEM), pl.BlockSpec(memory_space=pl.ANY)
    squares, skipped, packed = call(
        prepare_kernel,
        (
            shape((1, rows), F32),
            shape((wide, rows), BF16),
            shape((places, 5, width, rows) if piled else (5, wide, rows), BF16),
        ),
        10 * cells,
        32 * cells,
        features,
        pre_gate,
        norm_gain[None, :],
        skip_weight[None, :],
        spectrum,
        limit=WHOLE_VMEM,
        in_specs=[anywhere] * 5,
        out_specs=(anywhere, anywhere, anywhere),
        scratch_shapes=[
            pltpu.VMEM(features.shape, BF16),
            pltpu.VMEM(pre_gate.shape, BF16),
            pltpu.VMEM((1, wide), F32),
            pltpu.VMEM((1, wide), F32),
            pltpu.VMEM(spectrum.shape, F32),
            pltpu.VMEM((1, rows), F32),
            pltpu.VMEM((wide, rows), BF16),
            pltpu.VMEM((5, places, width, rows) if piled else (5, wide, rows), BF16),
            pltpu.SemaphoreType.DMA((8,)),
            pltpu.SemaphoreType.DMA((7,)),
        ],
    )
    if not piled:
        packed = packed.reshape(5, places, width, rows).transpose(1, 0, 2, 3)
    gathered = exchange(packed)
    others = [swap(squares, "chan", apart) for apart in range(1, groups)]
    scale = call(
        functools.partial(scale_kernel, wide * groups), shape((1, rows), F32), 8 * rows, 32 * rows, squares, *others
    )
    if piled:
        near = jnp.concatenate([scale, swap(scale, "seq", 1)])
        scales = [near] + [swap(near, "seq", steps[0]) for steps in hops(places)[1:]]
    else:
        scales = [jnp.repeat(lax.all_gather(scale, "seq", axis=0, tiled=True), width, axis=0)]
        response = gathered[:, :4].reshape(places, 2, 2, width, rows).transpose(1, 0, 2, 3, 4)
        gathered = jnp.concatenate([response.reshape(4, wide, rows), gathered[:, 4].reshape(1, wide, rows)])
    if piled:
        constants = folded_tables(places, rows, width)
        half = constants[0].shape[0] // 2
        scratch = [
            pltpu.VMEM((places, 1, rows), F32),
            pltpu.VMEM((wide, rows), BF16),
            pltpu.VMEM((8 * (half - 2 * width), rows // 4), BF16),
            pltpu.VMEM((4 * half, rows // 2), BF16),
            pltpu.VMEM((4 * half, rows // 2), BF16),
            pltpu.VMEM((2 * half, rows), BF16),
        ]
    else:
        constants = tables(places, rows, width)
        scratch = [pltpu.VMEM((4 * wide, 2 * rows), BF16)] * 2
    conv = call(
        folded_kernel if piled else convolve_kernel,
        shape((wide, rows), BF16),
        20 * cells * rows,
        20 * cells,
        gathered,
        *constants,
        *scales,
        scratch_shapes=scratch,
    )
    conv = exchange(conv.reshape(places, width, rows), back=True)
    if not piled:
        conv = conv.reshape(wide, rows)
    return call(finish_kernel, shape((rows, wide), BF16), 10 * cells, 8 * cells, conv, skipped, scale, post_gate)


def solution(mesh):
    return jax.shard_map(
        local,
        mesh=mesh,
        in_specs=(
            P("seq", "chan"),
            P("seq", "chan"),
            P("seq", "chan"),
            P("chan"),
            P("chan"),
            P(None, "seq", None, "chan"),
        ),
        out_specs=P("seq", "chan"),
        check_vma=False,
    )
```

```python
import functools

import jax
import jax.numpy as jnp
import numpy as np
from jax import lax
from jax.experimental import pallas as pl
from jax.experimental.pallas import tpu as pltpu
from jax.sharding import PartitionSpec as P

EPS = 1e-06
BF16 = jnp.bfloat16
F32 = jnp.float32
VMEM_LIMIT = 48 * 1024 * 1024
WHOLE_VMEM = 63 * 1024 * 1024 + 512 * 1024


def order_of(places, odd, back=False):
    if places != 8:
        return tuple(range(places))
    order = (5, 1, 3, 6, 2, 4, 0, 7) if back else (4, 7, 1, 2, 5, 6, 0, 3)
    return tuple(place ^ (4 if odd and not back else 0) for place in order)


def rank_of(place, places, odd, back=False):
    return jnp.where(odd, order_of(places, True, back).index(place), order_of(places, False, back).index(place))


def is_odd():
    return lax.axis_index("chan") % 2 == 1


def reverse_bits(index, levels):
    return sum((index >> bit & 1) << levels - 1 - bit for bit in range(levels))


@functools.lru_cache(maxsize=None)
def tables(places, rows, width):
    levels = places.bit_length() - 1
    stride = 2 * places
    bins = stride * rows
    residues = np.array([2 * reverse_bits(place, levels) + parity for place in range(places) for parity in range(2)])
    angle = 2.0 * np.pi * ((residues[:, None] * np.arange(places)[None, :]) % stride) / stride
    same = np.eye(width)
    first = np.concatenate([np.kron(np.cos(angle), same), np.kron(-np.sin(angle), same)])
    last = first.T / bins
    angle = 2.0 * np.pi * ((residues[:, None] * np.arange(rows)[None, :]) % bins) / bins
    twist = np.repeat(np.stack([np.cos(angle), np.sin(angle)]), width, axis=1)
    series = np.arange(rows)
    angle = 2.0 * np.pi * ((series[:, None] * series[None, :]) % rows) / rows
    dft = np.concatenate([np.cos(angle), np.sin(angle)])
    return (
        first.astype(jnp.bfloat16),
        last.astype(jnp.bfloat16),
        twist.astype(np.float32),
        dft.astype(jnp.bfloat16),
    )


def pair_rows(places):
    levels = places.bit_length() - 1

    def holder(residue):
        return reverse_bits(residue // 2, levels), residue % 2

    mirrors = [None if residue % places == 0 else holder(2 * places - residue) for residue in range(places + 1)]
    return [holder(residue) for residue in range(places + 1)], mirrors


@functools.lru_cache(maxsize=None)
def folded_tables(places, rows, width):
    stride = 2 * places
    bins = stride * rows
    residues = np.arange(places + 1)
    angle = 2.0 * np.pi * ((residues[:, None] * np.arange(places)[None, :]) % stride) / stride
    parts = np.stack([np.cos(angle), -np.sin(angle)], axis=1)
    first = np.kron(parts.reshape(-1, places), np.eye(width))
    last = first.T / bins
    angle = 2.0 * np.pi * ((residues[:, None] * np.arange(rows)[None, :]) % bins) / bins
    twist = np.stack([np.cos(angle), np.sin(angle)])
    block = rows // 4
    series = np.arange(block)
    angle = 2.0 * np.pi * ((np.arange(4)[:, None] * series[None, :]) % rows) / rows
    spin = np.stack([np.cos(angle), np.sin(angle)])
    angle = 2.0 * np.pi * ((series[:, None] * series[None, :]) % block) / block
    cos, sin = np.cos(angle), np.sin(angle)
    there = np.block([[cos, -sin], [sin, cos]])
    back = np.block([[cos, sin], [-sin, cos]])
    reverse = np.eye(block)[::-1]
    return (
        first.astype(jnp.bfloat16),
        last.astype(jnp.bfloat16),
        twist.astype(np.float32),
        spin.astype(np.float32),
        np.stack([there, back]).astype(jnp.bfloat16),
        reverse.astype(jnp.bfloat16),
    )


def hops(places):
    return [[apart, apart + 1] for apart in range(0, places, 2)]


def prepare_kernel(
    features_ref,
    pre_ref,
    gain_ref,
    skip_ref,
    spectrum_ref,
    squares_ref,
    skipped_ref,
    packed_ref,
    features_in,
    pre_in,
    gain_in,
    skip_in,
    spectrum_in,
    squares_out,
    skipped_out,
    packed_out,
    in_sems,
    out_sems,
):
    blocks = [(part, parity) for part in range(2) for parity in range(2)]
    pairs = [(features_ref, features_in), (pre_ref, pre_in), (gain_ref, gain_in), (skip_ref, skip_in)]
    pairs += [(spectrum_ref.at[block], spectrum_in.at[block]) for block in blocks]
    arriving = [pltpu.make_async_copy(*pair, in_sems.at[slot]) for slot, pair in enumerate(pairs)]
    for copy in arriving:
        copy.start()
    leaving = []

    def leave(source, target):
        copy = pltpu.make_async_copy(source, target, out_sems.at[len(leaving)])
        copy.start()
        leaving.append(copy)

    odd = is_odd()

    def pack(slot, turned):
        if len(packed_ref.shape) == 4:
            places, width = packed_out.shape[1:3]
            for place in range(places):
                packed_out[slot, rank_of(place, places, odd)] = turned[place * width : (place + 1) * width]
            leave(packed_out.at[slot], packed_ref.at[:, slot])
        else:
            packed_out[slot] = turned
            leave(packed_out.at[slot], packed_ref.at[slot])

    for copy in arriving[:4]:
        copy.wait()
    features = features_in[...].astype(F32)
    scaled = features * gain_in[...] * pre_in[...].astype(F32)
    pack(4, scaled.astype(BF16).T)
    skipped_out[...] = (scaled * skip_in[...]).astype(BF16).T
    leave(skipped_out, skipped_ref)
    turned = features_in[...].T.astype(F32)
    squares_out[...] = jnp.sum(turned * turned, axis=0, keepdims=True)
    leave(squares_out, squares_ref)
    for slot, block in enumerate(blocks):
        arriving[4 + slot].wait()
        if len(packed_ref.shape) == 4:
            quarter = spectrum_in.shape[2] // 4
            rows = [spectrum_in[(*block, pl.ds(turn, quarter, stride=4), slice(None))] for turn in range(4)]
            pack(slot, jnp.concatenate([row.astype(BF16).T for row in rows], axis=1))
        else:
            pack(slot, spectrum_in[block].astype(BF16).T)
    for copy in leaving:
        copy.wait()


def scale_kernel(channels, *refs):
    square_refs, scale_ref = refs[:-1], refs[-1]
    total = square_refs[0][...]
    for square_ref in square_refs[1:]:
        total = total + square_ref[...]
    scale_ref[...] = lax.rsqrt(total / channels + EPS)


def matmul(left, right):
    return jnp.dot(left, right, preferred_element_type=F32)


def butterfly(values, direction):
    (real0, imag0), (real1, imag1), (real2, imag2), (real3, imag3) = values
    even, odd = (real0 + real2, imag0 + imag2), (real1 + real3, imag1 + imag3)
    even_gap, odd_gap = (real0 - real2, imag0 - imag2), (real1 - real3, imag1 - imag3)
    lower = (even_gap[0] + odd_gap[1], even_gap[1] - odd_gap[0])
    upper = (even_gap[0] - odd_gap[1], even_gap[1] + odd_gap[0])
    total, gap = (even[0] + odd[0], even[1] + odd[1]), (even[0] - odd[0], even[1] - odd[1])
    return [total, lower, gap, upper] if direction > 0 else [total, upper, gap, lower]


def folded_kernel(packed_ref, first_ref, last_ref, twist_ref, spin_ref, dft_ref, reverse_ref, *refs):
    scale_refs, (out_ref, scales, signal, mirror, forward, backward, both) = refs[:-7], refs[-7:]
    wide, rows = out_ref.shape
    places, width = scales.shape[0], wide // scales.shape[0]
    block, inner = rows // 4, mirror.shape[0] // 8
    odd = is_odd()
    ranks = [rank_of(at, places, odd) for at in range(places)]
    direct, mirrors = pair_rows(places)
    quarters = [pl.ds(turn * block, block) for turn in range(4)]
    groups = [range(begin, min(begin + 3, places + 1)) for begin in range(0, places + 1, 3)]
    for row, holder in enumerate(mirrors[1:places]):
        for part in range(2):
            for turn in range(4):
                at = pl.ds((part * 4 + 3 - turn) * inner + row * width, width)
                mirror[at, :] = packed_ref[ranks[holder[0]], 2 * part + holder[1], :, quarters[turn]]
    reversed_bins = matmul(mirror[...], reverse_ref[...])
    place = lax.axis_index("seq")
    for scale_ref, steps in zip(scale_refs, hops(places)):
        for at, step in enumerate(steps):
            scales[place ^ step] = scale_ref[pl.ds(at, 1), :]
    for at in range(places):
        signal[pl.ds(at * width, width), :] = (packed_ref[ranks[at], 4].astype(F32) * scales[at]).astype(BF16)
    spectral = []
    for group in groups:
        begin = group[0] * width
        mixed = matmul(first_ref[pl.ds(2 * begin, 2 * len(group) * width), :], signal[...])
        for at, residue in enumerate(group):
            over, under = mixed[2 * at * width : (2 * at + 1) * width], mixed[(2 * at + 1) * width : (2 * at + 2) * width]
            values = []
            for turn in range(4):
                real, imag = (part[:, turn * block : (turn + 1) * block] for part in (over, under))
                cos, sin = (twist_ref[part, pl.ds(residue, 1), quarters[turn]] for part in range(2))
                values.append((real * cos + imag * sin, imag * cos - real * sin))
            for turn, (real, imag) in enumerate(butterfly(values, 1)):
                if turn > 0:
                    cos, sin = spin_ref[0, pl.ds(turn, 1), :], spin_ref[1, pl.ds(turn, 1), :]
                    real, imag = real * cos + imag * sin, imag * cos - real * sin
                row = pl.ds(4 * begin + (turn * len(group) + at) * width, width)
                forward[row, pl.ds(0, block)] = real.astype(BF16)
                forward[row, pl.ds(block, block)] = imag.astype(BF16)
        spectral.append(matmul(forward[pl.ds(4 * begin, 4 * len(group) * width), :], dft_ref[0]))
    restored = []
    for group, values in zip(groups, spectral):
        begin = group[0] * width
        for turn in range(4):
            for at, residue in enumerate(group):
                row = (turn * len(group) + at) * width
                real, imag = values[row : row + width, :block], values[row : row + width, block:]
                holder = direct[residue]
                response_real = packed_ref[ranks[holder[0]], holder[1], :, quarters[turn]].astype(F32)
                response_imag = packed_ref[ranks[holder[0]], 2 + holder[1], :, quarters[turn]].astype(F32)
                if mirrors[residue] is not None:
                    other = turn * inner + (residue - 1) * width
                    response_real = response_real + reversed_bins[other : other + width]
                    other = other + 4 * inner
                    response_imag = response_imag - reversed_bins[other : other + width]
                target = pl.ds(4 * begin + row, width)
                backward[target, pl.ds(0, block)] = (real * response_real - imag * response_imag).astype(BF16)
                backward[target, pl.ds(block, block)] = (real * response_imag + imag * response_real).astype(BF16)
        restored.append(matmul(backward[pl.ds(4 * begin, 4 * len(group) * width), :], dft_ref[1]))
    for group, turned in zip(groups, restored):
        for at, residue in enumerate(group):
            values = []
            for turn in range(4):
                row = (turn * len(group) + at) * width
                real, imag = turned[row : row + width, :block], turned[row : row + width, block:]
                if turn > 0:
                    cos, sin = spin_ref[0, pl.ds(turn, 1), :], spin_ref[1, pl.ds(turn, 1), :]
                    real, imag = real * cos - imag * sin, imag * cos + real * sin
                values.append((real, imag))
            for lanes, (real, imag) in zip(quarters, butterfly(values, -1)):
                cos, sin = twist_ref[0, pl.ds(residue, 1), lanes], twist_ref[1, pl.ds(residue, 1), lanes]
                both[pl.ds(2 * residue * width, width), lanes] = (real * cos - imag * sin).astype(BF16)
                both[pl.ds((2 * residue + 1) * width, width), lanes] = (imag * cos + real * sin).astype(BF16)
    result = matmul(last_ref[...], both[...]).astype(BF16)
    for rank, at in enumerate(order_of(places, False, back=True)):
        out_ref[pl.ds(rank * width, width), :] = result[at * width : (at + 1) * width]


def convolve_kernel(packed_ref, first_ref, last_ref, twist_ref, dft_ref, scale_ref, out_ref, left, right):
    wide, rows = out_ref.shape
    half = 2 * wide
    signal = (packed_ref[4].astype(F32) * scale_ref[...]).astype(BF16)
    mixed = matmul(first_ref[...], signal)
    real, imag = mixed[:half], mixed[half:]
    cos_twist, sin_twist = twist_ref[0], twist_ref[1]
    turned_real = (real * cos_twist + imag * sin_twist).astype(BF16)
    turned_imag = (imag * cos_twist - real * sin_twist).astype(BF16)
    left[pl.ds(0, half), pl.ds(0, rows)] = turned_real
    left[pl.ds(0, half), pl.ds(rows, rows)] = turned_imag
    left[pl.ds(half, half), pl.ds(0, rows)] = turned_imag
    left[pl.ds(half, half), pl.ds(rows, rows)] = -turned_real
    mixed = matmul(left[...], dft_ref[...])
    real, imag = mixed[:half], mixed[half:]
    response_real = packed_ref[0:2].reshape(half, rows).astype(F32)
    response_imag = packed_ref[2:4].reshape(half, rows).astype(F32)
    product_real = (real * response_real - imag * response_imag).astype(BF16)
    product_imag = (real * response_imag + imag * response_real).astype(BF16)
    right[pl.ds(0, half), pl.ds(0, rows)] = product_real
    right[pl.ds(0, half), pl.ds(rows, rows)] = -product_imag
    right[pl.ds(half, half), pl.ds(0, rows)] = product_imag
    right[pl.ds(half, half), pl.ds(rows, rows)] = product_real
    mixed = matmul(right[...], dft_ref[...])
    real, imag = mixed[:half], mixed[half:]
    turned_real = (real * cos_twist - imag * sin_twist).astype(BF16)
    turned_imag = (imag * cos_twist + real * sin_twist).astype(BF16)
    both = jnp.concatenate([turned_real, turned_imag], axis=0)
    out_ref[...] = matmul(last_ref[...], both).astype(BF16)


def finish_kernel(conv_ref, skipped_ref, scale_ref, post_ref, out_ref):
    conv = conv_ref[...]
    if len(conv_ref.shape) == 3:
        order = order_of(conv_ref.shape[0], False, back=True)
        conv = jnp.concatenate([conv_ref[order.index(place)] for place in range(len(order))])
    turned = conv.astype(F32) + skipped_ref[...].astype(F32) * scale_ref[...]
    out_ref[...] = (post_ref[...].astype(F32) * turned.T).astype(BF16)


def call(kernel, out_shape, flops, moved, *operands, limit=VMEM_LIMIT, **options):
    return pl.pallas_call(
        kernel,
        out_shape=out_shape,
        compiler_params=pltpu.CompilerParams(vmem_limit_bytes=limit),
        cost_estimate=pl.CostEstimate(flops=flops, bytes_accessed=moved, transcendentals=0),
        **options,
    )(*operands)


def exchange(value, back=False):
    places, groups = lax.axis_size("seq"), lax.axis_size("chan")
    lists = [[place * groups + index for place in order_of(places, index % 2, back)] for index in range(groups)]
    both = ("seq", "chan")
    return lax.all_to_all(value, both, split_axis=0, concat_axis=0, tiled=True, axis_index_groups=lists)


def swap(value, axis, apart):
    return lax.ppermute(value, axis, [(place, place ^ apart) for place in range(lax.axis_size(axis))])


def local(features, pre_gate, post_gate, norm_gain, skip_weight, spectrum):
    rows, wide = features.shape
    places = lax.axis_size("seq")
    groups = lax.axis_size("chan")
    width = wide // places
    piled = width % 16 == 0
    cells = rows * wide
    shape = jax.ShapeDtypeStruct
    vmem, anywhere = pl.BlockSpec(memory_space=pltpu.VMEM), pl.BlockSpec(memory_space=pl.ANY)
    squares, skipped, packed = call(
        prepare_kernel,
        (
            shape((1, rows), F32),
            shape((wide, rows), BF16),
            shape((places, 5, width, rows) if piled else (5, wide, rows), BF16),
        ),
        10 * cells,
        32 * cells,
        features,
        pre_gate,
        norm_gain[None, :],
        skip_weight[None, :],
        spectrum,
        limit=WHOLE_VMEM,
        in_specs=[anywhere] * 5,
        out_specs=(anywhere, anywhere, anywhere),
        scratch_shapes=[
            pltpu.VMEM(features.shape, BF16),
            pltpu.VMEM(pre_gate.shape, BF16),
            pltpu.VMEM((1, wide), F32),
            pltpu.VMEM((1, wide), F32),
            pltpu.VMEM(spectrum.shape, F32),
            pltpu.VMEM((1, rows), F32),
            pltpu.VMEM((wide, rows), BF16),
            pltpu.VMEM((5, places, width, rows) if piled else (5, wide, rows), BF16),
            pltpu.SemaphoreType.DMA((8,)),
            pltpu.SemaphoreType.DMA((7,)),
        ],
    )
    if not piled:
        packed = packed.reshape(5, places, width, rows).transpose(1, 0, 2, 3)
    gathered = exchange(packed)
    others = [swap(squares, "chan", apart) for apart in range(1, groups)]
    scale = call(
        functools.partial(scale_kernel, wide * groups), shape((1, rows), F32), 8 * rows, 32 * rows, squares, *others
    )
    if piled:
        near = jnp.concatenate([scale, swap(scale, "seq", 1)])
        scales = [near] + [swap(near, "seq", steps[0]) for steps in hops(places)[1:]]
    else:
        scales = [jnp.repeat(lax.all_gather(scale, "seq", axis=0, tiled=True), width, axis=0)]
        response = gathered[:, :4].reshape(places, 2, 2, width, rows).transpose(1, 0, 2, 3, 4)
        gathered = jnp.concatenate([response.reshape(4, wide, rows), gathered[:, 4].reshape(1, wide, rows)])
    if piled:
        constants = folded_tables(places, rows, width)
        half = constants[0].shape[0] // 2
        scratch = [
            pltpu.VMEM((places, 1, rows), F32),
            pltpu.VMEM((wide, rows), BF16),
            pltpu.VMEM((8 * (half - 2 * width), rows // 4), BF16),
            pltpu.VMEM((4 * half, rows // 2), BF16),
            pltpu.VMEM((4 * half, rows // 2), BF16),
            pltpu.VMEM((2 * half, rows), BF16),
        ]
    else:
        constants = tables(places, rows, width)
        scratch = [pltpu.VMEM((4 * wide, 2 * rows), BF16)] * 2
    conv = call(
        folded_kernel if piled else convolve_kernel,
        shape((wide, rows), BF16),
        20 * cells * rows,
        20 * cells,
        gathered,
        *constants,
        *scales,
        scratch_shapes=scratch,
    )
    conv = exchange(conv.reshape(places, width, rows), back=True)
    if not piled:
        conv = conv.reshape(wide, rows)
    return call(finish_kernel, shape((rows, wide), BF16), 10 * cells, 8 * cells, conv, skipped, scale, post_gate)


def solution(mesh):
    return jax.shard_map(
        local,
        mesh=mesh,
        in_specs=(
            P("seq", "chan"),
            P("seq", "chan"),
            P("seq", "chan"),
            P("chan"),
            P("chan"),
            P(None, "seq", None, "chan"),
        ),
        out_specs=P("seq", "chan"),
        check_vma=False,
    )
```

```python
import functools

import jax
import jax.numpy as jnp
import numpy as np
from jax import lax
from jax.experimental import pallas as pl
from jax.experimental.pallas import tpu as pltpu
from jax.sharding import PartitionSpec as P

EPS = 1e-06
BF16 = jnp.bfloat16
F32 = jnp.float32
VMEM_LIMIT = 48 * 1024 * 1024
WHOLE_VMEM = 63 * 1024 * 1024 + 512 * 1024


def order_of(places, back=False):
    if places != 8:
        return tuple(range(places))
    return (5, 3, 4, 6, 7, 0, 1, 2) if back else (4, 7, 1, 2, 5, 6, 0, 3)


def reverse_bits(index, levels):
    return sum((index >> bit & 1) << levels - 1 - bit for bit in range(levels))


@functools.lru_cache(maxsize=None)
def tables(places, rows, width):
    levels = places.bit_length() - 1
    stride = 2 * places
    bins = stride * rows
    residues = np.array([2 * reverse_bits(place, levels) + parity for place in range(places) for parity in range(2)])
    angle = 2.0 * np.pi * ((residues[:, None] * np.arange(places)[None, :]) % stride) / stride
    same = np.eye(width)
    first = np.concatenate([np.kron(np.cos(angle), same), np.kron(-np.sin(angle), same)])
    last = first.T / bins
    angle = 2.0 * np.pi * ((residues[:, None] * np.arange(rows)[None, :]) % bins) / bins
    twist = np.repeat(np.stack([np.cos(angle), np.sin(angle)]), width, axis=1)
    series = np.arange(rows)
    angle = 2.0 * np.pi * ((series[:, None] * series[None, :]) % rows) / rows
    dft = np.concatenate([np.cos(angle), np.sin(angle)])
    return (
        first.astype(jnp.bfloat16),
        last.astype(jnp.bfloat16),
        twist.astype(np.float32),
        dft.astype(jnp.bfloat16),
    )


def pair_rows(places):
    levels = places.bit_length() - 1

    def holder(residue):
        return order_of(places).index(reverse_bits(residue // 2, levels)), residue % 2

    mirrors = [None if residue % places == 0 else holder(2 * places - residue) for residue in range(places + 1)]
    return [holder(residue) for residue in range(places + 1)], mirrors


@functools.lru_cache(maxsize=None)
def folded_tables(places, rows, width):
    stride = 2 * places
    bins = stride * rows
    residues = np.arange(places + 1)
    angle = 2.0 * np.pi * ((residues[:, None] * np.arange(places)[None, :]) % stride) / stride
    parts = np.stack([np.cos(angle), -np.sin(angle)], axis=1)
    first = np.kron(parts.reshape(-1, places), np.eye(width))
    last = first.T / bins
    angle = 2.0 * np.pi * ((residues[:, None] * np.arange(rows)[None, :]) % bins) / bins
    twist = np.stack([np.cos(angle), np.sin(angle)])
    block = rows // 4
    series = np.arange(block)
    angle = 2.0 * np.pi * ((np.arange(4)[:, None] * series[None, :]) % rows) / rows
    spin = np.stack([np.cos(angle), np.sin(angle)])
    angle = 2.0 * np.pi * ((series[:, None] * series[None, :]) % block) / block
    cos, sin = np.cos(angle), np.sin(angle)
    there = np.block([[cos, -sin], [sin, cos]])
    back = np.block([[cos, sin], [-sin, cos]])
    reverse = np.eye(block)[::-1]
    return (
        first.astype(jnp.bfloat16),
        last.astype(jnp.bfloat16),
        twist.astype(np.float32),
        spin.astype(np.float32),
        np.stack([there, back]).astype(jnp.bfloat16),
        reverse.astype(jnp.bfloat16),
    )


def hops(places):
    return [[apart, apart + 1] for apart in range(0, places, 2)]


def prepare_kernel(
    features_ref,
    pre_ref,
    gain_ref,
    skip_ref,
    spectrum_ref,
    squares_ref,
    skipped_ref,
    packed_ref,
    features_in,
    pre_in,
    gain_in,
    skip_in,
    spectrum_in,
    squares_out,
    skipped_out,
    packed_out,
    in_sems,
    out_sems,
):
    blocks = [(part, parity) for part in range(2) for parity in range(2)]
    pairs = [(features_ref, features_in), (pre_ref, pre_in), (gain_ref, gain_in), (skip_ref, skip_in)]
    pairs += [(spectrum_ref.at[block], spectrum_in.at[block]) for block in blocks]
    arriving = [pltpu.make_async_copy(*pair, in_sems.at[slot]) for slot, pair in enumerate(pairs)]
    for copy in arriving:
        copy.start()
    leaving = []

    def leave(source, target):
        copy = pltpu.make_async_copy(source, target, out_sems.at[len(leaving)])
        copy.start()
        leaving.append(copy)

    def pack(slot, turned):
        if len(packed_ref.shape) == 4:
            places, width = packed_out.shape[1:3]
            for rank, place in enumerate(order_of(places)):
                packed_out[slot, rank] = turned[place * width : (place + 1) * width]
            leave(packed_out.at[slot], packed_ref.at[:, slot])
        else:
            packed_out[slot] = turned
            leave(packed_out.at[slot], packed_ref.at[slot])

    for copy in arriving[:4]:
        copy.wait()
    features = features_in[...].astype(F32)
    scaled = features * gain_in[...] * pre_in[...].astype(F32)
    pack(4, scaled.astype(BF16).T)
    skipped_out[...] = (scaled * skip_in[...]).astype(BF16).T
    leave(skipped_out, skipped_ref)
    turned = features_in[...].T.astype(F32)
    squares_out[...] = jnp.sum(turned * turned, axis=0, keepdims=True)
    leave(squares_out, squares_ref)
    for slot, block in enumerate(blocks):
        arriving[4 + slot].wait()
        if len(packed_ref.shape) == 4:
            quarter = spectrum_in.shape[2] // 4
            rows = [spectrum_in[(*block, pl.ds(turn, quarter, stride=4), slice(None))] for turn in range(4)]
            pack(slot, jnp.concatenate([row.astype(BF16).T for row in rows], axis=1))
        else:
            pack(slot, spectrum_in[block].astype(BF16).T)
    for copy in leaving:
        copy.wait()


def scale_kernel(channels, *refs):
    square_refs, scale_ref = refs[:-1], refs[-1]
    total = square_refs[0][...]
    for square_ref in square_refs[1:]:
        total = total + square_ref[...]
    scale_ref[...] = lax.rsqrt(total / channels + EPS)


def matmul(left, right):
    return jnp.dot(left, right, preferred_element_type=F32)


def butterfly(values, direction):
    (real0, imag0), (real1, imag1), (real2, imag2), (real3, imag3) = values
    even, odd = (real0 + real2, imag0 + imag2), (real1 + real3, imag1 + imag3)
    even_gap, odd_gap = (real0 - real2, imag0 - imag2), (real1 - real3, imag1 - imag3)
    lower = (even_gap[0] + odd_gap[1], even_gap[1] - odd_gap[0])
    upper = (even_gap[0] - odd_gap[1], even_gap[1] + odd_gap[0])
    total, gap = (even[0] + odd[0], even[1] + odd[1]), (even[0] - odd[0], even[1] - odd[1])
    return [total, lower, gap, upper] if direction > 0 else [total, upper, gap, lower]


def folded_kernel(packed_ref, first_ref, last_ref, twist_ref, spin_ref, dft_ref, reverse_ref, *refs):
    scale_refs, (out_ref, scales, signal, mirror, forward, backward, both) = refs[:-7], refs[-7:]
    wide, rows = out_ref.shape
    places, width = scales.shape[0], wide // scales.shape[0]
    block, inner = rows // 4, mirror.shape[0] // 8
    order = order_of(places)
    direct, mirrors = pair_rows(places)
    quarters = [pl.ds(turn * block, block) for turn in range(4)]
    groups = [range(begin, min(begin + 3, places + 1)) for begin in range(0, places + 1, 3)]
    for row, holder in enumerate(mirrors[1:places]):
        for part in range(2):
            for turn in range(4):
                at = pl.ds((part * 4 + 3 - turn) * inner + row * width, width)
                mirror[at, :] = packed_ref[holder[0], 2 * part + holder[1], :, quarters[turn]]
    reversed_bins = matmul(mirror[...], reverse_ref[...])
    place = lax.axis_index("seq")
    for scale_ref, steps in zip(scale_refs, hops(places)):
        for at, step in enumerate(steps):
            scales[place ^ step] = scale_ref[pl.ds(at, 1), :]
    for rank, at in enumerate(order):
        signal[pl.ds(at * width, width), :] = (packed_ref[rank, 4].astype(F32) * scales[at]).astype(BF16)
    spectral = []
    for group in groups:
        begin = group[0] * width
        mixed = matmul(first_ref[pl.ds(2 * begin, 2 * len(group) * width), :], signal[...])
        for at, residue in enumerate(group):
            over, under = mixed[2 * at * width : (2 * at + 1) * width], mixed[(2 * at + 1) * width : (2 * at + 2) * width]
            values = []
            for turn in range(4):
                real, imag = (part[:, turn * block : (turn + 1) * block] for part in (over, under))
                cos, sin = (twist_ref[part, pl.ds(residue, 1), quarters[turn]] for part in range(2))
                values.append((real * cos + imag * sin, imag * cos - real * sin))
            for turn, (real, imag) in enumerate(butterfly(values, 1)):
                if turn > 0:
                    cos, sin = spin_ref[0, pl.ds(turn, 1), :], spin_ref[1, pl.ds(turn, 1), :]
                    real, imag = real * cos + imag * sin, imag * cos - real * sin
                row = pl.ds(4 * begin + (turn * len(group) + at) * width, width)
                forward[row, pl.ds(0, block)] = real.astype(BF16)
                forward[row, pl.ds(block, block)] = imag.astype(BF16)
        spectral.append(matmul(forward[pl.ds(4 * begin, 4 * len(group) * width), :], dft_ref[0]))
    restored = []
    for group, values in zip(groups, spectral):
        begin = group[0] * width
        for turn in range(4):
            for at, residue in enumerate(group):
                row = (turn * len(group) + at) * width
                real, imag = values[row : row + width, :block], values[row : row + width, block:]
                holder = direct[residue]
                response_real = packed_ref[holder[0], holder[1], :, quarters[turn]].astype(F32)
                response_imag = packed_ref[holder[0], 2 + holder[1], :, quarters[turn]].astype(F32)
                if mirrors[residue] is not None:
                    other = turn * inner + (residue - 1) * width
                    response_real = response_real + reversed_bins[other : other + width]
                    other = other + 4 * inner
                    response_imag = response_imag - reversed_bins[other : other + width]
                target = pl.ds(4 * begin + row, width)
                backward[target, pl.ds(0, block)] = (real * response_real - imag * response_imag).astype(BF16)
                backward[target, pl.ds(block, block)] = (real * response_imag + imag * response_real).astype(BF16)
        restored.append(matmul(backward[pl.ds(4 * begin, 4 * len(group) * width), :], dft_ref[1]))
    for group, turned in zip(groups, restored):
        for at, residue in enumerate(group):
            values = []
            for turn in range(4):
                row = (turn * len(group) + at) * width
                real, imag = turned[row : row + width, :block], turned[row : row + width, block:]
                if turn > 0:
                    cos, sin = spin_ref[0, pl.ds(turn, 1), :], spin_ref[1, pl.ds(turn, 1), :]
                    real, imag = real * cos - imag * sin, imag * cos + real * sin
                values.append((real, imag))
            for lanes, (real, imag) in zip(quarters, butterfly(values, -1)):
                cos, sin = twist_ref[0, pl.ds(residue, 1), lanes], twist_ref[1, pl.ds(residue, 1), lanes]
                both[pl.ds(2 * residue * width, width), lanes] = (real * cos - imag * sin).astype(BF16)
                both[pl.ds((2 * residue + 1) * width, width), lanes] = (imag * cos + real * sin).astype(BF16)
    result = matmul(last_ref[...], both[...]).astype(BF16)
    for rank, at in enumerate(order_of(places, back=True)):
        out_ref[pl.ds(rank * width, width), :] = result[at * width : (at + 1) * width]


def convolve_kernel(packed_ref, first_ref, last_ref, twist_ref, dft_ref, scale_ref, out_ref, left, right):
    wide, rows = out_ref.shape
    half = 2 * wide
    signal = (packed_ref[4].astype(F32) * scale_ref[...]).astype(BF16)
    mixed = matmul(first_ref[...], signal)
    real, imag = mixed[:half], mixed[half:]
    cos_twist, sin_twist = twist_ref[0], twist_ref[1]
    turned_real = (real * cos_twist + imag * sin_twist).astype(BF16)
    turned_imag = (imag * cos_twist - real * sin_twist).astype(BF16)
    left[pl.ds(0, half), pl.ds(0, rows)] = turned_real
    left[pl.ds(0, half), pl.ds(rows, rows)] = turned_imag
    left[pl.ds(half, half), pl.ds(0, rows)] = turned_imag
    left[pl.ds(half, half), pl.ds(rows, rows)] = -turned_real
    mixed = matmul(left[...], dft_ref[...])
    real, imag = mixed[:half], mixed[half:]
    response_real = packed_ref[0:2].reshape(half, rows).astype(F32)
    response_imag = packed_ref[2:4].reshape(half, rows).astype(F32)
    product_real = (real * response_real - imag * response_imag).astype(BF16)
    product_imag = (real * response_imag + imag * response_real).astype(BF16)
    right[pl.ds(0, half), pl.ds(0, rows)] = product_real
    right[pl.ds(0, half), pl.ds(rows, rows)] = -product_imag
    right[pl.ds(half, half), pl.ds(0, rows)] = product_imag
    right[pl.ds(half, half), pl.ds(rows, rows)] = product_real
    mixed = matmul(right[...], dft_ref[...])
    real, imag = mixed[:half], mixed[half:]
    turned_real = (real * cos_twist - imag * sin_twist).astype(BF16)
    turned_imag = (imag * cos_twist + real * sin_twist).astype(BF16)
    both = jnp.concatenate([turned_real, turned_imag], axis=0)
    out_ref[...] = matmul(last_ref[...], both).astype(BF16)


def finish_kernel(conv_ref, skipped_ref, scale_ref, post_ref, out_ref):
    conv = conv_ref[...]
    if len(conv_ref.shape) == 3:
        order = order_of(conv_ref.shape[0], back=True)
        conv = jnp.concatenate([conv_ref[order.index(place)] for place in range(len(order))])
    turned = conv.astype(F32) + skipped_ref[...].astype(F32) * scale_ref[...]
    out_ref[...] = (post_ref[...].astype(F32) * turned.T).astype(BF16)


def call(kernel, out_shape, flops, moved, *operands, limit=VMEM_LIMIT, **options):
    return pl.pallas_call(
        kernel,
        out_shape=out_shape,
        compiler_params=pltpu.CompilerParams(vmem_limit_bytes=limit),
        cost_estimate=pl.CostEstimate(flops=flops, bytes_accessed=moved, transcendentals=0),
        **options,
    )(*operands)


def exchange(value, back=False):
    ranks = [list(order_of(lax.axis_size("seq"), back))]
    return lax.all_to_all(value, "seq", split_axis=0, concat_axis=0, tiled=True, axis_index_groups=ranks)


def swap(value, axis, apart):
    return lax.ppermute(value, axis, [(place, place ^ apart) for place in range(lax.axis_size(axis))])


def local(features, pre_gate, post_gate, norm_gain, skip_weight, spectrum):
    rows, wide = features.shape
    places = lax.axis_size("seq")
    groups = lax.axis_size("chan")
    width = wide // places
    piled = width % 16 == 0
    cells = rows * wide
    shape = jax.ShapeDtypeStruct
    vmem, anywhere = pl.BlockSpec(memory_space=pltpu.VMEM), pl.BlockSpec(memory_space=pl.ANY)
    squares, skipped, packed = call(
        prepare_kernel,
        (
            shape((1, rows), F32),
            shape((wide, rows), BF16),
            shape((places, 5, width, rows) if piled else (5, wide, rows), BF16),
        ),
        10 * cells,
        32 * cells,
        features,
        pre_gate,
        norm_gain[None, :],
        skip_weight[None, :],
        spectrum,
        limit=WHOLE_VMEM,
        in_specs=[anywhere] * 5,
        out_specs=(anywhere, anywhere, anywhere),
        scratch_shapes=[
            pltpu.VMEM(features.shape, BF16),
            pltpu.VMEM(pre_gate.shape, BF16),
            pltpu.VMEM((1, wide), F32),
            pltpu.VMEM((1, wide), F32),
            pltpu.VMEM(spectrum.shape, F32),
            pltpu.VMEM((1, rows), F32),
            pltpu.VMEM((wide, rows), BF16),
            pltpu.VMEM((5, places, width, rows) if piled else (5, wide, rows), BF16),
            pltpu.SemaphoreType.DMA((8,)),
            pltpu.SemaphoreType.DMA((7,)),
        ],
    )
    if not piled:
        packed = packed.reshape(5, places, width, rows).transpose(1, 0, 2, 3)
    gathered = exchange(packed)
    others = [swap(squares, "chan", apart) for apart in range(1, groups)]
    scale = call(
        functools.partial(scale_kernel, wide * groups), shape((1, rows), F32), 8 * rows, 32 * rows, squares, *others
    )
    if piled:
        near = jnp.concatenate([scale, swap(scale, "seq", 1)])
        scales = [near] + [swap(near, "seq", steps[0]) for steps in hops(places)[1:]]
    else:
        scales = [jnp.repeat(lax.all_gather(scale, "seq", axis=0, tiled=True), width, axis=0)]
        response = gathered[:, :4].reshape(places, 2, 2, width, rows).transpose(1, 0, 2, 3, 4)
        gathered = jnp.concatenate([response.reshape(4, wide, rows), gathered[:, 4].reshape(1, wide, rows)])
    if piled:
        constants = folded_tables(places, rows, width)
        half = constants[0].shape[0] // 2
        scratch = [
            pltpu.VMEM((places, 1, rows), F32),
            pltpu.VMEM((wide, rows), BF16),
            pltpu.VMEM((8 * (half - 2 * width), rows // 4), BF16),
            pltpu.VMEM((4 * half, rows // 2), BF16),
            pltpu.VMEM((4 * half, rows // 2), BF16),
            pltpu.VMEM((2 * half, rows), BF16),
        ]
    else:
        constants = tables(places, rows, width)
        scratch = [pltpu.VMEM((4 * wide, 2 * rows), BF16)] * 2
    conv = call(
        folded_kernel if piled else convolve_kernel,
        shape((wide, rows), BF16),
        20 * cells * rows,
        20 * cells,
        gathered,
        *constants,
        *scales,
        scratch_shapes=scratch,
    )
    conv = exchange(conv.reshape(places, width, rows), back=True)
    if not piled:
        conv = conv.reshape(wide, rows)
    return call(finish_kernel, shape((rows, wide), BF16), 10 * cells, 8 * cells, conv, skipped, scale, post_gate)


def solution(mesh):
    return jax.shard_map(
        local,
        mesh=mesh,
        in_specs=(
            P("seq", "chan"),
            P("seq", "chan"),
            P("seq", "chan"),
            P("chan"),
            P("chan"),
            P(None, "seq", None, "chan"),
        ),
        out_specs=P("seq", "chan"),
        check_vma=False,
    )
```

```python
import functools

import jax
import jax.numpy as jnp
import numpy as np
from jax import lax
from jax.experimental import pallas as pl
from jax.experimental.pallas import tpu as pltpu
from jax.sharding import PartitionSpec as P

EPS = 1e-06
BF16 = jnp.bfloat16
F32 = jnp.float32
VMEM_LIMIT = 48 * 1024 * 1024
WHOLE_VMEM = 63 * 1024 * 1024 + 512 * 1024


def order_of(places, back=False):
    if places != 8:
        return tuple(range(places))
    return (5, 4, 3, 2, 1, 0, 7, 6) if back else (4, 7, 1, 2, 5, 6, 0, 3)


def reverse_bits(index, levels):
    return sum((index >> bit & 1) << levels - 1 - bit for bit in range(levels))


@functools.lru_cache(maxsize=None)
def tables(places, rows, width):
    levels = places.bit_length() - 1
    stride = 2 * places
    bins = stride * rows
    residues = np.array([2 * reverse_bits(place, levels) + parity for place in range(places) for parity in range(2)])
    angle = 2.0 * np.pi * ((residues[:, None] * np.arange(places)[None, :]) % stride) / stride
    same = np.eye(width)
    first = np.concatenate([np.kron(np.cos(angle), same), np.kron(-np.sin(angle), same)])
    last = first.T / bins
    angle = 2.0 * np.pi * ((residues[:, None] * np.arange(rows)[None, :]) % bins) / bins
    twist = np.repeat(np.stack([np.cos(angle), np.sin(angle)]), width, axis=1)
    series = np.arange(rows)
    angle = 2.0 * np.pi * ((series[:, None] * series[None, :]) % rows) / rows
    dft = np.concatenate([np.cos(angle), np.sin(angle)])
    return (
        first.astype(jnp.bfloat16),
        last.astype(jnp.bfloat16),
        twist.astype(np.float32),
        dft.astype(jnp.bfloat16),
    )


def pair_rows(places):
    levels = places.bit_length() - 1

    def holder(residue):
        return order_of(places).index(reverse_bits(residue // 2, levels)), residue % 2

    mirrors = [None if residue % places == 0 else holder(2 * places - residue) for residue in range(places + 1)]
    return [holder(residue) for residue in range(places + 1)], mirrors


@functools.lru_cache(maxsize=None)
def folded_tables(places, rows, width):
    stride = 2 * places
    bins = stride * rows
    residues = np.arange(places + 1)
    angle = 2.0 * np.pi * ((residues[:, None] * np.arange(places)[None, :]) % stride) / stride
    parts = np.stack([np.cos(angle), -np.sin(angle)], axis=1)
    first = np.kron(parts.reshape(-1, places), np.eye(width))
    last = first.T / bins
    angle = 2.0 * np.pi * ((residues[:, None] * np.arange(rows)[None, :]) % bins) / bins
    twist = np.stack([np.cos(angle), np.sin(angle)])
    block = rows // 4
    series = np.arange(block)
    angle = 2.0 * np.pi * ((np.arange(4)[:, None] * series[None, :]) % rows) / rows
    spin = np.stack([np.cos(angle), np.sin(angle)])
    angle = 2.0 * np.pi * ((series[:, None] * series[None, :]) % block) / block
    cos, sin = np.cos(angle), np.sin(angle)
    there = np.block([[cos, -sin], [sin, cos]])
    back = np.block([[cos, sin], [-sin, cos]])
    reverse = np.eye(block)[::-1]
    return (
        first.astype(jnp.bfloat16),
        last.astype(jnp.bfloat16),
        twist.astype(np.float32),
        spin.astype(np.float32),
        np.stack([there, back]).astype(jnp.bfloat16),
        reverse.astype(jnp.bfloat16),
    )


def hops(places):
    return [[apart, apart + 1] for apart in range(0, places, 2)]


def prepare_kernel(
    features_ref,
    pre_ref,
    gain_ref,
    skip_ref,
    spectrum_ref,
    squares_ref,
    skipped_ref,
    packed_ref,
    features_in,
    pre_in,
    gain_in,
    skip_in,
    spectrum_in,
    squares_out,
    skipped_out,
    packed_out,
    in_sems,
    out_sems,
):
    blocks = [(part, parity) for part in range(2) for parity in range(2)]
    pairs = [(features_ref, features_in), (pre_ref, pre_in), (gain_ref, gain_in), (skip_ref, skip_in)]
    pairs += [(spectrum_ref.at[block], spectrum_in.at[block]) for block in blocks]
    arriving = [pltpu.make_async_copy(*pair, in_sems.at[slot]) for slot, pair in enumerate(pairs)]
    for copy in arriving:
        copy.start()
    leaving = []

    def leave(source, target):
        copy = pltpu.make_async_copy(source, target, out_sems.at[len(leaving)])
        copy.start()
        leaving.append(copy)

    def pack(slot, turned):
        if len(packed_ref.shape) == 4:
            places, width = packed_out.shape[1:3]
            for rank, place in enumerate(order_of(places)):
                packed_out[slot, rank] = turned[place * width : (place + 1) * width]
            leave(packed_out.at[slot], packed_ref.at[:, slot])
        else:
            packed_out[slot] = turned
            leave(packed_out.at[slot], packed_ref.at[slot])

    for copy in arriving[:4]:
        copy.wait()
    features = features_in[...].astype(F32)
    scaled = features * gain_in[...] * pre_in[...].astype(F32)
    pack(4, scaled.astype(BF16).T)
    skipped_out[...] = (scaled * skip_in[...]).astype(BF16).T
    leave(skipped_out, skipped_ref)
    turned = features_in[...].T.astype(F32)
    squares_out[...] = jnp.sum(turned * turned, axis=0, keepdims=True)
    leave(squares_out, squares_ref)
    for slot, block in enumerate(blocks):
        arriving[4 + slot].wait()
        if len(packed_ref.shape) == 4:
            quarter = spectrum_in.shape[2] // 4
            rows = [spectrum_in[(*block, pl.ds(turn, quarter, stride=4), slice(None))] for turn in range(4)]
            pack(slot, jnp.concatenate([row.astype(BF16).T for row in rows], axis=1))
        else:
            pack(slot, spectrum_in[block].astype(BF16).T)
    for copy in leaving:
        copy.wait()


def scale_kernel(channels, *refs):
    square_refs, scale_ref = refs[:-1], refs[-1]
    total = square_refs[0][...]
    for square_ref in square_refs[1:]:
        total = total + square_ref[...]
    scale_ref[...] = lax.rsqrt(total / channels + EPS)


def matmul(left, right):
    return jnp.dot(left, right, preferred_element_type=F32)


def butterfly(values, direction):
    (real0, imag0), (real1, imag1), (real2, imag2), (real3, imag3) = values
    even, odd = (real0 + real2, imag0 + imag2), (real1 + real3, imag1 + imag3)
    even_gap, odd_gap = (real0 - real2, imag0 - imag2), (real1 - real3, imag1 - imag3)
    lower = (even_gap[0] + odd_gap[1], even_gap[1] - odd_gap[0])
    upper = (even_gap[0] - odd_gap[1], even_gap[1] + odd_gap[0])
    total, gap = (even[0] + odd[0], even[1] + odd[1]), (even[0] - odd[0], even[1] - odd[1])
    return [total, lower, gap, upper] if direction > 0 else [total, upper, gap, lower]


def folded_kernel(packed_ref, first_ref, last_ref, twist_ref, spin_ref, dft_ref, reverse_ref, *refs):
    scale_refs, (out_ref, scales, signal, mirror, forward, backward, both) = refs[:-7], refs[-7:]
    wide, rows = out_ref.shape
    places, width = scales.shape[0], wide // scales.shape[0]
    block, inner = rows // 4, mirror.shape[0] // 8
    order = order_of(places)
    direct, mirrors = pair_rows(places)
    quarters = [pl.ds(turn * block, block) for turn in range(4)]
    groups = [range(begin, min(begin + 3, places + 1)) for begin in range(0, places + 1, 3)]
    for row, holder in enumerate(mirrors[1:places]):
        for part in range(2):
            for turn in range(4):
                at = pl.ds((part * 4 + 3 - turn) * inner + row * width, width)
                mirror[at, :] = packed_ref[holder[0], 2 * part + holder[1], :, quarters[turn]]
    reversed_bins = matmul(mirror[...], reverse_ref[...])
    place = lax.axis_index("seq")
    for scale_ref, steps in zip(scale_refs, hops(places)):
        for at, step in enumerate(steps):
            scales[place ^ step] = scale_ref[pl.ds(at, 1), :]
    for rank, at in enumerate(order):
        signal[pl.ds(at * width, width), :] = (packed_ref[rank, 4].astype(F32) * scales[at]).astype(BF16)
    spectral = []
    for group in groups:
        begin = group[0] * width
        mixed = matmul(first_ref[pl.ds(2 * begin, 2 * len(group) * width), :], signal[...])
        for at, residue in enumerate(group):
            over, under = mixed[2 * at * width : (2 * at + 1) * width], mixed[(2 * at + 1) * width : (2 * at + 2) * width]
            values = []
            for turn in range(4):
                real, imag = (part[:, turn * block : (turn + 1) * block] for part in (over, under))
                cos, sin = (twist_ref[part, pl.ds(residue, 1), quarters[turn]] for part in range(2))
                values.append((real * cos + imag * sin, imag * cos - real * sin))
            for turn, (real, imag) in enumerate(butterfly(values, 1)):
                if turn > 0:
                    cos, sin = spin_ref[0, pl.ds(turn, 1), :], spin_ref[1, pl.ds(turn, 1), :]
                    real, imag = real * cos + imag * sin, imag * cos - real * sin
                row = pl.ds(4 * begin + (turn * len(group) + at) * width, width)
                forward[row, pl.ds(0, block)] = real.astype(BF16)
                forward[row, pl.ds(block, block)] = imag.astype(BF16)
        spectral.append(matmul(forward[pl.ds(4 * begin, 4 * len(group) * width), :], dft_ref[0]))
    restored = []
    for group, values in zip(groups, spectral):
        begin = group[0] * width
        for turn in range(4):
            for at, residue in enumerate(group):
                row = (turn * len(group) + at) * width
                real, imag = values[row : row + width, :block], values[row : row + width, block:]
                holder = direct[residue]
                response_real = packed_ref[holder[0], holder[1], :, quarters[turn]].astype(F32)
                response_imag = packed_ref[holder[0], 2 + holder[1], :, quarters[turn]].astype(F32)
                if mirrors[residue] is not None:
                    other = turn * inner + (residue - 1) * width
                    response_real = response_real + reversed_bins[other : other + width]
                    other = other + 4 * inner
                    response_imag = response_imag - reversed_bins[other : other + width]
                target = pl.ds(4 * begin + row, width)
                backward[target, pl.ds(0, block)] = (real * response_real - imag * response_imag).astype(BF16)
                backward[target, pl.ds(block, block)] = (real * response_imag + imag * response_real).astype(BF16)
        restored.append(matmul(backward[pl.ds(4 * begin, 4 * len(group) * width), :], dft_ref[1]))
    for group, turned in zip(groups, restored):
        for at, residue in enumerate(group):
            values = []
            for turn in range(4):
                row = (turn * len(group) + at) * width
                real, imag = turned[row : row + width, :block], turned[row : row + width, block:]
                if turn > 0:
                    cos, sin = spin_ref[0, pl.ds(turn, 1), :], spin_ref[1, pl.ds(turn, 1), :]
                    real, imag = real * cos - imag * sin, imag * cos + real * sin
                values.append((real, imag))
            for lanes, (real, imag) in zip(quarters, butterfly(values, -1)):
                cos, sin = twist_ref[0, pl.ds(residue, 1), lanes], twist_ref[1, pl.ds(residue, 1), lanes]
                both[pl.ds(2 * residue * width, width), lanes] = (real * cos - imag * sin).astype(BF16)
                both[pl.ds((2 * residue + 1) * width, width), lanes] = (imag * cos + real * sin).astype(BF16)
    result = matmul(last_ref[...], both[...]).astype(BF16)
    for rank, at in enumerate(order_of(places, back=True)):
        out_ref[pl.ds(rank * width, width), :] = result[at * width : (at + 1) * width]


def convolve_kernel(packed_ref, first_ref, last_ref, twist_ref, dft_ref, scale_ref, out_ref, left, right):
    wide, rows = out_ref.shape
    half = 2 * wide
    signal = (packed_ref[4].astype(F32) * scale_ref[...]).astype(BF16)
    mixed = matmul(first_ref[...], signal)
    real, imag = mixed[:half], mixed[half:]
    cos_twist, sin_twist = twist_ref[0], twist_ref[1]
    turned_real = (real * cos_twist + imag * sin_twist).astype(BF16)
    turned_imag = (imag * cos_twist - real * sin_twist).astype(BF16)
    left[pl.ds(0, half), pl.ds(0, rows)] = turned_real
    left[pl.ds(0, half), pl.ds(rows, rows)] = turned_imag
    left[pl.ds(half, half), pl.ds(0, rows)] = turned_imag
    left[pl.ds(half, half), pl.ds(rows, rows)] = -turned_real
    mixed = matmul(left[...], dft_ref[...])
    real, imag = mixed[:half], mixed[half:]
    response_real = packed_ref[0:2].reshape(half, rows).astype(F32)
    response_imag = packed_ref[2:4].reshape(half, rows).astype(F32)
    product_real = (real * response_real - imag * response_imag).astype(BF16)
    product_imag = (real * response_imag + imag * response_real).astype(BF16)
    right[pl.ds(0, half), pl.ds(0, rows)] = product_real
    right[pl.ds(0, half), pl.ds(rows, rows)] = -product_imag
    right[pl.ds(half, half), pl.ds(0, rows)] = product_imag
    right[pl.ds(half, half), pl.ds(rows, rows)] = product_real
    mixed = matmul(right[...], dft_ref[...])
    real, imag = mixed[:half], mixed[half:]
    turned_real = (real * cos_twist - imag * sin_twist).astype(BF16)
    turned_imag = (imag * cos_twist + real * sin_twist).astype(BF16)
    both = jnp.concatenate([turned_real, turned_imag], axis=0)
    out_ref[...] = matmul(last_ref[...], both).astype(BF16)


def finish_kernel(conv_ref, skipped_ref, scale_ref, post_ref, out_ref):
    conv = conv_ref[...]
    if len(conv_ref.shape) == 3:
        order = order_of(conv_ref.shape[0], back=True)
        conv = jnp.concatenate([conv_ref[order.index(place)] for place in range(len(order))])
    turned = conv.astype(F32) + skipped_ref[...].astype(F32) * scale_ref[...]
    out_ref[...] = (post_ref[...].astype(F32) * turned.T).astype(BF16)


def call(kernel, out_shape, flops, moved, *operands, limit=VMEM_LIMIT, **options):
    return pl.pallas_call(
        kernel,
        out_shape=out_shape,
        compiler_params=pltpu.CompilerParams(vmem_limit_bytes=limit),
        cost_estimate=pl.CostEstimate(flops=flops, bytes_accessed=moved, transcendentals=0),
        **options,
    )(*operands)


def exchange(value, back=False):
    ranks = [list(order_of(lax.axis_size("seq"), back))]
    return lax.all_to_all(value, "seq", split_axis=0, concat_axis=0, tiled=True, axis_index_groups=ranks)


def swap(value, axis, apart):
    return lax.ppermute(value, axis, [(place, place ^ apart) for place in range(lax.axis_size(axis))])


def local(features, pre_gate, post_gate, norm_gain, skip_weight, spectrum):
    rows, wide = features.shape
    places = lax.axis_size("seq")
    groups = lax.axis_size("chan")
    width = wide // places
    piled = width % 16 == 0
    cells = rows * wide
    shape = jax.ShapeDtypeStruct
    vmem, anywhere = pl.BlockSpec(memory_space=pltpu.VMEM), pl.BlockSpec(memory_space=pl.ANY)
    squares, skipped, packed = call(
        prepare_kernel,
        (
            shape((1, rows), F32),
            shape((wide, rows), BF16),
            shape((places, 5, width, rows) if piled else (5, wide, rows), BF16),
        ),
        10 * cells,
        32 * cells,
        features,
        pre_gate,
        norm_gain[None, :],
        skip_weight[None, :],
        spectrum,
        limit=WHOLE_VMEM,
        in_specs=[anywhere] * 5,
        out_specs=(anywhere, anywhere, anywhere),
        scratch_shapes=[
            pltpu.VMEM(features.shape, BF16),
            pltpu.VMEM(pre_gate.shape, BF16),
            pltpu.VMEM((1, wide), F32),
            pltpu.VMEM((1, wide), F32),
            pltpu.VMEM(spectrum.shape, F32),
            pltpu.VMEM((1, rows), F32),
            pltpu.VMEM((wide, rows), BF16),
            pltpu.VMEM((5, places, width, rows) if piled else (5, wide, rows), BF16),
            pltpu.SemaphoreType.DMA((8,)),
            pltpu.SemaphoreType.DMA((7,)),
        ],
    )
    if not piled:
        packed = packed.reshape(5, places, width, rows).transpose(1, 0, 2, 3)
    gathered = exchange(packed)
    others = [swap(squares, "chan", apart) for apart in range(1, groups)]
    scale = call(
        functools.partial(scale_kernel, wide * groups), shape((1, rows), F32), 8 * rows, 32 * rows, squares, *others
    )
    if piled:
        near = jnp.concatenate([scale, swap(scale, "seq", 1)])
        scales = [near] + [swap(near, "seq", steps[0]) for steps in hops(places)[1:]]
    else:
        scales = [jnp.repeat(lax.all_gather(scale, "seq", axis=0, tiled=True), width, axis=0)]
        response = gathered[:, :4].reshape(places, 2, 2, width, rows).transpose(1, 0, 2, 3, 4)
        gathered = jnp.concatenate([response.reshape(4, wide, rows), gathered[:, 4].reshape(1, wide, rows)])
    if piled:
        constants = folded_tables(places, rows, width)
        half = constants[0].shape[0] // 2
        scratch = [
            pltpu.VMEM((places, 1, rows), F32),
            pltpu.VMEM((wide, rows), BF16),
            pltpu.VMEM((8 * (half - 2 * width), rows // 4), BF16),
            pltpu.VMEM((4 * half, rows // 2), BF16),
            pltpu.VMEM((4 * half, rows // 2), BF16),
            pltpu.VMEM((2 * half, rows), BF16),
        ]
    else:
        constants = tables(places, rows, width)
        scratch = [pltpu.VMEM((4 * wide, 2 * rows), BF16)] * 2
    conv = call(
        folded_kernel if piled else convolve_kernel,
        shape((wide, rows), BF16),
        20 * cells * rows,
        20 * cells,
        gathered,
        *constants,
        *scales,
        scratch_shapes=scratch,
    )
    conv = exchange(conv.reshape(places, width, rows), back=True)
    if not piled:
        conv = conv.reshape(wide, rows)
    return call(finish_kernel, shape((rows, wide), BF16), 10 * cells, 8 * cells, conv, skipped, scale, post_gate)


def solution(mesh):
    return jax.shard_map(
        local,
        mesh=mesh,
        in_specs=(
            P("seq", "chan"),
            P("seq", "chan"),
            P("seq", "chan"),
            P("chan"),
            P("chan"),
            P(None, "seq", None, "chan"),
        ),
        out_specs=P("seq", "chan"),
        check_vma=False,
    )
```

```python
import functools

import jax
import jax.numpy as jnp
import numpy as np
from jax import lax
from jax.experimental import pallas as pl
from jax.experimental.pallas import tpu as pltpu
from jax.sharding import PartitionSpec as P

EPS = 1e-06
BF16 = jnp.bfloat16
F32 = jnp.float32
VMEM_LIMIT = 48 * 1024 * 1024
WHOLE_VMEM = 63 * 1024 * 1024 + 512 * 1024


def order_of(places, back=False):
    if places != 8:
        return tuple(range(places))
    return (5, 1, 3, 6, 2, 4, 0, 7) if back else (4, 7, 3, 6, 2, 1, 5, 0)


def reverse_bits(index, levels):
    return sum((index >> bit & 1) << levels - 1 - bit for bit in range(levels))


@functools.lru_cache(maxsize=None)
def tables(places, rows, width):
    levels = places.bit_length() - 1
    stride = 2 * places
    bins = stride * rows
    residues = np.array([2 * reverse_bits(place, levels) + parity for place in range(places) for parity in range(2)])
    angle = 2.0 * np.pi * ((residues[:, None] * np.arange(places)[None, :]) % stride) / stride
    same = np.eye(width)
    first = np.concatenate([np.kron(np.cos(angle), same), np.kron(-np.sin(angle), same)])
    last = first.T / bins
    angle = 2.0 * np.pi * ((residues[:, None] * np.arange(rows)[None, :]) % bins) / bins
    twist = np.repeat(np.stack([np.cos(angle), np.sin(angle)]), width, axis=1)
    series = np.arange(rows)
    angle = 2.0 * np.pi * ((series[:, None] * series[None, :]) % rows) / rows
    dft = np.concatenate([np.cos(angle), np.sin(angle)])
    return (
        first.astype(jnp.bfloat16),
        last.astype(jnp.bfloat16),
        twist.astype(np.float32),
        dft.astype(jnp.bfloat16),
    )


def pair_rows(places):
    levels = places.bit_length() - 1

    def holder(residue):
        return order_of(places).index(reverse_bits(residue // 2, levels)), residue % 2

    mirrors = [None if residue % places == 0 else holder(2 * places - residue) for residue in range(places + 1)]
    return [holder(residue) for residue in range(places + 1)], mirrors


@functools.lru_cache(maxsize=None)
def folded_tables(places, rows, width):
    stride = 2 * places
    bins = stride * rows
    residues = np.arange(places + 1)
    angle = 2.0 * np.pi * ((residues[:, None] * np.arange(places)[None, :]) % stride) / stride
    parts = np.stack([np.cos(angle), -np.sin(angle)], axis=1)
    first = np.kron(parts.reshape(-1, places), np.eye(width))
    last = first.T / bins
    angle = 2.0 * np.pi * ((residues[:, None] * np.arange(rows)[None, :]) % bins) / bins
    twist = np.stack([np.cos(angle), np.sin(angle)])
    block = rows // 4
    series = np.arange(block)
    angle = 2.0 * np.pi * ((np.arange(4)[:, None] * series[None, :]) % rows) / rows
    spin = np.stack([np.cos(angle), np.sin(angle)])
    angle = 2.0 * np.pi * ((series[:, None] * series[None, :]) % block) / block
    cos, sin = np.cos(angle), np.sin(angle)
    there = np.block([[cos, -sin], [sin, cos]])
    back = np.block([[cos, sin], [-sin, cos]])
    reverse = np.eye(block)[::-1]
    return (
        first.astype(jnp.bfloat16),
        last.astype(jnp.bfloat16),
        twist.astype(np.float32),
        spin.astype(np.float32),
        np.stack([there, back]).astype(jnp.bfloat16),
        reverse.astype(jnp.bfloat16),
    )


def hops(places):
    return [[apart, apart + 1] for apart in range(0, places, 2)]


def prepare_kernel(
    features_ref,
    pre_ref,
    gain_ref,
    skip_ref,
    spectrum_ref,
    squares_ref,
    skipped_ref,
    packed_ref,
    features_in,
    pre_in,
    gain_in,
    skip_in,
    spectrum_in,
    squares_out,
    skipped_out,
    packed_out,
    in_sems,
    out_sems,
):
    blocks = [(part, parity) for part in range(2) for parity in range(2)]
    pairs = [(features_ref, features_in), (pre_ref, pre_in), (gain_ref, gain_in), (skip_ref, skip_in)]
    pairs += [(spectrum_ref.at[block], spectrum_in.at[block]) for block in blocks]
    arriving = [pltpu.make_async_copy(*pair, in_sems.at[slot]) for slot, pair in enumerate(pairs)]
    for copy in arriving:
        copy.start()
    leaving = []

    def leave(source, target):
        copy = pltpu.make_async_copy(source, target, out_sems.at[len(leaving)])
        copy.start()
        leaving.append(copy)

    def pack(slot, turned):
        if len(packed_ref.shape) == 4:
            places, width = packed_out.shape[1:3]
            for rank, place in enumerate(order_of(places)):
                packed_out[slot, rank] = turned[place * width : (place + 1) * width]
            leave(packed_out.at[slot], packed_ref.at[:, slot])
        else:
            packed_out[slot] = turned
            leave(packed_out.at[slot], packed_ref.at[slot])

    for copy in arriving[:4]:
        copy.wait()
    features = features_in[...].astype(F32)
    scaled = features * gain_in[...] * pre_in[...].astype(F32)
    pack(4, scaled.astype(BF16).T)
    skipped_out[...] = (scaled * skip_in[...]).astype(BF16).T
    leave(skipped_out, skipped_ref)
    turned = features_in[...].T.astype(F32)
    squares_out[...] = jnp.sum(turned * turned, axis=0, keepdims=True)
    leave(squares_out, squares_ref)
    for slot, block in enumerate(blocks):
        arriving[4 + slot].wait()
        if len(packed_ref.shape) == 4:
            quarter = spectrum_in.shape[2] // 4
            rows = [spectrum_in[(*block, pl.ds(turn, quarter, stride=4), slice(None))] for turn in range(4)]
            pack(slot, jnp.concatenate([row.astype(BF16).T for row in rows], axis=1))
        else:
            pack(slot, spectrum_in[block].astype(BF16).T)
    for copy in leaving:
        copy.wait()


def scale_kernel(channels, *refs):
    square_refs, scale_ref = refs[:-1], refs[-1]
    total = square_refs[0][...]
    for square_ref in square_refs[1:]:
        total = total + square_ref[...]
    scale_ref[...] = lax.rsqrt(total / channels + EPS)


def matmul(left, right):
    return jnp.dot(left, right, preferred_element_type=F32)


def butterfly(values, direction):
    (real0, imag0), (real1, imag1), (real2, imag2), (real3, imag3) = values
    even, odd = (real0 + real2, imag0 + imag2), (real1 + real3, imag1 + imag3)
    even_gap, odd_gap = (real0 - real2, imag0 - imag2), (real1 - real3, imag1 - imag3)
    lower = (even_gap[0] + odd_gap[1], even_gap[1] - odd_gap[0])
    upper = (even_gap[0] - odd_gap[1], even_gap[1] + odd_gap[0])
    total, gap = (even[0] + odd[0], even[1] + odd[1]), (even[0] - odd[0], even[1] - odd[1])
    return [total, lower, gap, upper] if direction > 0 else [total, upper, gap, lower]


def folded_kernel(packed_ref, first_ref, last_ref, twist_ref, spin_ref, dft_ref, reverse_ref, *refs):
    scale_refs, (out_ref, scales, signal, mirror, forward, backward, both) = refs[:-7], refs[-7:]
    wide, rows = out_ref.shape
    places, width = scales.shape[0], wide // scales.shape[0]
    block, inner = rows // 4, mirror.shape[0] // 8
    order = order_of(places)
    direct, mirrors = pair_rows(places)
    quarters = [pl.ds(turn * block, block) for turn in range(4)]
    groups = [range(begin, min(begin + 3, places + 1)) for begin in range(0, places + 1, 3)]
    for row, holder in enumerate(mirrors[1:places]):
        for part in range(2):
            for turn in range(4):
                at = pl.ds((part * 4 + 3 - turn) * inner + row * width, width)
                mirror[at, :] = packed_ref[holder[0], 2 * part + holder[1], :, quarters[turn]]
    reversed_bins = matmul(mirror[...], reverse_ref[...])
    place = lax.axis_index("seq")
    for scale_ref, steps in zip(scale_refs, hops(places)):
        for at, step in enumerate(steps):
            scales[place ^ step] = scale_ref[pl.ds(at, 1), :]
    for rank, at in enumerate(order):
        signal[pl.ds(at * width, width), :] = (packed_ref[rank, 4].astype(F32) * scales[at]).astype(BF16)
    spectral = []
    for group in groups:
        begin = group[0] * width
        mixed = matmul(first_ref[pl.ds(2 * begin, 2 * len(group) * width), :], signal[...])
        for at, residue in enumerate(group):
            over, under = mixed[2 * at * width : (2 * at + 1) * width], mixed[(2 * at + 1) * width : (2 * at + 2) * width]
            values = []
            for turn in range(4):
                real, imag = (part[:, turn * block : (turn + 1) * block] for part in (over, under))
                cos, sin = (twist_ref[part, pl.ds(residue, 1), quarters[turn]] for part in range(2))
                values.append((real * cos + imag * sin, imag * cos - real * sin))
            for turn, (real, imag) in enumerate(butterfly(values, 1)):
                if turn > 0:
                    cos, sin = spin_ref[0, pl.ds(turn, 1), :], spin_ref[1, pl.ds(turn, 1), :]
                    real, imag = real * cos + imag * sin, imag * cos - real * sin
                row = pl.ds(4 * begin + (turn * len(group) + at) * width, width)
                forward[row, pl.ds(0, block)] = real.astype(BF16)
                forward[row, pl.ds(block, block)] = imag.astype(BF16)
        spectral.append(matmul(forward[pl.ds(4 * begin, 4 * len(group) * width), :], dft_ref[0]))
    restored = []
    for group, values in zip(groups, spectral):
        begin = group[0] * width
        for turn in range(4):
            for at, residue in enumerate(group):
                row = (turn * len(group) + at) * width
                real, imag = values[row : row + width, :block], values[row : row + width, block:]
                holder = direct[residue]
                response_real = packed_ref[holder[0], holder[1], :, quarters[turn]].astype(F32)
                response_imag = packed_ref[holder[0], 2 + holder[1], :, quarters[turn]].astype(F32)
                if mirrors[residue] is not None:
                    other = turn * inner + (residue - 1) * width
                    response_real = response_real + reversed_bins[other : other + width]
                    other = other + 4 * inner
                    response_imag = response_imag - reversed_bins[other : other + width]
                target = pl.ds(4 * begin + row, width)
                backward[target, pl.ds(0, block)] = (real * response_real - imag * response_imag).astype(BF16)
                backward[target, pl.ds(block, block)] = (real * response_imag + imag * response_real).astype(BF16)
        restored.append(matmul(backward[pl.ds(4 * begin, 4 * len(group) * width), :], dft_ref[1]))
    for group, turned in zip(groups, restored):
        for at, residue in enumerate(group):
            values = []
            for turn in range(4):
                row = (turn * len(group) + at) * width
                real, imag = turned[row : row + width, :block], turned[row : row + width, block:]
                if turn > 0:
                    cos, sin = spin_ref[0, pl.ds(turn, 1), :], spin_ref[1, pl.ds(turn, 1), :]
                    real, imag = real * cos - imag * sin, imag * cos + real * sin
                values.append((real, imag))
            for lanes, (real, imag) in zip(quarters, butterfly(values, -1)):
                cos, sin = twist_ref[0, pl.ds(residue, 1), lanes], twist_ref[1, pl.ds(residue, 1), lanes]
                both[pl.ds(2 * residue * width, width), lanes] = (real * cos - imag * sin).astype(BF16)
                both[pl.ds((2 * residue + 1) * width, width), lanes] = (imag * cos + real * sin).astype(BF16)
    result = matmul(last_ref[...], both[...]).astype(BF16)
    for rank, at in enumerate(order_of(places, back=True)):
        out_ref[pl.ds(rank * width, width), :] = result[at * width : (at + 1) * width]


def convolve_kernel(packed_ref, first_ref, last_ref, twist_ref, dft_ref, scale_ref, out_ref, left, right):
    wide, rows = out_ref.shape
    half = 2 * wide
    signal = (packed_ref[4].astype(F32) * scale_ref[...]).astype(BF16)
    mixed = matmul(first_ref[...], signal)
    real, imag = mixed[:half], mixed[half:]
    cos_twist, sin_twist = twist_ref[0], twist_ref[1]
    turned_real = (real * cos_twist + imag * sin_twist).astype(BF16)
    turned_imag = (imag * cos_twist - real * sin_twist).astype(BF16)
    left[pl.ds(0, half), pl.ds(0, rows)] = turned_real
    left[pl.ds(0, half), pl.ds(rows, rows)] = turned_imag
    left[pl.ds(half, half), pl.ds(0, rows)] = turned_imag
    left[pl.ds(half, half), pl.ds(rows, rows)] = -turned_real
    mixed = matmul(left[...], dft_ref[...])
    real, imag = mixed[:half], mixed[half:]
    response_real = packed_ref[0:2].reshape(half, rows).astype(F32)
    response_imag = packed_ref[2:4].reshape(half, rows).astype(F32)
    product_real = (real * response_real - imag * response_imag).astype(BF16)
    product_imag = (real * response_imag + imag * response_real).astype(BF16)
    right[pl.ds(0, half), pl.ds(0, rows)] = product_real
    right[pl.ds(0, half), pl.ds(rows, rows)] = -product_imag
    right[pl.ds(half, half), pl.ds(0, rows)] = product_imag
    right[pl.ds(half, half), pl.ds(rows, rows)] = product_real
    mixed = matmul(right[...], dft_ref[...])
    real, imag = mixed[:half], mixed[half:]
    turned_real = (real * cos_twist - imag * sin_twist).astype(BF16)
    turned_imag = (imag * cos_twist + real * sin_twist).astype(BF16)
    both = jnp.concatenate([turned_real, turned_imag], axis=0)
    out_ref[...] = matmul(last_ref[...], both).astype(BF16)


def finish_kernel(conv_ref, skipped_ref, scale_ref, post_ref, out_ref):
    conv = conv_ref[...]
    if len(conv_ref.shape) == 3:
        order = order_of(conv_ref.shape[0], back=True)
        conv = jnp.concatenate([conv_ref[order.index(place)] for place in range(len(order))])
    turned = conv.astype(F32) + skipped_ref[...].astype(F32) * scale_ref[...]
    out_ref[...] = (post_ref[...].astype(F32) * turned.T).astype(BF16)


def call(kernel, out_shape, flops, moved, *operands, limit=VMEM_LIMIT, **options):
    return pl.pallas_call(
        kernel,
        out_shape=out_shape,
        compiler_params=pltpu.CompilerParams(vmem_limit_bytes=limit),
        cost_estimate=pl.CostEstimate(flops=flops, bytes_accessed=moved, transcendentals=0),
        **options,
    )(*operands)


def exchange(value, back=False):
    ranks = [list(order_of(lax.axis_size("seq"), back))]
    return lax.all_to_all(value, "seq", split_axis=0, concat_axis=0, tiled=True, axis_index_groups=ranks)


def swap(value, axis, apart):
    return lax.ppermute(value, axis, [(place, place ^ apart) for place in range(lax.axis_size(axis))])


def local(features, pre_gate, post_gate, norm_gain, skip_weight, spectrum):
    rows, wide = features.shape
    places = lax.axis_size("seq")
    groups = lax.axis_size("chan")
    width = wide // places
    piled = width % 16 == 0
    cells = rows * wide
    shape = jax.ShapeDtypeStruct
    vmem, anywhere = pl.BlockSpec(memory_space=pltpu.VMEM), pl.BlockSpec(memory_space=pl.ANY)
    squares, skipped, packed = call(
        prepare_kernel,
        (
            shape((1, rows), F32),
            shape((wide, rows), BF16),
            shape((places, 5, width, rows) if piled else (5, wide, rows), BF16),
        ),
        10 * cells,
        32 * cells,
        features,
        pre_gate,
        norm_gain[None, :],
        skip_weight[None, :],
        spectrum,
        limit=WHOLE_VMEM,
        in_specs=[anywhere] * 5,
        out_specs=(anywhere, anywhere, anywhere),
        scratch_shapes=[
            pltpu.VMEM(features.shape, BF16),
            pltpu.VMEM(pre_gate.shape, BF16),
            pltpu.VMEM((1, wide), F32),
            pltpu.VMEM((1, wide), F32),
            pltpu.VMEM(spectrum.shape, F32),
            pltpu.VMEM((1, rows), F32),
            pltpu.VMEM((wide, rows), BF16),
            pltpu.VMEM((5, places, width, rows) if piled else (5, wide, rows), BF16),
            pltpu.SemaphoreType.DMA((8,)),
            pltpu.SemaphoreType.DMA((7,)),
        ],
    )
    if not piled:
        packed = packed.reshape(5, places, width, rows).transpose(1, 0, 2, 3)
    gathered = exchange(packed)
    others = [swap(squares, "chan", apart) for apart in range(1, groups)]
    scale = call(
        functools.partial(scale_kernel, wide * groups), shape((1, rows), F32), 8 * rows, 32 * rows, squares, *others
    )
    if piled:
        near = jnp.concatenate([scale, swap(scale, "seq", 1)])
        scales = [near] + [swap(near, "seq", steps[0]) for steps in hops(places)[1:]]
    else:
        scales = [jnp.repeat(lax.all_gather(scale, "seq", axis=0, tiled=True), width, axis=0)]
        response = gathered[:, :4].reshape(places, 2, 2, width, rows).transpose(1, 0, 2, 3, 4)
        gathered = jnp.concatenate([response.reshape(4, wide, rows), gathered[:, 4].reshape(1, wide, rows)])
    if piled:
        constants = folded_tables(places, rows, width)
        half = constants[0].shape[0] // 2
        scratch = [
            pltpu.VMEM((places, 1, rows), F32),
            pltpu.VMEM((wide, rows), BF16),
            pltpu.VMEM((8 * (half - 2 * width), rows // 4), BF16),
            pltpu.VMEM((4 * half, rows // 2), BF16),
            pltpu.VMEM((4 * half, rows // 2), BF16),
            pltpu.VMEM((2 * half, rows), BF16),
        ]
    else:
        constants = tables(places, rows, width)
        scratch = [pltpu.VMEM((4 * wide, 2 * rows), BF16)] * 2
    conv = call(
        folded_kernel if piled else convolve_kernel,
        shape((wide, rows), BF16),
        20 * cells * rows,
        20 * cells,
        gathered,
        *constants,
        *scales,
        scratch_shapes=scratch,
    )
    conv = exchange(conv.reshape(places, width, rows), back=True)
    if not piled:
        conv = conv.reshape(wide, rows)
    return call(finish_kernel, shape((rows, wide), BF16), 10 * cells, 8 * cells, conv, skipped, scale, post_gate)


def solution(mesh):
    return jax.shard_map(
        local,
        mesh=mesh,
        in_specs=(
            P("seq", "chan"),
            P("seq", "chan"),
            P("seq", "chan"),
            P("chan"),
            P("chan"),
            P(None, "seq", None, "chan"),
        ),
        out_specs=P("seq", "chan"),
        check_vma=False,
    )
```

```python
import functools

import jax
import jax.numpy as jnp
import numpy as np
from jax import lax
from jax.experimental import pallas as pl
from jax.experimental.pallas import tpu as pltpu
from jax.sharding import PartitionSpec as P

EPS = 1e-06
BF16 = jnp.bfloat16
F32 = jnp.float32
VMEM_LIMIT = 48 * 1024 * 1024
WHOLE_VMEM = 63 * 1024 * 1024 + 512 * 1024


def order_of(places, back=False):
    if places != 8:
        return tuple(range(places))
    return (5, 1, 3, 6, 2, 4, 0, 7) if back else (4, 7, 3, 6, 2, 1, 5, 0)


def reverse_bits(index, levels):
    return sum((index >> bit & 1) << levels - 1 - bit for bit in range(levels))


@functools.lru_cache(maxsize=None)
def tables(places, rows, width):
    levels = places.bit_length() - 1
    stride = 2 * places
    bins = stride * rows
    residues = np.array([2 * reverse_bits(place, levels) + parity for place in range(places) for parity in range(2)])
    angle = 2.0 * np.pi * ((residues[:, None] * np.arange(places)[None, :]) % stride) / stride
    same = np.eye(width)
    first = np.concatenate([np.kron(np.cos(angle), same), np.kron(-np.sin(angle), same)])
    last = first.T / bins
    angle = 2.0 * np.pi * ((residues[:, None] * np.arange(rows)[None, :]) % bins) / bins
    twist = np.repeat(np.stack([np.cos(angle), np.sin(angle)]), width, axis=1)
    series = np.arange(rows)
    angle = 2.0 * np.pi * ((series[:, None] * series[None, :]) % rows) / rows
    dft = np.concatenate([np.cos(angle), np.sin(angle)])
    return (
        first.astype(jnp.bfloat16),
        last.astype(jnp.bfloat16),
        twist.astype(np.float32),
        dft.astype(jnp.bfloat16),
    )


def pair_rows(places):
    levels = places.bit_length() - 1

    def holder(residue):
        return order_of(places).index(reverse_bits(residue // 2, levels)), residue % 2

    mirrors = [None if residue % places == 0 else holder(2 * places - residue) for residue in range(places + 1)]
    return [holder(residue) for residue in range(places + 1)], mirrors


@functools.lru_cache(maxsize=None)
def folded_tables(places, rows, width):
    stride = 2 * places
    bins = stride * rows
    residues = np.arange(places + 1)
    angle = 2.0 * np.pi * ((residues[:, None] * np.arange(places)[None, :]) % stride) / stride
    parts = np.stack([np.cos(angle), -np.sin(angle)], axis=1)
    first = np.kron(parts.reshape(-1, places), np.eye(width))
    last = first.T / bins
    angle = 2.0 * np.pi * ((residues[:, None] * np.arange(rows)[None, :]) % bins) / bins
    twist = np.stack([np.cos(angle), np.sin(angle)])
    block = rows // 4
    series = np.arange(block)
    angle = 2.0 * np.pi * ((np.arange(4)[:, None] * series[None, :]) % rows) / rows
    spin = np.stack([np.cos(angle), np.sin(angle)])
    angle = 2.0 * np.pi * ((series[:, None] * series[None, :]) % block) / block
    cos, sin = np.cos(angle), np.sin(angle)
    there = np.block([[cos, -sin], [sin, cos]])
    back = np.block([[cos, sin], [-sin, cos]])
    reverse = np.eye(block)[::-1]
    return (
        first.astype(jnp.bfloat16),
        last.astype(jnp.bfloat16),
        twist.astype(np.float32),
        spin.astype(np.float32),
        np.stack([there, back]).astype(jnp.bfloat16),
        reverse.astype(jnp.bfloat16),
    )


def hops(places):
    return [[apart, apart ^ 2] for apart in range(places) if apart & 2 == 0]


def prepare_kernel(
    features_ref,
    pre_ref,
    gain_ref,
    skip_ref,
    spectrum_ref,
    squares_ref,
    skipped_ref,
    packed_ref,
    features_in,
    pre_in,
    gain_in,
    skip_in,
    spectrum_in,
    squares_out,
    skipped_out,
    packed_out,
    in_sems,
    out_sems,
):
    blocks = [(part, parity) for part in range(2) for parity in range(2)]
    pairs = [(features_ref, features_in), (pre_ref, pre_in), (gain_ref, gain_in), (skip_ref, skip_in)]
    pairs += [(spectrum_ref.at[block], spectrum_in.at[block]) for block in blocks]
    arriving = [pltpu.make_async_copy(*pair, in_sems.at[slot]) for slot, pair in enumerate(pairs)]
    for copy in arriving:
        copy.start()
    leaving = []

    def leave(source, target):
        copy = pltpu.make_async_copy(source, target, out_sems.at[len(leaving)])
        copy.start()
        leaving.append(copy)

    def pack(slot, turned):
        if len(packed_ref.shape) == 4:
            places, width = packed_out.shape[1:3]
            for rank, place in enumerate(order_of(places)):
                packed_out[slot, rank] = turned[place * width : (place + 1) * width]
            leave(packed_out.at[slot], packed_ref.at[:, slot])
        else:
            packed_out[slot] = turned
            leave(packed_out.at[slot], packed_ref.at[slot])

    for copy in arriving[:4]:
        copy.wait()
    features = features_in[...].astype(F32)
    scaled = features * gain_in[...] * pre_in[...].astype(F32)
    pack(4, scaled.astype(BF16).T)
    skipped_out[...] = (scaled * skip_in[...]).astype(BF16).T
    leave(skipped_out, skipped_ref)
    turned = features_in[...].T.astype(F32)
    squares_out[...] = jnp.sum(turned * turned, axis=0, keepdims=True)
    leave(squares_out, squares_ref)
    for slot, block in enumerate(blocks):
        arriving[4 + slot].wait()
        if len(packed_ref.shape) == 4:
            quarter = spectrum_in.shape[2] // 4
            rows = [spectrum_in[(*block, pl.ds(turn, quarter, stride=4), slice(None))] for turn in range(4)]
            pack(slot, jnp.concatenate([row.astype(BF16).T for row in rows], axis=1))
        else:
            pack(slot, spectrum_in[block].astype(BF16).T)
    for copy in leaving:
        copy.wait()


def scale_kernel(channels, *refs):
    square_refs, scale_ref = refs[:-1], refs[-1]
    total = square_refs[0][...]
    for square_ref in square_refs[1:]:
        total = total + square_ref[...]
    scale_ref[...] = lax.rsqrt(total / channels + EPS)


def matmul(left, right):
    return jnp.dot(left, right, preferred_element_type=F32)


def butterfly(values, direction):
    (real0, imag0), (real1, imag1), (real2, imag2), (real3, imag3) = values
    even, odd = (real0 + real2, imag0 + imag2), (real1 + real3, imag1 + imag3)
    even_gap, odd_gap = (real0 - real2, imag0 - imag2), (real1 - real3, imag1 - imag3)
    lower = (even_gap[0] + odd_gap[1], even_gap[1] - odd_gap[0])
    upper = (even_gap[0] - odd_gap[1], even_gap[1] + odd_gap[0])
    total, gap = (even[0] + odd[0], even[1] + odd[1]), (even[0] - odd[0], even[1] - odd[1])
    return [total, lower, gap, upper] if direction > 0 else [total, upper, gap, lower]


def folded_kernel(packed_ref, first_ref, last_ref, twist_ref, spin_ref, dft_ref, reverse_ref, *refs):
    scale_refs, (out_ref, scales, signal, mirror, forward, backward, both) = refs[:-7], refs[-7:]
    wide, rows = out_ref.shape
    places, width = scales.shape[0], wide // scales.shape[0]
    block, inner = rows // 4, mirror.shape[0] // 8
    order = order_of(places)
    direct, mirrors = pair_rows(places)
    quarters = [pl.ds(turn * block, block) for turn in range(4)]
    groups = [range(begin, min(begin + 3, places + 1)) for begin in range(0, places + 1, 3)]
    for row, holder in enumerate(mirrors[1:places]):
        for part in range(2):
            for turn in range(4):
                at = pl.ds((part * 4 + 3 - turn) * inner + row * width, width)
                mirror[at, :] = packed_ref[holder[0], 2 * part + holder[1], :, quarters[turn]]
    reversed_bins = matmul(mirror[...], reverse_ref[...])
    place = lax.axis_index("seq")
    for scale_ref, steps in zip(scale_refs, hops(places)):
        for at, step in enumerate(steps):
            scales[place ^ step] = scale_ref[pl.ds(at, 1), :]
    for rank, at in enumerate(order):
        signal[pl.ds(at * width, width), :] = (packed_ref[rank, 4].astype(F32) * scales[at]).astype(BF16)
    spectral = []
    for group in groups:
        begin = group[0] * width
        mixed = matmul(first_ref[pl.ds(2 * begin, 2 * len(group) * width), :], signal[...])
        for at, residue in enumerate(group):
            over, under = mixed[2 * at * width : (2 * at + 1) * width], mixed[(2 * at + 1) * width : (2 * at + 2) * width]
            values = []
            for turn in range(4):
                real, imag = (part[:, turn * block : (turn + 1) * block] for part in (over, under))
                cos, sin = (twist_ref[part, pl.ds(residue, 1), quarters[turn]] for part in range(2))
                values.append((real * cos + imag * sin, imag * cos - real * sin))
            for turn, (real, imag) in enumerate(butterfly(values, 1)):
                if turn > 0:
                    cos, sin = spin_ref[0, pl.ds(turn, 1), :], spin_ref[1, pl.ds(turn, 1), :]
                    real, imag = real * cos + imag * sin, imag * cos - real * sin
                row = pl.ds(4 * begin + (turn * len(group) + at) * width, width)
                forward[row, pl.ds(0, block)] = real.astype(BF16)
                forward[row, pl.ds(block, block)] = imag.astype(BF16)
        spectral.append(matmul(forward[pl.ds(4 * begin, 4 * len(group) * width), :], dft_ref[0]))
    restored = []
    for group, values in zip(groups, spectral):
        begin = group[0] * width
        for turn in range(4):
            for at, residue in enumerate(group):
                row = (turn * len(group) + at) * width
                real, imag = values[row : row + width, :block], values[row : row + width, block:]
                holder = direct[residue]
                response_real = packed_ref[holder[0], holder[1], :, quarters[turn]].astype(F32)
                response_imag = packed_ref[holder[0], 2 + holder[1], :, quarters[turn]].astype(F32)
                if mirrors[residue] is not None:
                    other = turn * inner + (residue - 1) * width
                    response_real = response_real + reversed_bins[other : other + width]
                    other = other + 4 * inner
                    response_imag = response_imag - reversed_bins[other : other + width]
                target = pl.ds(4 * begin + row, width)
                backward[target, pl.ds(0, block)] = (real * response_real - imag * response_imag).astype(BF16)
                backward[target, pl.ds(block, block)] = (real * response_imag + imag * response_real).astype(BF16)
        restored.append(matmul(backward[pl.ds(4 * begin, 4 * len(group) * width), :], dft_ref[1]))
    for group, turned in zip(groups, restored):
        for at, residue in enumerate(group):
            values = []
            for turn in range(4):
                row = (turn * len(group) + at) * width
                real, imag = turned[row : row + width, :block], turned[row : row + width, block:]
                if turn > 0:
                    cos, sin = spin_ref[0, pl.ds(turn, 1), :], spin_ref[1, pl.ds(turn, 1), :]
                    real, imag = real * cos - imag * sin, imag * cos + real * sin
                values.append((real, imag))
            for lanes, (real, imag) in zip(quarters, butterfly(values, -1)):
                cos, sin = twist_ref[0, pl.ds(residue, 1), lanes], twist_ref[1, pl.ds(residue, 1), lanes]
                both[pl.ds(2 * residue * width, width), lanes] = (real * cos - imag * sin).astype(BF16)
                both[pl.ds((2 * residue + 1) * width, width), lanes] = (imag * cos + real * sin).astype(BF16)
    result = matmul(last_ref[...], both[...]).astype(BF16)
    for rank, at in enumerate(order_of(places, back=True)):
        out_ref[pl.ds(rank * width, width), :] = result[at * width : (at + 1) * width]


def convolve_kernel(packed_ref, first_ref, last_ref, twist_ref, dft_ref, scale_ref, out_ref, left, right):
    wide, rows = out_ref.shape
    half = 2 * wide
    signal = (packed_ref[4].astype(F32) * scale_ref[...]).astype(BF16)
    mixed = matmul(first_ref[...], signal)
    real, imag = mixed[:half], mixed[half:]
    cos_twist, sin_twist = twist_ref[0], twist_ref[1]
    turned_real = (real * cos_twist + imag * sin_twist).astype(BF16)
    turned_imag = (imag * cos_twist - real * sin_twist).astype(BF16)
    left[pl.ds(0, half), pl.ds(0, rows)] = turned_real
    left[pl.ds(0, half), pl.ds(rows, rows)] = turned_imag
    left[pl.ds(half, half), pl.ds(0, rows)] = turned_imag
    left[pl.ds(half, half), pl.ds(rows, rows)] = -turned_real
    mixed = matmul(left[...], dft_ref[...])
    real, imag = mixed[:half], mixed[half:]
    response_real = packed_ref[0:2].reshape(half, rows).astype(F32)
    response_imag = packed_ref[2:4].reshape(half, rows).astype(F32)
    product_real = (real * response_real - imag * response_imag).astype(BF16)
    product_imag = (real * response_imag + imag * response_real).astype(BF16)
    right[pl.ds(0, half), pl.ds(0, rows)] = product_real
    right[pl.ds(0, half), pl.ds(rows, rows)] = -product_imag
    right[pl.ds(half, half), pl.ds(0, rows)] = product_imag
    right[pl.ds(half, half), pl.ds(rows, rows)] = product_real
    mixed = matmul(right[...], dft_ref[...])
    real, imag = mixed[:half], mixed[half:]
    turned_real = (real * cos_twist - imag * sin_twist).astype(BF16)
    turned_imag = (imag * cos_twist + real * sin_twist).astype(BF16)
    both = jnp.concatenate([turned_real, turned_imag], axis=0)
    out_ref[...] = matmul(last_ref[...], both).astype(BF16)


def finish_kernel(conv_ref, skipped_ref, scale_ref, post_ref, out_ref):
    conv = conv_ref[...]
    if len(conv_ref.shape) == 3:
        order = order_of(conv_ref.shape[0], back=True)
        conv = jnp.concatenate([conv_ref[order.index(place)] for place in range(len(order))])
    turned = conv.astype(F32) + skipped_ref[...].astype(F32) * scale_ref[...]
    out_ref[...] = (post_ref[...].astype(F32) * turned.T).astype(BF16)


def call(kernel, out_shape, flops, moved, *operands, limit=VMEM_LIMIT, **options):
    return pl.pallas_call(
        kernel,
        out_shape=out_shape,
        compiler_params=pltpu.CompilerParams(vmem_limit_bytes=limit),
        cost_estimate=pl.CostEstimate(flops=flops, bytes_accessed=moved, transcendentals=0),
        **options,
    )(*operands)


def exchange(value, back=False):
    ranks = [list(order_of(lax.axis_size("seq"), back))]
    return lax.all_to_all(value, "seq", split_axis=0, concat_axis=0, tiled=True, axis_index_groups=ranks)


def swap(value, axis, apart):
    return lax.ppermute(value, axis, [(place, place ^ apart) for place in range(lax.axis_size(axis))])


def local(features, pre_gate, post_gate, norm_gain, skip_weight, spectrum):
    rows, wide = features.shape
    places = lax.axis_size("seq")
    groups = lax.axis_size("chan")
    width = wide // places
    piled = width % 16 == 0
    cells = rows * wide
    shape = jax.ShapeDtypeStruct
    vmem, anywhere = pl.BlockSpec(memory_space=pltpu.VMEM), pl.BlockSpec(memory_space=pl.ANY)
    squares, skipped, packed = call(
        prepare_kernel,
        (
            shape((1, rows), F32),
            shape((wide, rows), BF16),
            shape((places, 5, width, rows) if piled else (5, wide, rows), BF16),
        ),
        10 * cells,
        32 * cells,
        features,
        pre_gate,
        norm_gain[None, :],
        skip_weight[None, :],
        spectrum,
        limit=WHOLE_VMEM,
        in_specs=[anywhere] * 5,
        out_specs=(anywhere, anywhere, anywhere),
        scratch_shapes=[
            pltpu.VMEM(features.shape, BF16),
            pltpu.VMEM(pre_gate.shape, BF16),
            pltpu.VMEM((1, wide), F32),
            pltpu.VMEM((1, wide), F32),
            pltpu.VMEM(spectrum.shape, F32),
            pltpu.VMEM((1, rows), F32),
            pltpu.VMEM((wide, rows), BF16),
            pltpu.VMEM((5, places, width, rows) if piled else (5, wide, rows), BF16),
            pltpu.SemaphoreType.DMA((8,)),
            pltpu.SemaphoreType.DMA((7,)),
        ],
    )
    if not piled:
        packed = packed.reshape(5, places, width, rows).transpose(1, 0, 2, 3)
    gathered = exchange(packed)
    others = [swap(squares, "chan", apart) for apart in range(1, groups)]
    scale = call(
        functools.partial(scale_kernel, wide * groups), shape((1, rows), F32), 8 * rows, 32 * rows, squares, *others
    )
    if piled:
        near = jnp.concatenate([scale, swap(scale, "seq", 2)])
        scales = [near] + [swap(near, "seq", steps[0]) for steps in hops(places)[1:]]
    else:
        scales = [jnp.repeat(lax.all_gather(scale, "seq", axis=0, tiled=True), width, axis=0)]
        response = gathered[:, :4].reshape(places, 2, 2, width, rows).transpose(1, 0, 2, 3, 4)
        gathered = jnp.concatenate([response.reshape(4, wide, rows), gathered[:, 4].reshape(1, wide, rows)])
    if piled:
        constants = folded_tables(places, rows, width)
        half = constants[0].shape[0] // 2
        scratch = [
            pltpu.VMEM((places, 1, rows), F32),
            pltpu.VMEM((wide, rows), BF16),
            pltpu.VMEM((8 * (half - 2 * width), rows // 4), BF16),
            pltpu.VMEM((4 * half, rows // 2), BF16),
            pltpu.VMEM((4 * half, rows // 2), BF16),
            pltpu.VMEM((2 * half, rows), BF16),
        ]
    else:
        constants = tables(places, rows, width)
        scratch = [pltpu.VMEM((4 * wide, 2 * rows), BF16)] * 2
    conv = call(
        folded_kernel if piled else convolve_kernel,
        shape((wide, rows), BF16),
        20 * cells * rows,
        20 * cells,
        gathered,
        *constants,
        *scales,
        scratch_shapes=scratch,
    )
    conv = exchange(conv.reshape(places, width, rows), back=True)
    if not piled:
        conv = conv.reshape(wide, rows)
    return call(finish_kernel, shape((rows, wide), BF16), 10 * cells, 8 * cells, conv, skipped, scale, post_gate)


def solution(mesh):
    return jax.shard_map(
        local,
        mesh=mesh,
        in_specs=(
            P("seq", "chan"),
            P("seq", "chan"),
            P("seq", "chan"),
            P("chan"),
            P("chan"),
            P(None, "seq", None, "chan"),
        ),
        out_specs=P("seq", "chan"),
        check_vma=False,
    )
```

```python
import functools

import jax
import jax.numpy as jnp
import numpy as np
from jax import lax
from jax.experimental import pallas as pl
from jax.experimental.pallas import tpu as pltpu
from jax.sharding import PartitionSpec as P

EPS = 1e-06
BF16 = jnp.bfloat16
F32 = jnp.float32
VMEM_LIMIT = 48 * 1024 * 1024
WHOLE_VMEM = 63 * 1024 * 1024 + 512 * 1024


def order_of(places, back=False):
    if places != 8:
        return tuple(range(places))
    return (5, 3, 6, 2, 4, 0, 7, 1) if back else (4, 7, 3, 6, 2, 1, 5, 0)


def reverse_bits(index, levels):
    return sum((index >> bit & 1) << levels - 1 - bit for bit in range(levels))


@functools.lru_cache(maxsize=None)
def tables(places, rows, width):
    levels = places.bit_length() - 1
    stride = 2 * places
    bins = stride * rows
    residues = np.array([2 * reverse_bits(place, levels) + parity for place in range(places) for parity in range(2)])
    angle = 2.0 * np.pi * ((residues[:, None] * np.arange(places)[None, :]) % stride) / stride
    same = np.eye(width)
    first = np.concatenate([np.kron(np.cos(angle), same), np.kron(-np.sin(angle), same)])
    last = first.T / bins
    angle = 2.0 * np.pi * ((residues[:, None] * np.arange(rows)[None, :]) % bins) / bins
    twist = np.repeat(np.stack([np.cos(angle), np.sin(angle)]), width, axis=1)
    series = np.arange(rows)
    angle = 2.0 * np.pi * ((series[:, None] * series[None, :]) % rows) / rows
    dft = np.concatenate([np.cos(angle), np.sin(angle)])
    return (
        first.astype(jnp.bfloat16),
        last.astype(jnp.bfloat16),
        twist.astype(np.float32),
        dft.astype(jnp.bfloat16),
    )


def pair_rows(places):
    levels = places.bit_length() - 1

    def holder(residue):
        return order_of(places).index(reverse_bits(residue // 2, levels)), residue % 2

    mirrors = [None if residue % places == 0 else holder(2 * places - residue) for residue in range(places + 1)]
    return [holder(residue) for residue in range(places + 1)], mirrors


@functools.lru_cache(maxsize=None)
def folded_tables(places, rows, width):
    stride = 2 * places
    bins = stride * rows
    residues = np.arange(places + 1)
    angle = 2.0 * np.pi * ((residues[:, None] * np.arange(places)[None, :]) % stride) / stride
    parts = np.stack([np.cos(angle), -np.sin(angle)], axis=1)
    first = np.kron(parts.reshape(-1, places), np.eye(width))
    last = first.T / bins
    angle = 2.0 * np.pi * ((residues[:, None] * np.arange(rows)[None, :]) % bins) / bins
    twist = np.stack([np.cos(angle), np.sin(angle)])
    block = rows // 4
    series = np.arange(block)
    angle = 2.0 * np.pi * ((np.arange(4)[:, None] * series[None, :]) % rows) / rows
    spin = np.stack([np.cos(angle), np.sin(angle)])
    angle = 2.0 * np.pi * ((series[:, None] * series[None, :]) % block) / block
    cos, sin = np.cos(angle), np.sin(angle)
    there = np.block([[cos, -sin], [sin, cos]])
    back = np.block([[cos, sin], [-sin, cos]])
    reverse = np.eye(block)[::-1]
    return (
        first.astype(jnp.bfloat16),
        last.astype(jnp.bfloat16),
        twist.astype(np.float32),
        spin.astype(np.float32),
        np.stack([there, back]).astype(jnp.bfloat16),
        reverse.astype(jnp.bfloat16),
    )


def hops(places):
    return [[apart, apart + 1] for apart in range(0, places, 2)]


def prepare_kernel(
    features_ref,
    pre_ref,
    gain_ref,
    skip_ref,
    spectrum_ref,
    squares_ref,
    skipped_ref,
    packed_ref,
    features_in,
    pre_in,
    gain_in,
    skip_in,
    spectrum_in,
    squares_out,
    skipped_out,
    packed_out,
    in_sems,
    out_sems,
):
    blocks = [(part, parity) for part in range(2) for parity in range(2)]
    pairs = [(features_ref, features_in), (pre_ref, pre_in), (gain_ref, gain_in), (skip_ref, skip_in)]
    pairs += [(spectrum_ref.at[block], spectrum_in.at[block]) for block in blocks]
    arriving = [pltpu.make_async_copy(*pair, in_sems.at[slot]) for slot, pair in enumerate(pairs)]
    for copy in arriving:
        copy.start()
    leaving = []

    def leave(source, target):
        copy = pltpu.make_async_copy(source, target, out_sems.at[len(leaving)])
        copy.start()
        leaving.append(copy)

    def pack(slot, turned):
        if len(packed_ref.shape) == 4:
            places, width = packed_out.shape[1:3]
            for rank, place in enumerate(order_of(places)):
                packed_out[slot, rank] = turned[place * width : (place + 1) * width]
            leave(packed_out.at[slot], packed_ref.at[:, slot])
        else:
            packed_out[slot] = turned
            leave(packed_out.at[slot], packed_ref.at[slot])

    for copy in arriving[:4]:
        copy.wait()
    features = features_in[...].astype(F32)
    scaled = features * gain_in[...] * pre_in[...].astype(F32)
    pack(4, scaled.astype(BF16).T)
    skipped_out[...] = (scaled * skip_in[...]).astype(BF16).T
    leave(skipped_out, skipped_ref)
    turned = features_in[...].T.astype(F32)
    squares_out[...] = jnp.sum(turned * turned, axis=0, keepdims=True)
    leave(squares_out, squares_ref)
    for slot, block in enumerate(blocks):
        arriving[4 + slot].wait()
        if len(packed_ref.shape) == 4:
            quarter = spectrum_in.shape[2] // 4
            rows = [spectrum_in[(*block, pl.ds(turn, quarter, stride=4), slice(None))] for turn in range(4)]
            pack(slot, jnp.concatenate([row.astype(BF16).T for row in rows], axis=1))
        else:
            pack(slot, spectrum_in[block].astype(BF16).T)
    for copy in leaving:
        copy.wait()


def scale_kernel(channels, *refs):
    square_refs, scale_ref = refs[:-1], refs[-1]
    total = square_refs[0][...]
    for square_ref in square_refs[1:]:
        total = total + square_ref[...]
    scale_ref[...] = lax.rsqrt(total / channels + EPS)


def matmul(left, right):
    return jnp.dot(left, right, preferred_element_type=F32)


def butterfly(values, direction):
    (real0, imag0), (real1, imag1), (real2, imag2), (real3, imag3) = values
    even, odd = (real0 + real2, imag0 + imag2), (real1 + real3, imag1 + imag3)
    even_gap, odd_gap = (real0 - real2, imag0 - imag2), (real1 - real3, imag1 - imag3)
    lower = (even_gap[0] + odd_gap[1], even_gap[1] - odd_gap[0])
    upper = (even_gap[0] - odd_gap[1], even_gap[1] + odd_gap[0])
    total, gap = (even[0] + odd[0], even[1] + odd[1]), (even[0] - odd[0], even[1] - odd[1])
    return [total, lower, gap, upper] if direction > 0 else [total, upper, gap, lower]


def folded_kernel(packed_ref, first_ref, last_ref, twist_ref, spin_ref, dft_ref, reverse_ref, *refs):
    scale_refs, (out_ref, scales, signal, mirror, forward, backward, both) = refs[:-7], refs[-7:]
    wide, rows = out_ref.shape
    places, width = scales.shape[0], wide // scales.shape[0]
    block, inner = rows // 4, mirror.shape[0] // 8
    order = order_of(places)
    direct, mirrors = pair_rows(places)
    quarters = [pl.ds(turn * block, block) for turn in range(4)]
    groups = [range(begin, min(begin + 3, places + 1)) for begin in range(0, places + 1, 3)]
    for row, holder in enumerate(mirrors[1:places]):
        for part in range(2):
            for turn in range(4):
                at = pl.ds((part * 4 + 3 - turn) * inner + row * width, width)
                mirror[at, :] = packed_ref[holder[0], 2 * part + holder[1], :, quarters[turn]]
    reversed_bins = matmul(mirror[...], reverse_ref[...])
    place = lax.axis_index("seq")
    for scale_ref, steps in zip(scale_refs, hops(places)):
        for at, step in enumerate(steps):
            scales[place ^ step] = scale_ref[pl.ds(at, 1), :]
    for rank, at in enumerate(order):
        signal[pl.ds(at * width, width), :] = (packed_ref[rank, 4].astype(F32) * scales[at]).astype(BF16)
    spectral = []
    for group in groups:
        begin = group[0] * width
        mixed = matmul(first_ref[pl.ds(2 * begin, 2 * len(group) * width), :], signal[...])
        for at, residue in enumerate(group):
            over, under = mixed[2 * at * width : (2 * at + 1) * width], mixed[(2 * at + 1) * width : (2 * at + 2) * width]
            values = []
            for turn in range(4):
                real, imag = (part[:, turn * block : (turn + 1) * block] for part in (over, under))
                cos, sin = (twist_ref[part, pl.ds(residue, 1), quarters[turn]] for part in range(2))
                values.append((real * cos + imag * sin, imag * cos - real * sin))
            for turn, (real, imag) in enumerate(butterfly(values, 1)):
                if turn > 0:
                    cos, sin = spin_ref[0, pl.ds(turn, 1), :], spin_ref[1, pl.ds(turn, 1), :]
                    real, imag = real * cos + imag * sin, imag * cos - real * sin
                row = pl.ds(4 * begin + (turn * len(group) + at) * width, width)
                forward[row, pl.ds(0, block)] = real.astype(BF16)
                forward[row, pl.ds(block, block)] = imag.astype(BF16)
        spectral.append(matmul(forward[pl.ds(4 * begin, 4 * len(group) * width), :], dft_ref[0]))
    restored = []
    for group, values in zip(groups, spectral):
        begin = group[0] * width
        for turn in range(4):
            for at, residue in enumerate(group):
                row = (turn * len(group) + at) * width
                real, imag = values[row : row + width, :block], values[row : row + width, block:]
                holder = direct[residue]
                response_real = packed_ref[holder[0], holder[1], :, quarters[turn]].astype(F32)
                response_imag = packed_ref[holder[0], 2 + holder[1], :, quarters[turn]].astype(F32)
                if mirrors[residue] is not None:
                    other = turn * inner + (residue - 1) * width
                    response_real = response_real + reversed_bins[other : other + width]
                    other = other + 4 * inner
                    response_imag = response_imag - reversed_bins[other : other + width]
                target = pl.ds(4 * begin + row, width)
                backward[target, pl.ds(0, block)] = (real * response_real - imag * response_imag).astype(BF16)
                backward[target, pl.ds(block, block)] = (real * response_imag + imag * response_real).astype(BF16)
        restored.append(matmul(backward[pl.ds(4 * begin, 4 * len(group) * width), :], dft_ref[1]))
    for group, turned in zip(groups, restored):
        for at, residue in enumerate(group):
            values = []
            for turn in range(4):
                row = (turn * len(group) + at) * width
                real, imag = turned[row : row + width, :block], turned[row : row + width, block:]
                if turn > 0:
                    cos, sin = spin_ref[0, pl.ds(turn, 1), :], spin_ref[1, pl.ds(turn, 1), :]
                    real, imag = real * cos - imag * sin, imag * cos + real * sin
                values.append((real, imag))
            for lanes, (real, imag) in zip(quarters, butterfly(values, -1)):
                cos, sin = twist_ref[0, pl.ds(residue, 1), lanes], twist_ref[1, pl.ds(residue, 1), lanes]
                both[pl.ds(2 * residue * width, width), lanes] = (real * cos - imag * sin).astype(BF16)
                both[pl.ds((2 * residue + 1) * width, width), lanes] = (imag * cos + real * sin).astype(BF16)
    result = matmul(last_ref[...], both[...]).astype(BF16)
    for rank, at in enumerate(order_of(places, back=True)):
        out_ref[pl.ds(rank * width, width), :] = result[at * width : (at + 1) * width]


def convolve_kernel(packed_ref, first_ref, last_ref, twist_ref, dft_ref, scale_ref, out_ref, left, right):
    wide, rows = out_ref.shape
    half = 2 * wide
    signal = (packed_ref[4].astype(F32) * scale_ref[...]).astype(BF16)
    mixed = matmul(first_ref[...], signal)
    real, imag = mixed[:half], mixed[half:]
    cos_twist, sin_twist = twist_ref[0], twist_ref[1]
    turned_real = (real * cos_twist + imag * sin_twist).astype(BF16)
    turned_imag = (imag * cos_twist - real * sin_twist).astype(BF16)
    left[pl.ds(0, half), pl.ds(0, rows)] = turned_real
    left[pl.ds(0, half), pl.ds(rows, rows)] = turned_imag
    left[pl.ds(half, half), pl.ds(0, rows)] = turned_imag
    left[pl.ds(half, half), pl.ds(rows, rows)] = -turned_real
    mixed = matmul(left[...], dft_ref[...])
    real, imag = mixed[:half], mixed[half:]
    response_real = packed_ref[0:2].reshape(half, rows).astype(F32)
    response_imag = packed_ref[2:4].reshape(half, rows).astype(F32)
    product_real = (real * response_real - imag * response_imag).astype(BF16)
    product_imag = (real * response_imag + imag * response_real).astype(BF16)
    right[pl.ds(0, half), pl.ds(0, rows)] = product_real
    right[pl.ds(0, half), pl.ds(rows, rows)] = -product_imag
    right[pl.ds(half, half), pl.ds(0, rows)] = product_imag
    right[pl.ds(half, half), pl.ds(rows, rows)] = product_real
    mixed = matmul(right[...], dft_ref[...])
    real, imag = mixed[:half], mixed[half:]
    turned_real = (real * cos_twist - imag * sin_twist).astype(BF16)
    turned_imag = (imag * cos_twist + real * sin_twist).astype(BF16)
    both = jnp.concatenate([turned_real, turned_imag], axis=0)
    out_ref[...] = matmul(last_ref[...], both).astype(BF16)


def finish_kernel(conv_ref, skipped_ref, scale_ref, post_ref, out_ref):
    conv = conv_ref[...]
    if len(conv_ref.shape) == 3:
        order = order_of(conv_ref.shape[0], back=True)
        conv = jnp.concatenate([conv_ref[order.index(place)] for place in range(len(order))])
    turned = conv.astype(F32) + skipped_ref[...].astype(F32) * scale_ref[...]
    out_ref[...] = (post_ref[...].astype(F32) * turned.T).astype(BF16)


def call(kernel, out_shape, flops, moved, *operands, limit=VMEM_LIMIT, **options):
    return pl.pallas_call(
        kernel,
        out_shape=out_shape,
        compiler_params=pltpu.CompilerParams(vmem_limit_bytes=limit),
        cost_estimate=pl.CostEstimate(flops=flops, bytes_accessed=moved, transcendentals=0),
        **options,
    )(*operands)


def exchange(value, back=False):
    ranks = [list(order_of(lax.axis_size("seq"), back))]
    return lax.all_to_all(value, "seq", split_axis=0, concat_axis=0, tiled=True, axis_index_groups=ranks)


def swap(value, axis, apart):
    return lax.ppermute(value, axis, [(place, place ^ apart) for place in range(lax.axis_size(axis))])


def local(features, pre_gate, post_gate, norm_gain, skip_weight, spectrum):
    rows, wide = features.shape
    places = lax.axis_size("seq")
    groups = lax.axis_size("chan")
    width = wide // places
    piled = width % 16 == 0
    cells = rows * wide
    shape = jax.ShapeDtypeStruct
    vmem, anywhere = pl.BlockSpec(memory_space=pltpu.VMEM), pl.BlockSpec(memory_space=pl.ANY)
    squares, skipped, packed = call(
        prepare_kernel,
        (
            shape((1, rows), F32),
            shape((wide, rows), BF16),
            shape((places, 5, width, rows) if piled else (5, wide, rows), BF16),
        ),
        10 * cells,
        32 * cells,
        features,
        pre_gate,
        norm_gain[None, :],
        skip_weight[None, :],
        spectrum,
        limit=WHOLE_VMEM,
        in_specs=[anywhere] * 5,
        out_specs=(anywhere, anywhere, anywhere),
        scratch_shapes=[
            pltpu.VMEM(features.shape, BF16),
            pltpu.VMEM(pre_gate.shape, BF16),
            pltpu.VMEM((1, wide), F32),
            pltpu.VMEM((1, wide), F32),
            pltpu.VMEM(spectrum.shape, F32),
            pltpu.VMEM((1, rows), F32),
            pltpu.VMEM((wide, rows), BF16),
            pltpu.VMEM((5, places, width, rows) if piled else (5, wide, rows), BF16),
            pltpu.SemaphoreType.DMA((8,)),
            pltpu.SemaphoreType.DMA((7,)),
        ],
    )
    if not piled:
        packed = packed.reshape(5, places, width, rows).transpose(1, 0, 2, 3)
    gathered = exchange(packed)
    others = [swap(squares, "chan", apart) for apart in range(1, groups)]
    scale = call(
        functools.partial(scale_kernel, wide * groups), shape((1, rows), F32), 8 * rows, 32 * rows, squares, *others
    )
    if piled:
        near = jnp.concatenate([scale, swap(scale, "seq", 1)])
        scales = [near] + [swap(near, "seq", steps[0]) for steps in hops(places)[1:]]
    else:
        scales = [jnp.repeat(lax.all_gather(scale, "seq", axis=0, tiled=True), width, axis=0)]
        response = gathered[:, :4].reshape(places, 2, 2, width, rows).transpose(1, 0, 2, 3, 4)
        gathered = jnp.concatenate([response.reshape(4, wide, rows), gathered[:, 4].reshape(1, wide, rows)])
    if piled:
        constants = folded_tables(places, rows, width)
        half = constants[0].shape[0] // 2
        scratch = [
            pltpu.VMEM((places, 1, rows), F32),
            pltpu.VMEM((wide, rows), BF16),
            pltpu.VMEM((8 * (half - 2 * width), rows // 4), BF16),
            pltpu.VMEM((4 * half, rows // 2), BF16),
            pltpu.VMEM((4 * half, rows // 2), BF16),
            pltpu.VMEM((2 * half, rows), BF16),
        ]
    else:
        constants = tables(places, rows, width)
        scratch = [pltpu.VMEM((4 * wide, 2 * rows), BF16)] * 2
    conv = call(
        folded_kernel if piled else convolve_kernel,
        shape((wide, rows), BF16),
        20 * cells * rows,
        20 * cells,
        gathered,
        *constants,
        *scales,
        scratch_shapes=scratch,
    )
    conv = exchange(conv.reshape(places, width, rows), back=True)
    if not piled:
        conv = conv.reshape(wide, rows)
    return call(finish_kernel, shape((rows, wide), BF16), 10 * cells, 8 * cells, conv, skipped, scale, post_gate)


def solution(mesh):
    return jax.shard_map(
        local,
        mesh=mesh,
        in_specs=(
            P("seq", "chan"),
            P("seq", "chan"),
            P("seq", "chan"),
            P("chan"),
            P("chan"),
            P(None, "seq", None, "chan"),
        ),
        out_specs=P("seq", "chan"),
        check_vma=False,
    )
```

```python
import functools

import jax
import jax.numpy as jnp
import numpy as np
from jax import lax
from jax.experimental import pallas as pl
from jax.experimental.pallas import tpu as pltpu
from jax.sharding import PartitionSpec as P

EPS = 1e-06
BF16 = jnp.bfloat16
F32 = jnp.float32
VMEM_LIMIT = 48 * 1024 * 1024
WHOLE_VMEM = 63 * 1024 * 1024 + 512 * 1024


def order_of(places, back=False):
    if places != 8:
        return tuple(range(places))
    return (5, 1, 3, 6, 2, 4, 0, 7) if back else (5, 6, 2, 7, 3, 0, 4, 1)


def reverse_bits(index, levels):
    return sum((index >> bit & 1) << levels - 1 - bit for bit in range(levels))


@functools.lru_cache(maxsize=None)
def tables(places, rows, width):
    levels = places.bit_length() - 1
    stride = 2 * places
    bins = stride * rows
    residues = np.array([2 * reverse_bits(place, levels) + parity for place in range(places) for parity in range(2)])
    angle = 2.0 * np.pi * ((residues[:, None] * np.arange(places)[None, :]) % stride) / stride
    same = np.eye(width)
    first = np.concatenate([np.kron(np.cos(angle), same), np.kron(-np.sin(angle), same)])
    last = first.T / bins
    angle = 2.0 * np.pi * ((residues[:, None] * np.arange(rows)[None, :]) % bins) / bins
    twist = np.repeat(np.stack([np.cos(angle), np.sin(angle)]), width, axis=1)
    series = np.arange(rows)
    angle = 2.0 * np.pi * ((series[:, None] * series[None, :]) % rows) / rows
    dft = np.concatenate([np.cos(angle), np.sin(angle)])
    return (
        first.astype(jnp.bfloat16),
        last.astype(jnp.bfloat16),
        twist.astype(np.float32),
        dft.astype(jnp.bfloat16),
    )


def pair_rows(places):
    levels = places.bit_length() - 1

    def holder(residue):
        return order_of(places).index(reverse_bits(residue // 2, levels)), residue % 2

    mirrors = [None if residue % places == 0 else holder(2 * places - residue) for residue in range(places + 1)]
    return [holder(residue) for residue in range(places + 1)], mirrors


@functools.lru_cache(maxsize=None)
def folded_tables(places, rows, width):
    stride = 2 * places
    bins = stride * rows
    residues = np.arange(places + 1)
    angle = 2.0 * np.pi * ((residues[:, None] * np.arange(places)[None, :]) % stride) / stride
    parts = np.stack([np.cos(angle), -np.sin(angle)], axis=1)
    first = np.kron(parts.reshape(-1, places), np.eye(width))
    last = first.T / bins
    angle = 2.0 * np.pi * ((residues[:, None] * np.arange(rows)[None, :]) % bins) / bins
    twist = np.stack([np.cos(angle), np.sin(angle)])
    block = rows // 4
    series = np.arange(block)
    angle = 2.0 * np.pi * ((np.arange(4)[:, None] * series[None, :]) % rows) / rows
    spin = np.stack([np.cos(angle), np.sin(angle)])
    angle = 2.0 * np.pi * ((series[:, None] * series[None, :]) % block) / block
    cos, sin = np.cos(angle), np.sin(angle)
    there = np.block([[cos, -sin], [sin, cos]])
    back = np.block([[cos, sin], [-sin, cos]])
    reverse = np.eye(block)[::-1]
    return (
        first.astype(jnp.bfloat16),
        last.astype(jnp.bfloat16),
        twist.astype(np.float32),
        spin.astype(np.float32),
        np.stack([there, back]).astype(jnp.bfloat16),
        reverse.astype(jnp.bfloat16),
    )


def hops(places):
    return [[apart, apart + 1] for apart in range(0, places, 2)]


def prepare_kernel(
    features_ref,
    pre_ref,
    gain_ref,
    skip_ref,
    spectrum_ref,
    squares_ref,
    skipped_ref,
    packed_ref,
    features_in,
    pre_in,
    gain_in,
    skip_in,
    spectrum_in,
    squares_out,
    skipped_out,
    packed_out,
    in_sems,
    out_sems,
):
    blocks = [(part, parity) for part in range(2) for parity in range(2)]
    pairs = [(features_ref, features_in), (pre_ref, pre_in), (gain_ref, gain_in), (skip_ref, skip_in)]
    pairs += [(spectrum_ref.at[block], spectrum_in.at[block]) for block in blocks]
    arriving = [pltpu.make_async_copy(*pair, in_sems.at[slot]) for slot, pair in enumerate(pairs)]
    for copy in arriving:
        copy.start()
    leaving = []

    def leave(source, target):
        copy = pltpu.make_async_copy(source, target, out_sems.at[len(leaving)])
        copy.start()
        leaving.append(copy)

    def pack(slot, turned):
        if len(packed_ref.shape) == 4:
            places, width = packed_out.shape[1:3]
            for rank, place in enumerate(order_of(places)):
                packed_out[slot, rank] = turned[place * width : (place + 1) * width]
            leave(packed_out.at[slot], packed_ref.at[:, slot])
        else:
            packed_out[slot] = turned
            leave(packed_out.at[slot], packed_ref.at[slot])

    for copy in arriving[:4]:
        copy.wait()
    features = features_in[...].astype(F32)
    scaled = features * gain_in[...] * pre_in[...].astype(F32)
    pack(4, scaled.astype(BF16).T)
    skipped_out[...] = (scaled * skip_in[...]).astype(BF16).T
    leave(skipped_out, skipped_ref)
    turned = features_in[...].T.astype(F32)
    squares_out[...] = jnp.sum(turned * turned, axis=0, keepdims=True)
    leave(squares_out, squares_ref)
    for slot, block in enumerate(blocks):
        arriving[4 + slot].wait()
        if len(packed_ref.shape) == 4:
            quarter = spectrum_in.shape[2] // 4
            rows = [spectrum_in[(*block, pl.ds(turn, quarter, stride=4), slice(None))] for turn in range(4)]
            pack(slot, jnp.concatenate([row.astype(BF16).T for row in rows], axis=1))
        else:
            pack(slot, spectrum_in[block].astype(BF16).T)
    for copy in leaving:
        copy.wait()


def scale_kernel(channels, *refs):
    square_refs, scale_ref = refs[:-1], refs[-1]
    total = square_refs[0][...]
    for square_ref in square_refs[1:]:
        total = total + square_ref[...]
    scale_ref[...] = lax.rsqrt(total / channels + EPS)


def matmul(left, right):
    return jnp.dot(left, right, preferred_element_type=F32)


def butterfly(values, direction):
    (real0, imag0), (real1, imag1), (real2, imag2), (real3, imag3) = values
    even, odd = (real0 + real2, imag0 + imag2), (real1 + real3, imag1 + imag3)
    even_gap, odd_gap = (real0 - real2, imag0 - imag2), (real1 - real3, imag1 - imag3)
    lower = (even_gap[0] + odd_gap[1], even_gap[1] - odd_gap[0])
    upper = (even_gap[0] - odd_gap[1], even_gap[1] + odd_gap[0])
    total, gap = (even[0] + odd[0], even[1] + odd[1]), (even[0] - odd[0], even[1] - odd[1])
    return [total, lower, gap, upper] if direction > 0 else [total, upper, gap, lower]


def folded_kernel(packed_ref, first_ref, last_ref, twist_ref, spin_ref, dft_ref, reverse_ref, *refs):
    scale_refs, (out_ref, scales, signal, mirror, forward, backward, both) = refs[:-7], refs[-7:]
    wide, rows = out_ref.shape
    places, width = scales.shape[0], wide // scales.shape[0]
    block, inner = rows // 4, mirror.shape[0] // 8
    order = order_of(places)
    direct, mirrors = pair_rows(places)
    quarters = [pl.ds(turn * block, block) for turn in range(4)]
    groups = [range(begin, min(begin + 3, places + 1)) for begin in range(0, places + 1, 3)]
    for row, holder in enumerate(mirrors[1:places]):
        for part in range(2):
            for turn in range(4):
                at = pl.ds((part * 4 + 3 - turn) * inner + row * width, width)
                mirror[at, :] = packed_ref[holder[0], 2 * part + holder[1], :, quarters[turn]]
    reversed_bins = matmul(mirror[...], reverse_ref[...])
    place = lax.axis_index("seq")
    for scale_ref, steps in zip(scale_refs, hops(places)):
        for at, step in enumerate(steps):
            scales[place ^ step] = scale_ref[pl.ds(at, 1), :]
    for rank, at in enumerate(order):
        signal[pl.ds(at * width, width), :] = (packed_ref[rank, 4].astype(F32) * scales[at]).astype(BF16)
    spectral = []
    for group in groups:
        begin = group[0] * width
        mixed = matmul(first_ref[pl.ds(2 * begin, 2 * len(group) * width), :], signal[...])
        for at, residue in enumerate(group):
            over, under = mixed[2 * at * width : (2 * at + 1) * width], mixed[(2 * at + 1) * width : (2 * at + 2) * width]
            values = []
            for turn in range(4):
                real, imag = (part[:, turn * block : (turn + 1) * block] for part in (over, under))
                cos, sin = (twist_ref[part, pl.ds(residue, 1), quarters[turn]] for part in range(2))
                values.append((real * cos + imag * sin, imag * cos - real * sin))
            for turn, (real, imag) in enumerate(butterfly(values, 1)):
                if turn > 0:
                    cos, sin = spin_ref[0, pl.ds(turn, 1), :], spin_ref[1, pl.ds(turn, 1), :]
                    real, imag = real * cos + imag * sin, imag * cos - real * sin
                row = pl.ds(4 * begin + (turn * len(group) + at) * width, width)
                forward[row, pl.ds(0, block)] = real.astype(BF16)
                forward[row, pl.ds(block, block)] = imag.astype(BF16)
        spectral.append(matmul(forward[pl.ds(4 * begin, 4 * len(group) * width), :], dft_ref[0]))
    restored = []
    for group, values in zip(groups, spectral):
        begin = group[0] * width
        for turn in range(4):
            for at, residue in enumerate(group):
                row = (turn * len(group) + at) * width
                real, imag = values[row : row + width, :block], values[row : row + width, block:]
                holder = direct[residue]
                response_real = packed_ref[holder[0], holder[1], :, quarters[turn]].astype(F32)
                response_imag = packed_ref[holder[0], 2 + holder[1], :, quarters[turn]].astype(F32)
                if mirrors[residue] is not None:
                    other = turn * inner + (residue - 1) * width
                    response_real = response_real + reversed_bins[other : other + width]
                    other = other + 4 * inner
                    response_imag = response_imag - reversed_bins[other : other + width]
                target = pl.ds(4 * begin + row, width)
                backward[target, pl.ds(0, block)] = (real * response_real - imag * response_imag).astype(BF16)
                backward[target, pl.ds(block, block)] = (real * response_imag + imag * response_real).astype(BF16)
        restored.append(matmul(backward[pl.ds(4 * begin, 4 * len(group) * width), :], dft_ref[1]))
    for group, turned in zip(groups, restored):
        for at, residue in enumerate(group):
            values = []
            for turn in range(4):
                row = (turn * len(group) + at) * width
                real, imag = turned[row : row + width, :block], turned[row : row + width, block:]
                if turn > 0:
                    cos, sin = spin_ref[0, pl.ds(turn, 1), :], spin_ref[1, pl.ds(turn, 1), :]
                    real, imag = real * cos - imag * sin, imag * cos + real * sin
                values.append((real, imag))
            for lanes, (real, imag) in zip(quarters, butterfly(values, -1)):
                cos, sin = twist_ref[0, pl.ds(residue, 1), lanes], twist_ref[1, pl.ds(residue, 1), lanes]
                both[pl.ds(2 * residue * width, width), lanes] = (real * cos - imag * sin).astype(BF16)
                both[pl.ds((2 * residue + 1) * width, width), lanes] = (imag * cos + real * sin).astype(BF16)
    result = matmul(last_ref[...], both[...]).astype(BF16)
    for rank, at in enumerate(order_of(places, back=True)):
        out_ref[pl.ds(rank * width, width), :] = result[at * width : (at + 1) * width]


def convolve_kernel(packed_ref, first_ref, last_ref, twist_ref, dft_ref, scale_ref, out_ref, left, right):
    wide, rows = out_ref.shape
    half = 2 * wide
    signal = (packed_ref[4].astype(F32) * scale_ref[...]).astype(BF16)
    mixed = matmul(first_ref[...], signal)
    real, imag = mixed[:half], mixed[half:]
    cos_twist, sin_twist = twist_ref[0], twist_ref[1]
    turned_real = (real * cos_twist + imag * sin_twist).astype(BF16)
    turned_imag = (imag * cos_twist - real * sin_twist).astype(BF16)
    left[pl.ds(0, half), pl.ds(0, rows)] = turned_real
    left[pl.ds(0, half), pl.ds(rows, rows)] = turned_imag
    left[pl.ds(half, half), pl.ds(0, rows)] = turned_imag
    left[pl.ds(half, half), pl.ds(rows, rows)] = -turned_real
    mixed = matmul(left[...], dft_ref[...])
    real, imag = mixed[:half], mixed[half:]
    response_real = packed_ref[0:2].reshape(half, rows).astype(F32)
    response_imag = packed_ref[2:4].reshape(half, rows).astype(F32)
    product_real = (real * response_real - imag * response_imag).astype(BF16)
    product_imag = (real * response_imag + imag * response_real).astype(BF16)
    right[pl.ds(0, half), pl.ds(0, rows)] = product_real
    right[pl.ds(0, half), pl.ds(rows, rows)] = -product_imag
    right[pl.ds(half, half), pl.ds(0, rows)] = product_imag
    right[pl.ds(half, half), pl.ds(rows, rows)] = product_real
    mixed = matmul(right[...], dft_ref[...])
    real, imag = mixed[:half], mixed[half:]
    turned_real = (real * cos_twist - imag * sin_twist).astype(BF16)
    turned_imag = (imag * cos_twist + real * sin_twist).astype(BF16)
    both = jnp.concatenate([turned_real, turned_imag], axis=0)
    out_ref[...] = matmul(last_ref[...], both).astype(BF16)


def finish_kernel(conv_ref, skipped_ref, scale_ref, post_ref, out_ref):
    conv = conv_ref[...]
    if len(conv_ref.shape) == 3:
        order = order_of(conv_ref.shape[0], back=True)
        conv = jnp.concatenate([conv_ref[order.index(place)] for place in range(len(order))])
    turned = conv.astype(F32) + skipped_ref[...].astype(F32) * scale_ref[...]
    out_ref[...] = (post_ref[...].astype(F32) * turned.T).astype(BF16)


def call(kernel, out_shape, flops, moved, *operands, limit=VMEM_LIMIT, **options):
    return pl.pallas_call(
        kernel,
        out_shape=out_shape,
        compiler_params=pltpu.CompilerParams(vmem_limit_bytes=limit),
        cost_estimate=pl.CostEstimate(flops=flops, bytes_accessed=moved, transcendentals=0),
        **options,
    )(*operands)


def exchange(value, back=False):
    ranks = [list(order_of(lax.axis_size("seq"), back))]
    return lax.all_to_all(value, "seq", split_axis=0, concat_axis=0, tiled=True, axis_index_groups=ranks)


def swap(value, axis, apart):
    return lax.ppermute(value, axis, [(place, place ^ apart) for place in range(lax.axis_size(axis))])


def local(features, pre_gate, post_gate, norm_gain, skip_weight, spectrum):
    rows, wide = features.shape
    places = lax.axis_size("seq")
    groups = lax.axis_size("chan")
    width = wide // places
    piled = width % 16 == 0
    cells = rows * wide
    shape = jax.ShapeDtypeStruct
    vmem, anywhere = pl.BlockSpec(memory_space=pltpu.VMEM), pl.BlockSpec(memory_space=pl.ANY)
    squares, skipped, packed = call(
        prepare_kernel,
        (
            shape((1, rows), F32),
            shape((wide, rows), BF16),
            shape((places, 5, width, rows) if piled else (5, wide, rows), BF16),
        ),
        10 * cells,
        32 * cells,
        features,
        pre_gate,
        norm_gain[None, :],
        skip_weight[None, :],
        spectrum,
        limit=WHOLE_VMEM,
        in_specs=[anywhere] * 5,
        out_specs=(anywhere, anywhere, anywhere),
        scratch_shapes=[
            pltpu.VMEM(features.shape, BF16),
            pltpu.VMEM(pre_gate.shape, BF16),
            pltpu.VMEM((1, wide), F32),
            pltpu.VMEM((1, wide), F32),
            pltpu.VMEM(spectrum.shape, F32),
            pltpu.VMEM((1, rows), F32),
            pltpu.VMEM((wide, rows), BF16),
            pltpu.VMEM((5, places, width, rows) if piled else (5, wide, rows), BF16),
            pltpu.SemaphoreType.DMA((8,)),
            pltpu.SemaphoreType.DMA((7,)),
        ],
    )
    if not piled:
        packed = packed.reshape(5, places, width, rows).transpose(1, 0, 2, 3)
    gathered = exchange(packed)
    others = [swap(squares, "chan", apart) for apart in range(1, groups)]
    scale = call(
        functools.partial(scale_kernel, wide * groups), shape((1, rows), F32), 8 * rows, 32 * rows, squares, *others
    )
    if piled:
        near = jnp.concatenate([scale, swap(scale, "seq", 1)])
        scales = [near] + [swap(near, "seq", steps[0]) for steps in hops(places)[1:]]
    else:
        scales = [jnp.repeat(lax.all_gather(scale, "seq", axis=0, tiled=True), width, axis=0)]
        response = gathered[:, :4].reshape(places, 2, 2, width, rows).transpose(1, 0, 2, 3, 4)
        gathered = jnp.concatenate([response.reshape(4, wide, rows), gathered[:, 4].reshape(1, wide, rows)])
    if piled:
        constants = folded_tables(places, rows, width)
        half = constants[0].shape[0] // 2
        scratch = [
            pltpu.VMEM((places, 1, rows), F32),
            pltpu.VMEM((wide, rows), BF16),
            pltpu.VMEM((8 * (half - 2 * width), rows // 4), BF16),
            pltpu.VMEM((4 * half, rows // 2), BF16),
            pltpu.VMEM((4 * half, rows // 2), BF16),
            pltpu.VMEM((2 * half, rows), BF16),
        ]
    else:
        constants = tables(places, rows, width)
        scratch = [pltpu.VMEM((4 * wide, 2 * rows), BF16)] * 2
    conv = call(
        folded_kernel if piled else convolve_kernel,
        shape((wide, rows), BF16),
        20 * cells * rows,
        20 * cells,
        gathered,
        *constants,
        *scales,
        scratch_shapes=scratch,
    )
    conv = exchange(conv.reshape(places, width, rows), back=True)
    if not piled:
        conv = conv.reshape(wide, rows)
    return call(finish_kernel, shape((rows, wide), BF16), 10 * cells, 8 * cells, conv, skipped, scale, post_gate)


def solution(mesh):
    return jax.shard_map(
        local,
        mesh=mesh,
        in_specs=(
            P("seq", "chan"),
            P("seq", "chan"),
            P("seq", "chan"),
            P("chan"),
            P("chan"),
            P(None, "seq", None, "chan"),
        ),
        out_specs=P("seq", "chan"),
        check_vma=False,
    )
```

```python
import functools

import jax
import jax.numpy as jnp
import numpy as np
from jax import lax
from jax.experimental import pallas as pl
from jax.experimental.pallas import tpu as pltpu
from jax.sharding import PartitionSpec as P

EPS = 1e-06
BF16 = jnp.bfloat16
F32 = jnp.float32
VMEM_LIMIT = 48 * 1024 * 1024
WHOLE_VMEM = 63 * 1024 * 1024 + 512 * 1024


def order_of(places, back=False):
    if places != 8:
        return tuple(range(places))
    return (5, 1, 3, 6, 2, 4, 0, 7) if back else (4, 7, 3, 6, 2, 1, 5, 0)


def reverse_bits(index, levels):
    return sum((index >> bit & 1) << levels - 1 - bit for bit in range(levels))


@functools.lru_cache(maxsize=None)
def tables(places, rows, width):
    levels = places.bit_length() - 1
    stride = 2 * places
    bins = stride * rows
    residues = np.array([2 * reverse_bits(place, levels) + parity for place in range(places) for parity in range(2)])
    angle = 2.0 * np.pi * ((residues[:, None] * np.arange(places)[None, :]) % stride) / stride
    same = np.eye(width)
    first = np.concatenate([np.kron(np.cos(angle), same), np.kron(-np.sin(angle), same)])
    last = first.T / bins
    angle = 2.0 * np.pi * ((residues[:, None] * np.arange(rows)[None, :]) % bins) / bins
    twist = np.repeat(np.stack([np.cos(angle), np.sin(angle)]), width, axis=1)
    series = np.arange(rows)
    angle = 2.0 * np.pi * ((series[:, None] * series[None, :]) % rows) / rows
    dft = np.concatenate([np.cos(angle), np.sin(angle)])
    return (
        first.astype(jnp.bfloat16),
        last.astype(jnp.bfloat16),
        twist.astype(np.float32),
        dft.astype(jnp.bfloat16),
    )


def pair_rows(places):
    levels = places.bit_length() - 1

    def holder(residue):
        return order_of(places).index(reverse_bits(residue // 2, levels)), residue % 2

    mirrors = [None if residue % places == 0 else holder(2 * places - residue) for residue in range(places + 1)]
    return [holder(residue) for residue in range(places + 1)], mirrors


@functools.lru_cache(maxsize=None)
def folded_tables(places, rows, width):
    stride = 2 * places
    bins = stride * rows
    residues = np.arange(places + 1)
    angle = 2.0 * np.pi * ((residues[:, None] * np.arange(places)[None, :]) % stride) / stride
    parts = np.stack([np.cos(angle), -np.sin(angle)], axis=1)
    first = np.kron(parts.reshape(-1, places), np.eye(width))
    last = first.T / bins
    angle = 2.0 * np.pi * ((residues[:, None] * np.arange(rows)[None, :]) % bins) / bins
    twist = np.stack([np.cos(angle), np.sin(angle)])
    block = rows // 4
    series = np.arange(block)
    angle = 2.0 * np.pi * ((np.arange(4)[:, None] * series[None, :]) % rows) / rows
    spin = np.stack([np.cos(angle), np.sin(angle)])
    angle = 2.0 * np.pi * ((series[:, None] * series[None, :]) % block) / block
    cos, sin = np.cos(angle), np.sin(angle)
    there = np.block([[cos, -sin], [sin, cos]])
    back = np.block([[cos, sin], [-sin, cos]])
    reverse = np.eye(block)[::-1]
    return (
        first.astype(jnp.bfloat16),
        last.astype(jnp.bfloat16),
        twist.astype(np.float32),
        spin.astype(np.float32),
        np.stack([there, back]).astype(jnp.bfloat16),
        reverse.astype(jnp.bfloat16),
    )


def hops(places):
    return [[apart, apart + 1] for apart in range(0, places, 2)]


def prepare_kernel(
    features_ref,
    pre_ref,
    gain_ref,
    skip_ref,
    spectrum_ref,
    squares_ref,
    skipped_ref,
    packed_ref,
    features_in,
    pre_in,
    gain_in,
    skip_in,
    spectrum_in,
    squares_out,
    skipped_out,
    packed_out,
    in_sems,
    out_sems,
):
    blocks = [(part, parity) for part in range(2) for parity in range(2)]
    pairs = [(features_ref, features_in), (pre_ref, pre_in), (gain_ref, gain_in), (skip_ref, skip_in)]
    pairs += [(spectrum_ref.at[block], spectrum_in.at[block]) for block in blocks]
    arriving = [pltpu.make_async_copy(*pair, in_sems.at[slot]) for slot, pair in enumerate(pairs)]
    for copy in arriving:
        copy.start()
    leaving = []

    def leave(source, target):
        copy = pltpu.make_async_copy(source, target, out_sems.at[len(leaving)])
        copy.start()
        leaving.append(copy)

    def pack(slot, turned):
        if len(packed_ref.shape) == 4:
            places, width = packed_out.shape[1:3]
            for rank, place in enumerate(order_of(places)):
                packed_out[slot, rank] = turned[place * width : (place + 1) * width]
            leave(packed_out.at[slot], packed_ref.at[:, slot])
        else:
            packed_out[slot] = turned
            leave(packed_out.at[slot], packed_ref.at[slot])

    for copy in arriving[:4]:
        copy.wait()
    features = features_in[...].astype(F32)
    scaled = features * gain_in[...] * pre_in[...].astype(F32)
    pack(4, scaled.astype(BF16).T)
    skipped_out[...] = (scaled * skip_in[...]).astype(BF16).T
    leave(skipped_out, skipped_ref)
    turned = features_in[...].T.astype(F32)
    squares_out[...] = jnp.sum(turned * turned, axis=0, keepdims=True)
    leave(squares_out, squares_ref)
    for slot, block in enumerate(blocks):
        arriving[4 + slot].wait()
        if len(packed_ref.shape) == 4:
            quarter = spectrum_in.shape[2] // 4
            rows = [spectrum_in[(*block, pl.ds(turn, quarter, stride=4), slice(None))] for turn in range(4)]
            pack(slot, jnp.concatenate([row.astype(BF16).T for row in rows], axis=1))
        else:
            pack(slot, spectrum_in[block].astype(BF16).T)
    for copy in leaving:
        copy.wait()


def scale_kernel(channels, *refs):
    square_refs, scale_ref = refs[:-1], refs[-1]
    total = square_refs[0][...]
    for square_ref in square_refs[1:]:
        total = total + square_ref[...]
    scale_ref[...] = lax.rsqrt(total / channels + EPS)


def matmul(left, right):
    return jnp.dot(left, right, preferred_element_type=F32)


def butterfly(values, direction):
    (real0, imag0), (real1, imag1), (real2, imag2), (real3, imag3) = values
    even, odd = (real0 + real2, imag0 + imag2), (real1 + real3, imag1 + imag3)
    even_gap, odd_gap = (real0 - real2, imag0 - imag2), (real1 - real3, imag1 - imag3)
    lower = (even_gap[0] + odd_gap[1], even_gap[1] - odd_gap[0])
    upper = (even_gap[0] - odd_gap[1], even_gap[1] + odd_gap[0])
    total, gap = (even[0] + odd[0], even[1] + odd[1]), (even[0] - odd[0], even[1] - odd[1])
    return [total, lower, gap, upper] if direction > 0 else [total, upper, gap, lower]


def folded_kernel(packed_ref, first_ref, last_ref, twist_ref, spin_ref, dft_ref, reverse_ref, *refs):
    scale_refs, (out_ref, scales, signal, mirror, forward, backward, both) = refs[:-7], refs[-7:]
    wide, rows = out_ref.shape
    places, width = scales.shape[0], wide // scales.shape[0]
    block, inner = rows // 4, mirror.shape[0] // 8
    order = order_of(places)
    direct, mirrors = pair_rows(places)
    quarters = [pl.ds(turn * block, block) for turn in range(4)]
    groups = [range(begin, min(begin + 3, places + 1)) for begin in range(0, places + 1, 3)]
    for row, holder in enumerate(mirrors[1:places]):
        for part in range(2):
            for turn in range(4):
                at = pl.ds((part * 4 + 3 - turn) * inner + row * width, width)
                mirror[at, :] = packed_ref[holder[0], 2 * part + holder[1], :, quarters[turn]]
    reversed_bins = matmul(mirror[...], reverse_ref[...])
    place = lax.axis_index("seq")
    for scale_ref, steps in zip(scale_refs, hops(places)):
        for at, step in enumerate(steps):
            scales[place ^ step] = scale_ref[pl.ds(at, 1), :]
    for rank, at in enumerate(order):
        signal[pl.ds(at * width, width), :] = (packed_ref[rank, 4].astype(F32) * scales[at]).astype(BF16)
    spectral = []
    for group in groups:
        begin = group[0] * width
        mixed = matmul(first_ref[pl.ds(2 * begin, 2 * len(group) * width), :], signal[...])
        for at, residue in enumerate(group):
            over, under = mixed[2 * at * width : (2 * at + 1) * width], mixed[(2 * at + 1) * width : (2 * at + 2) * width]
            values = []
            for turn in range(4):
                real, imag = (part[:, turn * block : (turn + 1) * block] for part in (over, under))
                cos, sin = (twist_ref[part, pl.ds(residue, 1), quarters[turn]] for part in range(2))
                values.append((real * cos + imag * sin, imag * cos - real * sin))
            for turn, (real, imag) in enumerate(butterfly(values, 1)):
                if turn > 0:
                    cos, sin = spin_ref[0, pl.ds(turn, 1), :], spin_ref[1, pl.ds(turn, 1), :]
                    real, imag = real * cos + imag * sin, imag * cos - real * sin
                row = pl.ds(4 * begin + (turn * len(group) + at) * width, width)
                forward[row, pl.ds(0, block)] = real.astype(BF16)
                forward[row, pl.ds(block, block)] = imag.astype(BF16)
        spectral.append(matmul(forward[pl.ds(4 * begin, 4 * len(group) * width), :], dft_ref[0]))
    restored = []
    for group, values in zip(groups, spectral):
        begin = group[0] * width
        for turn in range(4):
            for at, residue in enumerate(group):
                row = (turn * len(group) + at) * width
                real, imag = values[row : row + width, :block], values[row : row + width, block:]
                holder = direct[residue]
                response_real = packed_ref[holder[0], holder[1], :, quarters[turn]].astype(F32)
                response_imag = packed_ref[holder[0], 2 + holder[1], :, quarters[turn]].astype(F32)
                if mirrors[residue] is not None:
                    other = turn * inner + (residue - 1) * width
                    response_real = response_real + reversed_bins[other : other + width]
                    other = other + 4 * inner
                    response_imag = response_imag - reversed_bins[other : other + width]
                target = pl.ds(4 * begin + row, width)
                backward[target, pl.ds(0, block)] = (real * response_real - imag * response_imag).astype(BF16)
                backward[target, pl.ds(block, block)] = (real * response_imag + imag * response_real).astype(BF16)
        restored.append(matmul(backward[pl.ds(4 * begin, 4 * len(group) * width), :], dft_ref[1]))
    for group, turned in zip(groups, restored):
        for at, residue in enumerate(group):
            values = []
            for turn in range(4):
                row = (turn * len(group) + at) * width
                real, imag = turned[row : row + width, :block], turned[row : row + width, block:]
                if turn > 0:
                    cos, sin = spin_ref[0, pl.ds(turn, 1), :], spin_ref[1, pl.ds(turn, 1), :]
                    real, imag = real * cos - imag * sin, imag * cos + real * sin
                values.append((real, imag))
            for lanes, (real, imag) in zip(quarters, butterfly(values, -1)):
                cos, sin = twist_ref[0, pl.ds(residue, 1), lanes], twist_ref[1, pl.ds(residue, 1), lanes]
                both[pl.ds(2 * residue * width, width), lanes] = (real * cos - imag * sin).astype(BF16)
                both[pl.ds((2 * residue + 1) * width, width), lanes] = (imag * cos + real * sin).astype(BF16)
    result = matmul(last_ref[...], both[...]).astype(BF16)
    for rank, at in enumerate(order_of(places, back=True)):
        out_ref[pl.ds(rank * width, width), :] = result[at * width : (at + 1) * width]


def convolve_kernel(packed_ref, first_ref, last_ref, twist_ref, dft_ref, scale_ref, out_ref, left, right):
    wide, rows = out_ref.shape
    half = 2 * wide
    signal = (packed_ref[4].astype(F32) * scale_ref[...]).astype(BF16)
    mixed = matmul(first_ref[...], signal)
    real, imag = mixed[:half], mixed[half:]
    cos_twist, sin_twist = twist_ref[0], twist_ref[1]
    turned_real = (real * cos_twist + imag * sin_twist).astype(BF16)
    turned_imag = (imag * cos_twist - real * sin_twist).astype(BF16)
    left[pl.ds(0, half), pl.ds(0, rows)] = turned_real
    left[pl.ds(0, half), pl.ds(rows, rows)] = turned_imag
    left[pl.ds(half, half), pl.ds(0, rows)] = turned_imag
    left[pl.ds(half, half), pl.ds(rows, rows)] = -turned_real
    mixed = matmul(left[...], dft_ref[...])
    real, imag = mixed[:half], mixed[half:]
    response_real = packed_ref[0:2].reshape(half, rows).astype(F32)
    response_imag = packed_ref[2:4].reshape(half, rows).astype(F32)
    product_real = (real * response_real - imag * response_imag).astype(BF16)
    product_imag = (real * response_imag + imag * response_real).astype(BF16)
    right[pl.ds(0, half), pl.ds(0, rows)] = product_real
    right[pl.ds(0, half), pl.ds(rows, rows)] = -product_imag
    right[pl.ds(half, half), pl.ds(0, rows)] = product_imag
    right[pl.ds(half, half), pl.ds(rows, rows)] = product_real
    mixed = matmul(right[...], dft_ref[...])
    real, imag = mixed[:half], mixed[half:]
    turned_real = (real * cos_twist - imag * sin_twist).astype(BF16)
    turned_imag = (imag * cos_twist + real * sin_twist).astype(BF16)
    both = jnp.concatenate([turned_real, turned_imag], axis=0)
    out_ref[...] = matmul(last_ref[...], both).astype(BF16)


def finish_kernel(conv_ref, skipped_ref, scale_ref, post_ref, out_ref):
    conv = conv_ref[...]
    if len(conv_ref.shape) == 3:
        order = order_of(conv_ref.shape[0], back=True)
        conv = jnp.concatenate([conv_ref[order.index(place)] for place in range(len(order))])
    turned = conv.astype(F32) + skipped_ref[...].astype(F32) * scale_ref[...]
    out_ref[...] = (post_ref[...].astype(F32) * turned.T).astype(BF16)


def call(kernel, out_shape, flops, moved, *operands, limit=VMEM_LIMIT, **options):
    return pl.pallas_call(
        kernel,
        out_shape=out_shape,
        compiler_params=pltpu.CompilerParams(vmem_limit_bytes=limit),
        cost_estimate=pl.CostEstimate(flops=flops, bytes_accessed=moved, transcendentals=0),
        **options,
    )(*operands)


def exchange(value, back=False):
    ranks = [list(order_of(lax.axis_size("seq"), back))]
    return lax.all_to_all(value, "seq", split_axis=0, concat_axis=0, tiled=True, axis_index_groups=ranks)


def swap(value, axis, apart):
    return lax.ppermute(value, axis, [(place, place ^ apart) for place in range(lax.axis_size(axis))])


def local(features, pre_gate, post_gate, norm_gain, skip_weight, spectrum):
    rows, wide = features.shape
    places = lax.axis_size("seq")
    groups = lax.axis_size("chan")
    width = wide // places
    piled = width % 16 == 0
    cells = rows * wide
    shape = jax.ShapeDtypeStruct
    vmem, anywhere = pl.BlockSpec(memory_space=pltpu.VMEM), pl.BlockSpec(memory_space=pl.ANY)
    squares, skipped, packed = call(
        prepare_kernel,
        (
            shape((1, rows), F32),
            shape((wide, rows), BF16),
            shape((places, 5, width, rows) if piled else (5, wide, rows), BF16),
        ),
        10 * cells,
        32 * cells,
        features,
        pre_gate,
        norm_gain[None, :],
        skip_weight[None, :],
        spectrum,
        limit=WHOLE_VMEM,
        in_specs=[anywhere] * 5,
        out_specs=(anywhere, anywhere, anywhere),
        scratch_shapes=[
            pltpu.VMEM(features.shape, BF16),
            pltpu.VMEM(pre_gate.shape, BF16),
            pltpu.VMEM((1, wide), F32),
            pltpu.VMEM((1, wide), F32),
            pltpu.VMEM(spectrum.shape, F32),
            pltpu.VMEM((1, rows), F32),
            pltpu.VMEM((wide, rows), BF16),
            pltpu.VMEM((5, places, width, rows) if piled else (5, wide, rows), BF16),
            pltpu.SemaphoreType.DMA((8,)),
            pltpu.SemaphoreType.DMA((7,)),
        ],
    )
    if not piled:
        packed = packed.reshape(5, places, width, rows).transpose(1, 0, 2, 3)
    gathered = exchange(packed)
    others = [swap(squares, "chan", apart) for apart in range(groups - 1, 0, -1)]
    scale = call(
        functools.partial(scale_kernel, wide * groups), shape((1, rows), F32), 8 * rows, 32 * rows, squares, *others
    )
    if piled:
        near = jnp.concatenate([scale, swap(scale, "seq", 1)])
        scales = [near] + [swap(near, "seq", steps[0]) for steps in hops(places)[1:]]
    else:
        scales = [jnp.repeat(lax.all_gather(scale, "seq", axis=0, tiled=True), width, axis=0)]
        response = gathered[:, :4].reshape(places, 2, 2, width, rows).transpose(1, 0, 2, 3, 4)
        gathered = jnp.concatenate([response.reshape(4, wide, rows), gathered[:, 4].reshape(1, wide, rows)])
    if piled:
        constants = folded_tables(places, rows, width)
        half = constants[0].shape[0] // 2
        scratch = [
            pltpu.VMEM((places, 1, rows), F32),
            pltpu.VMEM((wide, rows), BF16),
            pltpu.VMEM((8 * (half - 2 * width), rows // 4), BF16),
            pltpu.VMEM((4 * half, rows // 2), BF16),
            pltpu.VMEM((4 * half, rows // 2), BF16),
            pltpu.VMEM((2 * half, rows), BF16),
        ]
    else:
        constants = tables(places, rows, width)
        scratch = [pltpu.VMEM((4 * wide, 2 * rows), BF16)] * 2
    conv = call(
        folded_kernel if piled else convolve_kernel,
        shape((wide, rows), BF16),
        20 * cells * rows,
        20 * cells,
        gathered,
        *constants,
        *scales,
        scratch_shapes=scratch,
    )
    conv = exchange(conv.reshape(places, width, rows), back=True)
    if not piled:
        conv = conv.reshape(wide, rows)
    return call(finish_kernel, shape((rows, wide), BF16), 10 * cells, 8 * cells, conv, skipped, scale, post_gate)


def solution(mesh):
    return jax.shard_map(
        local,
        mesh=mesh,
        in_specs=(
            P("seq", "chan"),
            P("seq", "chan"),
            P("seq", "chan"),
            P("chan"),
            P("chan"),
            P(None, "seq", None, "chan"),
        ),
        out_specs=P("seq", "chan"),
        check_vma=False,
    )
```

```python
import functools

import jax
import jax.numpy as jnp
import numpy as np
from jax import lax
from jax.experimental import pallas as pl
from jax.experimental.pallas import tpu as pltpu
from jax.sharding import PartitionSpec as P

EPS = 1e-06
BF16 = jnp.bfloat16
F32 = jnp.float32
VMEM_LIMIT = 48 * 1024 * 1024
WHOLE_VMEM = 63 * 1024 * 1024 + 512 * 1024


def order_of(places, back=False):
    if places != 8:
        return tuple(range(places))
    return (5, 1, 3, 6, 2, 4, 0, 7) if back else (4, 7, 3, 6, 2, 1, 5, 0)


def reverse_bits(index, levels):
    return sum((index >> bit & 1) << levels - 1 - bit for bit in range(levels))


@functools.lru_cache(maxsize=None)
def tables(places, rows, width):
    levels = places.bit_length() - 1
    stride = 2 * places
    bins = stride * rows
    residues = np.array([2 * reverse_bits(place, levels) + parity for place in range(places) for parity in range(2)])
    angle = 2.0 * np.pi * ((residues[:, None] * np.arange(places)[None, :]) % stride) / stride
    same = np.eye(width)
    first = np.concatenate([np.kron(np.cos(angle), same), np.kron(-np.sin(angle), same)])
    last = first.T / bins
    angle = 2.0 * np.pi * ((residues[:, None] * np.arange(rows)[None, :]) % bins) / bins
    twist = np.repeat(np.stack([np.cos(angle), np.sin(angle)]), width, axis=1)
    series = np.arange(rows)
    angle = 2.0 * np.pi * ((series[:, None] * series[None, :]) % rows) / rows
    dft = np.concatenate([np.cos(angle), np.sin(angle)])
    return (
        first.astype(jnp.bfloat16),
        last.astype(jnp.bfloat16),
        twist.astype(np.float32),
        dft.astype(jnp.bfloat16),
    )


def pair_rows(places):
    levels = places.bit_length() - 1

    def holder(residue):
        return order_of(places).index(reverse_bits(residue // 2, levels)), residue % 2

    mirrors = [None if residue % places == 0 else holder(2 * places - residue) for residue in range(places + 1)]
    return [holder(residue) for residue in range(places + 1)], mirrors


@functools.lru_cache(maxsize=None)
def folded_tables(places, rows, width):
    stride = 2 * places
    bins = stride * rows
    residues = np.arange(places + 1)
    angle = 2.0 * np.pi * ((residues[:, None] * np.arange(places)[None, :]) % stride) / stride
    parts = np.stack([np.cos(angle), -np.sin(angle)], axis=1)
    first = np.kron(parts.reshape(-1, places), np.eye(width))
    last = first.T / bins
    angle = 2.0 * np.pi * ((residues[:, None] * np.arange(rows)[None, :]) % bins) / bins
    twist = np.stack([np.cos(angle), np.sin(angle)])
    block = rows // 4
    series = np.arange(block)
    angle = 2.0 * np.pi * ((np.arange(4)[:, None] * series[None, :]) % rows) / rows
    spin = np.stack([np.cos(angle), np.sin(angle)])
    angle = 2.0 * np.pi * ((series[:, None] * series[None, :]) % block) / block
    cos, sin = np.cos(angle), np.sin(angle)
    there = np.block([[cos, -sin], [sin, cos]])
    back = np.block([[cos, sin], [-sin, cos]])
    reverse = np.eye(block)[::-1]
    return (
        first.astype(jnp.bfloat16),
        last.astype(jnp.bfloat16),
        twist.astype(np.float32),
        spin.astype(np.float32),
        np.stack([there, back]).astype(jnp.bfloat16),
        reverse.astype(jnp.bfloat16),
    )


def hops(places):
    return [[apart, apart + 1] for apart in range(0, places, 2)]


def prepare_kernel(
    features_ref,
    pre_ref,
    gain_ref,
    skip_ref,
    spectrum_ref,
    squares_ref,
    skipped_ref,
    packed_ref,
    features_in,
    pre_in,
    gain_in,
    skip_in,
    spectrum_in,
    squares_out,
    skipped_out,
    packed_out,
    in_sems,
    out_sems,
):
    blocks = [(part, parity) for part in range(2) for parity in range(2)]
    pairs = [(features_ref, features_in), (pre_ref, pre_in), (gain_ref, gain_in), (skip_ref, skip_in)]
    pairs += [(spectrum_ref.at[block], spectrum_in.at[block]) for block in blocks]
    arriving = [pltpu.make_async_copy(*pair, in_sems.at[slot]) for slot, pair in enumerate(pairs)]
    for copy in arriving:
        copy.start()
    leaving = []

    def leave(source, target):
        copy = pltpu.make_async_copy(source, target, out_sems.at[len(leaving)])
        copy.start()
        leaving.append(copy)

    def pack(slot, turned):
        if len(packed_ref.shape) == 4:
            places, width = packed_out.shape[1:3]
            for rank, place in enumerate(order_of(places)):
                packed_out[slot, rank] = turned[place * width : (place + 1) * width]
            leave(packed_out.at[slot], packed_ref.at[:, slot])
        else:
            packed_out[slot] = turned
            leave(packed_out.at[slot], packed_ref.at[slot])

    for copy in arriving[:4]:
        copy.wait()
    features = features_in[...].astype(F32)
    scaled = features * gain_in[...] * pre_in[...].astype(F32)
    pack(4, scaled.astype(BF16).T)
    skipped_out[...] = (scaled * skip_in[...]).astype(BF16).T
    leave(skipped_out, skipped_ref)
    turned = features_in[...].T.astype(F32)
    squares_out[...] = jnp.sum(turned * turned, axis=0, keepdims=True)
    leave(squares_out, squares_ref)
    for slot, block in enumerate(blocks):
        arriving[4 + slot].wait()
        if len(packed_ref.shape) == 4:
            quarter = spectrum_in.shape[2] // 4
            rows = [spectrum_in[(*block, pl.ds(turn, quarter, stride=4), slice(None))] for turn in range(4)]
            pack(slot, jnp.concatenate([row.astype(BF16).T for row in rows], axis=1))
        else:
            pack(slot, spectrum_in[block].astype(BF16).T)
    for copy in leaving:
        copy.wait()


def scale_kernel(channels, *refs):
    square_refs, scale_ref = refs[:-1], refs[-1]
    total = square_refs[0][...]
    for square_ref in square_refs[1:]:
        total = total + square_ref[...]
    scale_ref[...] = lax.rsqrt(total / channels + EPS)


def matmul(left, right):
    return jnp.dot(left, right, preferred_element_type=F32)


def butterfly(values, direction):
    (real0, imag0), (real1, imag1), (real2, imag2), (real3, imag3) = values
    even, odd = (real0 + real2, imag0 + imag2), (real1 + real3, imag1 + imag3)
    even_gap, odd_gap = (real0 - real2, imag0 - imag2), (real1 - real3, imag1 - imag3)
    lower = (even_gap[0] + odd_gap[1], even_gap[1] - odd_gap[0])
    upper = (even_gap[0] - odd_gap[1], even_gap[1] + odd_gap[0])
    total, gap = (even[0] + odd[0], even[1] + odd[1]), (even[0] - odd[0], even[1] - odd[1])
    return [total, lower, gap, upper] if direction > 0 else [total, upper, gap, lower]


def folded_kernel(packed_ref, first_ref, last_ref, twist_ref, spin_ref, dft_ref, reverse_ref, *refs):
    scale_refs, (out_ref, scales, signal, mirror, forward, backward, both) = refs[:-7], refs[-7:]
    wide, rows = out_ref.shape
    places, width = scales.shape[0], wide // scales.shape[0]
    block, inner = rows // 4, mirror.shape[0] // 8
    order = order_of(places)
    direct, mirrors = pair_rows(places)
    quarters = [pl.ds(turn * block, block) for turn in range(4)]
    groups = [range(begin, min(begin + 5, places + 1)) for begin in range(0, places + 1, 5)]
    for row, holder in enumerate(mirrors[1:places]):
        for part in range(2):
            for turn in range(4):
                at = pl.ds((part * 4 + 3 - turn) * inner + row * width, width)
                mirror[at, :] = packed_ref[holder[0], 2 * part + holder[1], :, quarters[turn]]
    reversed_bins = matmul(mirror[...], reverse_ref[...])
    place = lax.axis_index("seq")
    for scale_ref, steps in zip(scale_refs, hops(places)):
        for at, step in enumerate(steps):
            scales[place ^ step] = scale_ref[pl.ds(at, 1), :]
    for rank, at in enumerate(order):
        signal[pl.ds(at * width, width), :] = (packed_ref[rank, 4].astype(F32) * scales[at]).astype(BF16)
    spectral = []
    for group in groups:
        begin = group[0] * width
        mixed = matmul(first_ref[pl.ds(2 * begin, 2 * len(group) * width), :], signal[...])
        for at, residue in enumerate(group):
            over, under = mixed[2 * at * width : (2 * at + 1) * width], mixed[(2 * at + 1) * width : (2 * at + 2) * width]
            values = []
            for turn in range(4):
                real, imag = (part[:, turn * block : (turn + 1) * block] for part in (over, under))
                cos, sin = (twist_ref[part, pl.ds(residue, 1), quarters[turn]] for part in range(2))
                values.append((real * cos + imag * sin, imag * cos - real * sin))
            for turn, (real, imag) in enumerate(butterfly(values, 1)):
                if turn > 0:
                    cos, sin = spin_ref[0, pl.ds(turn, 1), :], spin_ref[1, pl.ds(turn, 1), :]
                    real, imag = real * cos + imag * sin, imag * cos - real * sin
                row = pl.ds(4 * begin + (turn * len(group) + at) * width, width)
                forward[row, pl.ds(0, block)] = real.astype(BF16)
                forward[row, pl.ds(block, block)] = imag.astype(BF16)
        spectral.append(matmul(forward[pl.ds(4 * begin, 4 * len(group) * width), :], dft_ref[0]))
    restored = []
    for group, values in zip(groups, spectral):
        begin = group[0] * width
        for turn in range(4):
            for at, residue in enumerate(group):
                row = (turn * len(group) + at) * width
                real, imag = values[row : row + width, :block], values[row : row + width, block:]
                holder = direct[residue]
                response_real = packed_ref[holder[0], holder[1], :, quarters[turn]].astype(F32)
                response_imag = packed_ref[holder[0], 2 + holder[1], :, quarters[turn]].astype(F32)
                if mirrors[residue] is not None:
                    other = turn * inner + (residue - 1) * width
                    response_real = response_real + reversed_bins[other : other + width]
                    other = other + 4 * inner
                    response_imag = response_imag - reversed_bins[other : other + width]
                target = pl.ds(4 * begin + row, width)
                backward[target, pl.ds(0, block)] = (real * response_real - imag * response_imag).astype(BF16)
                backward[target, pl.ds(block, block)] = (real * response_imag + imag * response_real).astype(BF16)
        restored.append(matmul(backward[pl.ds(4 * begin, 4 * len(group) * width), :], dft_ref[1]))
    for group, turned in zip(groups, restored):
        for at, residue in enumerate(group):
            values = []
            for turn in range(4):
                row = (turn * len(group) + at) * width
                real, imag = turned[row : row + width, :block], turned[row : row + width, block:]
                if turn > 0:
                    cos, sin = spin_ref[0, pl.ds(turn, 1), :], spin_ref[1, pl.ds(turn, 1), :]
                    real, imag = real * cos - imag * sin, imag * cos + real * sin
                values.append((real, imag))
            for lanes, (real, imag) in zip(quarters, butterfly(values, -1)):
                cos, sin = twist_ref[0, pl.ds(residue, 1), lanes], twist_ref[1, pl.ds(residue, 1), lanes]
                both[pl.ds(2 * residue * width, width), lanes] = (real * cos - imag * sin).astype(BF16)
                both[pl.ds((2 * residue + 1) * width, width), lanes] = (imag * cos + real * sin).astype(BF16)
    result = matmul(last_ref[...], both[...]).astype(BF16)
    for rank, at in enumerate(order_of(places, back=True)):
        out_ref[pl.ds(rank * width, width), :] = result[at * width : (at + 1) * width]


def convolve_kernel(packed_ref, first_ref, last_ref, twist_ref, dft_ref, scale_ref, out_ref, left, right):
    wide, rows = out_ref.shape
    half = 2 * wide
    signal = (packed_ref[4].astype(F32) * scale_ref[...]).astype(BF16)
    mixed = matmul(first_ref[...], signal)
    real, imag = mixed[:half], mixed[half:]
    cos_twist, sin_twist = twist_ref[0], twist_ref[1]
    turned_real = (real * cos_twist + imag * sin_twist).astype(BF16)
    turned_imag = (imag * cos_twist - real * sin_twist).astype(BF16)
    left[pl.ds(0, half), pl.ds(0, rows)] = turned_real
    left[pl.ds(0, half), pl.ds(rows, rows)] = turned_imag
    left[pl.ds(half, half), pl.ds(0, rows)] = turned_imag
    left[pl.ds(half, half), pl.ds(rows, rows)] = -turned_real
    mixed = matmul(left[...], dft_ref[...])
    real, imag = mixed[:half], mixed[half:]
    response_real = packed_ref[0:2].reshape(half, rows).astype(F32)
    response_imag = packed_ref[2:4].reshape(half, rows).astype(F32)
    product_real = (real * response_real - imag * response_imag).astype(BF16)
    product_imag = (real * response_imag + imag * response_real).astype(BF16)
    right[pl.ds(0, half), pl.ds(0, rows)] = product_real
    right[pl.ds(0, half), pl.ds(rows, rows)] = -product_imag
    right[pl.ds(half, half), pl.ds(0, rows)] = product_imag
    right[pl.ds(half, half), pl.ds(rows, rows)] = product_real
    mixed = matmul(right[...], dft_ref[...])
    real, imag = mixed[:half], mixed[half:]
    turned_real = (real * cos_twist - imag * sin_twist).astype(BF16)
    turned_imag = (imag * cos_twist + real * sin_twist).astype(BF16)
    both = jnp.concatenate([turned_real, turned_imag], axis=0)
    out_ref[...] = matmul(last_ref[...], both).astype(BF16)


def finish_kernel(conv_ref, skipped_ref, scale_ref, post_ref, out_ref):
    conv = conv_ref[...]
    if len(conv_ref.shape) == 3:
        order = order_of(conv_ref.shape[0], back=True)
        conv = jnp.concatenate([conv_ref[order.index(place)] for place in range(len(order))])
    turned = conv.astype(F32) + skipped_ref[...].astype(F32) * scale_ref[...]
    out_ref[...] = (post_ref[...].astype(F32) * turned.T).astype(BF16)


def call(kernel, out_shape, flops, moved, *operands, limit=VMEM_LIMIT, **options):
    return pl.pallas_call(
        kernel,
        out_shape=out_shape,
        compiler_params=pltpu.CompilerParams(vmem_limit_bytes=limit),
        cost_estimate=pl.CostEstimate(flops=flops, bytes_accessed=moved, transcendentals=0),
        **options,
    )(*operands)


def exchange(value, back=False):
    ranks = [list(order_of(lax.axis_size("seq"), back))]
    return lax.all_to_all(value, "seq", split_axis=0, concat_axis=0, tiled=True, axis_index_groups=ranks)


def swap(value, axis, apart):
    return lax.ppermute(value, axis, [(place, place ^ apart) for place in range(lax.axis_size(axis))])


def local(features, pre_gate, post_gate, norm_gain, skip_weight, spectrum):
    rows, wide = features.shape
    places = lax.axis_size("seq")
    groups = lax.axis_size("chan")
    width = wide // places
    piled = width % 16 == 0
    cells = rows * wide
    shape = jax.ShapeDtypeStruct
    vmem, anywhere = pl.BlockSpec(memory_space=pltpu.VMEM), pl.BlockSpec(memory_space=pl.ANY)
    squares, skipped, packed = call(
        prepare_kernel,
        (
            shape((1, rows), F32),
            shape((wide, rows), BF16),
            shape((places, 5, width, rows) if piled else (5, wide, rows), BF16),
        ),
        10 * cells,
        32 * cells,
        features,
        pre_gate,
        norm_gain[None, :],
        skip_weight[None, :],
        spectrum,
        limit=WHOLE_VMEM,
        in_specs=[anywhere] * 5,
        out_specs=(anywhere, anywhere, anywhere),
        scratch_shapes=[
            pltpu.VMEM(features.shape, BF16),
            pltpu.VMEM(pre_gate.shape, BF16),
            pltpu.VMEM((1, wide), F32),
            pltpu.VMEM((1, wide), F32),
            pltpu.VMEM(spectrum.shape, F32),
            pltpu.VMEM((1, rows), F32),
            pltpu.VMEM((wide, rows), BF16),
            pltpu.VMEM((5, places, width, rows) if piled else (5, wide, rows), BF16),
            pltpu.SemaphoreType.DMA((8,)),
            pltpu.SemaphoreType.DMA((7,)),
        ],
    )
    if not piled:
        packed = packed.reshape(5, places, width, rows).transpose(1, 0, 2, 3)
    gathered = exchange(packed)
    others = [swap(squares, "chan", apart) for apart in range(1, groups)]
    scale = call(
        functools.partial(scale_kernel, wide * groups), shape((1, rows), F32), 8 * rows, 32 * rows, squares, *others
    )
    if piled:
        near = jnp.concatenate([scale, swap(scale, "seq", 1)])
        scales = [near] + [swap(near, "seq", steps[0]) for steps in hops(places)[1:]]
    else:
        scales = [jnp.repeat(lax.all_gather(scale, "seq", axis=0, tiled=True), width, axis=0)]
        response = gathered[:, :4].reshape(places, 2, 2, width, rows).transpose(1, 0, 2, 3, 4)
        gathered = jnp.concatenate([response.reshape(4, wide, rows), gathered[:, 4].reshape(1, wide, rows)])
    if piled:
        constants = folded_tables(places, rows, width)
        half = constants[0].shape[0] // 2
        scratch = [
            pltpu.VMEM((places, 1, rows), F32),
            pltpu.VMEM((wide, rows), BF16),
            pltpu.VMEM((8 * (half - 2 * width), rows // 4), BF16),
            pltpu.VMEM((4 * half, rows // 2), BF16),
            pltpu.VMEM((4 * half, rows // 2), BF16),
            pltpu.VMEM((2 * half, rows), BF16),
        ]
    else:
        constants = tables(places, rows, width)
        scratch = [pltpu.VMEM((4 * wide, 2 * rows), BF16)] * 2
    conv = call(
        folded_kernel if piled else convolve_kernel,
        shape((wide, rows), BF16),
        20 * cells * rows,
        20 * cells,
        gathered,
        *constants,
        *scales,
        scratch_shapes=scratch,
    )
    conv = exchange(conv.reshape(places, width, rows), back=True)
    if not piled:
        conv = conv.reshape(wide, rows)
    return call(finish_kernel, shape((rows, wide), BF16), 10 * cells, 8 * cells, conv, skipped, scale, post_gate)


def solution(mesh):
    return jax.shard_map(
        local,
        mesh=mesh,
        in_specs=(
            P("seq", "chan"),
            P("seq", "chan"),
            P("seq", "chan"),
            P("chan"),
            P("chan"),
            P(None, "seq", None, "chan"),
        ),
        out_specs=P("seq", "chan"),
        check_vma=False,
    )
```

```python
import functools

import jax
import jax.numpy as jnp
import numpy as np
from jax import lax
from jax.experimental import pallas as pl
from jax.experimental.pallas import tpu as pltpu
from jax.sharding import PartitionSpec as P

EPS = 1e-06
BF16 = jnp.bfloat16
F32 = jnp.float32
VMEM_LIMIT = 48 * 1024 * 1024
WHOLE_VMEM = 63 * 1024 * 1024 + 512 * 1024


def order_of(places, back=False):
    if places != 8:
        return tuple(range(places))
    return (5, 1, 3, 6, 2, 4, 0, 7) if back else (4, 7, 3, 6, 2, 1, 5, 0)


def reverse_bits(index, levels):
    return sum((index >> bit & 1) << levels - 1 - bit for bit in range(levels))


@functools.lru_cache(maxsize=None)
def tables(places, rows, width):
    levels = places.bit_length() - 1
    stride = 2 * places
    bins = stride * rows
    residues = np.array([2 * reverse_bits(place, levels) + parity for place in range(places) for parity in range(2)])
    angle = 2.0 * np.pi * ((residues[:, None] * np.arange(places)[None, :]) % stride) / stride
    same = np.eye(width)
    first = np.concatenate([np.kron(np.cos(angle), same), np.kron(-np.sin(angle), same)])
    last = first.T / bins
    angle = 2.0 * np.pi * ((residues[:, None] * np.arange(rows)[None, :]) % bins) / bins
    twist = np.repeat(np.stack([np.cos(angle), np.sin(angle)]), width, axis=1)
    series = np.arange(rows)
    angle = 2.0 * np.pi * ((series[:, None] * series[None, :]) % rows) / rows
    dft = np.concatenate([np.cos(angle), np.sin(angle)])
    return (
        first.astype(jnp.bfloat16),
        last.astype(jnp.bfloat16),
        twist.astype(np.float32),
        dft.astype(jnp.bfloat16),
    )


def pair_rows(places):
    levels = places.bit_length() - 1

    def holder(residue):
        return order_of(places).index(reverse_bits(residue // 2, levels)), residue % 2

    mirrors = [None if residue % places == 0 else holder(2 * places - residue) for residue in range(places + 1)]
    return [holder(residue) for residue in range(places + 1)], mirrors


@functools.lru_cache(maxsize=None)
def folded_tables(places, rows, width):
    stride = 2 * places
    bins = stride * rows
    residues = np.arange(places + 1)
    angle = 2.0 * np.pi * ((residues[:, None] * np.arange(places)[None, :]) % stride) / stride
    parts = np.stack([np.cos(angle), -np.sin(angle)], axis=1)
    first = np.kron(parts.reshape(-1, places), np.eye(width))
    last = first.T / bins
    angle = 2.0 * np.pi * ((residues[:, None] * np.arange(rows)[None, :]) % bins) / bins
    twist = np.stack([np.cos(angle), np.sin(angle)])
    block = rows // 4
    series = np.arange(block)
    angle = 2.0 * np.pi * ((np.arange(4)[:, None] * series[None, :]) % rows) / rows
    spin = np.stack([np.cos(angle), np.sin(angle)])
    angle = 2.0 * np.pi * ((series[:, None] * series[None, :]) % block) / block
    cos, sin = np.cos(angle), np.sin(angle)
    there = np.block([[cos, -sin], [sin, cos]])
    back = np.block([[cos, sin], [-sin, cos]])
    reverse = np.eye(block)[::-1]
    return (
        first.astype(jnp.bfloat16),
        last.astype(jnp.bfloat16),
        twist.astype(np.float32),
        spin.astype(np.float32),
        np.stack([there, back]).astype(jnp.bfloat16),
        reverse.astype(jnp.bfloat16),
    )


def hops(places):
    return [[apart, apart + 1] for apart in range(0, places, 2)]


def prepare_kernel(
    features_ref,
    pre_ref,
    gain_ref,
    skip_ref,
    spectrum_ref,
    squares_ref,
    skipped_ref,
    packed_ref,
    features_in,
    pre_in,
    gain_in,
    skip_in,
    spectrum_in,
    squares_out,
    skipped_out,
    packed_out,
    in_sems,
    out_sems,
):
    blocks = [(part, parity) for part in range(2) for parity in range(2)]
    pairs = [(features_ref, features_in), (pre_ref, pre_in), (gain_ref, gain_in), (skip_ref, skip_in)]
    pairs += [(spectrum_ref.at[block], spectrum_in.at[block]) for block in blocks]
    arriving = [pltpu.make_async_copy(*pair, in_sems.at[slot]) for slot, pair in enumerate(pairs)]
    for copy in arriving:
        copy.start()
    leaving = []

    def leave(source, target):
        copy = pltpu.make_async_copy(source, target, out_sems.at[len(leaving)])
        copy.start()
        leaving.append(copy)

    def pack(slot, turned):
        if len(packed_ref.shape) == 4:
            places, width = packed_out.shape[1:3]
            for rank, place in enumerate(order_of(places)):
                packed_out[slot, rank] = turned[place * width : (place + 1) * width]
            leave(packed_out.at[slot], packed_ref.at[:, slot])
        else:
            packed_out[slot] = turned
            leave(packed_out.at[slot], packed_ref.at[slot])

    for copy in arriving[:4]:
        copy.wait()
    features = features_in[...].astype(F32)
    scaled = features * gain_in[...] * pre_in[...].astype(F32)
    pack(4, scaled.astype(BF16).T)
    skipped_out[...] = (scaled * skip_in[...]).astype(BF16).T
    leave(skipped_out, skipped_ref)
    turned = features_in[...].T.astype(F32)
    squares_out[...] = jnp.sum(turned * turned, axis=0, keepdims=True)
    leave(squares_out, squares_ref)
    for slot, block in enumerate(blocks):
        arriving[4 + slot].wait()
        if len(packed_ref.shape) == 4:
            quarter = spectrum_in.shape[2] // 4
            rows = [spectrum_in[(*block, pl.ds(turn, quarter, stride=4), slice(None))] for turn in range(4)]
            pack(slot, jnp.concatenate([row.astype(BF16).T for row in rows], axis=1))
        else:
            pack(slot, spectrum_in[block].astype(BF16).T)
    for copy in leaving:
        copy.wait()


def scale_kernel(channels, *refs):
    square_refs, scale_ref = refs[:-1], refs[-1]
    total = square_refs[0][...]
    for square_ref in square_refs[1:]:
        total = total + square_ref[...]
    scale_ref[...] = lax.rsqrt(total / channels + EPS)


def matmul(left, right):
    return jnp.dot(left, right, preferred_element_type=F32)


def butterfly(values, direction):
    (real0, imag0), (real1, imag1), (real2, imag2), (real3, imag3) = values
    even, odd = (real0 + real2, imag0 + imag2), (real1 + real3, imag1 + imag3)
    even_gap, odd_gap = (real0 - real2, imag0 - imag2), (real1 - real3, imag1 - imag3)
    lower = (even_gap[0] + odd_gap[1], even_gap[1] - odd_gap[0])
    upper = (even_gap[0] - odd_gap[1], even_gap[1] + odd_gap[0])
    total, gap = (even[0] + odd[0], even[1] + odd[1]), (even[0] - odd[0], even[1] - odd[1])
    return [total, lower, gap, upper] if direction > 0 else [total, upper, gap, lower]


def folded_kernel(packed_ref, first_ref, last_ref, twist_ref, spin_ref, dft_ref, reverse_ref, *refs):
    scale_refs, (out_ref, scales, signal, mirror, forward, backward, both) = refs[:-7], refs[-7:]
    wide, rows = out_ref.shape
    places, width = scales.shape[0], wide // scales.shape[0]
    block, inner = rows // 4, mirror.shape[0] // 8
    order = order_of(places)
    direct, mirrors = pair_rows(places)
    quarters = [pl.ds(turn * block, block) for turn in range(4)]
    groups = [range(begin, min(begin + 5, places + 1)) for begin in range(0, places + 1, 5)]
    for row, holder in enumerate(mirrors[1:places]):
        for part in range(2):
            for turn in range(4):
                at = pl.ds((part * 4 + 3 - turn) * inner + row * width, width)
                mirror[at, :] = packed_ref[holder[0], 2 * part + holder[1], :, quarters[turn]]
    reversed_bins = matmul(mirror[...], reverse_ref[...])
    place = lax.axis_index("seq")
    for scale_ref, steps in zip(scale_refs, hops(places)):
        for at, step in enumerate(steps):
            scales[place ^ step] = scale_ref[pl.ds(at, 1), :]
    for rank, at in enumerate(order):
        signal[pl.ds(at * width, width), :] = (packed_ref[rank, 4].astype(F32) * scales[at]).astype(BF16)
    spectral = []
    for group in groups:
        begin = group[0] * width
        mixed = matmul(first_ref[pl.ds(2 * begin, 2 * len(group) * width), :], signal[...])
        for at, residue in enumerate(group):
            over, under = mixed[2 * at * width : (2 * at + 1) * width], mixed[(2 * at + 1) * width : (2 * at + 2) * width]
            values = []
            for turn in range(4):
                real, imag = (part[:, turn * block : (turn + 1) * block] for part in (over, under))
                cos, sin = (twist_ref[part, pl.ds(residue, 1), quarters[turn]] for part in range(2))
                values.append((real * cos + imag * sin, imag * cos - real * sin))
            for turn, (real, imag) in enumerate(butterfly(values, 1)):
                if turn > 0:
                    cos, sin = spin_ref[0, pl.ds(turn, 1), :], spin_ref[1, pl.ds(turn, 1), :]
                    real, imag = real * cos + imag * sin, imag * cos - real * sin
                row = pl.ds(4 * begin + (turn * len(group) + at) * width, width)
                forward[row, pl.ds(0, block)] = real.astype(BF16)
                forward[row, pl.ds(block, block)] = imag.astype(BF16)
        spectral.append(matmul(forward[pl.ds(4 * begin, 4 * len(group) * width), :], dft_ref[0]))
    restored = []
    for group, values in zip(groups, spectral):
        begin = group[0] * width
        for turn in range(4):
            for at, residue in enumerate(group):
                row = (turn * len(group) + at) * width
                real, imag = values[row : row + width, :block], values[row : row + width, block:]
                holder = direct[residue]
                response_real = packed_ref[holder[0], holder[1], :, quarters[turn]].astype(F32)
                response_imag = packed_ref[holder[0], 2 + holder[1], :, quarters[turn]].astype(F32)
                if mirrors[residue] is not None:
                    other = turn * inner + (residue - 1) * width
                    response_real = response_real + reversed_bins[other : other + width]
                    other = other + 4 * inner
                    response_imag = response_imag - reversed_bins[other : other + width]
                target = pl.ds(4 * begin + row, width)
                backward[target, pl.ds(0, block)] = (real * response_real - imag * response_imag).astype(BF16)
                backward[target, pl.ds(block, block)] = (real * response_imag + imag * response_real).astype(BF16)
        restored.append(matmul(backward[pl.ds(4 * begin, 4 * len(group) * width), :], dft_ref[1]))
    for group, turned in zip(groups, restored):
        for at, residue in enumerate(group):
            values = []
            for turn in range(4):
                row = (turn * len(group) + at) * width
                real, imag = turned[row : row + width, :block], turned[row : row + width, block:]
                if turn > 0:
                    cos, sin = spin_ref[0, pl.ds(turn, 1), :], spin_ref[1, pl.ds(turn, 1), :]
                    real, imag = real * cos - imag * sin, imag * cos + real * sin
                values.append((real, imag))
            for lanes, (real, imag) in zip(quarters, butterfly(values, -1)):
                cos, sin = twist_ref[0, pl.ds(residue, 1), lanes], twist_ref[1, pl.ds(residue, 1), lanes]
                both[pl.ds(2 * residue * width, width), lanes] = (real * cos - imag * sin).astype(BF16)
                both[pl.ds((2 * residue + 1) * width, width), lanes] = (imag * cos + real * sin).astype(BF16)
    result = matmul(last_ref[...], both[...]).astype(BF16)
    for rank, at in enumerate(order_of(places, back=True)):
        out_ref[pl.ds(rank * width, width), :] = result[at * width : (at + 1) * width]


def convolve_kernel(packed_ref, first_ref, last_ref, twist_ref, dft_ref, scale_ref, out_ref, left, right):
    wide, rows = out_ref.shape
    half = 2 * wide
    signal = (packed_ref[4].astype(F32) * scale_ref[...]).astype(BF16)
    mixed = matmul(first_ref[...], signal)
    real, imag = mixed[:half], mixed[half:]
    cos_twist, sin_twist = twist_ref[0], twist_ref[1]
    turned_real = (real * cos_twist + imag * sin_twist).astype(BF16)
    turned_imag = (imag * cos_twist - real * sin_twist).astype(BF16)
    left[pl.ds(0, half), pl.ds(0, rows)] = turned_real
    left[pl.ds(0, half), pl.ds(rows, rows)] = turned_imag
    left[pl.ds(half, half), pl.ds(0, rows)] = turned_imag
    left[pl.ds(half, half), pl.ds(rows, rows)] = -turned_real
    mixed = matmul(left[...], dft_ref[...])
    real, imag = mixed[:half], mixed[half:]
    response_real = packed_ref[0:2].reshape(half, rows).astype(F32)
    response_imag = packed_ref[2:4].reshape(half, rows).astype(F32)
    product_real = (real * response_real - imag * response_imag).astype(BF16)
    product_imag = (real * response_imag + imag * response_real).astype(BF16)
    right[pl.ds(0, half), pl.ds(0, rows)] = product_real
    right[pl.ds(0, half), pl.ds(rows, rows)] = -product_imag
    right[pl.ds(half, half), pl.ds(0, rows)] = product_imag
    right[pl.ds(half, half), pl.ds(rows, rows)] = product_real
    mixed = matmul(right[...], dft_ref[...])
    real, imag = mixed[:half], mixed[half:]
    turned_real = (real * cos_twist - imag * sin_twist).astype(BF16)
    turned_imag = (imag * cos_twist + real * sin_twist).astype(BF16)
    both = jnp.concatenate([turned_real, turned_imag], axis=0)
    out_ref[...] = matmul(last_ref[...], both).astype(BF16)


def finish_kernel(conv_ref, skipped_ref, scale_ref, post_ref, out_ref):
    conv = conv_ref[...]
    if len(conv_ref.shape) == 3:
        order = order_of(conv_ref.shape[0], back=True)
        conv = jnp.concatenate([conv_ref[order.index(place)] for place in range(len(order))])
    turned = conv.astype(F32) + skipped_ref[...].astype(F32) * scale_ref[...]
    out_ref[...] = (post_ref[...].astype(F32) * turned.T).astype(BF16)


def call(kernel, out_shape, flops, moved, *operands, limit=VMEM_LIMIT, **options):
    return pl.pallas_call(
        kernel,
        out_shape=out_shape,
        compiler_params=pltpu.CompilerParams(vmem_limit_bytes=limit),
        cost_estimate=pl.CostEstimate(flops=flops, bytes_accessed=moved, transcendentals=0),
        **options,
    )(*operands)


def exchange(value, back=False):
    ranks = [list(order_of(lax.axis_size("seq"), back))]
    return lax.all_to_all(value, "seq", split_axis=0, concat_axis=0, tiled=True, axis_index_groups=ranks)


def swap(value, axis, apart):
    return lax.ppermute(value, axis, [(place, place ^ apart) for place in range(lax.axis_size(axis))])


def local(features, pre_gate, post_gate, norm_gain, skip_weight, spectrum):
    rows, wide = features.shape
    places = lax.axis_size("seq")
    groups = lax.axis_size("chan")
    width = wide // places
    piled = width % 16 == 0
    cells = rows * wide
    shape = jax.ShapeDtypeStruct
    vmem, anywhere = pl.BlockSpec(memory_space=pltpu.VMEM), pl.BlockSpec(memory_space=pl.ANY)
    squares, skipped, packed = call(
        prepare_kernel,
        (
            shape((1, rows), F32),
            shape((wide, rows), BF16),
            shape((places, 5, width, rows) if piled else (5, wide, rows), BF16),
        ),
        10 * cells,
        32 * cells,
        features,
        pre_gate,
        norm_gain[None, :],
        skip_weight[None, :],
        spectrum,
        limit=WHOLE_VMEM,
        in_specs=[anywhere] * 5,
        out_specs=(anywhere, anywhere, anywhere),
        scratch_shapes=[
            pltpu.VMEM(features.shape, BF16),
            pltpu.VMEM(pre_gate.shape, BF16),
            pltpu.VMEM((1, wide), F32),
            pltpu.VMEM((1, wide), F32),
            pltpu.VMEM(spectrum.shape, F32),
            pltpu.VMEM((1, rows), F32),
            pltpu.VMEM((wide, rows), BF16),
            pltpu.VMEM((5, places, width, rows) if piled else (5, wide, rows), BF16),
            pltpu.SemaphoreType.DMA((8,)),
            pltpu.SemaphoreType.DMA((7,)),
        ],
    )
    if not piled:
        packed = packed.reshape(5, places, width, rows).transpose(1, 0, 2, 3)
    gathered = exchange(packed)
    others = [swap(squares, "chan", apart) for apart in range(groups - 1, 0, -1)]
    scale = call(
        functools.partial(scale_kernel, wide * groups), shape((1, rows), F32), 8 * rows, 32 * rows, squares, *others
    )
    if piled:
        near = jnp.concatenate([scale, swap(scale, "seq", 1)])
        scales = [near] + [swap(near, "seq", steps[0]) for steps in hops(places)[1:]]
    else:
        scales = [jnp.repeat(lax.all_gather(scale, "seq", axis=0, tiled=True), width, axis=0)]
        response = gathered[:, :4].reshape(places, 2, 2, width, rows).transpose(1, 0, 2, 3, 4)
        gathered = jnp.concatenate([response.reshape(4, wide, rows), gathered[:, 4].reshape(1, wide, rows)])
    if piled:
        constants = folded_tables(places, rows, width)
        half = constants[0].shape[0] // 2
        scratch = [
            pltpu.VMEM((places, 1, rows), F32),
            pltpu.VMEM((wide, rows), BF16),
            pltpu.VMEM((8 * (half - 2 * width), rows // 4), BF16),
            pltpu.VMEM((4 * half, rows // 2), BF16),
            pltpu.VMEM((4 * half, rows // 2), BF16),
            pltpu.VMEM((2 * half, rows), BF16),
        ]
    else:
        constants = tables(places, rows, width)
        scratch = [pltpu.VMEM((4 * wide, 2 * rows), BF16)] * 2
    conv = call(
        folded_kernel if piled else convolve_kernel,
        shape((wide, rows), BF16),
        20 * cells * rows,
        20 * cells,
        gathered,
        *constants,
        *scales,
        scratch_shapes=scratch,
    )
    conv = exchange(conv.reshape(places, width, rows), back=True)
    if not piled:
        conv = conv.reshape(wide, rows)
    return call(finish_kernel, shape((rows, wide), BF16), 10 * cells, 8 * cells, conv, skipped, scale, post_gate)


def solution(mesh):
    return jax.shard_map(
        local,
        mesh=mesh,
        in_specs=(
            P("seq", "chan"),
            P("seq", "chan"),
            P("seq", "chan"),
            P("chan"),
            P("chan"),
            P(None, "seq", None, "chan"),
        ),
        out_specs=P("seq", "chan"),
        check_vma=False,
    )
```
